32 devices in a mesh: fs: 8 (over y, x, core), sp: 4 (over z).
Axes of the slice: x: 2, y: 2, z: 4, core: 2. Of those that a mesh axis runs over, the one named last changes fastest.
Arguments:
- hidden: bfloat16 [6, 4096, 1536], P(None, ('fs', 'sp')), may hold values from -6 to 6
- norm_gain: bfloat16 [1536], P('fs'), may hold values from 0.5 to 1.5
- w_z: bfloat16 [1536, 3072], P('fs'), may hold values from -0.15625 to 0.15625
- w_x: bfloat16 [1536, 3072], P('fs'), may hold values from -0.15625 to 0.15625
- w_bc: bfloat16 [1536, 256], P('fs'), may hold values from -0.15625 to 0.15625
- w_dt: bfloat16 [1536, 48], P('fs'), may hold values from -0.15625 to 0.15625
- w_out: bfloat16 [1536, 3072], P('fs'), may hold values from -0.109375 to 0.109375
- conv_x: bfloat16 [3072, 4], P('fs'), may hold values from -3 to 3
- conv_x_bias: bfloat16 [3072], P('fs'), may hold values from -0.5 to 0.5
- conv_bc: bfloat16 [256, 4], P('fs'), may hold values from -3 to 3
- conv_bc_bias: bfloat16 [256], P('fs'), may hold values from -0.5 to 0.5
- dt_bias: bfloat16 [48], P('fs'), may hold values from -7 to -2.296875
- a_log: bfloat16 [48], P('fs'), may hold values from -2.6875 to -1.59375
- skip_d: bfloat16 [48], P('fs'), may hold values from 0.5 to 4
- gate_gain: bfloat16 [3072], P('fs'), may hold values from 0.5 to 1.5
- cotangent: bfloat16 [6, 4096, 1536], P(None, ('fs', 'sp')), may hold values from -6 to 6
Outputs:
- output: bfloat16 [6, 4096, 1536], P(None, ('fs', 'sp'))
- grad_hidden: float32 [6, 4096, 1536], P(None, ('fs', 'sp'))
- grad_norm_gain: float32 [1536], P('fs')
- grad_w_z: float32 [1536, 3072], P('fs')
- grad_w_x: float32 [1536, 3072], P('fs')
- grad_w_bc: float32 [1536, 256], P('fs')
- grad_w_dt: float32 [1536, 48], P('fs')
- grad_w_out: float32 [1536, 3072], P('fs')
- grad_conv_x: float32 [3072, 4], P('fs')
- grad_conv_x_bias: float32 [3072], P('fs')
- grad_conv_bc: float32 [256, 4], P('fs')
- grad_conv_bc_bias: float32 [256], P('fs')
- grad_dt_bias: float32 [48], P('fs')
- grad_a_log: float32 [48], P('fs')
- grad_skip_d: float32 [48], P('fs')
- grad_gate_gain: float32 [3072], P('fs')
The draws below stay inside these ranges and needn't reach their ends.
All inputs are finite; a program needn't handle non-finite values.
Results may differ from the reference program's by a relative error of at most 0.035.
Values may be sent and summed in bfloat16 or wider, within the bound.
A program may use at most 384 MiB of HBM per device.

```python
import jax
import jax.numpy as jnp
from jax import lax

D = 1536
HEADS = 48
HEAD_SIZE = 64
STATE = 128
CONV = 4
SPAN = 256
SEQS = 6
INNER = 3072
LEN = 4096


def block_scale(key, dims, cuts, low, high):
    level, own = 1.0, jax.random.fold_in(key, 6)
    for dim, shards_of in cuts:
        draws = jnp.exp(jax.random.uniform(jax.random.fold_in(own, dim), (shards_of,), jnp.float32, low / len(cuts), high / len(cuts)))
        level = level * jnp.repeat(draws, dims[dim] // shards_of).reshape([-1 if axis == dim else 1 for axis in range(len(dims))])
    return level


def bell_draw(own_key, dims, spread, most, cuts=(), kind=jnp.bfloat16):
    drawn = jax.random.normal(own_key, dims, jnp.float32) * spread
    if len(cuts) > 0:
        drawn = block_scale(own_key, dims, cuts, -0.22, 0.18) * drawn
    return jnp.clip(drawn, min=-most, max=most).astype(kind)


def setup_inputs(seed: int = 0) -> dict:
    arg_keys = jax.random.split(jax.random.key(seed), 17)
    return {
        "hidden": bell_draw(arg_keys[0], (SEQS, LEN, D), 1.0, 6.0, ((1, 32),)),
        "norm_gain": jnp.clip(1.0 + 0.1 * jax.random.normal(arg_keys[1], (D,), jnp.float32), 0.5, 1.5).astype(jnp.bfloat16),
        "w_z": bell_draw(arg_keys[2], (D, INNER), D ** -0.5, 0.15625, ((0, 8),)),
        "w_x": bell_draw(arg_keys[3], (D, INNER), D ** -0.5, 0.15625, ((0, 8),)),
        "w_bc": bell_draw(arg_keys[4], (D, 2 * STATE), D ** -0.5, 0.15625, ((0, 8),)),
        "w_dt": bell_draw(arg_keys[5], (D, HEADS), D ** -0.5, 0.15625, ((0, 8),)),
        "w_out": bell_draw(arg_keys[6], (D, INNER), INNER ** -0.5, 0.109375, ((0, 8),)),
        "conv_x": bell_draw(arg_keys[7], (INNER, CONV), CONV ** -0.5, 3.0, ((0, 8),)),
        "conv_x_bias": jnp.clip(jax.random.uniform(arg_keys[8], (INNER,), jnp.float32, -0.5, 0.5) * block_scale(arg_keys[8], (INNER,), ((0, 8),), -0.4, 0.0), -0.5, 0.5).astype(jnp.bfloat16),
        "conv_bc": bell_draw(arg_keys[9], (2 * STATE, CONV), CONV ** -0.5, 3.0, ((0, 8),)),
        "conv_bc_bias": jnp.clip(jax.random.uniform(arg_keys[10], (2 * STATE,), jnp.float32, -0.5, 0.5) * block_scale(arg_keys[10], (2 * STATE,), ((0, 8),), -0.4, 0.0), -0.5, 0.5).astype(jnp.bfloat16),
        "dt_bias": jnp.clip(-7.0 + 4.703125 * jax.random.uniform(arg_keys[11], (HEADS,), jnp.float32) ** block_scale(arg_keys[11], (HEADS,), ((0, 8),), -0.2, 0.2), -7.0, -2.296875).astype(jnp.bfloat16),
        "a_log": jnp.clip(-2.6875 + 1.09375 * jax.random.uniform(arg_keys[12], (HEADS,), jnp.float32) ** block_scale(arg_keys[12], (HEADS,), ((0, 8),), -0.2, 0.2), -2.6875, -1.59375).astype(jnp.bfloat16),
        "skip_d": jnp.clip(0.5 + 3.5 * jax.random.uniform(arg_keys[13], (HEADS,), jnp.float32) ** block_scale(arg_keys[13], (HEADS,), ((0, 8),), -0.2, 0.2), 0.5, 4.0).astype(jnp.bfloat16),
        "gate_gain": jnp.clip(1.0 + 0.1 * jax.random.normal(arg_keys[14], (INNER,), jnp.float32), 0.5, 1.5).astype(jnp.bfloat16),
        "cotangent": bell_draw(arg_keys[15], (SEQS, LEN, D), 1.0, 6.0, ((1, 32),)),
    }


@jax.custom_vjp
def low(v):
    return lax.optimization_barrier(v.astype(jnp.bfloat16)).astype(jnp.float32)

@jax.custom_vjp
def low_back(v):
    return v

def low_keep(v):
    return (low(v), None)

def low_pass(kept, grad):
    return (grad,)

def back_keep(v):
    return (v, None)

def back_low(kept, grad):
    return (low(grad),)
low.defvjp(low_keep, low_pass)
low_back.defvjp(back_keep, back_low)
EPSILON = 1e-05
HIGHEST = lax.Precision.HIGHEST

def row_scale(values):
    return lax.rsqrt(lax.optimization_barrier(jnp.mean(values * values, axis=-1, keepdims=True)) + EPSILON)

def causal_filter_apply(values, kernel, offset):
    tap_count = kernel.shape[1]
    length = values.shape[0]
    padded = jnp.pad(values, ((tap_count - 1, 0), (0, 0)))
    summed = offset[None, :]
    for position in range(tap_count):
        summed = summed + padded[position:position + length] * kernel[:, position][None, :]
    return summed

def span_update(carry_state, pieces):
    weighted, log_decay, key_rows, read_rows = pieces
    length = log_decay.shape[0]
    running = jnp.cumsum(log_decay, axis=0)
    indices = jnp.arange(length)
    causal = (indices[:, None] >= indices[None, :])[:, :, None]
    log_gaps = running[:, None, :] - running[None, :, :]
    decay_mix = jnp.where(causal, jnp.exp(jnp.where(causal, log_gaps, 0.0)), 0.0)
    scores = jnp.dot(read_rows, key_rows.T, precision=HIGHEST)
    within = jnp.einsum('tsh,shp->thp', scores[:, :, None] * decay_mix, weighted, precision=HIGHEST)
    carried = jnp.einsum('tn,hpn->thp', read_rows, carry_state, precision=HIGHEST) * jnp.exp(running)[:, :, None]
    tail_decay = jnp.exp(running[-1][None, :] - running)
    fresh_terms = jnp.einsum('sh,shp,sn->hpn', tail_decay, weighted, key_rows, precision=HIGHEST)
    new_state = jnp.exp(running[-1])[:, None, None] * carry_state + fresh_terms
    return (new_state, within + carried)

def mixer(params, sequence):
    gain_in, weight_z, weight_x, weight_bc, weight_dt, output_weight, kernel_x, offset_x, kernel_bc, offset_bc, shift_dt, decay_log, skip_weight, gain_out = params
    normed = low(sequence * row_scale(sequence) * gain_in)

    def project(weight_matrix):
        return low(low_back(jnp.dot(normed, weight_matrix, precision=HIGHEST)))
    gate_in = project(weight_z)
    x_in = project(weight_x)
    bc_in = project(weight_bc)
    dt_in = project(weight_dt)
    features = jax.nn.silu(causal_filter_apply(x_in, kernel_x, offset_x))
    shared = jax.nn.silu(causal_filter_apply(bc_in, kernel_bc, offset_bc))
    key_rows = shared[:, :STATE]
    read_rows = shared[:, STATE:]
    step_size = jax.nn.softplus(dt_in + shift_dt[None, :])
    log_decay = -step_size * jnp.exp(decay_log)[None, :]
    head_x = features.reshape(LEN, HEADS, HEAD_SIZE)
    weighted = head_x * step_size[:, :, None]
    blocks_count = LEN // SPAN
    blocks = (weighted.reshape(blocks_count, SPAN, HEADS, HEAD_SIZE), log_decay.reshape(blocks_count, SPAN, HEADS), key_rows.reshape(blocks_count, SPAN, STATE), read_rows.reshape(blocks_count, SPAN, STATE))
    start = jnp.zeros((HEADS, HEAD_SIZE, STATE), jnp.float32)
    _, mixed = lax.scan(jax.checkpoint(span_update), start, blocks)
    result = mixed.reshape(LEN, HEADS, HEAD_SIZE) + skip_weight[None, :, None] * head_x
    gated = low(low_back(result.reshape(LEN, INNER) * jax.nn.silu(gate_in)))
    normalized_output = low(gated * row_scale(gated) * gain_out)
    return sequence + jnp.dot(normalized_output, output_weight.T, precision=HIGHEST)

def reference(hidden, norm_gain, w_z, w_x, w_bc, w_dt, w_out, conv_x, conv_x_bias, conv_bc, conv_bc_bias, dt_bias, a_log, skip_d, gate_gain, cotangent):
    params = tuple((value.astype(jnp.float32) for value in (norm_gain, w_z, w_x, w_bc, w_dt, w_out, conv_x, conv_x_bias, conv_bc, conv_bc_bias, dt_bias, a_log, skip_d, gate_gain)))
    inputs = hidden.astype(jnp.float32)

    def forward(weights, sequences):
        return lax.map(lambda sequence: jax.checkpoint(mixer)(weights, sequence), sequences)
    result, pullback = jax.vjp(forward, params, inputs)
    grad_params, grad_inputs = pullback(cotangent.astype(jnp.float32))
    return (result.astype(jnp.bfloat16), grad_inputs, grad_params[0], grad_params[1], grad_params[2], grad_params[3], grad_params[4], grad_params[5], grad_params[6], grad_params[7], grad_params[8], grad_params[9], grad_params[10], grad_params[11], grad_params[12], grad_params[13])
```

```python
import functools

import jax
import jax.numpy as jnp
from jax import lax
from jax.experimental import pallas as pl
from jax.experimental.pallas import tpu as pltpu
from jax.sharding import PartitionSpec as P

EPSILON = 1e-05
F32, BF16 = jnp.float32, jnp.bfloat16
MESH = pl.DeviceIdType.MESH
CHUNK = 128
LANES = 128
PER_UNIT = 4
VMEM_LIMIT = 56 * 1024 * 1024


def dot(a, b):
    return jnp.dot(a, b, preferred_element_type=F32)


def dot_nt(a, b):
    return lax.dot_general(a, b, (((1,), (1,)), ((), ())), preferred_element_type=F32)


def dot_tn(a, b):
    return lax.dot_general(a, b, (((0,), (0,)), ((), ())), preferred_element_type=F32)


def pieces_of(v):
    high = v.astype(BF16)
    rest = v - high.astype(F32)
    middle = rest.astype(BF16)
    return high, middle, (rest - middle.astype(F32)).astype(BF16)


def exact_left(ones, v):
    return sum(dot(ones, part) for part in pieces_of(v))


def exact_right(v, ones):
    return sum(dot(part, ones) for part in pieces_of(v))


def sigmoid(v):
    return 0.5 * jnp.tanh(0.5 * v) + 0.5


def grid_iotas():
    rows = lax.broadcasted_iota(jnp.int32, (CHUNK, CHUNK), 0)
    columns = lax.broadcasted_iota(jnp.int32, (CHUNK, CHUNK), 1)
    return rows, columns


def two_heads(v, pair, low):
    return jnp.where(low, v[:, 2 * pair : 2 * pair + 1], v[:, 2 * pair + 1 : 2 * pair + 2])


def conv_of(ext, lanes, taps):
    total = taps[4:5, lanes]
    for k in range(4):
        total = total + ext[5 + k : 5 + k + CHUNK, lanes] * taps[k : k + 1, lanes]
    return total


def forward_kernel(
    x_ref, xp_ref, bc_ref, bcp_ref, step_ref, cx_ref, cbc_ref, hp_ref,
    y_ref, st_ref, own_ref, dec_ref, bcs_ref, acum_ref,
    xe, be, state, base,
):
    chunk = pl.program_id(1)
    inner = x_ref.shape[1]

    @pl.when(chunk == 0)
    def _():
        state[...] = jnp.zeros_like(state)
        base[...] = jnp.zeros_like(base)

    xe[0:8] = xp_ref[0]
    xe[8:] = x_ref[...].astype(F32)
    be[0:8] = bcp_ref[0]
    be[8:] = bc_ref[...].astype(F32)
    shared = []
    for k in range(2):
        pre = conv_of(be, slice(k * LANES, (k + 1) * LANES), cbc_ref)
        shared.append(pre * sigmoid(pre))
    keys, reads = shared
    bcs_ref[:, :LANES] = keys.astype(BF16)
    bcs_ref[:, LANES:] = reads.astype(BF16)
    keys_t = keys.T.astype(BF16)
    keys, reads = keys.astype(BF16), reads.astype(BF16)
    rows, columns = grid_iotas()
    causal = rows >= columns
    step = step_ref[...]
    running = exact_left(jnp.where(causal, 1.0, 0.0).astype(BF16), -step * hp_ref[0:1])
    acum_ref[...] = base[0:1] + running
    total = running[CHUNK - 1 : CHUNK]
    base[...] = base[...] + total
    running_t = running.T
    scores = jnp.where(causal, dot_nt(reads, keys), 0.0)
    low = columns < LANES // 2
    low_row = low[0:1]

    for pair in range(inner // LANES):
        lanes = slice(pair * LANES, (pair + 1) * LANES)
        pre = conv_of(xe, lanes, cx_ref)
        xs = pre * sigmoid(pre)
        weighted = xs * two_heads(step, pair, low)
        first = jnp.broadcast_to(running[:, 2 * pair : 2 * pair + 1], (CHUNK, CHUNK))
        second = jnp.broadcast_to(running[:, 2 * pair + 1 : 2 * pair + 2], (CHUNK, CHUNK))
        mix = jnp.concatenate(
            [
                (jnp.exp(jnp.minimum(first - running_t[2 * pair : 2 * pair + 1], 0.0)) * scores).astype(BF16),
                (jnp.exp(jnp.minimum(second - running_t[2 * pair + 1 : 2 * pair + 2], 0.0)) * scores).astype(BF16),
            ],
            axis=1,
        )
        own = weighted.astype(BF16)
        zero = jnp.zeros_like(own)
        stacked = jnp.concatenate([jnp.where(low, own, zero), jnp.where(low, zero, own)], axis=0)
        at = jnp.where(low, first, second)
        at_end = two_heads(total, pair, low_row)
        before = state[:, lanes]
        before_low = before.astype(BF16)
        st_ref[0, :, lanes] = before_low
        y = dot(mix, stacked) + dot(reads, before_low) * jnp.exp(at) + cx_ref[5:6, lanes] * xs
        y_ref[:, lanes] = y.astype(BF16)
        late = (weighted * jnp.exp(at_end - at)).astype(BF16)
        state[:, lanes] = before * jnp.exp(at_end) + dot(keys_t, late)

    @pl.when(chunk == PER_UNIT - 1)
    def _():
        own_ref[0] = state[...].astype(BF16)
        for pair in range(inner // LANES):
            lanes = slice(pair * LANES, (pair + 1) * LANES)
            dec_ref[0, :, lanes] = jnp.broadcast_to(
                jnp.exp(two_heads(base[0:1], pair, low_row)), (8, LANES)
            )


def gate_kernel(y0_ref, gate_ref, bcs_ref, acum_ref, in_ref, y_ref, gated_ref, ss_ref):
    _, columns = grid_iotas()
    low = columns < LANES // 2
    reads = bcs_ref[:, LANES:]
    reach = acum_ref[...]
    squares = jnp.zeros((CHUNK, LANES), F32)
    for pair in range(y0_ref.shape[1] // LANES):
        lanes = slice(pair * LANES, (pair + 1) * LANES)
        y = y0_ref[:, lanes].astype(F32) + dot(reads, in_ref[0, :, lanes]) * jnp.exp(
            two_heads(reach, pair, low)
        )
        y_ref[:, lanes] = y.astype(BF16)
        gate = gate_ref[:, lanes].astype(F32)
        gated = (y * gate * sigmoid(gate)).astype(BF16)
        gated_ref[:, lanes] = gated
        wide = gated.astype(F32)
        squares = squares + wide * wide
    ss_ref[...] = jnp.broadcast_to(jnp.sum(squares, axis=1, keepdims=True), (CHUNK, LANES))


def pull_kernel(
    dno_ref, gated_ref, gate_ref, y_ref, stats_ref, gain_ref, bcs_ref, acum_ref,
    dy_ref, dgate_ref, pull_ref,
    total,
):
    chunk = pl.program_id(1)

    @pl.when(chunk == 0)
    def _():
        total[...] = jnp.zeros_like(total)

    _, columns = grid_iotas()
    low = columns < LANES // 2
    scale = jnp.broadcast_to(stats_ref[:, 0:1], (CHUNK, LANES))
    mean = jnp.broadcast_to(stats_ref[:, 1:2], (CHUNK, LANES))
    reads_t = bcs_ref[:, LANES:].astype(F32).T.astype(BF16)
    reach = acum_ref[...]
    for pair in range(dno_ref.shape[1] // LANES):
        lanes = slice(pair * LANES, (pair + 1) * LANES)
        unit = gated_ref[:, lanes].astype(F32) * scale
        du = dno_ref[:, lanes].astype(F32) * gain_ref[0:1, lanes]
        d_gated = (scale * (du - unit * mean)).astype(BF16).astype(F32)
        gate = gate_ref[:, lanes].astype(F32)
        sg = sigmoid(gate)
        silu = gate * sg
        dy = d_gated * silu
        dy_ref[:, lanes] = dy.astype(BF16)
        dgate = d_gated * y_ref[:, lanes].astype(F32) * (sg + silu * (1.0 - sg))
        dgate_ref[:, lanes] = dgate.astype(BF16)
        total[:, lanes] += dot(reads_t, (dy * jnp.exp(two_heads(reach, pair, low))).astype(BF16))

    @pl.when(chunk == PER_UNIT - 1)
    def _():
        pull_ref[0] = total[...].astype(BF16)


def backward_kernel(
    x_ref, xp_ref, bc_ref, bcp_ref, step_ref, sig_ref, cx_ref, cbc_ref, hp_ref,
    dy_ref, y_ref, st_ref, in_ref, acum_ref, after_ref, pick_ref,
    dall_ref, head_ref, head_bc_ref, gx_ref, gbc_ref, gh_ref,
    xe, be, adjoint, dpx, dpb, ends,
):
    unit, chunk = pl.program_id(0), pl.program_id(1)
    inner = x_ref.shape[1]

    @pl.when((unit == 0) & (chunk == 0))
    def _():
        gx_ref[...] = jnp.zeros_like(gx_ref)
        gbc_ref[...] = jnp.zeros_like(gbc_ref)
        gh_ref[...] = jnp.zeros_like(gh_ref)

    @pl.when(chunk == 0)
    def _():
        adjoint[...] = after_ref[0].astype(F32)
        dpx[CHUNK:] = jnp.zeros((8, inner), F32)
        dpb[CHUNK:] = jnp.zeros((8, 2 * LANES), F32)

    xe[0:8] = xp_ref[0]
    xe[8:] = x_ref[...].astype(F32)
    be[0:8] = bcp_ref[0]
    be[8:] = bc_ref[...].astype(F32)
    shared, slopes = [], []
    for k in range(2):
        pre = conv_of(be, slice(k * LANES, (k + 1) * LANES), cbc_ref)
        sg = sigmoid(pre)
        shared.append(pre * sg)
        slopes.append(sg + pre * sg * (1.0 - sg))
    keys, reads = shared
    reads_t = reads.T.astype(BF16)
    keys, reads = keys.astype(BF16), reads.astype(BF16)
    rows, columns = grid_iotas()
    causal = rows >= columns
    step = step_ref[...]
    rate = hp_ref[0:1]
    log_decay = -step * rate
    running = exact_left(jnp.where(causal, 1.0, 0.0).astype(BF16), log_decay)
    total = running[CHUNK - 1 : CHUNK]
    base = acum_ref[0:1] - running[0:1]
    running_t = running.T
    scores_t = jnp.where(rows <= columns, dot_nt(keys, reads), 0.0)
    low = columns < LANES // 2
    low_row = low[0:1]
    d_scores = jnp.zeros((CHUNK, CHUNK), F32)
    d_reads = jnp.zeros((CHUNK, LANES), F32)
    d_keys = jnp.zeros((CHUNK, LANES), F32)
    sums = jnp.zeros((3 * CHUNK, LANES), F32)

    for pair in range(inner // LANES):
        lanes = slice(pair * LANES, (pair + 1) * LANES)
        shifted = [xe[5 + k : 5 + k + CHUNK, lanes] for k in range(4)]
        pre = cx_ref[4:5, lanes] + sum(shifted[k] * cx_ref[k : k + 1, lanes] for k in range(4))
        sg = sigmoid(pre)
        xs = pre * sg
        slope = sg + xs * (1.0 - sg)
        step_wide = two_heads(step, pair, low)
        weighted = xs * step_wide
        first = jnp.broadcast_to(running[:, 2 * pair : 2 * pair + 1], (CHUNK, CHUNK))
        second = jnp.broadcast_to(running[:, 2 * pair + 1 : 2 * pair + 2], (CHUNK, CHUNK))
        gap0 = first - running_t[2 * pair : 2 * pair + 1]
        gap1 = second - running_t[2 * pair + 1 : 2 * pair + 2]
        mix_t = jnp.concatenate(
            [
                (jnp.exp(jnp.minimum(-gap0, 0.0)) * scores_t).astype(BF16),
                (jnp.exp(jnp.minimum(-gap1, 0.0)) * scores_t).astype(BF16),
            ],
            axis=1,
        )
        dy_low = dy_ref[:, lanes]
        dy = dy_low.astype(F32)
        zero = jnp.zeros_like(dy_low)
        dy_two = jnp.concatenate([jnp.where(low, dy_low, zero), jnp.where(low, zero, dy_low)], axis=0)
        d_mix = dot_nt(dy_two, weighted.astype(BF16))
        d_scores = d_scores + (
            jnp.exp(jnp.minimum(gap0, 0.0)) * d_mix[:CHUNK]
            + jnp.exp(jnp.minimum(gap1, 0.0)) * d_mix[CHUNK:]
        )
        at = jnp.where(low, first, second)
        at_end = two_heads(total, pair, low_row)
        tail = jnp.exp(at_end - at)
        end_decay = jnp.exp(at_end)
        later = adjoint[:, lanes]
        later_low = later.astype(BF16)
        from_state = dot(keys, later_low) * tail
        d_weighted = dot(mix_t, dy_two) + from_state
        before = st_ref[0, :, lanes].astype(F32) + in_ref[0, :, lanes].astype(F32) * jnp.exp(
            two_heads(base, pair, low_row)
        )
        d_read = (dy * jnp.exp(at)).astype(BF16)
        d_reads = d_reads + dot_nt(d_read, before.astype(BF16))
        d_keys = d_keys + dot_nt((weighted * tail).astype(BF16), later_low)
        skip = cx_ref[5:6, lanes]
        y = y_ref[:, lanes].astype(F32) - skip * xs
        d_run = dy * y - weighted * d_weighted
        pick = pick_ref[lanes, :]
        sums = sums + dot(
            jnp.concatenate(
                [d_run.astype(BF16), (xs * d_weighted).astype(BF16), (dy * xs).astype(BF16)], axis=0
            ),
            pick,
        )
        ends[:, lanes] = jnp.broadcast_to(
            jnp.sum(weighted * from_state, axis=0, keepdims=True)
            + end_decay * jnp.sum(later * before, axis=0, keepdims=True),
            (8, LANES),
        )
        d_pre = (step_wide * d_weighted + skip * dy) * slope
        dpx[0:CHUNK, lanes] = d_pre
        adjoint[:, lanes] = later * end_decay + dot(reads_t, d_read)
        d_x = jnp.zeros((CHUNK, LANES), F32)
        for k in range(4):
            d_x = d_x + dpx[3 - k : 3 - k + CHUNK, lanes] * cx_ref[k : k + 1, lanes]
            gx_ref[8 * k : 8 * k + 8, lanes] += jnp.sum(
                (d_pre * shifted[k]).reshape(CHUNK // 8, 8, LANES), axis=0
            )
        gx_ref[32:40, lanes] += jnp.sum(d_pre.reshape(CHUNK // 8, 8, LANES), axis=0)
        dall_ref[:, lanes] = d_x.astype(BF16)

    d_scores_low = jnp.where(causal, d_scores, 0.0)
    d_reads = d_reads + dot(d_scores_low.astype(BF16), keys)
    d_keys = d_keys + dot(d_scores_low.T.astype(BF16), reads)
    for k, part in enumerate((d_keys, d_reads)):
        lanes = slice(k * LANES, (k + 1) * LANES)
        d_pre = part * slopes[k]
        dpb[0:CHUNK, lanes] = d_pre
        d_x = jnp.zeros((CHUNK, LANES), F32)
        for tap in range(4):
            d_x = d_x + dpb[3 - tap : 3 - tap + CHUNK, lanes] * cbc_ref[tap : tap + 1, lanes]
            gbc_ref[8 * tap : 8 * tap + 8, lanes] += jnp.sum(
                (d_pre * be[5 + tap : 5 + tap + CHUNK, lanes]).reshape(CHUNK // 8, 8, LANES), axis=0
            )
        gbc_ref[32:40, lanes] += jnp.sum(d_pre.reshape(CHUNK // 8, 8, LANES), axis=0)
        dall_ref[:, inner + k * LANES : inner + (k + 1) * LANES] = d_x.astype(BF16)

    at_end = exact_right(ends[...], pick_ref[...])[0:1]
    d_log = exact_left(jnp.where(rows <= columns, 1.0, 0.0).astype(BF16), sums[:CHUNK]) + at_end
    d_step = sums[CHUNK : 2 * CHUNK] - d_log * rate
    d_dt = d_step * sig_ref[...]
    dall_ref[:, inner + 2 * LANES :] = d_dt.astype(BF16)
    for k, part in enumerate((d_dt, d_log * log_decay, sums[2 * CHUNK :])):
        gh_ref[8 * k : 8 * k + 8] += jnp.sum(part.reshape(CHUNK // 8, 8, LANES), axis=0)
    dpx[CHUNK:] = dpx[0:8]
    dpb[CHUNK:] = dpb[0:8]

    @pl.when(chunk == PER_UNIT - 1)
    def _():
        head_ref[0] = dpx[0:8]
        head_bc_ref[0] = dpb[0:8]


def exchange_kernel(
    count, joints, back, own_ref, dec_ref, out_ref, dec_out_ref,
    parts, decs, results, sends, receives, dec_sends, dec_receives, back_sends, back_receives,
):
    f, z = lax.axis_index("fs"), lax.axis_index("sp")
    core, group = f % 2, z // joints
    me = (f // 2) * joints + z % joints
    units, share = own_ref.shape[0], parts.shape[2]

    def peer(k):
        other = (me + k) % count
        return other, ((other // joints) * 2 + core, group * joints + other % joints)

    barrier = pltpu.get_barrier_semaphore()
    for k in range(1, count):
        pl.semaphore_signal(barrier, inc=1, device_id=peer(k)[1], device_id_type=MESH)
    pl.semaphore_wait(barrier, count - 1)

    def rows_of(i):
        return pl.ds(pl.multiple_of(i * share, share), share)

    def out_copy(k):
        other, device = peer(k)
        return pltpu.make_async_remote_copy(
            src_ref=own_ref.at[:, rows_of(other)], dst_ref=parts.at[me],
            send_sem=sends.at[k], recv_sem=receives.at[me], device_id=device, device_id_type=MESH,
        )

    def dec_copy(k):
        return pltpu.make_async_remote_copy(
            src_ref=dec_ref, dst_ref=decs.at[me],
            send_sem=dec_sends.at[k], recv_sem=dec_receives.at[me],
            device_id=peer(k)[1], device_id_type=MESH,
        )

    def back_copy(k):
        other, device = peer(k)
        return pltpu.make_async_remote_copy(
            src_ref=results.at[other], dst_ref=out_ref.at[:, rows_of(me)],
            send_sem=back_sends.at[k], recv_sem=back_receives.at[me],
            device_id=device, device_id_type=MESH,
        )

    for k in range(1, count):
        if not back:
            dec_copy(k).start()
        out_copy(k).start()
    parts[me] = own_ref[:, rows_of(me)]
    if not back:
        decs[me] = dec_ref[...]
    else:
        decs[...] = dec_ref[...]
    for k in range(1, count):
        other = (me + k) % count
        if not back:
            pltpu.make_async_remote_copy(
                src_ref=dec_ref, dst_ref=decs.at[other],
                send_sem=dec_sends.at[k], recv_sem=dec_receives.at[other],
                device_id=peer(k)[1], device_id_type=MESH,
            ).wait_recv()
        pltpu.make_async_remote_copy(
            src_ref=own_ref.at[:, rows_of(other)], dst_ref=parts.at[other],
            send_sem=sends.at[k], recv_sem=receives.at[other],
            device_id=peer(k)[1], device_id_type=MESH,
        ).wait_recv()
    if not back:
        dec_out_ref[...] = decs[...]
    order = range(count - 1, -1, -1) if back else range(count)
    width = own_ref.shape[2]
    running = [jnp.zeros((share, width), F32) for _ in range(units)]
    for i in order:
        for u in range(units):
            results[i, u] = running[u].astype(BF16)
            running[u] = running[u] * decs[i, u : u + 1] + parts[i, u].astype(F32)
    out_ref[:, rows_of(me)] = results[me]
    for k in range(1, count):
        back_copy(k).start()
    for k in range(1, count):
        other = (me + k) % count
        pltpu.make_async_remote_copy(
            src_ref=results.at[other], dst_ref=out_ref.at[:, rows_of(other)],
            send_sem=back_sends.at[k], recv_sem=back_receives.at[other],
            device_id=peer(k)[1], device_id_type=MESH,
        ).wait_recv()
    for k in range(1, count):
        if not back:
            dec_copy(k).wait_send()
        out_copy(k).wait_send()
        back_copy(k).wait_send()


class Plan:
    def __init__(self, batch, tokens):
        self.shards, self.members = lax.axis_size("fs"), lax.axis_size("sp")
        self.f, self.z = lax.axis_index("fs"), lax.axis_index("sp")
        self.core = self.f % 2
        self.chips = self.shards // 2
        self.chip = self.f // 2
        self.batch, self.tokens = batch, tokens
        self.units = batch // 2
        self.joints = self.members // 2
        self.count = self.chips * self.joints
        self.group, self.joint = self.z // self.joints, self.z % self.joints
        self.fast = self.chips == 4 and self.members == 4

    def at(self, f, z):
        return f * self.members + z

    def send(self, x, pairs):
        return lax.ppermute(x, ("fs", "sp"), pairs)

    def swap(self, x, df=0, dz=0):
        pairs = [
            (self.at(f, z), self.at(f ^ df, z ^ dz))
            for f in range(self.shards)
            for z in range(self.members)
        ]
        return self.send(x, pairs)

    def along(self, x, by):
        pairs = []
        for f in range(self.shards):
            for z in range(self.members):
                place = (f // 2) * self.joints + z % self.joints + by
                if 0 <= place < self.count:
                    there = (place // self.joints) * 2 + f % 2
                    pairs.append(
                        (self.at(f, z), self.at(there, z - z % self.joints + place % self.joints))
                    )
        return self.send(x, pairs)

    def by_core(self, mine, other):
        first = self.core == 0
        return jnp.where(first, mine, other), jnp.where(first, other, mine)

    def turned(self, blocks):
        if not self.fast:
            return blocks
        x, y = (self.chip % 2) == 1, (self.chip // 2) == 1
        a, b, c, d = blocks
        a, b = jnp.where(x, b, a), jnp.where(x, a, b)
        c, d = jnp.where(x, d, c), jnp.where(x, c, d)
        return [jnp.where(y, c, a), jnp.where(y, d, b), jnp.where(y, a, c), jnp.where(y, b, d)]

    def turn(self, x):
        if not self.fast:
            return x
        return jnp.concatenate(self.turned(jnp.split(x, 4, axis=-1)), axis=-1)

    def gather(self, x):
        if not self.fast:
            groups = [list(range(c, self.shards, 2)) for c in range(2)]
            return lax.all_gather(x, "fs", axis=0, tiled=True, axis_index_groups=groups)
        half = x.shape[0] // 2
        by_x, by_y = self.swap(x, df=2), self.swap(x, df=4)
        top, bottom = self.swap(by_x[:half], df=4), self.swap(by_y[half:], df=2)
        return jnp.concatenate([x, by_x, by_y, top, bottom], axis=0)

    def reduce_chips(self, g):
        if not self.fast:
            groups = [list(range(c, self.shards, 2)) for c in range(2)]
            return lax.psum_scatter(
                g.astype(BF16), "fs", scatter_dimension=0, tiled=True, axis_index_groups=groups
            ).astype(F32)
        rows, width = g.shape[0] // 4, g.shape[1]
        cut = -(-width // (2 * LANES)) * LANES
        blocks = [g[i * rows : (i + 1) * rows] for i in range(4)]
        left, right = [b[:, :cut] for b in blocks], [b[:, cut:] for b in blocks]
        sent_left = self.swap(jnp.concatenate([left[1], left[3]], axis=0).astype(BF16), df=2)
        sent_right = self.swap(jnp.concatenate([right[2], right[3]], axis=0).astype(BF16), df=4)
        next_left = self.swap((left[2] + sent_left[rows:]).astype(BF16), df=4)
        next_right = self.swap((right[1] + sent_right[rows:]).astype(BF16), df=2)
        return jnp.concatenate(
            [left[0] + sent_left[:rows] + next_left, right[0] + sent_right[:rows] + next_right], axis=1
        )

    def reduce_members(self, g):
        if not self.fast:
            return lax.psum(g.astype(BF16), "sp").astype(F32)
        half = g.shape[0] // 2
        first = self.z % 2 == 0
        kept, given = jnp.where(first, g[:half], g[half:]), jnp.where(first, g[half:], g[:half])
        kept = kept + self.swap(given.astype(BF16), dz=1)
        low = kept.astype(BF16)
        kept = (low.astype(F32) + self.swap(low, dz=2)).astype(BF16)
        other = self.swap(kept, dz=1)
        return jnp.concatenate(
            [jnp.where(first, kept, other), jnp.where(first, other, kept)], axis=0
        ).astype(F32)

    def to_units(self, rows):
        half = rows.shape[-1] // 2
        left, right = rows[..., :half], rows[..., half:]
        first = self.core == 0
        mine = jnp.where(first, left, right)
        other = self.swap(jnp.where(first, right, left), df=1)
        both = jnp.stack(self.by_core(mine, other))
        if self.fast:
            parts = [both[t % 2, (t // 2) * self.units : (t // 2 + 1) * self.units] for t in range(4)]
            parts = self.across(parts)
            block = jnp.stack(parts, axis=1)
        else:
            everything = lax.all_gather(both, "sp")
            per_core = self.joints // 2
            block = lax.dynamic_slice(
                everything,
                ((self.joint % per_core) * 4, self.joint // per_core, self.group * self.units, 0, 0),
                (4, 1, self.units) + both.shape[2:],
            )[:, 0]
            block = jnp.moveaxis(block, 0, 1)
        block = block.reshape(self.units * 4 * self.tokens, half)
        pair = self.by_core(block, self.swap(block, df=1))
        return jnp.concatenate(pair, axis=1)

    def across(self, parts):
        low, high = (self.z % 2) == 1, (self.z // 2) == 1
        a, b, c, d = parts
        a, b = jnp.where(low, b, a), jnp.where(low, a, b)
        c, d = jnp.where(low, d, c), jnp.where(low, c, d)
        a, b, c, d = (
            jnp.where(high, c, a),
            jnp.where(high, d, b),
            jnp.where(high, a, c),
            jnp.where(high, b, d),
        )
        d, c, b = self.swap(d, dz=3), self.swap(c, dz=2), self.swap(b, dz=1)
        a, b = jnp.where(low, b, a), jnp.where(low, a, b)
        c, d = jnp.where(low, d, c), jnp.where(low, c, d)
        return [
            jnp.where(high, c, a),
            jnp.where(high, d, b),
            jnp.where(high, a, c),
            jnp.where(high, b, d),
        ]

    def from_units(self, partial):
        half = partial.shape[-1] // 2
        first = self.core == 0
        left, right = partial[:, :half], partial[:, half:]
        mine = jnp.where(first, left, right)
        total = (mine + self.swap(jnp.where(first, right, left).astype(BF16), df=1)).astype(BF16)
        block = total.reshape(self.units, 4, self.tokens, half)
        if self.fast:
            parts = self.across([block[:, t] for t in range(4)])
            both = [jnp.concatenate([parts[c], parts[2 + c]], axis=0) for c in range(2)]
        else:
            per_core = self.joints // 2
            wide = jnp.zeros((self.members, 2, self.batch, self.tokens, half), BF16)
            wide = lax.dynamic_update_slice(
                wide,
                jnp.moveaxis(block, 1, 0)[:, None],
                ((self.joint % per_core) * 4, self.joint // per_core, self.group * self.units, 0, 0),
            )
            summed = lax.psum_scatter(wide, "sp", scatter_dimension=0, tiled=False)
            both = [summed[0], summed[1]]
        mine, other = jnp.where(first, both[0], both[1]), jnp.where(first, both[1], both[0])
        return jnp.concatenate(self.by_core(mine, self.swap(other, df=1)), axis=-1)

    def sum_all(self, x):
        if not self.fast:
            groups = [list(range(c, self.shards, 2)) for c in range(2)]
            return lax.psum(lax.psum(x, "fs", axis_index_groups=groups), "sp")
        for df, dz in ((2, 0), (4, 0), (0, 1), (0, 2)):
            x = x + self.swap(x, df, dz)
        return x


def row_scale(values):
    return lax.rsqrt(jnp.mean(values * values, axis=-1, keepdims=True) + EPSILON)


def rows_spec(width, column=0, back=False):
    def place(u, c):
        return (u * PER_UNIT + (PER_UNIT - 1 - c if back else c), column)

    return pl.BlockSpec((CHUNK, width), place)


def chunk_spec(shape, back=False):
    def place(u, c):
        return (u * PER_UNIT + (PER_UNIT - 1 - c if back else c), 0, 0)

    return pl.BlockSpec((1,) + shape, place)


def unit_spec(shape):
    return pl.BlockSpec((1,) + shape, lambda u, c: (u, 0, 0))


def whole_spec(shape):
    return pl.BlockSpec(shape, lambda u, c: (0,) * len(shape))


def params():
    return pltpu.CompilerParams(
        dimension_semantics=("arbitrary", "arbitrary"), vmem_limit_bytes=VMEM_LIMIT
    )


def exchange(plan, own, decays, back):
    units, depth, width = own.shape
    count = plan.count
    if depth % (16 * count):
        rates, pieces = decays[:units, None], own.astype(F32)

        def hop(_, before):
            return plan.along((before * rates + pieces).astype(BF16), -1 if back else 1).astype(F32)

        found = lax.fori_loop(0, count - 1, hop, jnp.zeros(own.shape, F32))
        return found.astype(BF16), decays
    share = depth // count
    dec_shape = (count, 8, width)
    vmem = pl.BlockSpec(memory_space=pltpu.VMEM)
    scratch = [
        pltpu.VMEM((count, units, share, width), BF16),
        pltpu.VMEM(dec_shape, F32),
        pltpu.VMEM((count, units, share, width), BF16),
    ] + [pltpu.SemaphoreType.DMA((count,))] * 6
    out_shape = [jax.ShapeDtypeStruct(own.shape, BF16)]
    if not back:
        out_shape.append(jax.ShapeDtypeStruct(dec_shape, F32))
        kernel = functools.partial(exchange_kernel, count, plan.joints, False)
    else:

        def kernel(own_ref, dec_ref, out_ref, *rest):
            exchange_kernel(count, plan.joints, True, own_ref, dec_ref, out_ref, None, *rest)

    outs = pl.pallas_call(
        kernel,
        out_shape=out_shape,
        in_specs=[vmem, vmem],
        out_specs=[vmem] * len(out_shape),
        scratch_shapes=scratch,
        compiler_params=pltpu.CompilerParams(
            collective_id=1 if back else 0, has_side_effects=True, vmem_limit_bytes=VMEM_LIMIT
        ),
        name="states_back" if back else "states",
    )(own, decays)
    return (outs[0], decays) if back else (outs[0], outs[1])


def body(
    hidden, norm_gain, w_z, w_x, w_bc, w_dt, w_out, conv_x, conv_x_bias, conv_bc, conv_bc_bias,
    dt_bias, a_log, skip_d, gate_gain, cotangent,
):
    batch, tokens, model = hidden.shape
    plan = Plan(batch, tokens)
    core = plan.core
    inner = w_z.shape[1] // 2
    heads = w_dt.shape[1] // 2
    head_size = inner // heads
    units = plan.units
    rows = units * 4 * tokens
    chunks = rows // CHUNK

    def halves(w):
        half = w.shape[1] // 2
        return jnp.where(core == 0, w[:, :half], w[:, half:]), jnp.where(core == 0, w[:, half:], w[:, :half])

    small = [conv_x, conv_x_bias, conv_bc, conv_bc_bias, dt_bias, a_log, skip_d, gate_gain, norm_gain]
    flat = jnp.concatenate([part.reshape(-1) for part in small])
    length = flat.shape[0]
    padded = -(-length // LANES) * LANES
    flat = jnp.pad(flat, (0, padded - length)).reshape(padded // LANES, LANES)
    everyone = lax.all_gather(flat, "fs").reshape(plan.shards, padded)
    gathered, start = [], 0
    for part in small:
        gathered.append(
            everyone[:, start : start + part.size].reshape((-1,) + part.shape[1:]).astype(F32)
        )
        start += part.size
    taps_x, bias_x, taps_bc, bias_bc, shift, rate_log, skip, gain_out, gain_in = gathered

    x_mine, x_other = halves(w_x)
    dt_mine, dt_other = halves(w_dt)
    z_mine, z_other = halves(w_z)
    o_mine, o_other = halves(w_out)
    fill = jnp.zeros((w_dt.shape[0], LANES - heads), BF16)
    first_mine = jnp.concatenate([x_mine, w_bc, dt_mine, fill], axis=1)
    first_other = jnp.concatenate([x_other, w_bc, dt_other, fill], axis=1)

    def rows_of_chip(mine, other):
        return jnp.concatenate(plan.by_core(mine, plan.swap(other, df=1)), axis=0)

    weight_first = plan.gather(rows_of_chip(first_mine, first_other))
    weight_gate = plan.gather(rows_of_chip(z_mine, z_other))
    weight_out = plan.gather(rows_of_chip(o_mine, o_other))

    def mine_of(v):
        half = v.shape[0] // 2
        return lax.dynamic_slice_in_dim(v, core * half, half, 0)

    gain_in_turned = plan.turn(gain_in[None])
    taps_x, bias_x, gain_out, skip_mine = (mine_of(v) for v in (taps_x, bias_x, gain_out, skip))
    shift, rate_log = mine_of(shift), mine_of(rate_log)
    cx = jnp.concatenate(
        [taps_x.T, bias_x[None], jnp.repeat(skip_mine, head_size)[None], jnp.zeros((2, inner), F32)]
    )
    cbc = jnp.concatenate([taps_bc.T, bias_bc[None], jnp.zeros((3, taps_bc.shape[0]), F32)])
    pad_heads = (0, LANES - heads)
    rate = jnp.pad(jnp.exp(rate_log), pad_heads)
    hp = jnp.concatenate([rate[None], jnp.zeros((7, LANES), F32)])
    pick = (jnp.arange(inner)[:, None] // head_size == jnp.arange(LANES)[None, :]).astype(BF16)

    hidden_rows = plan.to_units(plan.turn(hidden)).astype(F32)
    scale_in = row_scale(hidden_rows)
    unit_in = hidden_rows * scale_in
    normed = (unit_in * gain_in_turned).astype(BF16)
    cot_rows = plan.to_units(plan.turn(cotangent))

    first = dot(normed, weight_first).astype(BF16)
    dt_shifted = first[:, inner + 2 * LANES :].astype(F32) + jnp.pad(shift, pad_heads)[None]
    step = jax.nn.softplus(dt_shifted)
    slope_dt = jax.nn.sigmoid(dt_shifted)

    tails = first[:, : inner + 2 * LANES].reshape(units, PER_UNIT, CHUNK, inner + 2 * LANES)[:, :, CHUNK - 8 :]
    before = plan.along(tails[:, PER_UNIT - 1], 1)
    tails = jnp.concatenate([before[:, None], tails[:, : PER_UNIT - 1]], axis=1).astype(F32)
    tails = tails.reshape(chunks, 8, inner + 2 * LANES)
    tail_x, tail_bc = tails[..., :inner], tails[..., inner:]

    def shaped(*shape, dtype=BF16):
        return jax.ShapeDtypeStruct(shape, dtype)

    states = (LANES, inner)
    y_own, starts, own, decays, shared, reach = pl.pallas_call(
        forward_kernel,
        grid=(units, PER_UNIT),
        in_specs=[
            rows_spec(inner), chunk_spec((8, inner)),
            rows_spec(2 * LANES, inner // (2 * LANES)), chunk_spec((8, 2 * LANES)),
            rows_spec(LANES), whole_spec(cx.shape), whole_spec(cbc.shape), whole_spec(hp.shape),
        ],
        out_specs=[
            rows_spec(inner), chunk_spec(states), unit_spec(states), unit_spec((8, inner)),
            rows_spec(2 * LANES), rows_spec(LANES),
        ],
        out_shape=[
            shaped(rows, inner), shaped(chunks, *states), shaped(units, *states),
            shaped(units, 8, inner, dtype=F32), shaped(rows, 2 * LANES), shaped(rows, LANES, dtype=F32),
        ],
        scratch_shapes=[
            pltpu.VMEM((CHUNK + 8, inner), F32), pltpu.VMEM((CHUNK + 8, 2 * LANES), F32),
            pltpu.VMEM(states, F32), pltpu.VMEM((8, LANES), F32),
        ],
        compiler_params=params(),
        name="scan_forward",
    )(first, tail_x, first, tail_bc, step, cx, cbc, hp)

    decay_rows = jnp.concatenate([decays[:, 0], jnp.zeros((8 - units, inner), F32)])
    incoming, all_decays = exchange(plan, own, decay_rows, False)
    gate_in = dot(normed, weight_gate).astype(BF16)

    y, gated, squares = pl.pallas_call(
        gate_kernel,
        grid=(units, PER_UNIT),
        in_specs=[
            rows_spec(inner), rows_spec(inner), rows_spec(2 * LANES), rows_spec(LANES), unit_spec(states),
        ],
        out_specs=[rows_spec(inner), rows_spec(inner), rows_spec(LANES)],
        out_shape=[shaped(rows, inner), shaped(rows, inner), shaped(rows, LANES, dtype=F32)],
        compiler_params=params(),
        name="gate_forward",
    )(y_own, gate_in, shared, reach, incoming)

    def pair_sum(v):
        return v + plan.swap(v, df=1)

    squares = pair_sum(squares[:, 0].reshape(chunks, CHUNK))
    scale_out = lax.rsqrt(squares / (2 * inner) + EPSILON).reshape(rows, 1)
    unit_out = gated.astype(F32) * scale_out
    normed_out = (unit_out * gain_out[None]).astype(BF16)
    projected = plan.from_units(dot_nt(normed_out, weight_out))
    output = (hidden.astype(F32) + plan.turn(projected).astype(F32)).astype(BF16)

    d_normed_out = dot(cot_rows, weight_out).astype(BF16)
    wide = d_normed_out.astype(F32)
    g_gate_gain = jnp.sum(wide * unit_out, axis=0)
    mean = pair_sum(jnp.sum(wide * gain_out[None] * unit_out, axis=1).reshape(chunks, CHUNK))
    mean = (mean / (2 * inner)).reshape(rows, 1)
    stats = jnp.concatenate([scale_out, mean, jnp.zeros((rows, LANES - 2), F32)], axis=1)
    gain_rows = jnp.broadcast_to(gain_out[None], (8, inner))

    dy, d_gate, pull = pl.pallas_call(
        pull_kernel,
        grid=(units, PER_UNIT),
        in_specs=[
            rows_spec(inner), rows_spec(inner), rows_spec(inner), rows_spec(inner), rows_spec(LANES),
            whole_spec((8, inner)), rows_spec(2 * LANES), rows_spec(LANES),
        ],
        out_specs=[rows_spec(inner), rows_spec(inner), unit_spec(states)],
        out_shape=[shaped(rows, inner), shaped(rows, inner), shaped(units, *states)],
        scratch_shapes=[pltpu.VMEM(states, F32)],
        compiler_params=params(),
        name="gate_backward",
    )(d_normed_out, gated, gate_in, y, stats, gain_rows, shared, reach)

    after, _ = exchange(plan, pull, all_decays, True)

    back = functools.partial(rows_spec, back=True)
    width = inner + 3 * LANES
    d_all, heads_x, heads_bc, g_x, g_bc, g_heads = pl.pallas_call(
        backward_kernel,
        grid=(units, PER_UNIT),
        in_specs=[
            back(inner), chunk_spec((8, inner), True),
            back(2 * LANES, inner // (2 * LANES)), chunk_spec((8, 2 * LANES), True),
            back(LANES), back(LANES), whole_spec(cx.shape), whole_spec(cbc.shape), whole_spec(hp.shape),
            back(inner), back(inner), chunk_spec(states, True), unit_spec(states), back(LANES),
            unit_spec(states), whole_spec(pick.shape),
        ],
        out_specs=[
            back(width), unit_spec((8, inner)), unit_spec((8, 2 * LANES)),
            whole_spec((40, inner)), whole_spec((40, 2 * LANES)), whole_spec((24, LANES)),
        ],
        out_shape=[
            shaped(rows, width), shaped(units, 8, inner, dtype=F32), shaped(units, 8, 2 * LANES, dtype=F32),
            shaped(40, inner, dtype=F32), shaped(40, 2 * LANES, dtype=F32), shaped(24, LANES, dtype=F32),
        ],
        scratch_shapes=[
            pltpu.VMEM((CHUNK + 8, inner), F32), pltpu.VMEM((CHUNK + 8, 2 * LANES), F32),
            pltpu.VMEM(states, F32),
            pltpu.VMEM((CHUNK + 8, inner), F32), pltpu.VMEM((CHUNK + 8, 2 * LANES), F32),
            pltpu.VMEM((8, inner), F32),
        ],
        compiler_params=params(),
        name="scan_backward",
    )(
        first, tail_x, first, tail_bc, step, slope_dt, cx, cbc, hp,
        dy, y, starts, incoming, reach, after, pick,
    )

    later = plan.along(jnp.concatenate([heads_x, heads_bc], axis=2)[:, :3].astype(BF16), -1).astype(F32)
    taps = jnp.concatenate([cx[:4], cbc[:4]], axis=1)
    extra = jnp.stack(
        [sum(taps[k][None] * later[:, i - k] for k in range(i + 1)) for i in range(3)], axis=1
    )
    tail_rows = d_all.reshape(units, 4 * tokens, width)[:, 4 * tokens - 16 :].astype(F32)
    extra = jnp.pad(extra, ((0, 0), (13, 0), (0, width - extra.shape[2])))
    d_all = d_all.reshape(units, 4 * tokens, width)
    d_all = lax.dynamic_update_slice(d_all, (tail_rows + extra).astype(BF16), (0, 4 * tokens - 16, 0))
    d_all = d_all.reshape(rows, width)

    d_normed = dot_nt(d_gate, weight_gate) + dot_nt(d_all, weight_first)
    g_norm_gain = jnp.sum(d_normed * unit_in, axis=0)

    def both_halves(g):
        half = g.shape[0] // 2
        first_core = core == 0
        mine = jnp.where(first_core, g[:half], g[half:])
        other = jnp.where(first_core, g[half:], g[:half]).astype(BF16)
        return mine, plan.swap(other, df=1)

    g_out_mine, g_out_other = both_halves(plan.reduce_chips(dot_tn(cot_rows, normed_out)))
    total_out = plan.reduce_members(jnp.concatenate(plan.by_core(g_out_mine, g_out_other), axis=1))
    g_z_mine, g_z_other = both_halves(plan.reduce_chips(dot_tn(normed, d_gate)))
    total_z = plan.reduce_members(jnp.concatenate(plan.by_core(g_z_mine, g_z_other), axis=1))

    grad_rows = plan.turn(plan.from_units(d_normed)).astype(F32)
    resid = hidden.astype(F32)
    own_scale = row_scale(resid)
    own_unit = resid * own_scale
    dv = grad_rows * gain_in[None, None]
    grad_hidden = cotangent.astype(F32) + own_scale * (
        dv - own_unit * jnp.mean(dv * own_unit, axis=-1, keepdims=True)
    )

    g_mine, g_other = both_halves(plan.reduce_chips(dot_tn(normed, d_all)))
    x_parts = plan.by_core(g_mine[:, :inner], g_other[:, :inner].astype(F32))
    bc_sum = g_mine[:, inner : inner + 2 * LANES] + g_other[:, inner : inner + 2 * LANES]
    dt_parts = plan.by_core(
        g_mine[:, inner + 2 * LANES : inner + 2 * LANES + heads],
        g_other[:, inner + 2 * LANES : inner + 2 * LANES + heads].astype(F32),
    )
    total = plan.reduce_members(
        jnp.concatenate(
            list(x_parts) + [bc_sum] + list(dt_parts) + [jnp.zeros((bc_sum.shape[0], LANES - 2 * heads), F32)],
            axis=1,
        )
    )
    total_x = total[:, : 2 * inner]
    total_bc = total[:, 2 * inner : 2 * inner + 2 * LANES]
    total_dt = total[:, 2 * inner + 2 * LANES : 2 * inner + 2 * LANES + 2 * heads]

    own_x = g_x.reshape(5, 8, inner).sum(axis=1)
    own_bc = g_bc.reshape(5, 8, 2 * LANES).sum(axis=1)
    own_heads = g_heads.reshape(3, 8, LANES).sum(axis=1)[:, :heads]
    norm_gain_sum = plan.turn(g_norm_gain[None])[0]
    half_parts = [own_x, g_gate_gain[None], own_heads]
    sum_parts = [norm_gain_sum, own_bc]
    vector = jnp.concatenate([v.reshape(-1) for v in half_parts + sum_parts])
    size = -(-vector.shape[0] // 1024) * 1024
    vector = jnp.pad(vector, (0, size - vector.shape[0])).reshape(-1, LANES)
    vector = plan.sum_all(vector)
    lower, upper = (v.reshape(-1) for v in plan.by_core(vector, plan.swap(vector, df=1)))

    def pieces(v):
        found, start = [], 0
        for part in half_parts + sum_parts:
            found.append(v[start : start + part.size].reshape(part.shape))
            start += part.size
        return found

    low_parts, high_parts = pieces(lower), pieces(upper)
    whole_x, whole_gain, whole_heads = (
        jnp.concatenate([a, b], axis=1) for a, b in zip(low_parts[:3], high_parts[:3])
    )
    whole_norm, whole_bc = (a + b for a, b in zip(low_parts[3:], high_parts[3:]))

    def shard(v):
        share = v.shape[-1] // plan.shards
        return lax.dynamic_slice_in_dim(v, plan.f * share, share, v.ndim - 1)

    shard_x, shard_bc, shard_heads = shard(whole_x), shard(whole_bc), shard(whole_heads)
    return (
        output,
        grad_hidden,
        shard(whole_norm),
        total_z,
        total_x,
        total_bc,
        total_dt,
        total_out,
        shard_x[:4].T,
        shard_x[4],
        shard_bc[:4].T,
        shard_bc[4],
        shard_heads[0],
        shard_heads[1],
        shard_heads[2],
        shard(whole_gain)[0],
    )


def solution(mesh):
    one, two = P("fs"), P("fs", None)
    tokens = P(None, ("fs", "sp"), None)
    return jax.shard_map(
        body,
        mesh=mesh,
        in_specs=(tokens, one, two, two, two, two, two, two, one, two, one, one, one, one, one, tokens),
        out_specs=(tokens, tokens, one, two, two, two, two, two, two, one, two, one, one, one, one, one),
        check_vma=False,
    )
```

```python
import functools

import jax
import jax.numpy as jnp
from jax import lax
from jax.experimental import pallas as pl
from jax.experimental.pallas import tpu as pltpu
from jax.sharding import PartitionSpec as P

EPSILON = 1e-05
F32, BF16 = jnp.float32, jnp.bfloat16
MESH = pl.DeviceIdType.MESH
CHUNK = 128
LANES = 128
PER_UNIT = 4
VMEM_LIMIT = 56 * 1024 * 1024


def dot(a, b):
    return jnp.dot(a, b, preferred_element_type=F32)


def dot_nt(a, b):
    return lax.dot_general(a, b, (((1,), (1,)), ((), ())), preferred_element_type=F32)


def dot_tn(a, b):
    return lax.dot_general(a, b, (((0,), (0,)), ((), ())), preferred_element_type=F32)


def pieces_of(v):
    high = v.astype(BF16)
    rest = v - high.astype(F32)
    middle = rest.astype(BF16)
    return high, middle, (rest - middle.astype(F32)).astype(BF16)


def exact_left(ones, v):
    return sum(dot(ones, part) for part in pieces_of(v))


def exact_right(v, ones):
    return sum(dot(part, ones) for part in pieces_of(v))


def sigmoid(v):
    return 0.5 * jnp.tanh(0.5 * v) + 0.5


def grid_iotas():
    rows = lax.broadcasted_iota(jnp.int32, (CHUNK, CHUNK), 0)
    columns = lax.broadcasted_iota(jnp.int32, (CHUNK, CHUNK), 1)
    return rows, columns


def two_heads(v, pair, low):
    return jnp.where(low, v[:, 2 * pair : 2 * pair + 1], v[:, 2 * pair + 1 : 2 * pair + 2])


def conv_of(ext, lanes, taps):
    total = taps[4:5, lanes]
    for k in range(4):
        total = total + ext[5 + k : 5 + k + CHUNK, lanes] * taps[k : k + 1, lanes]
    return total


def forward_kernel(
    x_ref, xp_ref, bc_ref, bcp_ref, step_ref, cx_ref, cbc_ref, hp_ref,
    y_ref, st_ref, own_ref, dec_ref, bcs_ref, acum_ref,
    xe, be, state, base,
):
    chunk = pl.program_id(1)
    inner = x_ref.shape[1]

    @pl.when(chunk == 0)
    def _():
        state[...] = jnp.zeros_like(state)
        base[...] = jnp.zeros_like(base)

    xe[0:8] = xp_ref[0]
    xe[8:] = x_ref[...].astype(F32)
    be[0:8] = bcp_ref[0]
    be[8:] = bc_ref[...].astype(F32)
    shared = []
    for k in range(2):
        pre = conv_of(be, slice(k * LANES, (k + 1) * LANES), cbc_ref)
        shared.append(pre * sigmoid(pre))
    keys, reads = shared
    bcs_ref[:, :LANES] = keys.astype(BF16)
    bcs_ref[:, LANES:] = reads.astype(BF16)
    keys_t = keys.T.astype(BF16)
    keys, reads = keys.astype(BF16), reads.astype(BF16)
    rows, columns = grid_iotas()
    causal = rows >= columns
    step = step_ref[...]
    running = exact_left(jnp.where(causal, 1.0, 0.0).astype(BF16), -step * hp_ref[0:1])
    acum_ref[...] = base[0:1] + running
    total = running[CHUNK - 1 : CHUNK]
    base[...] = base[...] + total
    running_t = running.T
    scores = jnp.where(causal, dot_nt(reads, keys), 0.0)
    low = columns < LANES // 2
    low_row = low[0:1]

    for pair in range(inner // LANES):
        lanes = slice(pair * LANES, (pair + 1) * LANES)
        pre = conv_of(xe, lanes, cx_ref)
        xs = pre * sigmoid(pre)
        weighted = xs * two_heads(step, pair, low)
        first = jnp.broadcast_to(running[:, 2 * pair : 2 * pair + 1], (CHUNK, CHUNK))
        second = jnp.broadcast_to(running[:, 2 * pair + 1 : 2 * pair + 2], (CHUNK, CHUNK))
        mix = jnp.concatenate(
            [
                (jnp.exp(jnp.minimum(first - running_t[2 * pair : 2 * pair + 1], 0.0)) * scores).astype(BF16),
                (jnp.exp(jnp.minimum(second - running_t[2 * pair + 1 : 2 * pair + 2], 0.0)) * scores).astype(BF16),
            ],
            axis=1,
        )
        own = weighted.astype(BF16)
        zero = jnp.zeros_like(own)
        stacked = jnp.concatenate([jnp.where(low, own, zero), jnp.where(low, zero, own)], axis=0)
        at = jnp.where(low, first, second)
        at_end = two_heads(total, pair, low_row)
        before = state[:, lanes]
        before_low = before.astype(BF16)
        st_ref[0, :, lanes] = before_low
        y = dot(mix, stacked) + dot(reads, before_low) * jnp.exp(at) + cx_ref[5:6, lanes] * xs
        y_ref[:, lanes] = y.astype(BF16)
        late = (weighted * jnp.exp(at_end - at)).astype(BF16)
        state[:, lanes] = before * jnp.exp(at_end) + dot(keys_t, late)

    @pl.when(chunk == PER_UNIT - 1)
    def _():
        own_ref[0] = state[...].astype(BF16)
        for pair in range(inner // LANES):
            lanes = slice(pair * LANES, (pair + 1) * LANES)
            dec_ref[0, :, lanes] = jnp.broadcast_to(
                jnp.exp(two_heads(base[0:1], pair, low_row)), (8, LANES)
            )


def gate_kernel(y0_ref, gate_ref, bcs_ref, acum_ref, in_ref, y_ref, gated_ref, ss_ref):
    _, columns = grid_iotas()
    low = columns < LANES // 2
    reads = bcs_ref[:, LANES:]
    reach = acum_ref[...]
    squares = jnp.zeros((CHUNK, LANES), F32)
    for pair in range(y0_ref.shape[1] // LANES):
        lanes = slice(pair * LANES, (pair + 1) * LANES)
        y = y0_ref[:, lanes].astype(F32) + dot(reads, in_ref[0, :, lanes]) * jnp.exp(
            two_heads(reach, pair, low)
        )
        y_ref[:, lanes] = y.astype(BF16)
        gate = gate_ref[:, lanes].astype(F32)
        gated = (y * gate * sigmoid(gate)).astype(BF16)
        gated_ref[:, lanes] = gated
        wide = gated.astype(F32)
        squares = squares + wide * wide
    ss_ref[...] = jnp.broadcast_to(jnp.sum(squares, axis=1, keepdims=True), (CHUNK, LANES))


def pull_kernel(
    dno_ref, gated_ref, gate_ref, y_ref, stats_ref, gain_ref, bcs_ref, acum_ref,
    dy_ref, dgate_ref, pull_ref,
    total,
):
    chunk = pl.program_id(1)

    @pl.when(chunk == 0)
    def _():
        total[...] = jnp.zeros_like(total)

    _, columns = grid_iotas()
    low = columns < LANES // 2
    scale = jnp.broadcast_to(stats_ref[:, 0:1], (CHUNK, LANES))
    mean = jnp.broadcast_to(stats_ref[:, 1:2], (CHUNK, LANES))
    reads_t = bcs_ref[:, LANES:].astype(F32).T.astype(BF16)
    reach = acum_ref[...]
    for pair in range(dno_ref.shape[1] // LANES):
        lanes = slice(pair * LANES, (pair + 1) * LANES)
        unit = gated_ref[:, lanes].astype(F32) * scale
        du = dno_ref[:, lanes].astype(F32) * gain_ref[0:1, lanes]
        d_gated = (scale * (du - unit * mean)).astype(BF16).astype(F32)
        gate = gate_ref[:, lanes].astype(F32)
        sg = sigmoid(gate)
        silu = gate * sg
        dy = d_gated * silu
        dy_ref[:, lanes] = dy.astype(BF16)
        dgate = d_gated * y_ref[:, lanes].astype(F32) * (sg + silu * (1.0 - sg))
        dgate_ref[:, lanes] = dgate.astype(BF16)
        total[:, lanes] += dot(reads_t, (dy * jnp.exp(two_heads(reach, pair, low))).astype(BF16))

    @pl.when(chunk == PER_UNIT - 1)
    def _():
        pull_ref[0] = total[...].astype(BF16)


def backward_kernel(
    x_ref, xp_ref, bc_ref, bcp_ref, step_ref, sig_ref, cx_ref, cbc_ref, hp_ref,
    dy_ref, y_ref, st_ref, in_ref, acum_ref, after_ref, pick_ref,
    dall_ref, head_ref, head_bc_ref, gx_ref, gbc_ref, gh_ref,
    xe, be, adjoint, dpx, dpb, ends,
):
    unit, chunk = pl.program_id(0), pl.program_id(1)
    inner = x_ref.shape[1]

    @pl.when((unit == 0) & (chunk == 0))
    def _():
        gx_ref[...] = jnp.zeros_like(gx_ref)
        gbc_ref[...] = jnp.zeros_like(gbc_ref)
        gh_ref[...] = jnp.zeros_like(gh_ref)

    @pl.when(chunk == 0)
    def _():
        adjoint[...] = after_ref[0].astype(F32)
        dpx[CHUNK:] = jnp.zeros((8, inner), F32)
        dpb[CHUNK:] = jnp.zeros((8, 2 * LANES), F32)

    xe[0:8] = xp_ref[0]
    xe[8:] = x_ref[...].astype(F32)
    be[0:8] = bcp_ref[0]
    be[8:] = bc_ref[...].astype(F32)
    shared, slopes = [], []
    for k in range(2):
        pre = conv_of(be, slice(k * LANES, (k + 1) * LANES), cbc_ref)
        sg = sigmoid(pre)
        shared.append(pre * sg)
        slopes.append(sg + pre * sg * (1.0 - sg))
    keys, reads = shared
    reads_t = reads.T.astype(BF16)
    keys, reads = keys.astype(BF16), reads.astype(BF16)
    rows, columns = grid_iotas()
    causal = rows >= columns
    step = step_ref[...]
    rate = hp_ref[0:1]
    log_decay = -step * rate
    running = exact_left(jnp.where(causal, 1.0, 0.0).astype(BF16), log_decay)
    total = running[CHUNK - 1 : CHUNK]
    base = acum_ref[0:1] - running[0:1]
    running_t = running.T
    scores_t = jnp.where(rows <= columns, dot_nt(keys, reads), 0.0)
    low = columns < LANES // 2
    low_row = low[0:1]
    d_scores = jnp.zeros((CHUNK, CHUNK), F32)
    d_reads = jnp.zeros((CHUNK, LANES), F32)
    d_keys = jnp.zeros((CHUNK, LANES), F32)
    sums = jnp.zeros((3 * CHUNK, LANES), F32)

    for pair in range(inner // LANES):
        lanes = slice(pair * LANES, (pair + 1) * LANES)
        shifted = [xe[5 + k : 5 + k + CHUNK, lanes] for k in range(4)]
        pre = cx_ref[4:5, lanes] + sum(shifted[k] * cx_ref[k : k + 1, lanes] for k in range(4))
        sg = sigmoid(pre)
        xs = pre * sg
        slope = sg + xs * (1.0 - sg)
        step_wide = two_heads(step, pair, low)
        weighted = xs * step_wide
        first = jnp.broadcast_to(running[:, 2 * pair : 2 * pair + 1], (CHUNK, CHUNK))
        second = jnp.broadcast_to(running[:, 2 * pair + 1 : 2 * pair + 2], (CHUNK, CHUNK))
        gap0 = first - running_t[2 * pair : 2 * pair + 1]
        gap1 = second - running_t[2 * pair + 1 : 2 * pair + 2]
        mix_t = jnp.concatenate(
            [
                (jnp.exp(jnp.minimum(-gap0, 0.0)) * scores_t).astype(BF16),
                (jnp.exp(jnp.minimum(-gap1, 0.0)) * scores_t).astype(BF16),
            ],
            axis=1,
        )
        dy_low = dy_ref[:, lanes]
        dy = dy_low.astype(F32)
        zero = jnp.zeros_like(dy_low)
        dy_two = jnp.concatenate([jnp.where(low, dy_low, zero), jnp.where(low, zero, dy_low)], axis=0)
        d_mix = dot_nt(dy_two, weighted.astype(BF16))
        d_scores = d_scores + (
            jnp.exp(jnp.minimum(gap0, 0.0)) * d_mix[:CHUNK]
            + jnp.exp(jnp.minimum(gap1, 0.0)) * d_mix[CHUNK:]
        )
        at = jnp.where(low, first, second)
        at_end = two_heads(total, pair, low_row)
        tail = jnp.exp(at_end - at)
        end_decay = jnp.exp(at_end)
        later = adjoint[:, lanes]
        later_low = later.astype(BF16)
        from_state = dot(keys, later_low) * tail
        d_weighted = dot(mix_t, dy_two) + from_state
        before = st_ref[0, :, lanes].astype(F32) + in_ref[0, :, lanes].astype(F32) * jnp.exp(
            two_heads(base, pair, low_row)
        )
        d_read = (dy * jnp.exp(at)).astype(BF16)
        d_reads = d_reads + dot_nt(d_read, before.astype(BF16))
        d_keys = d_keys + dot_nt((weighted * tail).astype(BF16), later_low)
        skip = cx_ref[5:6, lanes]
        y = y_ref[:, lanes].astype(F32) - skip * xs
        d_run = dy * y - weighted * d_weighted
        pick = pick_ref[lanes, :]
        sums = sums + dot(
            jnp.concatenate(
                [d_run.astype(BF16), (xs * d_weighted).astype(BF16), (dy * xs).astype(BF16)], axis=0
            ),
            pick,
        )
        ends[:, lanes] = jnp.broadcast_to(
            jnp.sum(weighted * from_state, axis=0, keepdims=True)
            + end_decay * jnp.sum(later * before, axis=0, keepdims=True),
            (8, LANES),
        )
        d_pre = (step_wide * d_weighted + skip * dy) * slope
        dpx[0:CHUNK, lanes] = d_pre
        adjoint[:, lanes] = later * end_decay + dot(reads_t, d_read)
        d_x = jnp.zeros((CHUNK, LANES), F32)
        for k in range(4):
            d_x = d_x + dpx[3 - k : 3 - k + CHUNK, lanes] * cx_ref[k : k + 1, lanes]
            gx_ref[8 * k : 8 * k + 8, lanes] += jnp.sum(
                (d_pre * shifted[k]).reshape(CHUNK // 8, 8, LANES), axis=0
            )
        gx_ref[32:40, lanes] += jnp.sum(d_pre.reshape(CHUNK // 8, 8, LANES), axis=0)
        dall_ref[:, lanes] = d_x.astype(BF16)

    d_scores_low = jnp.where(causal, d_scores, 0.0)
    d_reads = d_reads + dot(d_scores_low.astype(BF16), keys)
    d_keys = d_keys + dot(d_scores_low.T.astype(BF16), reads)
    for k, part in enumerate((d_keys, d_reads)):
        lanes = slice(k * LANES, (k + 1) * LANES)
        d_pre = part * slopes[k]
        dpb[0:CHUNK, lanes] = d_pre
        d_x = jnp.zeros((CHUNK, LANES), F32)
        for tap in range(4):
            d_x = d_x + dpb[3 - tap : 3 - tap + CHUNK, lanes] * cbc_ref[tap : tap + 1, lanes]
            gbc_ref[8 * tap : 8 * tap + 8, lanes] += jnp.sum(
                (d_pre * be[5 + tap : 5 + tap + CHUNK, lanes]).reshape(CHUNK // 8, 8, LANES), axis=0
            )
        gbc_ref[32:40, lanes] += jnp.sum(d_pre.reshape(CHUNK // 8, 8, LANES), axis=0)
        dall_ref[:, inner + k * LANES : inner + (k + 1) * LANES] = d_x.astype(BF16)

    at_end = exact_right(ends[...], pick_ref[...])[0:1]
    d_log = exact_left(jnp.where(rows <= columns, 1.0, 0.0).astype(BF16), sums[:CHUNK]) + at_end
    d_step = sums[CHUNK : 2 * CHUNK] - d_log * rate
    d_dt = d_step * sig_ref[...]
    dall_ref[:, inner + 2 * LANES :] = d_dt.astype(BF16)
    for k, part in enumerate((d_dt, d_log * log_decay, sums[2 * CHUNK :])):
        gh_ref[8 * k : 8 * k + 8] += jnp.sum(part.reshape(CHUNK // 8, 8, LANES), axis=0)
    dpx[CHUNK:] = dpx[0:8]
    dpb[CHUNK:] = dpb[0:8]

    @pl.when(chunk == PER_UNIT - 1)
    def _():
        head_ref[0] = dpx[0:8]
        head_bc_ref[0] = dpb[0:8]


def exchange_kernel(
    count, joints, back, own_ref, dec_ref, out_ref, dec_out_ref,
    parts, decs, results, sends, receives, dec_sends, dec_receives, back_sends, back_receives,
):
    f, z = lax.axis_index("fs"), lax.axis_index("sp")
    core, group = f % 2, z // joints
    me = (f // 2) * joints + z % joints
    units, share = own_ref.shape[0], parts.shape[2]

    def peer(k):
        other = (me + k) % count
        return other, ((other // joints) * 2 + core, group * joints + other % joints)

    barrier = pltpu.get_barrier_semaphore()
    for k in range(1, count):
        pl.semaphore_signal(barrier, inc=1, device_id=peer(k)[1], device_id_type=MESH)
    pl.semaphore_wait(barrier, count - 1)

    def rows_of(i):
        return pl.ds(pl.multiple_of(i * share, share), share)

    def out_copy(k):
        other, device = peer(k)
        return pltpu.make_async_remote_copy(
            src_ref=own_ref.at[:, rows_of(other)], dst_ref=parts.at[me],
            send_sem=sends.at[k], recv_sem=receives.at[me], device_id=device, device_id_type=MESH,
        )

    def dec_copy(k):
        return pltpu.make_async_remote_copy(
            src_ref=dec_ref, dst_ref=decs.at[me],
            send_sem=dec_sends.at[k], recv_sem=dec_receives.at[me],
            device_id=peer(k)[1], device_id_type=MESH,
        )

    def back_copy(k):
        other, device = peer(k)
        return pltpu.make_async_remote_copy(
            src_ref=results.at[other], dst_ref=out_ref.at[:, rows_of(me)],
            send_sem=back_sends.at[k], recv_sem=back_receives.at[me],
            device_id=device, device_id_type=MESH,
        )

    for k in range(1, count):
        if not back:
            dec_copy(k).start()
        out_copy(k).start()
    parts[me] = own_ref[:, rows_of(me)]
    if not back:
        decs[me] = dec_ref[...]
    else:
        decs[...] = dec_ref[...]
    for k in range(1, count):
        other = (me + k) % count
        if not back:
            pltpu.make_async_remote_copy(
                src_ref=dec_ref, dst_ref=decs.at[other],
                send_sem=dec_sends.at[k], recv_sem=dec_receives.at[other],
                device_id=peer(k)[1], device_id_type=MESH,
            ).wait_recv()
        pltpu.make_async_remote_copy(
            src_ref=own_ref.at[:, rows_of(other)], dst_ref=parts.at[other],
            send_sem=sends.at[k], recv_sem=receives.at[other],
            device_id=peer(k)[1], device_id_type=MESH,
        ).wait_recv()
    if not back:
        dec_out_ref[...] = decs[...]
    order = range(count - 1, -1, -1) if back else range(count)
    width = own_ref.shape[2]
    running = [jnp.zeros((share, width), F32) for _ in range(units)]
    for i in order:
        for u in range(units):
            results[i, u] = running[u].astype(BF16)
            running[u] = running[u] * decs[i, u : u + 1] + parts[i, u].astype(F32)
    out_ref[:, rows_of(me)] = results[me]
    for k in range(1, count):
        back_copy(k).start()
    for k in range(1, count):
        other = (me + k) % count
        pltpu.make_async_remote_copy(
            src_ref=results.at[other], dst_ref=out_ref.at[:, rows_of(other)],
            send_sem=back_sends.at[k], recv_sem=back_receives.at[other],
            device_id=peer(k)[1], device_id_type=MESH,
        ).wait_recv()
    for k in range(1, count):
        if not back:
            dec_copy(k).wait_send()
        out_copy(k).wait_send()
        back_copy(k).wait_send()


def places():
    f, z = lax.axis_index("fs"), lax.axis_index("sp")
    core, chip = f % 2, f // 2
    by_x, by_y = chip + 1 - 2 * (chip % 2), (chip + 2) % 4
    return f, z, core, chip, by_x, by_y


def remote(src, dst, sends, receives, slot, device):
    return pltpu.make_async_remote_copy(
        src_ref=src, dst_ref=dst, send_sem=sends.at[slot], recv_sem=receives.at[slot],
        device_id=device, device_id_type=MESH,
    )


def head_kernel(
    hidden, mine, other, small, rows_out, first_out, small_out, local, sends, receives, small_sends, small_receives
):
    f, z, core, chip, by_x, by_y = places()
    units = rows_out.shape[0]
    partner, over_x, over_y = (f + 1 - 2 * core, z), (2 * by_x + core, z), (2 * by_y + core, z)
    near_group, far_group = z // 2, 1 - z // 2
    near, far = (2 * chip + z % 2, 2 * near_group + core), (2 * chip + z % 2, 2 * far_group + core)
    stays = z % 2 == core
    shards = small_out.shape[0]

    barrier = pltpu.get_barrier_semaphore()
    for k in range(1, shards):
        pl.semaphore_signal(barrier, inc=1, device_id=((f + k) % shards, z), device_id_type=MESH)
    pl.semaphore_signal(barrier, inc=1, device_id=far, device_id_type=MESH)

    @pl.when(jnp.logical_not(stays))
    def _():
        pl.semaphore_signal(barrier, inc=1, device_id=near, device_id_type=MESH)

    pl.semaphore_wait(barrier, shards + (z + core) % 2)

    def group_of(g):
        return hidden.at[pl.ds(g * units, units)]

    def part(chip_at, core_at):
        return first_out.at[chip_at, core_at]

    def copy(src, dst, slot, device):
        return remote(src, dst, sends, receives, slot, device)

    to_far = copy(group_of(far_group), rows_out.at[:, z], 0, far)
    to_far.start()
    to_partner = copy(other, part(chip, core), 1, partner)
    to_partner.start()
    to_x = copy(mine, part(chip, core), 2, over_x)
    to_x.start()
    to_y = copy(mine, part(chip, core), 3, over_y)
    to_y.start()
    to_near = copy(group_of(near_group), rows_out.at[:, z], 4, near)
    keep_rows = pltpu.make_async_copy(group_of(near_group), rows_out.at[:, z], local.at[0])

    @pl.when(stays)
    def _():
        keep_rows.start()

    @pl.when(jnp.logical_not(stays))
    def _():
        to_near.start()

    keep_first = pltpu.make_async_copy(mine, part(chip, core), local.at[1])
    keep_first.start()
    keep_small = pltpu.make_async_copy(small, small_out.at[f], local.at[2])
    keep_small.start()

    def small_copy(k, at):
        return pltpu.make_async_remote_copy(
            src_ref=small, dst_ref=small_out.at[at],
            send_sem=small_sends.at[k], recv_sem=small_receives.at[at],
            device_id=((f + k) % shards, z), device_id_type=MESH,
        )

    for k in range(1, shards):
        small_copy(k, f).start()

    from_partner = copy(other, part(chip, 1 - core), 1, partner)
    from_partner.wait_recv()
    again_x = copy(part(chip, 1 - core), part(chip, 1 - core), 5, over_x)
    again_x.start()
    again_y = copy(part(chip, 1 - core), part(chip, 1 - core), 6, over_y)
    again_y.start()

    near_at, far_at = 2 * near_group + core, 2 * far_group + core

    @pl.when(stays)
    def _():
        keep_rows.wait()

    @pl.when(jnp.logical_not(stays))
    def _():
        copy(group_of(near_group), rows_out.at[:, near_at], 4, near).wait_recv()

    near_on = copy(rows_out.at[:, near_at], rows_out.at[:, near_at], 7, partner)
    near_on.start()

    copy(mine, part(by_x, core), 2, over_x).wait_recv()
    on_y = copy(part(by_x, core), part(by_x, core), 8, over_y)
    on_y.start()
    copy(mine, part(by_y, core), 3, over_y).wait_recv()
    copy(mine, part(by_x, 1 - core), 5, over_x).wait_recv()
    copy(mine, part(by_y, 1 - core), 6, over_y).wait_recv()
    on_x = copy(part(by_y, 1 - core), part(by_y, 1 - core), 9, over_x)
    on_x.start()

    copy(group_of(far_group), rows_out.at[:, far_at], 0, far).wait_recv()
    far_on = copy(rows_out.at[:, far_at], rows_out.at[:, far_at], 10, partner)
    far_on.start()

    corner = (by_x + 2) % 4
    for k in range(1, shards):
        small_copy(k, (f + k) % shards).wait_recv()
    copy(mine, part(corner, core), 8, over_y).wait_recv()
    copy(mine, part(corner, 1 - core), 9, over_x).wait_recv()
    copy(rows_out.at[:, near_at], rows_out.at[:, 2 * near_group + 1 - core], 7, partner).wait_recv()
    copy(rows_out.at[:, far_at], rows_out.at[:, 2 * far_group + 1 - core], 10, partner).wait_recv()
    for sent in (to_far, to_partner, to_x, to_y, again_x, again_y, near_on, on_y, on_x, far_on):
        sent.wait_send()

    @pl.when(jnp.logical_not(stays))
    def _():
        to_near.wait_send()

    for k in range(1, shards):
        small_copy(k, f).wait_send()
    keep_first.wait()
    keep_small.wait()


PIECES = ((0, 512, "x"), (1024, 512, "y"), (512, 512, "x"), (1536, 384, "y"))


def tail_kernel(
    g, g_x, g_bc, g_heads, g_gate, g_norm, d_part, out_x, out_bc, out_dt, vec_out, d_out,
    d_came, d_sum, local, r1, s2, r2, sp, rp, total, z1s, z1r, z2s, z2r, z3s, z3r, vs, vr,
    sends, receives, vec_sends, vec_receives,
):
    f, z, core, chip, by_x, by_y = places()
    corner = (by_x + 2) % 4
    rows = g.shape[0] // 4
    half = rows // 2
    quarter = half // 2
    inner = out_x.shape[1] // 2
    bit = z % 2
    partner = (f + 1 - 2 * core, z)
    over = {"x": (2 * by_x + core, z), "y": (2 * by_y + core, z)}
    near, far = (f, z + 1 - 2 * bit), (f, (z + 2) % 4)

    upper, units = z // 2, d_part.shape[0]
    token_near, token_far = (2 * chip + bit, 2 * upper + core), (2 * chip + bit, 2 * (1 - upper) + core)
    stays = bit == core

    barrier = pltpu.get_barrier_semaphore()
    for device in (partner, over["x"], over["y"], near, far, token_far):
        pl.semaphore_signal(barrier, inc=1, device_id=device, device_id_type=MESH)

    @pl.when(jnp.logical_not(stays))
    def _():
        pl.semaphore_signal(barrier, inc=1, device_id=token_near, device_id_type=MESH)

    pl.semaphore_wait(barrier, 6 + (bit + core) % 2)

    slot = 7 * len(PIECES)

    def d_pair(k, n):
        return remote(d_part.at[:, k, 1 - core], d_came.at[:, k], sends, receives, slot + n, partner)

    def d_trade(k, n, device, group):
        return remote(
            d_sum.at[:, k], d_out.at[pl.ds(group * units, units)], sends, receives, slot + 2 + n, device
        )

    def d_add(k):
        for u in range(units):
            d_sum[u, k] = (d_part[u, k, core].astype(F32) + d_came[u, k].astype(F32)).astype(BF16)

    d_pair(1 - upper, 0).start()
    d_pair(upper, 1).start()
    d_keep = pltpu.make_async_copy(d_sum.at[:, upper], d_out.at[pl.ds(upper * units, units)], local.at[0])

    def at(i, size):
        return pl.ds(pl.multiple_of(i * size, size), size)

    vs[0] = jnp.zeros(vs.shape[1:], F32)
    for k in range(5):
        vs[0, k : k + 1] = jnp.sum(g_x[8 * k : 8 * k + 8], axis=0, keepdims=True)
        vs[0, 8 + k : 9 + k, : 2 * LANES] = jnp.sum(g_bc[8 * k : 8 * k + 8], axis=0, keepdims=True)
    vs[0, 5:6] = g_gate[...]
    vs[0, 6:7] = g_norm[...]
    for k in range(3):
        vs[0, 7:8, k * LANES : (k + 1) * LANES] = jnp.sum(
            g_heads[8 * k : 8 * k + 8], axis=0, keepdims=True
        )
    vec_ways = [over["x"], over["y"], near, far]

    def vec_copy(k):
        return remote(vs.at[k], vr.at[k], vec_sends, vec_receives, k, vec_ways[k])

    def vec_last(side):
        return remote(vec_out.at[core], vec_out.at[side], vec_sends, vec_receives, 4, partner)

    layout = []
    z_start = 0
    for n, (start, width, way) in enumerate(PIECES):
        wide = 4 * LANES if start == inner else 2 * width
        layout.append((n, start, width, way, "y" if way == "x" else "x", z_start, wide))
        z_start += wide

    def first_copies(piece):
        n, start, width, way, _, _, _ = piece
        columns = pl.ds(start, width)
        to = by_x if way == "x" else by_y
        return [
            remote(g.at[at(i, rows), columns], r1.at[k, :, columns], sends, receives, 7 * n + k, over[way])
            for k, i in enumerate((to, corner))
        ]

    def second_copy(piece):
        n, start, width, _, other, _, _ = piece
        columns = pl.ds(start, width)
        return remote(s2.at[:, columns], r2.at[:, columns], sends, receives, 7 * n + 2, over[other])

    def pair_copy(piece):
        n, start, width, _, _, _, _ = piece
        columns = pl.ds(start, width)
        return remote(sp.at[:, columns], rp.at[:, columns], sends, receives, 7 * n + 3, partner)

    def z_copy(piece, k):
        n, _, _, _, _, start, wide = piece
        columns = pl.ds(start, wide)
        src, dst, device = ((z1s, z1r, near), (z2s, z2r, far), (z3s, z3r, near))[k]
        return remote(src.at[:, columns], dst.at[:, columns], sends, receives, 7 * n + 4 + k, device)

    def after_first(piece):
        _, start, width, way, _, _, _ = piece
        for copy in first_copies(piece):
            copy.wait_recv()
        columns = pl.ds(start, width)
        to = by_y if way == "x" else by_x
        s2[:, columns] = (g[at(to, rows), columns].astype(F32) + r1[1, :, columns].astype(F32)).astype(BF16)
        second_copy(piece).start()

    def chip_sum(piece, side):
        _, start, width, _, _, _, _ = piece
        columns = pl.ds(start, width)
        own = g[pl.ds(pl.multiple_of(chip * rows + side * half, half), half), columns].astype(F32)
        return own + r1[0, at(side, half), columns].astype(F32) + r2[at(side, half), columns].astype(F32)

    def lanes_at(start, side, width):
        return pl.ds(pl.multiple_of(start + side * width, LANES), width)

    def after_second(piece):
        _, start, width, _, _, z_at, _ = piece
        second_copy(piece).wait_recv()
        sp[:, pl.ds(start, width)] = chip_sum(piece, 1 - core).astype(BF16)
        pair_copy(piece).start()
        own = chip_sum(piece, core)
        if start == inner:
            total[:, pl.ds(z_at, 2 * LANES)] = own[:, : 2 * LANES]
            total[:, lanes_at(z_at + 2 * LANES, core, LANES)] = own[:, 2 * LANES :]
        else:
            total[:, lanes_at(z_at, core, width)] = own

    def after_pair(piece):
        _, start, width, _, _, z_at, wide = piece
        pair_copy(piece).wait_recv()
        came = rp[:, pl.ds(start, width)].astype(F32)
        if start == inner:
            total[:, pl.ds(z_at, 2 * LANES)] += came[:, : 2 * LANES]
            total[:, lanes_at(z_at + 2 * LANES, 1 - core, LANES)] = came[:, 2 * LANES :]
        else:
            total[:, lanes_at(z_at, 1 - core, width)] = came
        columns = pl.ds(z_at, wide)
        z1s[:, columns] = total[at(1 - bit, quarter), columns].astype(BF16)
        z_copy(piece, 0).start()

    def after_near(piece):
        columns = pl.ds(piece[5], piece[6])
        z_copy(piece, 0).wait_recv()
        z2s[:, columns] = (total[at(bit, quarter), columns] + z1r[:, columns].astype(F32)).astype(BF16)
        z_copy(piece, 1).start()

    def store(piece, side, values):
        _, start, width, _, _, _, _ = piece
        there = at(side, quarter)
        if start == inner:
            out_bc[there, :] = values[:, : 2 * LANES]
            out_dt[there, :] = values[:, 2 * LANES :]
        else:
            out_x[there, pl.ds(start, width)] = values[:, :width]
            out_x[there, pl.ds(inner + start, width)] = values[:, width:]

    def after_far(piece):
        columns = pl.ds(piece[5], piece[6])
        z_copy(piece, 1).wait_recv()
        low = (z2s[:, columns].astype(F32) + z2r[:, columns].astype(F32)).astype(BF16)
        z3s[:, columns] = low
        z_copy(piece, 2).start()
        store(piece, bit, low.astype(F32))

    def after_last(piece):
        z_copy(piece, 2).wait_recv()
        store(piece, 1 - bit, z3r[:, pl.ds(piece[5], piece[6])].astype(F32))

    def vec_step(k):
        if k:
            vec_copy(k - 1).wait_recv()
            summed = vs[k - 1] + vr[k - 1]
            if k < 4:
                vs[k] = summed
            else:
                vec_out[core] = summed
        if k < 4:
            vec_copy(k).start()
        else:
            vec_last(core).start()

    for piece in layout:
        for copy in first_copies(piece):
            copy.start()
    vec_step(0)
    d_pair(1 - upper, 0).wait_recv()
    d_add(1 - upper)
    d_trade(1 - upper, 0, token_far, upper).start()
    d_pair(upper, 1).wait_recv()
    d_add(upper)

    @pl.when(stays)
    def _():
        d_keep.start()

    @pl.when(jnp.logical_not(stays))
    def _():
        d_trade(upper, 1, token_near, upper).start()

    early, late = layout[:2], layout[2:]
    order = (
        (after_first, early), (1, ()), (after_first, late), (2, ()), (after_second, early), (3, ()),
        (after_pair, early), (after_second, late), (4, ()), (after_near, early), (after_pair, late),
        (after_far, early), (after_near, late), (after_last, early), (after_far, late), (after_last, late),
    )
    for stage, pieces in order:
        if not pieces:
            vec_step(stage)
        for piece in pieces:
            stage(piece)
    vec_last(1 - core).wait_recv()
    d_trade(1 - upper, 0, token_far, 1 - upper).wait_recv()

    @pl.when(stays)
    def _():
        d_keep.wait()

    @pl.when(jnp.logical_not(stays))
    def _():
        d_trade(upper, 1, token_near, upper).wait()

    d_trade(1 - upper, 0, token_far, upper).wait_send()
    d_pair(1 - upper, 0).wait_send()
    d_pair(upper, 1).wait_send()
    for piece in layout:
        for copy in first_copies(piece) + [second_copy(piece), pair_copy(piece)]:
            copy.wait_send()
        for k in range(3):
            z_copy(piece, k).wait_send()
    for k in range(4):
        vec_copy(k).wait_send()
    vec_last(core).wait_send()


def trade_steps(source, target, local, sends, receives):
    f, z, core, chip, _, _ = places()
    units = source.shape[0]
    bit, upper = z % 2, z // 2
    near, far = (2 * chip + bit, 2 * upper + core), (2 * chip + bit, 2 * (1 - upper) + core)
    stays = bit == core

    def copy(k, n, device, group):
        return remote(source.at[:, k], target.at[pl.ds(group * units, units)], sends, receives, n, device)

    keep = pltpu.make_async_copy(source.at[:, upper], target.at[pl.ds(upper * units, units)], local.at[0])

    def start():
        barrier = pltpu.get_barrier_semaphore()
        pl.semaphore_signal(barrier, inc=1, device_id=far, device_id_type=MESH)

        @pl.when(jnp.logical_not(stays))
        def _():
            pl.semaphore_signal(barrier, inc=1, device_id=near, device_id_type=MESH)

        pl.semaphore_wait(barrier, 1 + (bit + core) % 2)
        copy(1 - upper, 0, far, upper).start()

        @pl.when(stays)
        def _():
            keep.start()

        @pl.when(jnp.logical_not(stays))
        def _():
            copy(upper, 1, near, upper).start()

    def finish():
        copy(1 - upper, 0, far, 1 - upper).wait_recv()
        copy(1 - upper, 0, far, upper).wait_send()

        @pl.when(stays)
        def _():
            keep.wait()

        @pl.when(jnp.logical_not(stays))
        def _():
            copy(upper, 1, near, upper).wait()

    return start, finish


def backward_sending_kernel(*refs):
    inputs, source, outputs, target = refs[:16], refs[16], refs[17:23], refs[23]
    scratch, sems = refs[24:30], refs[30:]
    unit, chunk = pl.program_id(0), pl.program_id(1)
    start, finish = trade_steps(source, target, *sems)

    @pl.when((unit == 0) & (chunk == 0))
    def _():
        start()

    backward_kernel(*inputs, *outputs, *scratch)

    @pl.when((unit == pl.num_programs(0) - 1) & (chunk == PER_UNIT - 1))
    def _():
        finish()


class Plan:
    def __init__(self, batch, tokens):
        self.shards, self.members = lax.axis_size("fs"), lax.axis_size("sp")
        self.f, self.z = lax.axis_index("fs"), lax.axis_index("sp")
        self.core = self.f % 2
        self.chips = self.shards // 2
        self.chip = self.f // 2
        self.batch, self.tokens = batch, tokens
        self.units = batch // 2
        self.joints = self.members // 2
        self.count = self.chips * self.joints
        self.group, self.joint = self.z // self.joints, self.z % self.joints
        self.fast = self.chips == 4 and self.members == 4

    def at(self, f, z):
        return f * self.members + z

    def send(self, x, pairs):
        return lax.ppermute(x, ("fs", "sp"), pairs)

    def swap(self, x, df=0, dz=0):
        pairs = [
            (self.at(f, z), self.at(f ^ df, z ^ dz))
            for f in range(self.shards)
            for z in range(self.members)
        ]
        return self.send(x, pairs)

    def along(self, x, by):
        pairs = []
        for f in range(self.shards):
            for z in range(self.members):
                place = (f // 2) * self.joints + z % self.joints + by
                if 0 <= place < self.count:
                    there = (place // self.joints) * 2 + f % 2
                    pairs.append(
                        (self.at(f, z), self.at(there, z - z % self.joints + place % self.joints))
                    )
        return self.send(x, pairs)

    def by_core(self, mine, other):
        first = self.core == 0
        return jnp.where(first, mine, other), jnp.where(first, other, mine)

    def head(self, hidden, mine, other, small):
        if not self.fast:
            both = jnp.concatenate(self.by_core(mine, self.swap(other, df=1)), axis=0)
            return self.to_units(hidden), self.gather(both), lax.all_gather(small, "fs")
        anywhere = pl.BlockSpec(memory_space=pl.ANY)
        rows, first, everyone = pl.pallas_call(
            head_kernel,
            out_shape=[
                jax.ShapeDtypeStruct((self.units, 4, self.tokens, hidden.shape[-1]), BF16),
                jax.ShapeDtypeStruct((4, 2) + mine.shape, BF16),
                jax.ShapeDtypeStruct((self.shards,) + small.shape, BF16),
            ],
            in_specs=[anywhere] * 4,
            out_specs=[anywhere] * 3,
            scratch_shapes=[
                pltpu.SemaphoreType.DMA((3,)),
                pltpu.SemaphoreType.DMA((11,)),
                pltpu.SemaphoreType.DMA((11,)),
                pltpu.SemaphoreType.DMA((self.shards,)),
                pltpu.SemaphoreType.DMA((self.shards,)),
            ],
            compiler_params=pltpu.CompilerParams(collective_id=2, has_side_effects=True),
            cost_estimate=cost(55),
            name="head",
        )(hidden, mine, other, small)
        return (
            rows.reshape(-1, rows.shape[-1]),
            first.reshape(-1, first.shape[-1]),
            everyone,
        )

    def tail(self, g, g_x, g_bc, g_heads, g_gate, g_norm, d_normed):
        rows, inner = g.shape[0] // self.shards, g_x.shape[1]
        if not self.fast:
            g = self.reduce_chips(g)
            low = self.core == 0
            kept, given = jnp.where(low, g[:rows], g[rows:]), jnp.where(low, g[rows:], g[:rows])
            came = self.swap(given.astype(BF16), df=1).astype(F32)
            total = self.reduce_members(
                jnp.concatenate(
                    list(self.by_core(kept[:, :inner], came[:, :inner]))
                    + [kept[:, inner : inner + 2 * LANES] + came[:, inner : inner + 2 * LANES]]
                    + list(self.by_core(kept[:, inner + 2 * LANES :], came[:, inner + 2 * LANES :])),
                    axis=1,
                )
            )
            wide = ((0, 0), (0, inner - 2 * LANES))
            heads = g_heads.reshape(3, 8, LANES).sum(axis=1).reshape(1, -1)
            vec = jnp.concatenate(
                [
                    g_x.reshape(5, 8, inner).sum(axis=1), g_gate, g_norm,
                    jnp.pad(heads, ((0, 0), (0, inner - 3 * LANES))),
                    jnp.pad(g_bc.reshape(5, 8, 2 * LANES).sum(axis=1), wide),
                ]
            )
            vec = self.sum_all(jnp.pad(vec, ((0, 3), (0, 0))))
            vec = jnp.stack(self.by_core(vec, self.swap(vec, df=1)))
            cut = 2 * inner + 2 * LANES
            d_rows = self.to_tokens(self.cores_sum(d_normed))
            return total[:, : 2 * inner], total[:, 2 * inner : cut], total[:, cut:], vec, d_rows
        width = g.shape[1]
        half, whole = rows // 2, 2 * inner + 4 * LANES
        vmem = pl.BlockSpec(memory_space=pltpu.VMEM)
        vec = (16, inner)
        return pl.pallas_call(
            tail_kernel,
            out_shape=[
                jax.ShapeDtypeStruct((rows, 2 * inner), F32),
                jax.ShapeDtypeStruct((rows, 2 * LANES), F32),
                jax.ShapeDtypeStruct((rows, 2 * LANES), F32),
                jax.ShapeDtypeStruct((2,) + vec, F32),
                jax.ShapeDtypeStruct((self.batch, self.tokens, d_normed.shape[1]), BF16),
            ],
            in_specs=[vmem] * 7,
            out_specs=[vmem] * 5,
            scratch_shapes=[
                pltpu.VMEM((self.units, 2, self.tokens, d_normed.shape[1]), BF16),
                pltpu.VMEM((self.units, 2, self.tokens, d_normed.shape[1]), BF16),
                pltpu.SemaphoreType.DMA((1,)),
                pltpu.VMEM((2, 2 * rows, width), BF16),
                pltpu.VMEM((2 * rows, width), BF16),
                pltpu.VMEM((2 * rows, width), BF16),
                pltpu.VMEM((rows, width), BF16),
                pltpu.VMEM((rows, width), BF16),
                pltpu.VMEM((rows, whole), F32),
            ]
            + [pltpu.VMEM((half, whole), BF16)] * 6
            + [pltpu.VMEM((4,) + vec, F32)] * 2
            + [pltpu.SemaphoreType.DMA((7 * len(PIECES) + 4,))] * 2
            + [pltpu.SemaphoreType.DMA((5,))] * 2,
            compiler_params=pltpu.CompilerParams(
                collective_id=3, has_side_effects=True, vmem_limit_bytes=VMEM_LIMIT
            ),
            cost_estimate=cost(90),
            name="tail",
        )(
            g, g_x, g_bc, g_heads, g_gate, g_norm,
            d_normed.reshape(self.units, 2, 2, self.tokens, d_normed.shape[1]),
        )

    def gather(self, x):
        groups = [list(range(c, self.shards, 2)) for c in range(2)]
        return lax.all_gather(x, "fs", axis=0, tiled=True, axis_index_groups=groups)

    def reduce_chips(self, g):
        groups = [list(range(c, self.shards, 2)) for c in range(2)]
        return lax.psum_scatter(
            g, "fs", scatter_dimension=0, tiled=True, axis_index_groups=groups
        ).astype(F32)

    def reduce_members(self, g):
        return lax.psum(g.astype(BF16), "sp").astype(F32)

    def traded(self, x, far):
        pairs = [
            (self.at(f, z), self.at(f - f % 2 + z % 2, ((z // 2) ^ far) * 2 + f % 2))
            for f in range(self.shards)
            for z in range(self.members)
        ]
        return self.send(x, pairs)

    def to_units(self, rows):
        units, width = self.units, rows.shape[-1]
        if self.fast:
            low, high = rows[:units], rows[units:]
            upper = self.z // 2 == 1
            far = self.traded(jnp.where(upper, low, high), 1)
            near = self.traded(jnp.where(upper, high, low), 0)
            mine = jnp.stack([jnp.where(upper, far, near), jnp.where(upper, near, far)], axis=1)
            pair = self.by_core(mine, self.swap(mine, df=1))
            block = jnp.stack(pair, axis=2)
        else:
            other = self.swap(rows, df=1)
            everything = lax.all_gather(jnp.stack(self.by_core(rows, other)), "sp")
            per_core = self.joints // 2
            block = lax.dynamic_slice(
                everything,
                ((self.joint % per_core) * 4, self.joint // per_core, self.group * units, 0, 0),
                (4, 1, units) + rows.shape[1:],
            )[:, 0]
            block = jnp.moveaxis(block, 0, 1)
        return block.reshape(units * 4 * self.tokens, width)

    def cores_sum(self, partial):
        units, width = self.units, partial.shape[-1]
        if self.fast:
            block = partial.reshape(units, 2, 2, self.tokens, width)
            even = self.core == 0
            mine = jnp.where(even, block[:, :, 0], block[:, :, 1])
            given = jnp.where(even, block[:, :, 1], block[:, :, 0]).astype(BF16)
            return (mine.astype(F32) + self.swap(given, df=1).astype(F32)).astype(BF16)
        return partial.astype(BF16).reshape(units, 4, self.tokens, width)

    def to_tokens(self, total):
        units, width = self.units, total.shape[-1]
        if self.fast:
            upper = self.z // 2 == 1
            far = self.traded(jnp.where(upper, total[:, 0], total[:, 1]), 1)
            near = self.traded(jnp.where(upper, total[:, 1], total[:, 0]), 0)
            return jnp.concatenate(
                [jnp.where(upper, far, near), jnp.where(upper, near, far)], axis=0
            )
        per_core = self.joints // 2
        block = total
        wide = jnp.zeros((self.members, 2, self.batch, self.tokens, width), BF16)
        wide = lax.dynamic_update_slice(
            wide,
            jnp.moveaxis(block, 1, 0)[:, None],
            ((self.joint % per_core) * 4, self.joint // per_core, self.group * units, 0, 0),
        )
        summed = lax.psum_scatter(wide, "sp", scatter_dimension=0, tiled=False)
        first = self.core == 0
        mine, given = jnp.where(first, summed[0], summed[1]), jnp.where(first, summed[1], summed[0])
        return (mine.astype(F32) + self.swap(given, df=1).astype(F32)).astype(BF16)

    def sum_all(self, x):
        if not self.fast:
            groups = [list(range(c, self.shards, 2)) for c in range(2)]
            return lax.psum(lax.psum(x, "fs", axis_index_groups=groups), "sp")
        for df, dz in ((2, 0), (4, 0), (0, 1), (0, 2)):
            x = x + self.swap(x, df, dz)
        return x


def row_scale(values):
    return lax.rsqrt(jnp.mean(values * values, axis=-1, keepdims=True) + EPSILON)


def rows_spec(width, column=0, back=False):
    def place(u, c):
        return (u * PER_UNIT + (PER_UNIT - 1 - c if back else c), column)

    return pl.BlockSpec((CHUNK, width), place)


def chunk_spec(shape, back=False):
    def place(u, c):
        return (u * PER_UNIT + (PER_UNIT - 1 - c if back else c), 0, 0)

    return pl.BlockSpec((1,) + shape, place)


def unit_spec(shape):
    return pl.BlockSpec((1,) + shape, lambda u, c: (u, 0, 0))


def whole_spec(shape):
    return pl.BlockSpec(shape, lambda u, c: (0,) * len(shape))


def cost(microseconds):
    return pl.CostEstimate(flops=int(microseconds * 1.15e9), bytes_accessed=0, transcendentals=0)


def params():
    return pltpu.CompilerParams(
        dimension_semantics=("arbitrary", "arbitrary"), vmem_limit_bytes=VMEM_LIMIT
    )


def exchange(plan, own, decays, back):
    units, depth, width = own.shape
    count = plan.count
    if depth % (16 * count):
        rates, pieces = decays[:units, None], own.astype(F32)

        def hop(_, before):
            return plan.along((before * rates + pieces).astype(BF16), -1 if back else 1).astype(F32)

        found = lax.fori_loop(0, count - 1, hop, jnp.zeros(own.shape, F32))
        return found.astype(BF16), decays
    share = depth // count
    dec_shape = (count, 8, width)
    vmem = pl.BlockSpec(memory_space=pltpu.VMEM)
    scratch = [
        pltpu.VMEM((count, units, share, width), BF16),
        pltpu.VMEM(dec_shape, F32),
        pltpu.VMEM((count, units, share, width), BF16),
    ] + [pltpu.SemaphoreType.DMA((count,))] * 6
    out_shape = [jax.ShapeDtypeStruct(own.shape, BF16)]
    if not back:
        out_shape.append(jax.ShapeDtypeStruct(dec_shape, F32))
        kernel = functools.partial(exchange_kernel, count, plan.joints, False)
    else:

        def kernel(own_ref, dec_ref, out_ref, *rest):
            exchange_kernel(count, plan.joints, True, own_ref, dec_ref, out_ref, None, *rest)

    outs = pl.pallas_call(
        kernel,
        out_shape=out_shape,
        in_specs=[vmem, vmem],
        out_specs=[vmem] * len(out_shape),
        scratch_shapes=scratch,
        compiler_params=pltpu.CompilerParams(
            collective_id=1 if back else 0, has_side_effects=True, vmem_limit_bytes=VMEM_LIMIT
        ),
        cost_estimate=cost(35),
        name="states_back" if back else "states",
    )(own, decays)
    return (outs[0], decays) if back else (outs[0], outs[1])


def body(
    hidden, norm_gain, w_z, w_x, w_bc, w_dt, w_out, conv_x, conv_x_bias, conv_bc, conv_bc_bias,
    dt_bias, a_log, skip_d, gate_gain, cotangent,
):
    batch, tokens, model = hidden.shape
    plan = Plan(batch, tokens)
    core = plan.core
    inner = w_z.shape[1] // 2
    heads = w_dt.shape[1] // 2
    head_size = inner // heads
    units = plan.units
    rows = units * 4 * tokens
    chunks = rows // CHUNK

    def halves(w):
        half = w.shape[1] // 2
        return jnp.where(core == 0, w[:, :half], w[:, half:]), jnp.where(core == 0, w[:, half:], w[:, :half])

    misc = jnp.concatenate([conv_bc_bias, dt_bias, a_log, skip_d])
    flat = jnp.concatenate(
        [conv_x.T.reshape(-1), conv_x_bias, gate_gain, norm_gain, conv_bc.T.reshape(-1), misc]
    )
    length = flat.shape[0]
    padded = -(-length // (16 * LANES)) * 16 * LANES
    flat = jnp.pad(flat, (0, padded - length)).reshape(padded // LANES, LANES)

    x_mine, x_other = halves(w_x)
    dt_mine, dt_other = halves(w_dt)
    z_mine, z_other = halves(w_z)
    o_mine, o_other = halves(w_out)
    fill = jnp.zeros((w_dt.shape[0], LANES - heads), BF16)
    first_mine = jnp.concatenate([x_mine, w_bc, dt_mine, fill], axis=1)
    first_other = jnp.concatenate([x_other, w_bc, dt_other, fill], axis=1)

    def rows_of_chip(mine, other):
        return jnp.concatenate(plan.by_core(mine, plan.swap(other, df=1)), axis=0)

    rows_gate, rows_out = rows_of_chip(z_mine, z_other), rows_of_chip(o_mine, o_other)
    weight_gate, weight_out = plan.gather(rows_gate), plan.gather(rows_out)
    hidden_rows, weight_first, everyone = plan.head(hidden, first_mine, first_other, flat)
    everyone = everyone.reshape(plan.shards, padded).astype(F32)

    parts, start = [], 0
    for shape in (
        conv_x.shape[::-1], conv_x_bias.shape, gate_gain.shape, norm_gain.shape, conv_bc.shape[::-1],
        conv_bc_bias.shape, dt_bias.shape, a_log.shape, skip_d.shape,
    ):
        size = shape[0] * (shape[1] if len(shape) > 1 else 1)
        parts.append(everyone[:, start : start + size].reshape((plan.shards,) + shape))
        start += size
    taps_x, bias_x, gain_out, gain_in, taps_bc, bias_bc, shift, rate_log, skip = parts
    gain_in = gain_in.reshape(-1)

    def mine_of(v):
        half = v.shape[0] // 2
        return lax.dynamic_slice_in_dim(v, core * half, half, 0)

    def flat_taps(v):
        return jnp.moveaxis(v, 0, 1).reshape(v.shape[1], -1)

    bias_x, gain_out, skip_mine = (mine_of(v).reshape(-1) for v in (bias_x, gain_out, skip))
    shift, rate_log = mine_of(shift).reshape(-1), mine_of(rate_log).reshape(-1)
    cx = jnp.concatenate(
        [
            flat_taps(mine_of(taps_x)), bias_x[None],
            jnp.repeat(skip_mine, head_size)[None], jnp.zeros((2, inner), F32),
        ]
    )
    cbc = jnp.concatenate(
        [flat_taps(taps_bc), bias_bc.reshape(1, -1), jnp.zeros((3, bias_bc.size), F32)]
    )
    pad_heads = (0, LANES - heads)
    rate = jnp.pad(jnp.exp(rate_log), pad_heads)
    hp = jnp.concatenate([rate[None], jnp.zeros((7, LANES), F32)])
    pick = (jnp.arange(inner)[:, None] // head_size == jnp.arange(LANES)[None, :]).astype(BF16)

    hidden_rows, cot_late = lax.optimization_barrier((hidden_rows, cotangent))
    cot_rows = plan.to_units(cot_late)

    hidden_rows = hidden_rows.astype(F32)
    scale_in = row_scale(hidden_rows)
    unit_in = hidden_rows * scale_in
    normed = (unit_in * gain_in[None]).astype(BF16)

    first = dot(normed, weight_first).astype(BF16)
    dt_shifted = first[:, inner + 2 * LANES :].astype(F32) + jnp.pad(shift, pad_heads)[None]
    step = jax.nn.softplus(dt_shifted)
    slope_dt = jax.nn.sigmoid(dt_shifted)

    tails = first[:, : inner + 2 * LANES].reshape(units, PER_UNIT, CHUNK, inner + 2 * LANES)[:, :, CHUNK - 8 :]
    before = plan.along(tails[:, PER_UNIT - 1], 1)
    tails = jnp.concatenate([before[:, None], tails[:, : PER_UNIT - 1]], axis=1).astype(F32)
    tails = tails.reshape(chunks, 8, inner + 2 * LANES)
    tail_x, tail_bc = tails[..., :inner], tails[..., inner:]

    def shaped(*shape, dtype=BF16):
        return jax.ShapeDtypeStruct(shape, dtype)

    states = (LANES, inner)
    y_own, starts, own, decays, shared, reach = pl.pallas_call(
        forward_kernel,
        grid=(units, PER_UNIT),
        in_specs=[
            rows_spec(inner), chunk_spec((8, inner)),
            rows_spec(2 * LANES, inner // (2 * LANES)), chunk_spec((8, 2 * LANES)),
            rows_spec(LANES), whole_spec(cx.shape), whole_spec(cbc.shape), whole_spec(hp.shape),
        ],
        out_specs=[
            rows_spec(inner), chunk_spec(states), unit_spec(states), unit_spec((8, inner)),
            rows_spec(2 * LANES), rows_spec(LANES),
        ],
        out_shape=[
            shaped(rows, inner), shaped(chunks, *states), shaped(units, *states),
            shaped(units, 8, inner, dtype=F32), shaped(rows, 2 * LANES), shaped(rows, LANES, dtype=F32),
        ],
        scratch_shapes=[
            pltpu.VMEM((CHUNK + 8, inner), F32), pltpu.VMEM((CHUNK + 8, 2 * LANES), F32),
            pltpu.VMEM(states, F32), pltpu.VMEM((8, LANES), F32),
        ],
        compiler_params=params(),
        cost_estimate=cost(31),
        name="scan_forward",
    )(first, tail_x, first, tail_bc, step, cx, cbc, hp)

    decay_rows = jnp.concatenate([decays[:, 0], jnp.zeros((8 - units, inner), F32)])
    incoming, all_decays = exchange(plan, own, decay_rows, False)
    gate_in = dot(normed, weight_gate).astype(BF16)

    y, gated, squares = pl.pallas_call(
        gate_kernel,
        grid=(units, PER_UNIT),
        in_specs=[
            rows_spec(inner), rows_spec(inner), rows_spec(2 * LANES), rows_spec(LANES), unit_spec(states),
        ],
        out_specs=[rows_spec(inner), rows_spec(inner), rows_spec(LANES)],
        out_shape=[shaped(rows, inner), shaped(rows, inner), shaped(rows, LANES, dtype=F32)],
        compiler_params=params(),
        cost_estimate=cost(14),
        name="gate_forward",
    )(y_own, gate_in, shared, reach, incoming)

    def pair_sum(v):
        return v + plan.swap(v, df=1)

    squares = pair_sum(squares[:, 0].reshape(chunks, CHUNK))
    scale_out = lax.rsqrt(squares / (2 * inner) + EPSILON).reshape(rows, 1)
    unit_out = gated.astype(F32) * scale_out
    normed_out = (unit_out * gain_out[None]).astype(BF16)
    projected = plan.cores_sum(dot_nt(normed_out, weight_out))

    g_out = dot_tn(cot_rows, normed_out).astype(BF16)
    g_out, weight_out, cot_rows = lax.optimization_barrier((g_out, weight_out, cot_rows))
    d_normed_out = dot(cot_rows, weight_out).astype(BF16)
    wide = d_normed_out.astype(F32)
    g_gate_gain = jnp.sum(wide * unit_out, axis=0)
    mean = pair_sum(jnp.sum(wide * gain_out[None] * unit_out, axis=1).reshape(chunks, CHUNK))
    mean = (mean / (2 * inner)).reshape(rows, 1)
    stats = jnp.concatenate([scale_out, mean, jnp.zeros((rows, LANES - 2), F32)], axis=1)
    gain_rows = jnp.broadcast_to(gain_out[None], (8, inner))

    dy, d_gate, pull = pl.pallas_call(
        pull_kernel,
        grid=(units, PER_UNIT),
        in_specs=[
            rows_spec(inner), rows_spec(inner), rows_spec(inner), rows_spec(inner), rows_spec(LANES),
            whole_spec((8, inner)), rows_spec(2 * LANES), rows_spec(LANES),
        ],
        out_specs=[rows_spec(inner), rows_spec(inner), unit_spec(states)],
        out_shape=[shaped(rows, inner), shaped(rows, inner), shaped(units, *states)],
        scratch_shapes=[pltpu.VMEM(states, F32)],
        compiler_params=params(),
        cost_estimate=cost(19),
        name="gate_backward",
    )(d_normed_out, gated, gate_in, y, stats, gain_rows, shared, reach)

    def both_halves(g):
        half = g.shape[0] // 2
        first_core = core == 0
        mine = jnp.where(first_core, g[:half], g[half:])
        other = jnp.where(first_core, g[half:], g[:half]).astype(BF16)
        return mine, plan.swap(other, df=1)

    g_z = dot_tn(normed, d_gate).astype(BF16)
    pull, g_z, g_out = lax.optimization_barrier((pull, g_z, plan.reduce_chips(g_out)))
    after, _ = exchange(plan, pull, all_decays, True)
    after, projected, g_z, g_out = lax.optimization_barrier((after, projected, plan.reduce_chips(g_z), g_out))
    g_out_mine, g_out_other = both_halves(g_out)
    g_out = jnp.concatenate(plan.by_core(g_out_mine, g_out_other), axis=1).astype(BF16)
    total_out = lax.psum(g_out, "sp")
    g_z_mine, g_z_other = both_halves(g_z)
    g_z = jnp.concatenate(plan.by_core(g_z_mine, g_z_other), axis=1).astype(BF16)

    back = functools.partial(rows_spec, back=True)
    width = inner + 3 * LANES
    anywhere = pl.BlockSpec(memory_space=pl.ANY)
    in_specs = [
        back(inner), chunk_spec((8, inner), True),
        back(2 * LANES, inner // (2 * LANES)), chunk_spec((8, 2 * LANES), True),
        back(LANES), back(LANES), whole_spec(cx.shape), whole_spec(cbc.shape), whole_spec(hp.shape),
        back(inner), back(inner), chunk_spec(states, True), unit_spec(states), back(LANES),
        unit_spec(states), whole_spec(pick.shape),
    ]
    out_specs = [
        back(width), unit_spec((8, inner)), unit_spec((8, 2 * LANES)),
        whole_spec((40, inner)), whole_spec((40, 2 * LANES)), whole_spec((24, LANES)),
    ]
    out_shape = [
        shaped(rows, width), shaped(units, 8, inner, dtype=F32), shaped(units, 8, 2 * LANES, dtype=F32),
        shaped(40, inner, dtype=F32), shaped(40, 2 * LANES, dtype=F32), shaped(24, LANES, dtype=F32),
    ]
    scratch = [
        pltpu.VMEM((CHUNK + 8, inner), F32), pltpu.VMEM((CHUNK + 8, 2 * LANES), F32),
        pltpu.VMEM(states, F32),
        pltpu.VMEM((CHUNK + 8, inner), F32), pltpu.VMEM((CHUNK + 8, 2 * LANES), F32),
        pltpu.VMEM((8, inner), F32),
    ]
    operands = [
        first, tail_x, first, tail_bc, step, slope_dt, cx, cbc, hp,
        dy, y, starts, incoming, reach, after, pick,
    ]
    sending = params()
    if plan.fast:
        in_specs, operands = in_specs + [anywhere], operands + [projected]
        out_specs, out_shape = out_specs + [anywhere], out_shape + [shaped(batch, tokens, model)]
        scratch = scratch + [
            pltpu.SemaphoreType.DMA((1,)), pltpu.SemaphoreType.DMA((2,)), pltpu.SemaphoreType.DMA((2,)),
        ]
        sending = pltpu.CompilerParams(
            dimension_semantics=("arbitrary", "arbitrary"), vmem_limit_bytes=VMEM_LIMIT,
            collective_id=4, has_side_effects=True,
        )
    d_all, heads_x, heads_bc, g_x, g_bc, g_heads, *sent = pl.pallas_call(
        backward_sending_kernel if plan.fast else backward_kernel,
        grid=(units, PER_UNIT),
        in_specs=in_specs,
        out_specs=out_specs,
        out_shape=out_shape,
        scratch_shapes=scratch,
        compiler_params=sending,
        cost_estimate=cost(70),
        name="scan_backward",
    )(*operands)
    projected = sent[0] if plan.fast else plan.to_tokens(projected)

    later = plan.along(jnp.concatenate([heads_x, heads_bc], axis=2)[:, :3].astype(BF16), -1).astype(F32)
    taps = jnp.concatenate([cx[:4], cbc[:4]], axis=1)
    extra = jnp.stack(
        [sum(taps[k][None] * later[:, i - k] for k in range(i + 1)) for i in range(3)], axis=1
    )
    tail_rows = d_all.reshape(units, 4 * tokens, width)[:, 4 * tokens - 16 :].astype(F32)
    extra = jnp.pad(extra, ((0, 0), (13, 0), (0, width - extra.shape[2])))
    d_all = d_all.reshape(units, 4 * tokens, width)
    d_all = lax.dynamic_update_slice(d_all, (tail_rows + extra).astype(BF16), (0, 4 * tokens - 16, 0))
    d_all = d_all.reshape(rows, width)

    total_z = lax.psum(g_z, "sp")
    output = (hidden.astype(F32) + projected.astype(F32)).astype(BF16)
    g_first = dot_tn(normed, d_all).astype(BF16)
    d_normed = dot_nt(d_gate, weight_gate) + dot_nt(d_all, weight_first)
    g_norm_gain = jnp.sum(d_normed * unit_in, axis=0)

    total_x, total_bc, total_dt, vec, grad_rows = plan.tail(
        g_first, g_x, g_bc, g_heads, g_gate_gain[None], g_norm_gain[None], d_normed.astype(BF16)
    )
    grad_rows = grad_rows.astype(F32)
    resid = hidden.astype(F32)
    own_scale = row_scale(resid)
    own_unit = resid * own_scale
    dv = grad_rows * gain_in[None, None]
    grad_hidden = cotangent.astype(F32) + own_scale * (
        dv - own_unit * jnp.mean(dv * own_unit, axis=-1, keepdims=True)
    )

    total_dt = jnp.concatenate([total_dt[:, :heads], total_dt[:, LANES : LANES + heads]], axis=1)
    whole_x = jnp.moveaxis(vec[:, :6], 0, 1).reshape(6, 2 * inner)
    whole_heads = jnp.moveaxis(vec[:, 7, : 3 * LANES].reshape(2, 3, LANES)[:, :, :heads], 0, 1)
    whole_heads = whole_heads.reshape(3, 2 * heads)
    whole_norm = vec[0, 6] + vec[1, 6]
    whole_bc = vec[0, 8:13, : 2 * LANES] + vec[1, 8:13, : 2 * LANES]

    def shard(v):
        share = v.shape[-1] // plan.shards
        return lax.dynamic_slice_in_dim(v, plan.f * share, share, v.ndim - 1)

    shard_x, shard_bc, shard_heads = shard(whole_x), shard(whole_bc), shard(whole_heads)
    return (
        output,
        grad_hidden,
        shard(whole_norm),
        total_z.astype(F32),
        total_x,
        total_bc,
        total_dt,
        total_out.astype(F32),
        shard_x[:4].T,
        shard_x[4],
        shard_bc[:4].T,
        shard_bc[4],
        shard_heads[0],
        shard_heads[1],
        shard_heads[2],
        shard_x[5],
    )


def solution(mesh):
    one, two = P("fs"), P("fs", None)
    tokens = P(None, ("fs", "sp"), None)
    return jax.shard_map(
        body,
        mesh=mesh,
        in_specs=(tokens, one, two, two, two, two, two, two, one, two, one, one, one, one, one, tokens),
        out_specs=(tokens, tokens, one, two, two, two, two, two, two, one, two, one, one, one, one, one),
        check_vma=False,
    )
```

```python
import functools

import jax
import jax.numpy as jnp
from jax import lax
from jax.experimental import pallas as pl
from jax.experimental.pallas import tpu as pltpu
from jax.sharding import PartitionSpec as P

EPSILON = 1e-05
F32, BF16 = jnp.float32, jnp.bfloat16
MESH = pl.DeviceIdType.MESH
CHUNK = 128
LANES = 128
PER_UNIT = 4
VMEM_LIMIT = 56 * 1024 * 1024


def dot(a, b):
    return jnp.dot(a, b, preferred_element_type=F32)


def dot_nt(a, b):
    return lax.dot_general(a, b, (((1,), (1,)), ((), ())), preferred_element_type=F32)


def dot_tn(a, b):
    return lax.dot_general(a, b, (((0,), (0,)), ((), ())), preferred_element_type=F32)


def pieces_of(v):
    high = v.astype(BF16)
    rest = v - high.astype(F32)
    middle = rest.astype(BF16)
    return high, middle, (rest - middle.astype(F32)).astype(BF16)


def exact_left(ones, v):
    return sum(dot(ones, part) for part in pieces_of(v))


def exact_right(v, ones):
    return sum(dot(part, ones) for part in pieces_of(v))


def sigmoid(v):
    return 0.5 * jnp.tanh(0.5 * v) + 0.5


def grid_iotas():
    rows = lax.broadcasted_iota(jnp.int32, (CHUNK, CHUNK), 0)
    columns = lax.broadcasted_iota(jnp.int32, (CHUNK, CHUNK), 1)
    return rows, columns


def two_heads(v, pair, low):
    return jnp.where(low, v[:, 2 * pair : 2 * pair + 1], v[:, 2 * pair + 1 : 2 * pair + 2])


def conv_of(ext, lanes, taps):
    total = taps[4:5, lanes]
    for k in range(4):
        total = total + ext[5 + k : 5 + k + CHUNK, lanes] * taps[k : k + 1, lanes]
    return total


def forward_kernel(
    x_ref, xp_ref, bc_ref, bcp_ref, step_ref, cx_ref, cbc_ref, hp_ref,
    y_ref, st_ref, own_ref, dec_ref, bcs_ref, acum_ref,
    xe, be, state, base,
):
    chunk = pl.program_id(1)
    inner = x_ref.shape[1]

    @pl.when(chunk == 0)
    def _():
        state[...] = jnp.zeros_like(state)
        base[...] = jnp.zeros_like(base)

    xe[0:8] = xp_ref[0]
    xe[8:] = x_ref[...].astype(F32)
    be[0:8] = bcp_ref[0]
    be[8:] = bc_ref[...].astype(F32)
    shared = []
    for k in range(2):
        pre = conv_of(be, slice(k * LANES, (k + 1) * LANES), cbc_ref)
        shared.append(pre * sigmoid(pre))
    keys, reads = shared
    bcs_ref[:, :LANES] = keys.astype(BF16)
    bcs_ref[:, LANES:] = reads.astype(BF16)
    keys_t = keys.T.astype(BF16)
    keys, reads = keys.astype(BF16), reads.astype(BF16)
    rows, columns = grid_iotas()
    causal = rows >= columns
    step = step_ref[...]
    running = exact_left(jnp.where(causal, 1.0, 0.0).astype(BF16), -step * hp_ref[0:1])
    acum_ref[...] = base[0:1] + running
    total = running[CHUNK - 1 : CHUNK]
    base[...] = base[...] + total
    running_t = running.T
    scores = jnp.where(causal, dot_nt(reads, keys), 0.0)
    low = columns < LANES // 2
    low_row = low[0:1]

    for pair in range(inner // LANES):
        lanes = slice(pair * LANES, (pair + 1) * LANES)
        pre = conv_of(xe, lanes, cx_ref)
        xs = pre * sigmoid(pre)
        weighted = xs * two_heads(step, pair, low)
        first = jnp.broadcast_to(running[:, 2 * pair : 2 * pair + 1], (CHUNK, CHUNK))
        second = jnp.broadcast_to(running[:, 2 * pair + 1 : 2 * pair + 2], (CHUNK, CHUNK))
        mix = jnp.concatenate(
            [
                (jnp.exp(jnp.minimum(first - running_t[2 * pair : 2 * pair + 1], 0.0)) * scores).astype(BF16),
                (jnp.exp(jnp.minimum(second - running_t[2 * pair + 1 : 2 * pair + 2], 0.0)) * scores).astype(BF16),
            ],
            axis=1,
        )
        own = weighted.astype(BF16)
        zero = jnp.zeros_like(own)
        stacked = jnp.concatenate([jnp.where(low, own, zero), jnp.where(low, zero, own)], axis=0)
        at = jnp.where(low, first, second)
        at_end = two_heads(total, pair, low_row)
        before = state[:, lanes]
        before_low = before.astype(BF16)
        st_ref[0, :, lanes] = before_low
        y = dot(mix, stacked) + dot(reads, before_low) * jnp.exp(at) + cx_ref[5:6, lanes] * xs
        y_ref[:, lanes] = y.astype(BF16)
        late = (weighted * jnp.exp(at_end - at)).astype(BF16)
        state[:, lanes] = before * jnp.exp(at_end) + dot(keys_t, late)

    @pl.when(chunk == PER_UNIT - 1)
    def _():
        own_ref[0] = state[...].astype(BF16)
        for pair in range(inner // LANES):
            lanes = slice(pair * LANES, (pair + 1) * LANES)
            dec_ref[0, :, lanes] = jnp.broadcast_to(
                jnp.exp(two_heads(base[0:1], pair, low_row)), (8, LANES)
            )


def gate_kernel(y0_ref, gate_ref, bcs_ref, acum_ref, in_ref, y_ref, gated_ref, ss_ref):
    _, columns = grid_iotas()
    low = columns < LANES // 2
    reads = bcs_ref[:, LANES:]
    reach = acum_ref[...]
    squares = jnp.zeros((CHUNK, LANES), F32)
    for pair in range(y0_ref.shape[1] // LANES):
        lanes = slice(pair * LANES, (pair + 1) * LANES)
        y = y0_ref[:, lanes].astype(F32) + dot(reads, in_ref[0, :, lanes]) * jnp.exp(
            two_heads(reach, pair, low)
        )
        y_ref[:, lanes] = y.astype(BF16)
        gate = gate_ref[:, lanes].astype(F32)
        gated = (y * gate * sigmoid(gate)).astype(BF16)
        gated_ref[:, lanes] = gated
        wide = gated.astype(F32)
        squares = squares + wide * wide
    ss_ref[...] = jnp.broadcast_to(jnp.sum(squares, axis=1, keepdims=True), (CHUNK, LANES))


def pull_kernel(
    dno_ref, gated_ref, gate_ref, y_ref, stats_ref, gain_ref, bcs_ref, acum_ref,
    dy_ref, dgate_ref, pull_ref,
    total, chunk=None,
):
    chunk = pl.program_id(1) if chunk is None else chunk

    @pl.when(chunk == 0)
    def _():
        total[...] = jnp.zeros_like(total)

    _, columns = grid_iotas()
    low = columns < LANES // 2
    scale = jnp.broadcast_to(stats_ref[:, 0:1], (CHUNK, LANES))
    mean = jnp.broadcast_to(stats_ref[:, 1:2], (CHUNK, LANES))
    reads_t = bcs_ref[:, LANES:].astype(F32).T.astype(BF16)
    reach = acum_ref[...]
    for pair in range(dno_ref.shape[1] // LANES):
        lanes = slice(pair * LANES, (pair + 1) * LANES)
        unit = gated_ref[:, lanes].astype(F32) * scale
        du = dno_ref[:, lanes].astype(F32) * gain_ref[0:1, lanes]
        d_gated = (scale * (du - unit * mean)).astype(BF16).astype(F32)
        gate = gate_ref[:, lanes].astype(F32)
        sg = sigmoid(gate)
        silu = gate * sg
        dy = d_gated * silu
        dy_ref[:, lanes] = dy.astype(BF16)
        dgate = d_gated * y_ref[:, lanes].astype(F32) * (sg + silu * (1.0 - sg))
        dgate_ref[:, lanes] = dgate.astype(BF16)
        total[:, lanes] += dot(reads_t, (dy * jnp.exp(two_heads(reach, pair, low))).astype(BF16))

    @pl.when(chunk == PER_UNIT - 1)
    def _():
        pull_ref[0] = total[...].astype(BF16)


def backward_kernel(
    x_ref, xp_ref, bc_ref, bcp_ref, step_ref, sig_ref, cx_ref, cbc_ref, hp_ref,
    dy_ref, y_ref, st_ref, in_ref, acum_ref, after_ref, pick_ref,
    dall_ref, head_ref, head_bc_ref, gx_ref, gbc_ref, gh_ref,
    xe, be, adjoint, dpx, dpb, ends, place=None,
):
    unit, chunk = (pl.program_id(0), pl.program_id(1)) if place is None else place
    inner = x_ref.shape[1]

    @pl.when((unit == 0) & (chunk == 0))
    def _():
        gx_ref[...] = jnp.zeros_like(gx_ref)
        gbc_ref[...] = jnp.zeros_like(gbc_ref)
        gh_ref[...] = jnp.zeros_like(gh_ref)

    @pl.when(chunk == 0)
    def _():
        adjoint[...] = after_ref[0].astype(F32)
        dpx[CHUNK:] = jnp.zeros((8, inner), F32)
        dpb[CHUNK:] = jnp.zeros((8, 2 * LANES), F32)

    xe[0:8] = xp_ref[0]
    xe[8:] = x_ref[...].astype(F32)
    be[0:8] = bcp_ref[0]
    be[8:] = bc_ref[...].astype(F32)
    shared, slopes = [], []
    for k in range(2):
        pre = conv_of(be, slice(k * LANES, (k + 1) * LANES), cbc_ref)
        sg = sigmoid(pre)
        shared.append(pre * sg)
        slopes.append(sg + pre * sg * (1.0 - sg))
    keys, reads = shared
    reads_t = reads.T.astype(BF16)
    keys, reads = keys.astype(BF16), reads.astype(BF16)
    rows, columns = grid_iotas()
    causal = rows >= columns
    step = step_ref[...]
    rate = hp_ref[0:1]
    log_decay = -step * rate
    running = exact_left(jnp.where(causal, 1.0, 0.0).astype(BF16), log_decay)
    total = running[CHUNK - 1 : CHUNK]
    base = acum_ref[0:1] - running[0:1]
    running_t = running.T
    scores_t = jnp.where(rows <= columns, dot_nt(keys, reads), 0.0)
    low = columns < LANES // 2
    low_row = low[0:1]
    d_scores = jnp.zeros((CHUNK, CHUNK), F32)
    d_reads = jnp.zeros((CHUNK, LANES), F32)
    d_keys = jnp.zeros((CHUNK, LANES), F32)
    sums = jnp.zeros((3 * CHUNK, LANES), F32)

    for pair in range(inner // LANES):
        lanes = slice(pair * LANES, (pair + 1) * LANES)
        shifted = [xe[5 + k : 5 + k + CHUNK, lanes] for k in range(4)]
        pre = cx_ref[4:5, lanes] + sum(shifted[k] * cx_ref[k : k + 1, lanes] for k in range(4))
        sg = sigmoid(pre)
        xs = pre * sg
        slope = sg + xs * (1.0 - sg)
        step_wide = two_heads(step, pair, low)
        weighted = xs * step_wide
        first = jnp.broadcast_to(running[:, 2 * pair : 2 * pair + 1], (CHUNK, CHUNK))
        second = jnp.broadcast_to(running[:, 2 * pair + 1 : 2 * pair + 2], (CHUNK, CHUNK))
        gap0 = first - running_t[2 * pair : 2 * pair + 1]
        gap1 = second - running_t[2 * pair + 1 : 2 * pair + 2]
        mix_t = jnp.concatenate(
            [
                (jnp.exp(jnp.minimum(-gap0, 0.0)) * scores_t).astype(BF16),
                (jnp.exp(jnp.minimum(-gap1, 0.0)) * scores_t).astype(BF16),
            ],
            axis=1,
        )
        dy_low = dy_ref[:, lanes]
        dy = dy_low.astype(F32)
        zero = jnp.zeros_like(dy_low)
        dy_two = jnp.concatenate([jnp.where(low, dy_low, zero), jnp.where(low, zero, dy_low)], axis=0)
        d_mix = dot_nt(dy_two, weighted.astype(BF16))
        d_scores = d_scores + (
            jnp.exp(jnp.minimum(gap0, 0.0)) * d_mix[:CHUNK]
            + jnp.exp(jnp.minimum(gap1, 0.0)) * d_mix[CHUNK:]
        )
        at = jnp.where(low, first, second)
        at_end = two_heads(total, pair, low_row)
        tail = jnp.exp(at_end - at)
        end_decay = jnp.exp(at_end)
        later = adjoint[:, lanes]
        later_low = later.astype(BF16)
        from_state = dot(keys, later_low) * tail
        d_weighted = dot(mix_t, dy_two) + from_state
        before = st_ref[0, :, lanes].astype(F32) + in_ref[0, :, lanes].astype(F32) * jnp.exp(
            two_heads(base, pair, low_row)
        )
        d_read = (dy * jnp.exp(at)).astype(BF16)
        d_reads = d_reads + dot_nt(d_read, before.astype(BF16))
        d_keys = d_keys + dot_nt((weighted * tail).astype(BF16), later_low)
        skip = cx_ref[5:6, lanes]
        y = y_ref[:, lanes].astype(F32) - skip * xs
        d_run = dy * y - weighted * d_weighted
        pick = pick_ref[lanes, :]
        sums = sums + dot(
            jnp.concatenate(
                [d_run.astype(BF16), (xs * d_weighted).astype(BF16), (dy * xs).astype(BF16)], axis=0
            ),
            pick,
        )
        ends[:, lanes] = jnp.broadcast_to(
            jnp.sum(weighted * from_state, axis=0, keepdims=True)
            + end_decay * jnp.sum(later * before, axis=0, keepdims=True),
            (8, LANES),
        )
        d_pre = (step_wide * d_weighted + skip * dy) * slope
        dpx[0:CHUNK, lanes] = d_pre
        adjoint[:, lanes] = later * end_decay + dot(reads_t, d_read)
        d_x = jnp.zeros((CHUNK, LANES), F32)
        for k in range(4):
            d_x = d_x + dpx[3 - k : 3 - k + CHUNK, lanes] * cx_ref[k : k + 1, lanes]
            gx_ref[8 * k : 8 * k + 8, lanes] += jnp.sum(
                (d_pre * shifted[k]).reshape(CHUNK // 8, 8, LANES), axis=0
            )
        gx_ref[32:40, lanes] += jnp.sum(d_pre.reshape(CHUNK // 8, 8, LANES), axis=0)
        dall_ref[:, lanes] = d_x.astype(BF16)

    d_scores_low = jnp.where(causal, d_scores, 0.0)
    d_reads = d_reads + dot(d_scores_low.astype(BF16), keys)
    d_keys = d_keys + dot(d_scores_low.T.astype(BF16), reads)
    for k, part in enumerate((d_keys, d_reads)):
        lanes = slice(k * LANES, (k + 1) * LANES)
        d_pre = part * slopes[k]
        dpb[0:CHUNK, lanes] = d_pre
        d_x = jnp.zeros((CHUNK, LANES), F32)
        for tap in range(4):
            d_x = d_x + dpb[3 - tap : 3 - tap + CHUNK, lanes] * cbc_ref[tap : tap + 1, lanes]
            gbc_ref[8 * tap : 8 * tap + 8, lanes] += jnp.sum(
                (d_pre * be[5 + tap : 5 + tap + CHUNK, lanes]).reshape(CHUNK // 8, 8, LANES), axis=0
            )
        gbc_ref[32:40, lanes] += jnp.sum(d_pre.reshape(CHUNK // 8, 8, LANES), axis=0)
        dall_ref[:, inner + k * LANES : inner + (k + 1) * LANES] = d_x.astype(BF16)

    at_end = exact_right(ends[...], pick_ref[...])[0:1]
    d_log = exact_left(jnp.where(rows <= columns, 1.0, 0.0).astype(BF16), sums[:CHUNK]) + at_end
    d_step = sums[CHUNK : 2 * CHUNK] - d_log * rate
    d_dt = d_step * sig_ref[...]
    dall_ref[:, inner + 2 * LANES :] = d_dt.astype(BF16)
    for k, part in enumerate((d_dt, d_log * log_decay, sums[2 * CHUNK :])):
        gh_ref[8 * k : 8 * k + 8] += jnp.sum(part.reshape(CHUNK // 8, 8, LANES), axis=0)
    dpx[CHUNK:] = dpx[0:8]
    dpb[CHUNK:] = dpb[0:8]

    @pl.when(chunk == PER_UNIT - 1)
    def _():
        head_ref[0] = dpx[0:8]
        head_bc_ref[0] = dpb[0:8]


def exchange_kernel(
    count, joints, back, own_ref, dec_ref, out_ref, dec_out_ref,
    parts, decs, results, sends, receives, dec_sends, dec_receives, back_sends, back_receives,
):
    f, z = lax.axis_index("fs"), lax.axis_index("sp")
    core, group = f % 2, z // joints
    me = (f // 2) * joints + z % joints
    units, share = own_ref.shape[0], parts.shape[2]

    def peer(k):
        other = (me + k) % count
        return other, ((other // joints) * 2 + core, group * joints + other % joints)

    barrier = pltpu.get_barrier_semaphore()
    for k in range(1, count):
        pl.semaphore_signal(barrier, inc=1, device_id=peer(k)[1], device_id_type=MESH)
    pl.semaphore_wait(barrier, count - 1)

    def rows_of(i):
        return pl.ds(pl.multiple_of(i * share, share), share)

    def out_copy(k):
        other, device = peer(k)
        return pltpu.make_async_remote_copy(
            src_ref=own_ref.at[:, rows_of(other)], dst_ref=parts.at[me],
            send_sem=sends.at[k], recv_sem=receives.at[me], device_id=device, device_id_type=MESH,
        )

    def dec_copy(k):
        return pltpu.make_async_remote_copy(
            src_ref=dec_ref, dst_ref=decs.at[me],
            send_sem=dec_sends.at[k], recv_sem=dec_receives.at[me],
            device_id=peer(k)[1], device_id_type=MESH,
        )

    def back_copy(k):
        other, device = peer(k)
        return pltpu.make_async_remote_copy(
            src_ref=results.at[other], dst_ref=out_ref.at[:, rows_of(me)],
            send_sem=back_sends.at[k], recv_sem=back_receives.at[me],
            device_id=device, device_id_type=MESH,
        )

    for k in range(1, count):
        if not back:
            dec_copy(k).start()
        out_copy(k).start()
    parts[me] = own_ref[:, rows_of(me)]
    if not back:
        decs[me] = dec_ref[...]
    else:
        decs[...] = dec_ref[...]
    for k in range(1, count):
        other = (me + k) % count
        if not back:
            pltpu.make_async_remote_copy(
                src_ref=dec_ref, dst_ref=decs.at[other],
                send_sem=dec_sends.at[k], recv_sem=dec_receives.at[other],
                device_id=peer(k)[1], device_id_type=MESH,
            ).wait_recv()
        pltpu.make_async_remote_copy(
            src_ref=own_ref.at[:, rows_of(other)], dst_ref=parts.at[other],
            send_sem=sends.at[k], recv_sem=receives.at[other],
            device_id=peer(k)[1], device_id_type=MESH,
        ).wait_recv()
    if not back:
        dec_out_ref[...] = decs[...]
    order = range(count - 1, -1, -1) if back else range(count)
    width = own_ref.shape[2]
    running = [jnp.zeros((share, width), F32) for _ in range(units)]
    for i in order:
        for u in range(units):
            results[i, u] = running[u].astype(BF16)
            running[u] = running[u] * decs[i, u : u + 1] + parts[i, u].astype(F32)
    out_ref[:, rows_of(me)] = results[me]
    for k in range(1, count):
        back_copy(k).start()
    for k in range(1, count):
        other = (me + k) % count
        pltpu.make_async_remote_copy(
            src_ref=results.at[other], dst_ref=out_ref.at[:, rows_of(other)],
            send_sem=back_sends.at[k], recv_sem=back_receives.at[other],
            device_id=peer(k)[1], device_id_type=MESH,
        ).wait_recv()
    for k in range(1, count):
        if not back:
            dec_copy(k).wait_send()
        out_copy(k).wait_send()
        back_copy(k).wait_send()


def places():
    f, z = lax.axis_index("fs"), lax.axis_index("sp")
    core, chip = f % 2, f // 2
    by_x, by_y = chip + 1 - 2 * (chip % 2), (chip + 2) % 4
    return f, z, core, chip, by_x, by_y


def remote(src, dst, sends, receives, slot, device):
    return pltpu.make_async_remote_copy(
        src_ref=src, dst_ref=dst, send_sem=sends.at[slot], recv_sem=receives.at[slot],
        device_id=device, device_id_type=MESH,
    )


def head_kernel(
    hidden, mine, other, small, rows_out, first_out, small_out, local, sends, receives, small_sends, small_receives
):
    f, z, core, chip, by_x, by_y = places()
    units = rows_out.shape[0]
    partner, over_x, over_y = (f + 1 - 2 * core, z), (2 * by_x + core, z), (2 * by_y + core, z)
    near_group, far_group = z // 2, 1 - z // 2
    near, far = (2 * chip + z % 2, 2 * near_group + core), (2 * chip + z % 2, 2 * far_group + core)
    stays = z % 2 == core
    shards = small_out.shape[0]

    barrier = pltpu.get_barrier_semaphore()
    for k in range(1, shards):
        pl.semaphore_signal(barrier, inc=1, device_id=((f + k) % shards, z), device_id_type=MESH)
    pl.semaphore_signal(barrier, inc=1, device_id=far, device_id_type=MESH)

    @pl.when(jnp.logical_not(stays))
    def _():
        pl.semaphore_signal(barrier, inc=1, device_id=near, device_id_type=MESH)

    pl.semaphore_wait(barrier, shards + (z + core) % 2)

    def group_of(g):
        return hidden.at[pl.ds(g * units, units)]

    def part(chip_at, core_at):
        return first_out.at[chip_at, core_at]

    def copy(src, dst, slot, device):
        return remote(src, dst, sends, receives, slot, device)

    to_far = copy(group_of(far_group), rows_out.at[:, z], 0, far)
    to_far.start()
    to_partner = copy(other, part(chip, core), 1, partner)
    to_partner.start()
    to_x = copy(mine, part(chip, core), 2, over_x)
    to_x.start()
    to_y = copy(mine, part(chip, core), 3, over_y)
    to_y.start()
    to_near = copy(group_of(near_group), rows_out.at[:, z], 4, near)
    keep_rows = pltpu.make_async_copy(group_of(near_group), rows_out.at[:, z], local.at[0])

    @pl.when(stays)
    def _():
        keep_rows.start()

    @pl.when(jnp.logical_not(stays))
    def _():
        to_near.start()

    keep_first = pltpu.make_async_copy(mine, part(chip, core), local.at[1])
    keep_first.start()
    keep_small = pltpu.make_async_copy(small, small_out.at[f], local.at[2])
    keep_small.start()

    def small_copy(k, at):
        return pltpu.make_async_remote_copy(
            src_ref=small, dst_ref=small_out.at[at],
            send_sem=small_sends.at[k], recv_sem=small_receives.at[at],
            device_id=((f + k) % shards, z), device_id_type=MESH,
        )

    for k in range(1, shards):
        small_copy(k, f).start()

    from_partner = copy(other, part(chip, 1 - core), 1, partner)
    from_partner.wait_recv()
    again_x = copy(part(chip, 1 - core), part(chip, 1 - core), 5, over_x)
    again_x.start()
    again_y = copy(part(chip, 1 - core), part(chip, 1 - core), 6, over_y)
    again_y.start()

    near_at, far_at = 2 * near_group + core, 2 * far_group + core

    @pl.when(stays)
    def _():
        keep_rows.wait()

    @pl.when(jnp.logical_not(stays))
    def _():
        copy(group_of(near_group), rows_out.at[:, near_at], 4, near).wait_recv()

    near_on = copy(rows_out.at[:, near_at], rows_out.at[:, near_at], 7, partner)
    near_on.start()

    copy(mine, part(by_x, core), 2, over_x).wait_recv()
    on_y = copy(part(by_x, core), part(by_x, core), 8, over_y)
    on_y.start()
    copy(mine, part(by_y, core), 3, over_y).wait_recv()
    copy(mine, part(by_x, 1 - core), 5, over_x).wait_recv()
    copy(mine, part(by_y, 1 - core), 6, over_y).wait_recv()
    on_x = copy(part(by_y, 1 - core), part(by_y, 1 - core), 9, over_x)
    on_x.start()

    copy(group_of(far_group), rows_out.at[:, far_at], 0, far).wait_recv()
    far_on = copy(rows_out.at[:, far_at], rows_out.at[:, far_at], 10, partner)
    far_on.start()

    corner = (by_x + 2) % 4
    for k in range(1, shards):
        small_copy(k, (f + k) % shards).wait_recv()
    copy(mine, part(corner, core), 8, over_y).wait_recv()
    copy(mine, part(corner, 1 - core), 9, over_x).wait_recv()
    copy(rows_out.at[:, near_at], rows_out.at[:, 2 * near_group + 1 - core], 7, partner).wait_recv()
    copy(rows_out.at[:, far_at], rows_out.at[:, 2 * far_group + 1 - core], 10, partner).wait_recv()
    for sent in (to_far, to_partner, to_x, to_y, again_x, again_y, near_on, on_y, on_x, far_on):
        sent.wait_send()

    @pl.when(jnp.logical_not(stays))
    def _():
        to_near.wait_send()

    for k in range(1, shards):
        small_copy(k, f).wait_send()
    keep_first.wait()
    keep_small.wait()


class Reduction:
    def __init__(self, pieces, sends, receives, base, special=None):
        self.f, self.z, self.core, self.chip, self.by_x, self.by_y = places()
        self.corner, self.bit = (self.by_x + 2) % 4, self.z % 2
        self.sends, self.receives, self.base, self.special = sends, receives, base, special
        self.pieces, z_start = [], 0
        for n, (start, width, way) in enumerate(pieces):
            wide = width + LANES if start == special else 2 * width
            self.pieces.append((n, start, width, way, z_start, wide))
            z_start += wide
        self.wide = z_start
        self.partner = (self.f + 1 - 2 * self.core, self.z)
        self.over = {"x": (2 * self.by_x + self.core, self.z), "y": (2 * self.by_y + self.core, self.z)}
        self.near, self.far = (self.f, self.z + 1 - 2 * self.bit), (self.f, (self.z + 2) % 4)

    @staticmethod
    def at(i, size):
        return pl.ds(pl.multiple_of(i * size, size), size)

    def copy(self, src, dst, n, k, device):
        return remote(src, dst, self.sends, self.receives, self.base + 7 * n + k, device)

    def over_chips(self, source, own, passed, r1, s2, r2, sp, rp, total):
        self.source, self.own, self.passed = source, own, passed
        self.r1, self.s2, self.r2, self.sp, self.rp, self.total = r1, s2, r2, sp, rp, total
        self.rows = r2.shape[0]

    def first_copies(self, piece):
        n, start, width, way, _, _ = piece
        columns = pl.ds(start, width)
        to = self.by_x if way == "x" else self.by_y
        return [
            self.copy(self.source(i, columns), self.r1.at[k, :, columns], n, k, self.over[way])
            for k, i in enumerate((to, self.corner))
        ]

    def second_copy(self, piece):
        n, start, width, way, _, _ = piece
        columns = pl.ds(start, width)
        other = "y" if way == "x" else "x"
        return self.copy(self.s2.at[:, columns], self.r2.at[:, columns], n, 2, self.over[other])

    def pair_copy(self, piece):
        n, start, width, _, _, _ = piece
        columns = pl.ds(start, width)
        return self.copy(self.sp.at[:, columns], self.rp.at[:, columns], n, 3, self.partner)

    def start(self):
        for piece in self.pieces:
            for copy in self.first_copies(piece):
                copy.start()

    def after_first(self, piece):
        _, start, width, way, _, _ = piece
        if self.source is not None:
            for copy in self.first_copies(piece):
                copy.wait_recv()
        columns = pl.ds(start, width)
        passed = self.passed(self.by_y if way == "x" else self.by_x, columns)
        self.s2[:, columns] = (passed.astype(F32) + self.r1[1, :, columns].astype(F32)).astype(BF16)
        self.second_copy(piece).start()

    def chip_sum(self, piece, side):
        columns = pl.ds(piece[1], piece[2])
        there = self.at(side, self.rows // 2)
        own = self.own(side, columns).astype(F32)
        return own + self.r1[0, there, columns].astype(F32) + self.r2[there, columns].astype(F32)

    def lanes_at(self, start, side, width):
        return pl.ds(pl.multiple_of(start + side * width, LANES), width)

    def after_second(self, piece):
        _, start, width, _, z_at, _ = piece
        self.second_copy(piece).wait_recv()
        self.sp[:, pl.ds(start, width)] = self.chip_sum(piece, 1 - self.core).astype(BF16)
        self.pair_copy(piece).start()

    def after_pair(self, piece):
        _, start, width, _, z_at, _ = piece
        self.pair_copy(piece).wait_recv()
        own = self.chip_sum(piece, self.core)
        came = self.rp[:, pl.ds(start, width)]
        if start == self.special:
            both = 2 * LANES
            self.total[:, pl.ds(z_at, both)] = (own[:, :both] + came[:, :both].astype(F32)).astype(BF16)
            self.total[:, self.lanes_at(z_at + both, self.core, LANES)] = own[:, both:].astype(BF16)
            self.total[:, self.lanes_at(z_at + both, 1 - self.core, LANES)] = came[:, both:]
        else:
            self.total[:, self.lanes_at(z_at, self.core, width)] = own.astype(BF16)
            self.total[:, self.lanes_at(z_at, 1 - self.core, width)] = came

    def drain_chips(self):
        for piece in self.pieces:
            firsts = [] if self.source is None else self.first_copies(piece)
            for copy in firsts + [self.second_copy(piece), self.pair_copy(piece)]:
                copy.wait_send()

    def over_members(self, total, came, sums, across, last, store):
        self.total, self.store = total, store
        self.came, self.sums, self.across, self.last = came, sums, across, last
        self.half = total.shape[0] // 2

    def z_copy(self, piece, k):
        n, _, _, _, start, wide = piece
        columns = pl.ds(start, wide)
        src, dst, device = (
            (self.total.at[self.at(1 - self.bit, self.half), columns], self.came, self.near),
            (self.sums.at[0, :, columns], self.across, self.far),
            (self.sums.at[1, :, columns], self.last, self.near),
        )[k]
        return self.copy(src, dst.at[:, columns], n, 4 + k, device)

    def start_members(self, piece):
        self.z_copy(piece, 0).start()

    def after_near(self, piece):
        columns = pl.ds(piece[4], piece[5])
        self.z_copy(piece, 0).wait_recv()
        own = self.total[self.at(self.bit, self.half), columns].astype(F32)
        self.sums[0, :, columns] = (own + self.came[:, columns].astype(F32)).astype(BF16)
        self.z_copy(piece, 1).start()

    def after_far(self, piece):
        columns = pl.ds(piece[4], piece[5])
        self.z_copy(piece, 1).wait_recv()
        total = self.sums[0, :, columns].astype(F32) + self.across[:, columns].astype(F32)
        self.sums[1, :, columns] = total.astype(BF16)
        self.z_copy(piece, 2).start()
        self.store(piece, self.at(self.bit, self.half), total.astype(BF16).astype(F32))

    def after_last(self, piece):
        self.z_copy(piece, 2).wait_recv()
        values = self.last[:, pl.ds(piece[4], piece[5])].astype(F32)
        self.store(piece, self.at(1 - self.bit, self.half), values)

    def drain_members(self):
        for piece in self.pieces:
            for k in range(3):
                self.z_copy(piece, k).wait_send()


def chip_scratch(rows, width):
    return [
        pltpu.VMEM((2, 2 * rows, width), BF16),
        pltpu.VMEM((2 * rows, width), BF16),
        pltpu.VMEM((2 * rows, width), BF16),
        pltpu.VMEM((rows, width), BF16),
        pltpu.VMEM((rows, width), BF16),
    ]


def member_scratch(rows, wide):
    half = (rows // 2, wide)
    return [
        pltpu.VMEM(half, BF16), pltpu.VMEM((2,) + half, BF16),
        pltpu.VMEM(half, BF16), pltpu.VMEM(half, BF16),
    ]


FIRST_PIECES = ((0, 512, "x"), (1024, 512, "y"), (512, 512, "x"), (1536, 384, "y"))
HALF_PIECES = ((0, 768, "x"), (768, 768, "y"))


def tail_kernel(
    g, g_x, g_bc, g_heads, g_gate, g_norm, d_part, out_x, out_bc, out_dt, vec_out, d_out,
    d_came, d_sum, local, r1, s2, r2, sp, rp, total, came, sums, across, last,
    vs, vr, sends, receives, vec_sends, vec_receives,
):
    f, z, core, chip, by_x, by_y = places()
    rows = g.shape[0] // 4
    inner = out_x.shape[1] // 2
    bit, upper, units = z % 2, z // 2, d_part.shape[0]
    first = Reduction(FIRST_PIECES, sends, receives, 0, inner)
    slot = 7 * len(FIRST_PIECES)
    partner, near, far = first.partner, first.near, first.far
    token_near, token_far = (2 * chip + bit, 2 * upper + core), (2 * chip + bit, 2 * (1 - upper) + core)
    stays = bit == core

    barrier = pltpu.get_barrier_semaphore()
    for device in (partner, first.over["x"], first.over["y"], near, far, token_far):
        pl.semaphore_signal(barrier, inc=1, device_id=device, device_id_type=MESH)

    @pl.when(jnp.logical_not(stays))
    def _():
        pl.semaphore_signal(barrier, inc=1, device_id=token_near, device_id_type=MESH)

    pl.semaphore_wait(barrier, 6 + (bit + core) % 2)

    def d_pair(k, n):
        return remote(d_part.at[:, k, 1 - core], d_came.at[:, k], sends, receives, slot + n, partner)

    def d_trade(k, n, device, group):
        return remote(
            d_sum.at[:, k], d_out.at[pl.ds(group * units, units)], sends, receives, slot + 2 + n, device
        )

    def d_add(k):
        for u in range(units):
            d_sum[u, k] = (d_part[u, k, core].astype(F32) + d_came[u, k].astype(F32)).astype(BF16)

    d_pair(1 - upper, 0).start()
    d_pair(upper, 1).start()
    d_keep = pltpu.make_async_copy(d_sum.at[:, upper], d_out.at[pl.ds(upper * units, units)], local.at[0])

    first.over_chips(
        lambda i, columns: g.at[first.at(i, rows), columns],
        lambda side, columns: g[pl.ds(pl.multiple_of(chip * rows + side * (rows // 2), rows // 2), rows // 2), columns],
        lambda i, columns: g[first.at(i, rows), columns],
        r1, s2, r2, sp, rp, total,
    )

    def store_first(piece, there, values):
        _, start, width, _, _, _ = piece
        if start == inner:
            out_bc[there, :] = values[:, : 2 * LANES]
            out_dt[there, :] = values[:, 2 * LANES :]
        else:
            out_x[there, pl.ds(start, width)] = values[:, :width]
            out_x[there, pl.ds(inner + start, width)] = values[:, width:]

    first.over_members(total, came, sums, across, last, store_first)

    vs[0] = jnp.zeros(vs.shape[1:], F32)
    for k in range(5):
        vs[0, k : k + 1] = jnp.sum(g_x[8 * k : 8 * k + 8], axis=0, keepdims=True)
        vs[0, 8 + k : 9 + k, : 2 * LANES] = jnp.sum(g_bc[8 * k : 8 * k + 8], axis=0, keepdims=True)
    vs[0, 5:6] = g_gate[...]
    vs[0, 6:7] = g_norm[...]
    for k in range(3):
        vs[0, 7:8, k * LANES : (k + 1) * LANES] = jnp.sum(
            g_heads[8 * k : 8 * k + 8], axis=0, keepdims=True
        )
    vec_ways = [first.over["x"], first.over["y"], near, far]

    def vec_copy(k):
        return remote(vs.at[k], vr.at[k], vec_sends, vec_receives, k, vec_ways[k])

    def vec_last(side):
        return remote(vec_out.at[core], vec_out.at[side], vec_sends, vec_receives, 4, partner)

    def vec_step(k):
        if k:
            vec_copy(k - 1).wait_recv()
            summed = vs[k - 1] + vr[k - 1]
            if k < 4:
                vs[k] = summed
            else:
                vec_out[core] = summed
        if k < 4:
            vec_copy(k).start()
        else:
            vec_last(core).start()

    first.start()
    vec_step(0)
    d_pair(1 - upper, 0).wait_recv()
    d_add(1 - upper)
    d_trade(1 - upper, 0, token_far, upper).start()
    d_pair(upper, 1).wait_recv()
    d_add(upper)

    @pl.when(stays)
    def _():
        d_keep.start()

    @pl.when(jnp.logical_not(stays))
    def _():
        d_trade(upper, 1, token_near, upper).start()

    early, late = first.pieces[:2], first.pieces[2:]

    def pair_on(piece):
        first.after_pair(piece)
        first.start_members(piece)

    order = (
        (first.after_first, early), (1, ()), (first.after_first, late), (2, ()),
        (first.after_second, early), (3, ()), (pair_on, early), (first.after_second, late), (4, ()),
        (first.after_near, early), (pair_on, late), (first.after_far, early),
        (first.after_near, late), (first.after_last, early),
        (first.after_far, late), (first.after_last, late),
    )
    for stage, pieces in order:
        if not pieces:
            vec_step(stage)
        for piece in pieces:
            stage(piece)
    vec_last(1 - core).wait_recv()
    d_trade(1 - upper, 0, token_far, 1 - upper).wait_recv()

    @pl.when(stays)
    def _():
        d_keep.wait()

    @pl.when(jnp.logical_not(stays))
    def _():
        d_trade(upper, 1, token_near, upper).wait()

    d_trade(1 - upper, 0, token_far, upper).wait_send()
    d_pair(1 - upper, 0).wait_send()
    d_pair(upper, 1).wait_send()
    first.drain_chips()
    first.drain_members()
    for k in range(4):
        vec_copy(k).wait_send()
    vec_last(core).wait_send()


def trade_steps(source, target, local, sends, receives):
    f, z, core, chip, _, _ = places()
    units = source.shape[0]
    bit, upper = z % 2, z // 2
    near, far = (2 * chip + bit, 2 * upper + core), (2 * chip + bit, 2 * (1 - upper) + core)
    stays = bit == core

    def copy(k, n, device, group):
        return remote(source.at[:, k], target.at[pl.ds(group * units, units)], sends, receives, n, device)

    keep = pltpu.make_async_copy(source.at[:, upper], target.at[pl.ds(upper * units, units)], local.at[0])

    def start():
        copy(1 - upper, 0, far, upper).start()

        @pl.when(stays)
        def _():
            keep.start()

        @pl.when(jnp.logical_not(stays))
        def _():
            copy(upper, 1, near, upper).start()

    def finish():
        copy(1 - upper, 0, far, 1 - upper).wait_recv()
        copy(1 - upper, 0, far, upper).wait_send()

        @pl.when(stays)
        def _():
            keep.wait()

        @pl.when(jnp.logical_not(stays))
        def _():
            copy(upper, 1, near, upper).wait()

    return start, finish, far, near, stays


class Segments:
    def __init__(self):
        self.f, self.z, self.core, self.chip, _, _ = places()
        self.group = self.z // 2
        self.me = self.chip * 2 + self.z % 2
        self.count = 8

    def peer(self, k):
        other = (self.me + k) % self.count
        return other, ((other // 2) * 2 + self.core, self.group * 2 + other % 2)


def middle_kernel(
    dno, gated, gate, y_pull, stats, gain, bcs, acum_pull, decays, normed, g_out, came_left, came_right, projected,
    x, xp, bc, bcp, step, sig, cx, cbc, hp, y, st, incoming, acum, pick,
    d_all, heads_x, heads_bc, g_x, g_bc, g_heads, d_gate_out, tokens_out, total_out, z_out,
    dy_all, dgate_all, pulled, own, after, parts, results, blocks, g_z, out_own, out_passed,
    o_r1, o_s2, o_r2, o_sp, o_rp, o_total, o_came, o_sums, o_across, o_last,
    z_r1, z_s2, z_r2, z_sp, z_rp, z_total, z_came, z_sums, z_across, z_last,
    xe, be, adjoint, dpx, dpb, ends,
    local, block_sems, trade_local, trade_sends, trade_receives, sends, receives,
    state_sends, state_receives, back_sends, back_receives,
):
    i = pl.program_id(0)
    chunks = (pl.num_programs(0) - 1) // 2
    f, z, core, chip, by_x, by_y = places()
    segments = Segments()
    me, count = segments.me, segments.count
    units, share = own.shape[0], parts.shape[2]
    rows = g_z.shape[0] // 4
    half = rows // 2
    inner = g_z.shape[1]

    def at(k, size):
        return pl.ds(pl.multiple_of(k * size, size), size)

    start_trade, finish_trade, trade_far, trade_near, stays = trade_steps(
        projected, tokens_out, trade_local, trade_sends, trade_receives
    )
    out = Reduction(HALF_PIECES, sends, receives, 0)
    gz = Reduction(HALF_PIECES, sends, receives, 7 * len(HALF_PIECES))
    out.over_chips(
        None,
        lambda side, columns: out_own[at(side, half), columns],
        lambda k, columns: out_passed[:, columns],
        o_r1, o_s2, o_r2, o_sp, o_rp, o_total,
    )

    def store_to(target):
        def store(piece, there, values):
            _, start, width, _, _, _ = piece
            target[there, pl.ds(start, width)] = values[:, :width].astype(BF16)
            target[there, pl.ds(inner + start, width)] = values[:, width:].astype(BF16)

        return store

    out.over_members(o_total, o_came, o_sums, o_across, o_last, store_to(total_out))
    gz.over_chips(
        lambda k, columns: g_z.at[at(k, rows), columns],
        lambda side, columns: g_z[pl.ds(pl.multiple_of(chip * rows + side * half, half), half), columns],
        lambda k, columns: g_z[at(k, rows), columns],
        z_r1, z_s2, z_r2, z_sp, z_rp, z_total,
    )
    gz.over_members(z_total, z_came, z_sums, z_across, z_last, store_to(z_out))
    left, right = (pl.ds(start, width) for start, width, _ in HALF_PIECES)
    own_rows = pltpu.make_async_copy(g_out.at[at(chip, rows)], out_own, local.at[0])
    pass_left = pltpu.make_async_copy(g_out.at[at(by_y, rows), left], out_passed.at[:, left], local.at[1])
    pass_right = pltpu.make_async_copy(g_out.at[at(by_x, rows), right], out_passed.at[:, right], local.at[2])
    keep_gate = pltpu.make_async_copy(dgate_all, d_gate_out, local.at[3])
    take_left = pltpu.make_async_copy(came_left, o_r1.at[:, :, left], local.at[4])
    take_right = pltpu.make_async_copy(came_right, o_r1.at[:, :, right], local.at[5])
    taken = (own_rows, pass_left, pass_right, take_left, take_right)

    def fetch(k):
        columns = pl.ds(k * rows, rows) if isinstance(k, int) else at(k, rows)
        return pltpu.make_async_copy(normed.at[:, columns], blocks.at[k % 2], block_sems.at[k % 2])

    @pl.when(i == 0)
    def _():
        barrier = pltpu.get_barrier_semaphore()
        for k in range(1, count):
            pl.semaphore_signal(barrier, inc=1, device_id=segments.peer(k)[1], device_id_type=MESH)
        for device in (out.partner, out.far, trade_far):
            pl.semaphore_signal(barrier, inc=1, device_id=device, device_id_type=MESH)

        @pl.when(jnp.logical_not(stays))
        def _():
            pl.semaphore_signal(barrier, inc=1, device_id=trade_near, device_id_type=MESH)

        pl.semaphore_wait(barrier, count + 2 + (z + core) % 2)
        for copy in taken:
            copy.start()
        start_trade()

    @pl.when(i == 2)
    def _():
        for copy in taken:
            copy.wait()
        for piece in out.pieces:
            out.after_first(piece)

    @pl.when(i == chunks - 2)
    def _():
        for piece in out.pieces:
            out.after_second(piece)

    @pl.when(i < chunks)
    def _():
        place = at(i, CHUNK)
        pull_kernel(
            dno, gated, gate, y_pull, stats, gain, bcs, acum_pull,
            dy_all.at[place], dgate_all.at[place], own.at[pl.ds(i // PER_UNIT, 1)],
            pulled, chunk=i % PER_UNIT,
        )

    def state_copy(k, at_me):
        other, device = segments.peer(k)
        src, slot = (own.at[:, at(other, share)], me) if at_me else (own.at[:, at(me, share)], other)
        return pltpu.make_async_remote_copy(
            src_ref=src, dst_ref=parts.at[slot],
            send_sem=state_sends.at[k], recv_sem=state_receives.at[slot],
            device_id=device, device_id_type=MESH,
        )

    def back_copy(k, at_me):
        other, device = segments.peer(k)
        slot = me if at_me else other
        return pltpu.make_async_remote_copy(
            src_ref=results.at[other], dst_ref=after.at[:, at(slot, share)],
            send_sem=back_sends.at[k], recv_sem=back_receives.at[slot],
            device_id=device, device_id_type=MESH,
        )

    def multiply(k):
        if k < 3:
            fetch(k + 1).start()
        fetch(k).wait()

        def part(n, carry):
            columns = pl.ds(pl.multiple_of(n * 256, 256), 256)
            product = dot_tn(blocks[k % 2], dgate_all[:, columns])
            g_z[pl.ds(k * rows, rows), columns] = product.astype(BF16)
            return carry

        lax.fori_loop(0, inner // 256, part, 0)

    @pl.when(i == chunks)
    def _():
        for k in range(1, count):
            state_copy(k, True).start()
        fetch(0).start()
        keep_gate.start()
        parts[me] = own[:, at(me, share)]
        multiply(0)
        multiply(1)
        for piece in out.pieces:
            out.after_pair(piece)
        for k in range(1, count):
            state_copy(k, False).wait_recv()
        running = [jnp.zeros((share, inner), F32) for _ in range(units)]
        for n in range(count - 1, -1, -1):
            for u in range(units):
                results[n, u] = running[u].astype(BF16)
                running[u] = running[u] * decays[n, u : u + 1] + parts[n, u].astype(F32)
        after[:, at(me, share)] = results[me]
        for k in range(1, count):
            back_copy(k, True).start()
        multiply(2)
        multiply(3)
        gz.start()
        for k in range(1, count):
            back_copy(k, False).wait_recv()
        for k in range(1, count):
            state_copy(k, True).wait_send()
            back_copy(k, True).wait_send()
        for piece in out.pieces:
            out.start_members(piece)

    def at_step(n, *stages):
        @pl.when(i == chunks + 1 + n)
        def _():
            for stage, reduction in stages:
                for piece in reduction.pieces:
                    stage(piece)

    @pl.when(i > chunks)
    def _():
        n = i - chunks - 1
        unit, chunk = n // PER_UNIT, n % PER_UNIT
        place = at(unit * PER_UNIT + PER_UNIT - 1 - chunk, CHUNK)
        backward_kernel(
            x, xp, bc, bcp, step, sig, cx, cbc, hp, dy_all.at[place], y, st, incoming, acum,
            after.at[pl.ds(unit, 1)], pick, d_all, heads_x, heads_bc, g_x, g_bc, g_heads,
            xe, be, adjoint, dpx, dpb, ends, place=(unit, chunk),
        )

    at_step(2, (out.after_near, out))
    at_step(4, (gz.after_first, gz))
    at_step(6, (out.after_far, out), (gz.after_second, gz))
    at_step(7, (gz.after_pair, gz), (gz.start_members, gz))
    at_step(8, (out.after_last, out))
    at_step(9, (gz.after_near, gz))

    @pl.when(i == 2 * chunks)
    def _():
        finish_trade()
        out.drain_chips()
        out.drain_members()
        gz.drain_chips()
        for stage in (gz.after_far, gz.after_last):
            for piece in gz.pieces:
                stage(piece)
        gz.drain_members()
        keep_gate.wait()


class Plan:
    def __init__(self, batch, tokens):
        self.shards, self.members = lax.axis_size("fs"), lax.axis_size("sp")
        self.f, self.z = lax.axis_index("fs"), lax.axis_index("sp")
        self.core = self.f % 2
        self.chips = self.shards // 2
        self.chip = self.f // 2
        self.batch, self.tokens = batch, tokens
        self.units = batch // 2
        self.joints = self.members // 2
        self.count = self.chips * self.joints
        self.group, self.joint = self.z // self.joints, self.z % self.joints
        self.fast = self.chips == 4 and self.members == 4

    def at(self, f, z):
        return f * self.members + z

    def send(self, x, pairs):
        return lax.ppermute(x, ("fs", "sp"), pairs)

    def swap(self, x, df=0, dz=0):
        pairs = [
            (self.at(f, z), self.at(f ^ df, z ^ dz))
            for f in range(self.shards)
            for z in range(self.members)
        ]
        return self.send(x, pairs)

    def along(self, x, by):
        pairs = []
        for f in range(self.shards):
            for z in range(self.members):
                place = (f // 2) * self.joints + z % self.joints + by
                if 0 <= place < self.count:
                    there = (place // self.joints) * 2 + f % 2
                    pairs.append(
                        (self.at(f, z), self.at(there, z - z % self.joints + place % self.joints))
                    )
        return self.send(x, pairs)

    def by_core(self, mine, other):
        first = self.core == 0
        return jnp.where(first, mine, other), jnp.where(first, other, mine)

    def head(self, hidden, mine, other, small):
        if not self.fast:
            both = jnp.concatenate(self.by_core(mine, self.swap(other, df=1)), axis=0)
            return self.to_units(hidden), self.gather(both), lax.all_gather(small, "fs")
        anywhere = pl.BlockSpec(memory_space=pl.ANY)
        rows, first, everyone = pl.pallas_call(
            head_kernel,
            out_shape=[
                jax.ShapeDtypeStruct((self.units, 4, self.tokens, hidden.shape[-1]), BF16),
                jax.ShapeDtypeStruct((4, 2) + mine.shape, BF16),
                jax.ShapeDtypeStruct((self.shards,) + small.shape, BF16),
            ],
            in_specs=[anywhere] * 4,
            out_specs=[anywhere] * 3,
            scratch_shapes=[
                pltpu.SemaphoreType.DMA((3,)),
                pltpu.SemaphoreType.DMA((11,)),
                pltpu.SemaphoreType.DMA((11,)),
                pltpu.SemaphoreType.DMA((self.shards,)),
                pltpu.SemaphoreType.DMA((self.shards,)),
            ],
            compiler_params=pltpu.CompilerParams(collective_id=2, has_side_effects=True),
            cost_estimate=cost(55),
            name="head",
        )(hidden, mine, other, small)
        return (
            rows.reshape(-1, rows.shape[-1]),
            first.reshape(-1, first.shape[-1]),
            everyone,
        )

    def tail(self, g, g_x, g_bc, g_heads, g_gate, g_norm, d_normed):
        rows, inner = g.shape[0] // self.shards, g_x.shape[1]
        if not self.fast:
            g = self.reduce_chips(g)
            low = self.core == 0
            kept, given = jnp.where(low, g[:rows], g[rows:]), jnp.where(low, g[rows:], g[:rows])
            came = self.swap(given.astype(BF16), df=1).astype(F32)
            total = self.reduce_members(
                jnp.concatenate(
                    list(self.by_core(kept[:, :inner], came[:, :inner]))
                    + [kept[:, inner : inner + 2 * LANES] + came[:, inner : inner + 2 * LANES]]
                    + list(self.by_core(kept[:, inner + 2 * LANES :], came[:, inner + 2 * LANES :])),
                    axis=1,
                )
            )
            wide = ((0, 0), (0, inner - 2 * LANES))
            heads = g_heads.reshape(3, 8, LANES).sum(axis=1).reshape(1, -1)
            vec = jnp.concatenate(
                [
                    g_x.reshape(5, 8, inner).sum(axis=1), g_gate, g_norm,
                    jnp.pad(heads, ((0, 0), (0, inner - 3 * LANES))),
                    jnp.pad(g_bc.reshape(5, 8, 2 * LANES).sum(axis=1), wide),
                ]
            )
            vec = self.sum_all(jnp.pad(vec, ((0, 3), (0, 0))))
            vec = jnp.stack(self.by_core(vec, self.swap(vec, df=1)))
            cut = 2 * inner + 2 * LANES
            d_rows = self.to_tokens(self.cores_sum(d_normed))
            return total[:, : 2 * inner], total[:, 2 * inner : cut], total[:, cut:], vec, d_rows
        width = g.shape[1]
        wide = 2 * inner + 4 * LANES
        vmem = pl.BlockSpec(memory_space=pltpu.VMEM)
        vec = (16, inner)
        d_shape = (self.units, 2, self.tokens, d_normed.shape[1])
        slots = 7 * len(FIRST_PIECES) + 4
        return pl.pallas_call(
            tail_kernel,
            out_shape=[
                jax.ShapeDtypeStruct((rows, 2 * inner), F32),
                jax.ShapeDtypeStruct((rows, 2 * LANES), F32),
                jax.ShapeDtypeStruct((rows, 2 * LANES), F32),
                jax.ShapeDtypeStruct((2,) + vec, F32),
                jax.ShapeDtypeStruct((self.batch, self.tokens, d_normed.shape[1]), BF16),
            ],
            in_specs=[vmem] * 7,
            out_specs=[vmem] * 5,
            scratch_shapes=[pltpu.VMEM(d_shape, BF16)] * 2
            + [pltpu.SemaphoreType.DMA((1,))]
            + chip_scratch(rows, width)
            + [pltpu.VMEM((rows, wide), BF16)]
            + member_scratch(rows, wide)
            + [pltpu.VMEM((4,) + vec, F32)] * 2
            + [pltpu.SemaphoreType.DMA((slots,))] * 2
            + [pltpu.SemaphoreType.DMA((5,))] * 2,
            compiler_params=pltpu.CompilerParams(
                collective_id=3, has_side_effects=True, vmem_limit_bytes=VMEM_LIMIT
            ),
            cost_estimate=cost(90),
            name="tail",
        )(
            g, g_x, g_bc, g_heads, g_gate, g_norm,
            d_normed.reshape(self.units, 2, 2, self.tokens, d_normed.shape[1]),
        )

    def first_hop(self, g):
        rows = g.shape[0] // 4
        by_x, by_y = self.chip + 1 - 2 * (self.chip % 2), (self.chip + 2) % 4
        corner = (by_x + 2) % 4
        blocks = g.reshape(4, rows, g.shape[1])
        found = []
        for (start, width, _), to, df in zip(HALF_PIECES, (by_x, by_y), (2, 4)):
            columns = blocks[:, :, start : start + width]
            given = [lax.dynamic_index_in_dim(columns, k, 0, False) for k in (to, corner)]
            found.append(self.swap(jnp.stack(given), df=df))
        return found

    def gather(self, x):
        groups = [list(range(c, self.shards, 2)) for c in range(2)]
        return lax.all_gather(x, "fs", axis=0, tiled=True, axis_index_groups=groups)

    def reduce_chips(self, g):
        groups = [list(range(c, self.shards, 2)) for c in range(2)]
        return lax.psum_scatter(
            g, "fs", scatter_dimension=0, tiled=True, axis_index_groups=groups
        ).astype(F32)

    def reduce_members(self, g):
        return lax.psum(g.astype(BF16), "sp").astype(F32)

    def traded(self, x, far):
        pairs = [
            (self.at(f, z), self.at(f - f % 2 + z % 2, ((z // 2) ^ far) * 2 + f % 2))
            for f in range(self.shards)
            for z in range(self.members)
        ]
        return self.send(x, pairs)

    def to_units(self, rows):
        units, width = self.units, rows.shape[-1]
        if self.fast:
            low, high = rows[:units], rows[units:]
            upper = self.z // 2 == 1
            far = self.traded(jnp.where(upper, low, high), 1)
            near = self.traded(jnp.where(upper, high, low), 0)
            mine = jnp.stack([jnp.where(upper, far, near), jnp.where(upper, near, far)], axis=1)
            pair = self.by_core(mine, self.swap(mine, df=1))
            block = jnp.stack(pair, axis=2)
        else:
            other = self.swap(rows, df=1)
            everything = lax.all_gather(jnp.stack(self.by_core(rows, other)), "sp")
            per_core = self.joints // 2
            block = lax.dynamic_slice(
                everything,
                ((self.joint % per_core) * 4, self.joint // per_core, self.group * units, 0, 0),
                (4, 1, units) + rows.shape[1:],
            )[:, 0]
            block = jnp.moveaxis(block, 0, 1)
        return block.reshape(units * 4 * self.tokens, width)

    def cores_sum(self, partial):
        units, width = self.units, partial.shape[-1]
        if self.fast:
            block = partial.reshape(units, 2, 2, self.tokens, width)
            even = self.core == 0
            mine = jnp.where(even, block[:, :, 0], block[:, :, 1])
            given = jnp.where(even, block[:, :, 1], block[:, :, 0]).astype(BF16)
            return (mine.astype(F32) + self.swap(given, df=1).astype(F32)).astype(BF16)
        return partial.astype(BF16).reshape(units, 4, self.tokens, width)

    def to_tokens(self, total):
        units, width = self.units, total.shape[-1]
        if self.fast:
            upper = self.z // 2 == 1
            far = self.traded(jnp.where(upper, total[:, 0], total[:, 1]), 1)
            near = self.traded(jnp.where(upper, total[:, 1], total[:, 0]), 0)
            return jnp.concatenate(
                [jnp.where(upper, far, near), jnp.where(upper, near, far)], axis=0
            )
        per_core = self.joints // 2
        block = total
        wide = jnp.zeros((self.members, 2, self.batch, self.tokens, width), BF16)
        wide = lax.dynamic_update_slice(
            wide,
            jnp.moveaxis(block, 1, 0)[:, None],
            ((self.joint % per_core) * 4, self.joint // per_core, self.group * units, 0, 0),
        )
        summed = lax.psum_scatter(wide, "sp", scatter_dimension=0, tiled=False)
        first = self.core == 0
        mine, given = jnp.where(first, summed[0], summed[1]), jnp.where(first, summed[1], summed[0])
        return (mine.astype(F32) + self.swap(given, df=1).astype(F32)).astype(BF16)

    def sum_all(self, x):
        if not self.fast:
            groups = [list(range(c, self.shards, 2)) for c in range(2)]
            return lax.psum(lax.psum(x, "fs", axis_index_groups=groups), "sp")
        for df, dz in ((2, 0), (4, 0), (0, 1), (0, 2)):
            x = x + self.swap(x, df, dz)
        return x


def row_scale(values):
    return lax.rsqrt(jnp.mean(values * values, axis=-1, keepdims=True) + EPSILON)


def rows_spec(width, column=0, back=False):
    def place(u, c):
        return (u * PER_UNIT + (PER_UNIT - 1 - c if back else c), column)

    return pl.BlockSpec((CHUNK, width), place)


def chunk_spec(shape, back=False):
    def place(u, c):
        return (u * PER_UNIT + (PER_UNIT - 1 - c if back else c), 0, 0)

    return pl.BlockSpec((1,) + shape, place)


def unit_spec(shape):
    return pl.BlockSpec((1,) + shape, lambda u, c: (u, 0, 0))


def whole_spec(shape):
    return pl.BlockSpec(shape, lambda u, c: (0,) * len(shape))


def cost(microseconds):
    return pl.CostEstimate(flops=int(microseconds * 1.15e9), bytes_accessed=0, transcendentals=0)


def params():
    return pltpu.CompilerParams(
        dimension_semantics=("arbitrary", "arbitrary"), vmem_limit_bytes=VMEM_LIMIT
    )


def exchange(plan, own, decays, back):
    units, depth, width = own.shape
    count = plan.count
    if depth % (16 * count):
        rates, pieces = decays[:units, None], own.astype(F32)

        def hop(_, before):
            return plan.along((before * rates + pieces).astype(BF16), -1 if back else 1).astype(F32)

        found = lax.fori_loop(0, count - 1, hop, jnp.zeros(own.shape, F32))
        return found.astype(BF16), decays
    share = depth // count
    dec_shape = (count, 8, width)
    vmem = pl.BlockSpec(memory_space=pltpu.VMEM)
    scratch = [
        pltpu.VMEM((count, units, share, width), BF16),
        pltpu.VMEM(dec_shape, F32),
        pltpu.VMEM((count, units, share, width), BF16),
    ] + [pltpu.SemaphoreType.DMA((count,))] * 6
    out_shape = [jax.ShapeDtypeStruct(own.shape, BF16)]
    if not back:
        out_shape.append(jax.ShapeDtypeStruct(dec_shape, F32))
        kernel = functools.partial(exchange_kernel, count, plan.joints, False)
    else:

        def kernel(own_ref, dec_ref, out_ref, *rest):
            exchange_kernel(count, plan.joints, True, own_ref, dec_ref, out_ref, None, *rest)

    outs = pl.pallas_call(
        kernel,
        out_shape=out_shape,
        in_specs=[vmem, vmem],
        out_specs=[vmem] * len(out_shape),
        scratch_shapes=scratch,
        compiler_params=pltpu.CompilerParams(
            collective_id=1 if back else 0, has_side_effects=True, vmem_limit_bytes=VMEM_LIMIT
        ),
        cost_estimate=cost(35),
        name="states_back" if back else "states",
    )(own, decays)
    return (outs[0], decays) if back else (outs[0], outs[1])


def body(
    hidden, norm_gain, w_z, w_x, w_bc, w_dt, w_out, conv_x, conv_x_bias, conv_bc, conv_bc_bias,
    dt_bias, a_log, skip_d, gate_gain, cotangent,
):
    batch, tokens, model = hidden.shape
    plan = Plan(batch, tokens)
    core = plan.core
    inner = w_z.shape[1] // 2
    heads = w_dt.shape[1] // 2
    head_size = inner // heads
    units = plan.units
    rows = units * 4 * tokens
    chunks = rows // CHUNK

    def halves(w):
        half = w.shape[1] // 2
        return jnp.where(core == 0, w[:, :half], w[:, half:]), jnp.where(core == 0, w[:, half:], w[:, :half])

    misc = jnp.concatenate([conv_bc_bias, dt_bias, a_log, skip_d])
    flat = jnp.concatenate(
        [conv_x.T.reshape(-1), conv_x_bias, gate_gain, norm_gain, conv_bc.T.reshape(-1), misc]
    )
    length = flat.shape[0]
    padded = -(-length // (16 * LANES)) * 16 * LANES
    flat = jnp.pad(flat, (0, padded - length)).reshape(padded // LANES, LANES)

    x_mine, x_other = halves(w_x)
    dt_mine, dt_other = halves(w_dt)
    z_mine, z_other = halves(w_z)
    o_mine, o_other = halves(w_out)
    fill = jnp.zeros((w_dt.shape[0], LANES - heads), BF16)
    first_mine = jnp.concatenate([x_mine, w_bc, dt_mine, fill], axis=1)
    first_other = jnp.concatenate([x_other, w_bc, dt_other, fill], axis=1)

    def rows_of_chip(mine, other):
        return jnp.concatenate(plan.by_core(mine, plan.swap(other, df=1)), axis=0)

    rows_gate, rows_out = rows_of_chip(z_mine, z_other), rows_of_chip(o_mine, o_other)
    weight_gate, weight_out = plan.gather(rows_gate), plan.gather(rows_out)
    hidden_rows, weight_first, everyone = plan.head(hidden, first_mine, first_other, flat)
    everyone = everyone.reshape(plan.shards, padded).astype(F32)

    parts, start = [], 0
    for shape in (
        conv_x.shape[::-1], conv_x_bias.shape, gate_gain.shape, norm_gain.shape, conv_bc.shape[::-1],
        conv_bc_bias.shape, dt_bias.shape, a_log.shape, skip_d.shape,
    ):
        size = shape[0] * (shape[1] if len(shape) > 1 else 1)
        parts.append(everyone[:, start : start + size].reshape((plan.shards,) + shape))
        start += size
    taps_x, bias_x, gain_out, gain_in, taps_bc, bias_bc, shift, rate_log, skip = parts
    gain_in = gain_in.reshape(-1)

    def mine_of(v):
        half = v.shape[0] // 2
        return lax.dynamic_slice_in_dim(v, core * half, half, 0)

    def flat_taps(v):
        return jnp.moveaxis(v, 0, 1).reshape(v.shape[1], -1)

    bias_x, gain_out, skip_mine = (mine_of(v).reshape(-1) for v in (bias_x, gain_out, skip))
    shift, rate_log = mine_of(shift).reshape(-1), mine_of(rate_log).reshape(-1)
    cx = jnp.concatenate(
        [
            flat_taps(mine_of(taps_x)), bias_x[None],
            jnp.repeat(skip_mine, head_size)[None], jnp.zeros((2, inner), F32),
        ]
    )
    cbc = jnp.concatenate(
        [flat_taps(taps_bc), bias_bc.reshape(1, -1), jnp.zeros((3, bias_bc.size), F32)]
    )
    pad_heads = (0, LANES - heads)
    rate = jnp.pad(jnp.exp(rate_log), pad_heads)
    hp = jnp.concatenate([rate[None], jnp.zeros((7, LANES), F32)])
    pick = (jnp.arange(inner)[:, None] // head_size == jnp.arange(LANES)[None, :]).astype(BF16)

    hidden_rows, cot_late = lax.optimization_barrier((hidden_rows, cotangent))
    cot_rows = plan.to_units(cot_late)

    hidden_rows = hidden_rows.astype(F32)
    scale_in = row_scale(hidden_rows)
    unit_in = hidden_rows * scale_in
    normed = (unit_in * gain_in[None]).astype(BF16)

    first = dot(normed, weight_first).astype(BF16)
    dt_shifted = first[:, inner + 2 * LANES :].astype(F32) + jnp.pad(shift, pad_heads)[None]
    step = jax.nn.softplus(dt_shifted)
    slope_dt = jax.nn.sigmoid(dt_shifted)

    tails = first[:, : inner + 2 * LANES].reshape(units, PER_UNIT, CHUNK, inner + 2 * LANES)[:, :, CHUNK - 8 :]
    before = plan.along(tails[:, PER_UNIT - 1], 1)
    tails = jnp.concatenate([before[:, None], tails[:, : PER_UNIT - 1]], axis=1).astype(F32)
    tails = tails.reshape(chunks, 8, inner + 2 * LANES)
    tail_x, tail_bc = tails[..., :inner], tails[..., inner:]

    def shaped(*shape, dtype=BF16):
        return jax.ShapeDtypeStruct(shape, dtype)

    states = (LANES, inner)
    y_own, starts, own, decays, shared, reach = pl.pallas_call(
        forward_kernel,
        grid=(units, PER_UNIT),
        in_specs=[
            rows_spec(inner), chunk_spec((8, inner)),
            rows_spec(2 * LANES, inner // (2 * LANES)), chunk_spec((8, 2 * LANES)),
            rows_spec(LANES), whole_spec(cx.shape), whole_spec(cbc.shape), whole_spec(hp.shape),
        ],
        out_specs=[
            rows_spec(inner), chunk_spec(states), unit_spec(states), unit_spec((8, inner)),
            rows_spec(2 * LANES), rows_spec(LANES),
        ],
        out_shape=[
            shaped(rows, inner), shaped(chunks, *states), shaped(units, *states),
            shaped(units, 8, inner, dtype=F32), shaped(rows, 2 * LANES), shaped(rows, LANES, dtype=F32),
        ],
        scratch_shapes=[
            pltpu.VMEM((CHUNK + 8, inner), F32), pltpu.VMEM((CHUNK + 8, 2 * LANES), F32),
            pltpu.VMEM(states, F32), pltpu.VMEM((8, LANES), F32),
        ],
        compiler_params=params(),
        cost_estimate=cost(31),
        name="scan_forward",
    )(first, tail_x, first, tail_bc, step, cx, cbc, hp)

    decay_rows = jnp.concatenate([decays[:, 0], jnp.zeros((8 - units, inner), F32)])
    incoming, all_decays = exchange(plan, own, decay_rows, False)
    gate_in = dot(normed, weight_gate).astype(BF16)

    y, gated, squares = pl.pallas_call(
        gate_kernel,
        grid=(units, PER_UNIT),
        in_specs=[
            rows_spec(inner), rows_spec(inner), rows_spec(2 * LANES), rows_spec(LANES), unit_spec(states),
        ],
        out_specs=[rows_spec(inner), rows_spec(inner), rows_spec(LANES)],
        out_shape=[shaped(rows, inner), shaped(rows, inner), shaped(rows, LANES, dtype=F32)],
        compiler_params=params(),
        cost_estimate=cost(14),
        name="gate_forward",
    )(y_own, gate_in, shared, reach, incoming)

    def pair_sum(v):
        return v + plan.swap(v, df=1)

    squares = pair_sum(squares[:, 0].reshape(chunks, CHUNK))
    scale_out = lax.rsqrt(squares / (2 * inner) + EPSILON).reshape(rows, 1)
    unit_out = gated.astype(F32) * scale_out
    normed_out = (unit_out * gain_out[None]).astype(BF16)
    projected = plan.cores_sum(dot_nt(normed_out, weight_out))

    g_out = dot_tn(cot_rows, normed_out).astype(BF16)
    g_out, weight_out, cot_rows = lax.optimization_barrier((g_out, weight_out, cot_rows))
    d_normed_out = dot(cot_rows, weight_out).astype(BF16)
    wide = d_normed_out.astype(F32)
    g_gate_gain = jnp.sum(wide * unit_out, axis=0)
    mean = pair_sum(jnp.sum(wide * gain_out[None] * unit_out, axis=1).reshape(chunks, CHUNK))
    mean = (mean / (2 * inner)).reshape(rows, 1)
    stats = jnp.concatenate([scale_out, mean, jnp.zeros((rows, LANES - 2), F32)], axis=1)
    gain_rows = jnp.broadcast_to(gain_out[None], (8, inner))

    width = inner + 3 * LANES
    back = functools.partial(rows_spec, back=True)
    if plan.fast:
        came_left, came_right = plan.first_hop(g_out)
        spots = 2 * chunks + 1
        shard_rows = model // plan.shards
        segments = plan.count
        share = LANES // segments

        def pulls(columns, column=0):
            return pl.BlockSpec((CHUNK, columns), lambda i: (jnp.minimum(i, chunks - 1), column))

        def scan_at(i):
            n = jnp.maximum(i - chunks - 1, 0)
            return n - n % PER_UNIT + PER_UNIT - 1 - n % PER_UNIT

        def scans(columns, column=0):
            return pl.BlockSpec((CHUNK, columns), lambda i: (scan_at(i), column))

        def scan_chunk(shape):
            return pl.BlockSpec((1,) + shape, lambda i: (scan_at(i), 0, 0))

        def scan_unit(shape):
            return pl.BlockSpec((1,) + shape, lambda i: (scan_at(i) // PER_UNIT, 0, 0))

        def every(shape):
            return pl.BlockSpec(shape, lambda i: (0,) * len(shape))

        anywhere = pl.BlockSpec(memory_space=pl.ANY)
        dma = pltpu.SemaphoreType.DMA
        d_all, heads_x, heads_bc, g_x, g_bc, g_heads, d_gate, projected, total_out, total_z = pl.pallas_call(
            middle_kernel,
            grid=(spots,),
            in_specs=[
                pulls(inner), pulls(inner), pulls(inner), pulls(inner), pulls(LANES), every((8, inner)),
                pulls(2 * LANES), pulls(LANES), every(all_decays.shape), anywhere, anywhere, anywhere, anywhere, anywhere,
                scans(inner), scan_chunk((8, inner)),
                scans(2 * LANES, inner // (2 * LANES)), scan_chunk((8, 2 * LANES)),
                scans(LANES), scans(LANES), every(cx.shape), every(cbc.shape), every(hp.shape),
                scans(inner), scan_chunk(states), scan_unit(states), scans(LANES), every(pick.shape),
            ],
            out_specs=[
                scans(width), scan_unit((8, inner)), scan_unit((8, 2 * LANES)),
                every((40, inner)), every((40, 2 * LANES)), every((24, LANES)),
                anywhere, anywhere, every((shard_rows, 2 * inner)), every((shard_rows, 2 * inner)),
            ],
            out_shape=[
                shaped(rows, width), shaped(units, 8, inner, dtype=F32), shaped(units, 8, 2 * LANES, dtype=F32),
                shaped(40, inner, dtype=F32), shaped(40, 2 * LANES, dtype=F32), shaped(24, LANES, dtype=F32),
                shaped(rows, inner), shaped(batch, tokens, model),
                shaped(shard_rows, 2 * inner), shaped(shard_rows, 2 * inner),
            ],
            scratch_shapes=[
                pltpu.VMEM((rows, inner), BF16), pltpu.VMEM((rows, inner), BF16), pltpu.VMEM(states, F32),
                pltpu.VMEM((units,) + states, BF16), pltpu.VMEM((units,) + states, BF16),
                pltpu.VMEM((segments, units, share, inner), BF16),
                pltpu.VMEM((segments, units, share, inner), BF16),
                pltpu.VMEM((2, rows, model // 4), BF16), pltpu.VMEM((model, inner), BF16),
                pltpu.VMEM((model // 4, inner), BF16), pltpu.VMEM((model // 4, inner), BF16),
            ]
            + chip_scratch(shard_rows, inner)
            + [pltpu.VMEM((shard_rows, 2 * inner), BF16)]
            + member_scratch(shard_rows, 2 * inner)
            + chip_scratch(shard_rows, inner)
            + [pltpu.VMEM((shard_rows, 2 * inner), BF16)]
            + member_scratch(shard_rows, 2 * inner)
            + [
                pltpu.VMEM((CHUNK + 8, inner), F32), pltpu.VMEM((CHUNK + 8, 2 * LANES), F32),
                pltpu.VMEM(states, F32),
                pltpu.VMEM((CHUNK + 8, inner), F32), pltpu.VMEM((CHUNK + 8, 2 * LANES), F32),
                pltpu.VMEM((8, inner), F32),
                dma((6,)), dma((2,)), dma((1,)), dma((2,)), dma((2,)),
                dma((14 * len(HALF_PIECES),)), dma((14 * len(HALF_PIECES),)),
                dma((segments,)), dma((segments,)), dma((segments,)), dma((segments,)),
            ],
            compiler_params=pltpu.CompilerParams(
                dimension_semantics=("arbitrary",), vmem_limit_bytes=62 * 1024 * 1024,
                collective_id=4, has_side_effects=True,
            ),
            cost_estimate=cost(125),
            name="middle",
        )(
            d_normed_out, gated, gate_in, y, stats, gain_rows, shared, reach, all_decays, normed, g_out,
            came_left, came_right, projected, first, tail_x, first, tail_bc, step, slope_dt, cx, cbc, hp, y, starts, incoming,
            reach, pick,
        )
    else:
        dy, d_gate, pull = pl.pallas_call(
            pull_kernel,
            grid=(units, PER_UNIT),
            in_specs=[
                rows_spec(inner), rows_spec(inner), rows_spec(inner), rows_spec(inner), rows_spec(LANES),
                whole_spec((8, inner)), rows_spec(2 * LANES), rows_spec(LANES),
            ],
            out_specs=[rows_spec(inner), rows_spec(inner), unit_spec(states)],
            out_shape=[shaped(rows, inner), shaped(rows, inner), shaped(units, *states)],
            scratch_shapes=[pltpu.VMEM(states, F32)],
            compiler_params=params(),
            name="gate_backward",
        )(d_normed_out, gated, gate_in, y, stats, gain_rows, shared, reach)
        after, _ = exchange(plan, pull, all_decays, True)
        d_all, heads_x, heads_bc, g_x, g_bc, g_heads = pl.pallas_call(
            backward_kernel,
            grid=(units, PER_UNIT),
            in_specs=[
                back(inner), chunk_spec((8, inner), True),
                back(2 * LANES, inner // (2 * LANES)), chunk_spec((8, 2 * LANES), True),
                back(LANES), back(LANES), whole_spec(cx.shape), whole_spec(cbc.shape), whole_spec(hp.shape),
                back(inner), back(inner), chunk_spec(states, True), unit_spec(states), back(LANES),
                unit_spec(states), whole_spec(pick.shape),
            ],
            out_specs=[
                back(width), unit_spec((8, inner)), unit_spec((8, 2 * LANES)),
                whole_spec((40, inner)), whole_spec((40, 2 * LANES)), whole_spec((24, LANES)),
            ],
            out_shape=[
                shaped(rows, width), shaped(units, 8, inner, dtype=F32), shaped(units, 8, 2 * LANES, dtype=F32),
                shaped(40, inner, dtype=F32), shaped(40, 2 * LANES, dtype=F32), shaped(24, LANES, dtype=F32),
            ],
            scratch_shapes=[
                pltpu.VMEM((CHUNK + 8, inner), F32), pltpu.VMEM((CHUNK + 8, 2 * LANES), F32),
                pltpu.VMEM(states, F32),
                pltpu.VMEM((CHUNK + 8, inner), F32), pltpu.VMEM((CHUNK + 8, 2 * LANES), F32),
                pltpu.VMEM((8, inner), F32),
            ],
            compiler_params=params(),
            name="scan_backward",
        )(
            first, tail_x, first, tail_bc, step, slope_dt, cx, cbc, hp,
            dy, y, starts, incoming, reach, after, pick,
        )
        projected = plan.to_tokens(projected)

        def over_everything(g):
            g = plan.reduce_chips(g)
            half = g.shape[0] // 2
            low = core == 0
            mine, other = jnp.where(low, g[:half], g[half:]), jnp.where(low, g[half:], g[:half])
            other = plan.swap(other.astype(BF16), df=1).astype(F32)
            return plan.reduce_members(jnp.concatenate(plan.by_core(mine, other), axis=1))

        total_out = over_everything(g_out)
        total_z = over_everything(dot_tn(normed, d_gate).astype(BF16))
    output = (hidden.astype(F32) + projected.astype(F32)).astype(BF16)

    later = plan.along(jnp.concatenate([heads_x, heads_bc], axis=2)[:, :3].astype(BF16), -1).astype(F32)
    taps = jnp.concatenate([cx[:4], cbc[:4]], axis=1)
    extra = jnp.stack(
        [sum(taps[k][None] * later[:, i - k] for k in range(i + 1)) for i in range(3)], axis=1
    )
    tail_rows = d_all.reshape(units, 4 * tokens, width)[:, 4 * tokens - 16 :].astype(F32)
    extra = jnp.pad(extra, ((0, 0), (13, 0), (0, width - extra.shape[2])))
    d_all = d_all.reshape(units, 4 * tokens, width)
    d_all = lax.dynamic_update_slice(d_all, (tail_rows + extra).astype(BF16), (0, 4 * tokens - 16, 0))
    d_all = d_all.reshape(rows, width)

    g_first = dot_tn(normed, d_all).astype(BF16)
    d_normed = dot_nt(d_gate, weight_gate) + dot_nt(d_all, weight_first)
    g_norm_gain = jnp.sum(d_normed * unit_in, axis=0)

    total_x, total_bc, total_dt, vec, grad_rows = plan.tail(
        g_first, g_x, g_bc, g_heads, g_gate_gain[None], g_norm_gain[None], d_normed.astype(BF16)
    )
    grad_rows = grad_rows.astype(F32)
    resid = hidden.astype(F32)
    own_scale = row_scale(resid)
    own_unit = resid * own_scale
    dv = grad_rows * gain_in[None, None]
    grad_hidden = cotangent.astype(F32) + own_scale * (
        dv - own_unit * jnp.mean(dv * own_unit, axis=-1, keepdims=True)
    )

    total_dt = jnp.concatenate([total_dt[:, :heads], total_dt[:, LANES : LANES + heads]], axis=1)
    whole_x = jnp.moveaxis(vec[:, :6], 0, 1).reshape(6, 2 * inner)
    whole_heads = jnp.moveaxis(vec[:, 7, : 3 * LANES].reshape(2, 3, LANES)[:, :, :heads], 0, 1)
    whole_heads = whole_heads.reshape(3, 2 * heads)
    whole_norm = vec[0, 6] + vec[1, 6]
    whole_bc = vec[0, 8:13, : 2 * LANES] + vec[1, 8:13, : 2 * LANES]

    def shard(v):
        share = v.shape[-1] // plan.shards
        return lax.dynamic_slice_in_dim(v, plan.f * share, share, v.ndim - 1)

    shard_x, shard_bc, shard_heads = shard(whole_x), shard(whole_bc), shard(whole_heads)
    return (
        output,
        grad_hidden,
        shard(whole_norm),
        total_z.astype(F32),
        total_x,
        total_bc,
        total_dt,
        total_out.astype(F32),
        shard_x[:4].T,
        shard_x[4],
        shard_bc[:4].T,
        shard_bc[4],
        shard_heads[0],
        shard_heads[1],
        shard_heads[2],
        shard_x[5],
    )


def solution(mesh):
    one, two = P("fs"), P("fs", None)
    tokens = P(None, ("fs", "sp"), None)
    return jax.shard_map(
        body,
        mesh=mesh,
        in_specs=(tokens, one, two, two, two, two, two, two, one, two, one, one, one, one, one, tokens),
        out_specs=(tokens, tokens, one, two, two, two, two, two, two, one, two, one, one, one, one, one),
        check_vma=False,
    )
```

```python
import functools

import jax
import jax.numpy as jnp
from jax import lax
from jax.experimental import pallas as pl
from jax.experimental.pallas import tpu as pltpu
from jax.sharding import PartitionSpec as P

EPSILON = 1e-05
F32, BF16 = jnp.float32, jnp.bfloat16
MESH = pl.DeviceIdType.MESH
CHUNK = 128
LANES = 128
PER_UNIT = 4
VMEM_LIMIT = 24 * 1024 * 1024
TAIL_LIMIT = 44 * 1024 * 1024
MIDDLE_LIMIT = 55 * 1024 * 1024


def dot(a, b):
    return jnp.dot(a, b, preferred_element_type=F32)


def dot_nt(a, b):
    return lax.dot_general(a, b, (((1,), (1,)), ((), ())), preferred_element_type=F32)


def dot_tn(a, b):
    return lax.dot_general(a, b, (((0,), (0,)), ((), ())), preferred_element_type=F32)


def pieces_of(v):
    high = v.astype(BF16)
    rest = v - high.astype(F32)
    middle = rest.astype(BF16)
    return high, middle, (rest - middle.astype(F32)).astype(BF16)


def exact_left(ones, v):
    return sum(dot(ones, part) for part in pieces_of(v))


def exact_right(v, ones):
    return sum(dot(part, ones) for part in pieces_of(v))


def sigmoid(v):
    return 0.5 * jnp.tanh(0.5 * v) + 0.5


def grid_iotas():
    rows = lax.broadcasted_iota(jnp.int32, (CHUNK, CHUNK), 0)
    columns = lax.broadcasted_iota(jnp.int32, (CHUNK, CHUNK), 1)
    return rows, columns


def two_heads(v, pair, low):
    return jnp.where(low, v[:, 2 * pair : 2 * pair + 1], v[:, 2 * pair + 1 : 2 * pair + 2])


def conv_of(ext, lanes, taps):
    total = taps[4:5, lanes]
    for k in range(4):
        total = total + ext[5 + k : 5 + k + CHUNK, lanes] * taps[k : k + 1, lanes]
    return total


def step_of(dt_ref, hp_ref):
    shifted = dt_ref[...].astype(F32) + hp_ref[1:2]
    return shifted, jnp.maximum(shifted, 0.0) + jnp.log1p(jnp.exp(-jnp.abs(shifted)))


def forward_kernel(
    x_ref, bc_ref, dt_ref, halo_ref, cx_ref, cbc_ref, hp_ref,
    y_ref, st_ref, own_ref, dec_ref, bcs_ref, acum_ref,
    xe, be, state, base,
):
    unit, chunk = pl.program_id(0), pl.program_id(1)
    inner = x_ref.shape[1]

    @pl.when(chunk == 0)
    def _():
        state[...] = jnp.zeros_like(state)
        base[...] = jnp.zeros_like(base)
        xe[0:8] = halo_ref[unit, :, :inner].astype(F32)[8:]
        be[0:8] = halo_ref[unit, :, inner:].astype(F32)[8:]

    @pl.when(chunk != 0)
    def _():
        xe[0:8] = xe[CHUNK:]
        be[0:8] = be[CHUNK:]

    xe[8:] = x_ref[...].astype(F32)
    be[8:] = bc_ref[...].astype(F32)
    shared = []
    for k in range(2):
        pre = conv_of(be, slice(k * LANES, (k + 1) * LANES), cbc_ref)
        shared.append(pre * sigmoid(pre))
    keys, reads = shared
    bcs_ref[:, :LANES] = keys.astype(BF16)
    bcs_ref[:, LANES:] = reads.astype(BF16)
    keys_t = keys.T.astype(BF16)
    keys, reads = keys.astype(BF16), reads.astype(BF16)
    rows, columns = grid_iotas()
    causal = rows >= columns
    _, step = step_of(dt_ref, hp_ref)
    running = exact_left(jnp.where(causal, 1.0, 0.0).astype(BF16), -step * hp_ref[0:1])
    acum_ref[...] = base[0:1] + running
    total = running[CHUNK - 1 : CHUNK]
    base[...] = base[...] + total
    running_t = running.T
    scores = jnp.where(causal, dot_nt(reads, keys), 0.0)
    low = columns < LANES // 2
    low_row = low[0:1]

    for pair in range(inner // LANES):
        lanes = slice(pair * LANES, (pair + 1) * LANES)
        pre = conv_of(xe, lanes, cx_ref)
        xs = pre * sigmoid(pre)
        weighted = xs * two_heads(step, pair, low)
        first = jnp.broadcast_to(running[:, 2 * pair : 2 * pair + 1], (CHUNK, CHUNK))
        second = jnp.broadcast_to(running[:, 2 * pair + 1 : 2 * pair + 2], (CHUNK, CHUNK))
        mix = jnp.concatenate(
            [
                (jnp.exp(jnp.minimum(first - running_t[2 * pair : 2 * pair + 1], 0.0)) * scores).astype(BF16),
                (jnp.exp(jnp.minimum(second - running_t[2 * pair + 1 : 2 * pair + 2], 0.0)) * scores).astype(BF16),
            ],
            axis=1,
        )
        own = weighted.astype(BF16)
        zero = jnp.zeros_like(own)
        stacked = jnp.concatenate([jnp.where(low, own, zero), jnp.where(low, zero, own)], axis=0)
        at = jnp.where(low, first, second)
        at_end = two_heads(total, pair, low_row)
        before = state[:, lanes]
        before_low = before.astype(BF16)
        st_ref[0, :, lanes] = before_low
        y = dot(mix, stacked) + dot(reads, before_low) * jnp.exp(at) + cx_ref[5:6, lanes] * xs
        y_ref[:, lanes] = y.astype(BF16)
        late = (weighted * jnp.exp(at_end - at)).astype(BF16)
        state[:, lanes] = before * jnp.exp(at_end) + dot(keys_t, late)

    @pl.when(chunk == PER_UNIT - 1)
    def _():
        own_ref[0] = state[...].astype(BF16)
        for pair in range(inner // LANES):
            lanes = slice(pair * LANES, (pair + 1) * LANES)
            dec_ref[0, :, lanes] = jnp.broadcast_to(
                jnp.exp(two_heads(base[0:1], pair, low_row)), (8, LANES)
            )


def gate_kernel(y0_ref, gate_ref, bcs_ref, acum_ref, in_ref, y_ref, gated_ref, ss_ref):
    _, columns = grid_iotas()
    low = columns < LANES // 2
    reads = bcs_ref[:, LANES:]
    reach = acum_ref[...]
    squares = jnp.zeros((CHUNK, LANES), F32)
    for pair in range(y0_ref.shape[1] // LANES):
        lanes = slice(pair * LANES, (pair + 1) * LANES)
        y = y0_ref[:, lanes].astype(F32) + dot(reads, in_ref[0, :, lanes]) * jnp.exp(
            two_heads(reach, pair, low)
        )
        y_ref[:, lanes] = y.astype(BF16)
        gate = gate_ref[:, lanes].astype(F32)
        gated = (y * gate * sigmoid(gate)).astype(BF16)
        gated_ref[:, lanes] = gated
        wide = gated.astype(F32)
        squares = squares + wide * wide
    ss_ref[...] = jnp.broadcast_to(jnp.sum(squares, axis=1, keepdims=True), (CHUNK, LANES))


def pull_kernel(
    dno_ref, gated_ref, gate_ref, y_ref, stats_ref, gain_ref, bcs_ref, acum_ref,
    dy_ref, dgate_ref, pull_ref,
    total, chunk=None,
):
    chunk = pl.program_id(1) if chunk is None else chunk

    @pl.when(chunk == 0)
    def _():
        total[...] = jnp.zeros_like(total)

    _, columns = grid_iotas()
    low = columns < LANES // 2
    scale = jnp.broadcast_to(stats_ref[:, 0:1], (CHUNK, LANES))
    mean = jnp.broadcast_to(stats_ref[:, 1:2], (CHUNK, LANES))
    reads_t = bcs_ref[:, LANES:].astype(F32).T.astype(BF16)
    reach = acum_ref[...]
    for pair in range(dno_ref.shape[1] // LANES):
        lanes = slice(pair * LANES, (pair + 1) * LANES)
        unit = gated_ref[:, lanes].astype(F32) * scale
        du = dno_ref[:, lanes].astype(F32) * gain_ref[0:1, lanes]
        d_gated = (scale * (du - unit * mean)).astype(BF16).astype(F32)
        gate = gate_ref[:, lanes].astype(F32)
        sg = sigmoid(gate)
        silu = gate * sg
        dy = d_gated * silu
        dy_ref[:, lanes] = dy.astype(BF16)
        dgate = d_gated * y_ref[:, lanes].astype(F32) * (sg + silu * (1.0 - sg))
        dgate_ref[:, lanes] = dgate.astype(BF16)
        total[:, lanes] += dot(reads_t, (dy * jnp.exp(two_heads(reach, pair, low))).astype(BF16))

    @pl.when(chunk == PER_UNIT - 1)
    def _():
        pull_ref[0] = total[...].astype(BF16)


def backward_kernel(
    x_ref, xp_ref, bc_ref, bcp_ref, dt_ref, halo_ref, cx_ref, cbc_ref, hp_ref,
    dy_ref, y_ref, st_ref, in_ref, acum_ref, after_ref, pick_ref,
    dall_ref, head_ref, head_bc_ref, gx_ref, gbc_ref, gh_ref,
    xe, be, adjoint, dpx, dpb, ends, place=None,
):
    unit, chunk = (pl.program_id(0), pl.program_id(1)) if place is None else place
    inner = x_ref.shape[1]

    @pl.when((unit == 0) & (chunk == 0))
    def _():
        gx_ref[...] = jnp.zeros_like(gx_ref)
        gbc_ref[...] = jnp.zeros_like(gbc_ref)
        gh_ref[...] = jnp.zeros_like(gh_ref)

    @pl.when(chunk == 0)
    def _():
        adjoint[...] = after_ref[0].astype(F32)
        dpx[CHUNK:] = jnp.zeros((8, inner), F32)
        dpb[CHUNK:] = jnp.zeros((8, 2 * LANES), F32)

    inside = chunk != PER_UNIT - 1
    xe[0:8] = jnp.where(inside, xp_ref[...].astype(F32)[8:], halo_ref[unit, :, :inner].astype(F32)[8:])
    xe[8:] = x_ref[...].astype(F32)
    be[0:8] = jnp.where(inside, bcp_ref[...].astype(F32)[8:], halo_ref[unit, :, inner:].astype(F32)[8:])
    be[8:] = bc_ref[...].astype(F32)
    shared, slopes = [], []
    for k in range(2):
        pre = conv_of(be, slice(k * LANES, (k + 1) * LANES), cbc_ref)
        sg = sigmoid(pre)
        shared.append(pre * sg)
        slopes.append(sg + pre * sg * (1.0 - sg))
    keys, reads = shared
    reads_t = reads.T.astype(BF16)
    keys, reads = keys.astype(BF16), reads.astype(BF16)
    rows, columns = grid_iotas()
    causal = rows >= columns
    shifted_dt, step = step_of(dt_ref, hp_ref)
    rate = hp_ref[0:1]
    log_decay = -step * rate
    running = exact_left(jnp.where(causal, 1.0, 0.0).astype(BF16), log_decay)
    total = running[CHUNK - 1 : CHUNK]
    base = acum_ref[0:1] - running[0:1]
    running_t = running.T
    scores_t = jnp.where(rows <= columns, dot_nt(keys, reads), 0.0)
    low = columns < LANES // 2
    low_row = low[0:1]
    d_scores = jnp.zeros((CHUNK, CHUNK), F32)
    d_reads = jnp.zeros((CHUNK, LANES), F32)
    d_keys = jnp.zeros((CHUNK, LANES), F32)
    sums = jnp.zeros((3 * CHUNK, LANES), F32)

    for pair in range(inner // LANES):
        lanes = slice(pair * LANES, (pair + 1) * LANES)
        shifted = [xe[5 + k : 5 + k + CHUNK, lanes] for k in range(4)]
        pre = cx_ref[4:5, lanes] + sum(shifted[k] * cx_ref[k : k + 1, lanes] for k in range(4))
        sg = sigmoid(pre)
        xs = pre * sg
        slope = sg + xs * (1.0 - sg)
        step_wide = two_heads(step, pair, low)
        weighted = xs * step_wide
        first = jnp.broadcast_to(running[:, 2 * pair : 2 * pair + 1], (CHUNK, CHUNK))
        second = jnp.broadcast_to(running[:, 2 * pair + 1 : 2 * pair + 2], (CHUNK, CHUNK))
        gap0 = first - running_t[2 * pair : 2 * pair + 1]
        gap1 = second - running_t[2 * pair + 1 : 2 * pair + 2]
        mix_t = jnp.concatenate(
            [
                (jnp.exp(jnp.minimum(-gap0, 0.0)) * scores_t).astype(BF16),
                (jnp.exp(jnp.minimum(-gap1, 0.0)) * scores_t).astype(BF16),
            ],
            axis=1,
        )
        dy_low = dy_ref[:, lanes]
        dy = dy_low.astype(F32)
        zero = jnp.zeros_like(dy_low)
        dy_two = jnp.concatenate([jnp.where(low, dy_low, zero), jnp.where(low, zero, dy_low)], axis=0)
        d_mix = dot_nt(dy_two, weighted.astype(BF16))
        d_scores = d_scores + (
            jnp.exp(jnp.minimum(gap0, 0.0)) * d_mix[:CHUNK]
            + jnp.exp(jnp.minimum(gap1, 0.0)) * d_mix[CHUNK:]
        )
        at = jnp.where(low, first, second)
        at_end = two_heads(total, pair, low_row)
        tail = jnp.exp(at_end - at)
        end_decay = jnp.exp(at_end)
        later = adjoint[:, lanes]
        later_low = later.astype(BF16)
        from_state = dot(keys, later_low) * tail
        d_weighted = dot(mix_t, dy_two) + from_state
        before = st_ref[0, :, lanes].astype(F32) + in_ref[0, :, lanes].astype(F32) * jnp.exp(
            two_heads(base, pair, low_row)
        )
        d_read = (dy * jnp.exp(at)).astype(BF16)
        d_reads = d_reads + dot_nt(d_read, before.astype(BF16))
        d_keys = d_keys + dot_nt((weighted * tail).astype(BF16), later_low)
        skip = cx_ref[5:6, lanes]
        y = y_ref[:, lanes].astype(F32) - skip * xs
        d_run = dy * y - weighted * d_weighted
        pick = pick_ref[lanes, :]
        sums = sums + dot(
            jnp.concatenate(
                [d_run.astype(BF16), (xs * d_weighted).astype(BF16), (dy * xs).astype(BF16)], axis=0
            ),
            pick,
        )
        ends[:, lanes] = jnp.broadcast_to(
            jnp.sum(weighted * from_state, axis=0, keepdims=True)
            + end_decay * jnp.sum(later * before, axis=0, keepdims=True),
            (8, LANES),
        )
        d_pre = (step_wide * d_weighted + skip * dy) * slope
        dpx[0:CHUNK, lanes] = d_pre
        adjoint[:, lanes] = later * end_decay + dot(reads_t, d_read)
        d_x = jnp.zeros((CHUNK, LANES), F32)
        for k in range(4):
            d_x = d_x + dpx[3 - k : 3 - k + CHUNK, lanes] * cx_ref[k : k + 1, lanes]
            gx_ref[8 * k : 8 * k + 8, lanes] += jnp.sum(
                (d_pre * shifted[k]).reshape(CHUNK // 8, 8, LANES), axis=0
            )
        gx_ref[32:40, lanes] += jnp.sum(d_pre.reshape(CHUNK // 8, 8, LANES), axis=0)
        dall_ref[:, lanes] = d_x.astype(BF16)

    d_scores_low = jnp.where(causal, d_scores, 0.0)
    d_reads = d_reads + dot(d_scores_low.astype(BF16), keys)
    d_keys = d_keys + dot(d_scores_low.T.astype(BF16), reads)
    for k, part in enumerate((d_keys, d_reads)):
        lanes = slice(k * LANES, (k + 1) * LANES)
        d_pre = part * slopes[k]
        dpb[0:CHUNK, lanes] = d_pre
        d_x = jnp.zeros((CHUNK, LANES), F32)
        for tap in range(4):
            d_x = d_x + dpb[3 - tap : 3 - tap + CHUNK, lanes] * cbc_ref[tap : tap + 1, lanes]
            gbc_ref[8 * tap : 8 * tap + 8, lanes] += jnp.sum(
                (d_pre * be[5 + tap : 5 + tap + CHUNK, lanes]).reshape(CHUNK // 8, 8, LANES), axis=0
            )
        gbc_ref[32:40, lanes] += jnp.sum(d_pre.reshape(CHUNK // 8, 8, LANES), axis=0)
        dall_ref[:, inner + k * LANES : inner + (k + 1) * LANES] = d_x.astype(BF16)

    at_end = exact_right(ends[...], pick_ref[...])[0:1]
    d_log = exact_left(jnp.where(rows <= columns, 1.0, 0.0).astype(BF16), sums[:CHUNK]) + at_end
    d_step = sums[CHUNK : 2 * CHUNK] - d_log * rate
    d_dt = d_step * sigmoid(shifted_dt)
    dall_ref[:, inner + 2 * LANES :] = d_dt.astype(BF16)
    for k, part in enumerate((d_dt, d_log * log_decay, sums[2 * CHUNK :])):
        gh_ref[8 * k : 8 * k + 8] += jnp.sum(part.reshape(CHUNK // 8, 8, LANES), axis=0)
    dpx[CHUNK:] = dpx[0:8]
    dpb[CHUNK:] = dpb[0:8]

    @pl.when(chunk == PER_UNIT - 1)
    def _():
        head_ref[0] = dpx[0:8]
        head_bc_ref[0] = dpb[0:8]


def exchange_kernel(
    own_ref, dec_ref, cot, near_ref, far_ref, out_ref, dec_out_ref, rows_out,
    parts, decs, results, sends, receives, dec_sends, dec_receives, back_sends, back_receives,
    row_sends, row_receives, local,
):
    count, joints, back = 8, 2, False
    trade = Trade(cot, row_sends, row_receives)
    f, z = lax.axis_index("fs"), lax.axis_index("sp")
    core, group = f % 2, z // joints
    me = (f // 2) * joints + z % joints
    units, share = own_ref.shape[0], parts.shape[2]

    def peer(k):
        other = (me + k) % count
        return other, ((other // joints) * 2 + core, group * joints + other % joints)

    barrier = pltpu.get_barrier_semaphore()
    for k in range(1, count):
        pl.semaphore_signal(barrier, inc=1, device_id=peer(k)[1], device_id_type=MESH)
    for device in (trade.partner, trade.far):
        pl.semaphore_signal(barrier, inc=1, device_id=device, device_id_type=MESH)
    pl.semaphore_wait(barrier, count + 1)
    early = far_ref.shape[0]
    near_at, far_at = trade.near_at, trade.far_at
    last = trade.send(trade.rows_for(trade.far_group, early, units), rows_out.at[early:, z], 0, trade.far)
    last.start()
    near_on = trade.send(near_ref, rows_out.at[:, near_at], 1, trade.partner)
    near_on.start()
    far_on = trade.send(far_ref, rows_out.at[:early, far_at], 2, trade.partner)
    far_on.start()
    near_keep = pltpu.make_async_copy(near_ref, rows_out.at[:, near_at], local.at[0])
    near_keep.start()
    far_keep = pltpu.make_async_copy(far_ref, rows_out.at[:early, far_at], local.at[1])
    far_keep.start()

    def rows_of(i):
        return pl.ds(pl.multiple_of(i * share, share), share)

    def out_copy(k):
        other, device = peer(k)
        return pltpu.make_async_remote_copy(
            src_ref=own_ref.at[:, rows_of(other)], dst_ref=parts.at[me],
            send_sem=sends.at[k], recv_sem=receives.at[me], device_id=device, device_id_type=MESH,
        )

    def dec_copy(k):
        return pltpu.make_async_remote_copy(
            src_ref=dec_ref, dst_ref=decs.at[me],
            send_sem=dec_sends.at[k], recv_sem=dec_receives.at[me],
            device_id=peer(k)[1], device_id_type=MESH,
        )

    def back_copy(k):
        other, device = peer(k)
        return pltpu.make_async_remote_copy(
            src_ref=results.at[other], dst_ref=out_ref.at[:, rows_of(me)],
            send_sem=back_sends.at[k], recv_sem=back_receives.at[me],
            device_id=device, device_id_type=MESH,
        )

    for k in range(1, count):
        if not back:
            dec_copy(k).start()
        out_copy(k).start()
    parts[me] = own_ref[:, rows_of(me)]
    if not back:
        decs[me] = dec_ref[...]
    else:
        decs[...] = dec_ref[...]
    for k in range(1, count):
        other = (me + k) % count
        if not back:
            pltpu.make_async_remote_copy(
                src_ref=dec_ref, dst_ref=decs.at[other],
                send_sem=dec_sends.at[k], recv_sem=dec_receives.at[other],
                device_id=peer(k)[1], device_id_type=MESH,
            ).wait_recv()
        pltpu.make_async_remote_copy(
            src_ref=own_ref.at[:, rows_of(other)], dst_ref=parts.at[other],
            send_sem=sends.at[k], recv_sem=receives.at[other],
            device_id=peer(k)[1], device_id_type=MESH,
        ).wait_recv()
    if not back:
        dec_out_ref[...] = decs[...]
    order = range(count - 1, -1, -1) if back else range(count)
    width = own_ref.shape[2]
    running = [jnp.zeros((share, width), F32) for _ in range(units)]
    for i in order:
        for u in range(units):
            results[i, u] = running[u].astype(BF16)
            running[u] = running[u] * decs[i, u : u + 1] + parts[i, u].astype(F32)
    out_ref[:, rows_of(me)] = results[me]
    for k in range(1, count):
        back_copy(k).start()
    trade.send(trade.rows_for(trade.far_group, early, units), rows_out.at[early:, far_at], 0, trade.far).wait_recv()
    last_on = trade.send(rows_out.at[early:, far_at], rows_out.at[early:, far_at], 3, trade.partner)
    last_on.start()
    for k in range(1, count):
        other = (me + k) % count
        pltpu.make_async_remote_copy(
            src_ref=results.at[other], dst_ref=out_ref.at[:, rows_of(other)],
            send_sem=back_sends.at[k], recv_sem=back_receives.at[other],
            device_id=peer(k)[1], device_id_type=MESH,
        ).wait_recv()
    for k in range(1, count):
        if not back:
            dec_copy(k).wait_send()
        out_copy(k).wait_send()
        back_copy(k).wait_send()
    other_near, other_far = trade.swapped(near_at), trade.swapped(far_at)
    trade.send(near_ref, rows_out.at[:, other_near], 1, trade.partner).wait_recv()
    trade.send(far_ref, rows_out.at[:early, other_far], 2, trade.partner).wait_recv()
    trade.send(rows_out.at[early:, far_at], rows_out.at[early:, other_far], 3, trade.partner).wait_recv()
    for copy in (last, near_on, far_on, last_on):
        copy.wait_send()
    near_keep.wait()
    far_keep.wait()


def places():
    f, z = lax.axis_index("fs"), lax.axis_index("sp")
    core, chip = f % 2, f // 2
    by_x, by_y = chip + 1 - 2 * (chip % 2), (chip + 2) % 4
    return f, z, core, chip, by_x, by_y


def remote(src, dst, sends, receives, slot, device):
    return pltpu.make_async_remote_copy(
        src_ref=src, dst_ref=dst, send_sem=sends.at[slot], recv_sem=receives.at[slot],
        device_id=device, device_id_type=MESH,
    )


class Trade:
    def __init__(self, source, sends, receives):
        self.f, self.z, self.core, self.chip, _, _ = places()
        self.source, self.sends, self.receives = source, sends, receives
        self.units = source.shape[0] // 2
        self.near_group, self.far_group = self.z // 2, 1 - self.z // 2
        across = 2 * self.chip + self.z % 2
        self.near, self.far = (across, 2 * self.near_group + self.core), (across, 2 * self.far_group + self.core)
        self.near_at, self.far_at = 2 * self.near_group + self.core, 2 * self.far_group + self.core
        self.partner = (self.f + 1 - 2 * self.core, self.z)
        self.stays = self.z % 2 == self.core
        self.moves = (self.z + self.core) % 2

    def rows_for(self, group, first, last):
        return self.source.at[pl.ds(group * self.units + first, last - first)]

    def swapped(self, at):
        return at + 1 - 2 * (at % 2)

    def send(self, src, dst, slot, device):
        return remote(src, dst, self.sends, self.receives, slot, device)


EARLY_UNITS = 2


def scan_forward_kernel(
    x, bc, dt, first, cot, cx, cbc, hp,
    y, st, own, dec, bcs, acum, halo_out, near_out, far_out,
    xe, be, state, base, halo, halo_sends, halo_receives, sends, receives, local,
):
    unit, chunk = pl.program_id(0), pl.program_id(1)
    segments, trade = Segments(), Trade(cot, sends, receives)
    me, last = segments.me, segments.count - 1
    units, depth, width = halo.shape

    def halo_copy():
        at = pl.ds(first.shape[1] - depth, depth)
        device = segments.device((me + 1) % segments.count)
        return remote(first.at[:, at, pl.ds(0, width)], halo, halo_sends, halo_receives, 0, device)

    far_copy = trade.send(trade.rows_for(trade.far_group, 0, EARLY_UNITS), far_out, 0, trade.far)
    near_copy = trade.send(trade.rows_for(trade.near_group, 0, units), near_out, 1, trade.near)
    keep = pltpu.make_async_copy(trade.rows_for(trade.near_group, 0, units), near_out, local.at[0])

    @pl.when((unit == 0) & (chunk == 0))
    def _():
        barrier = pltpu.get_barrier_semaphore()
        pl.semaphore_signal(barrier, inc=1, device_id=trade.far, device_id_type=MESH)

        @pl.when(jnp.logical_not(trade.stays))
        def _():
            pl.semaphore_signal(barrier, inc=1, device_id=trade.near, device_id_type=MESH)

        @pl.when(me > 0)
        def _():
            pl.semaphore_signal(
                barrier, inc=1, device_id=segments.device((me + last) % segments.count), device_id_type=MESH
            )

        pl.semaphore_wait(barrier, 1 + trade.moves + jnp.where(me < last, 1, 0))

        @pl.when(me < last)
        def _():
            halo_copy().start()

        far_copy.start()

        @pl.when(trade.stays)
        def _():
            keep.start()

        @pl.when(jnp.logical_not(trade.stays))
        def _():
            near_copy.start()

        @pl.when(me > 0)
        def _():
            halo_copy().wait_recv()

        @pl.when(me == 0)
        def _():
            halo[...] = jnp.zeros_like(halo)

        halo_out[...] = halo[...]

    forward_kernel(x, bc, dt, halo, cx, cbc, hp, y, st, own, dec, bcs, acum, xe, be, state, base)

    @pl.when((unit == units - 1) & (chunk == PER_UNIT - 1))
    def _():
        @pl.when(me < last)
        def _():
            halo_copy().wait_send()

        far_copy.wait()

        @pl.when(trade.stays)
        def _():
            keep.wait()

        @pl.when(jnp.logical_not(trade.stays))
        def _():
            near_copy.wait()


def one_hot(rows, columns, offset):
    i = lax.broadcasted_iota(jnp.int32, (rows, columns), 0)
    j = lax.broadcasted_iota(jnp.int32, (rows, columns), 1)
    return jnp.where(j == i + offset, 1.0, 0.0).astype(BF16)


SMALL_ROWS = 32


def head_kernel(
    hidden, w_x, w_bc, w_dt, conv_x, conv_x_bias, gate_gain, norm_gain, conv_bc, conv_bc_bias, dt_bias, a_log, skip_d,
    rows_out, first_out, cx, cbc, hp, gain_in, gain_rows,
    dt_mine, dt_other, small, small_all, local, sends, receives, small_sends, small_receives,
):
    f, z, core, chip, by_x, by_y = places()
    trade = Trade(hidden, sends, receives)
    partner, over_x, over_y = trade.partner, (2 * by_x + core, z), (2 * by_y + core, z)
    far, near, stays = trade.far, trade.near, trade.stays
    units, inner, shards = rows_out.shape[0], cx.shape[1], small_all.shape[0]
    heads = w_dt.shape[1] // 2

    barrier = pltpu.get_barrier_semaphore()
    for k in range(1, shards):
        pl.semaphore_signal(barrier, inc=1, device_id=((f + k) % shards, z), device_id_type=MESH)
    pl.semaphore_signal(barrier, inc=1, device_id=far, device_id_type=MESH)

    @pl.when(jnp.logical_not(stays))
    def _():
        pl.semaphore_signal(barrier, inc=1, device_id=near, device_id_type=MESH)

    pl.semaphore_wait(barrier, shards + trade.moves)

    def part(chip_at, core_at):
        return first_out.at[chip_at, core_at]

    def copy(src, dst, slot, device):
        return remote(src, dst, sends, receives, slot, device)

    class Thirds:
        def __init__(self, side, slot, device):
            columns = pl.ds(pl.multiple_of(side * inner, inner), inner)
            self.whole = copy(part(chip, core), part(chip, core), slot, device)
            dst, wide = part(chip, core), 2 * LANES
            dt = dt_mine if device is not partner else dt_other
            self.copies = [
                copy(w_x.at[:, columns], dst.at[:, pl.ds(0, inner)], slot, device),
                copy(w_bc, dst.at[:, pl.ds(inner, wide)], slot, device),
                copy(dt, dst.at[:, pl.ds(inner + wide, LANES)], slot, device),
            ]

        def start(self):
            for one in self.copies:
                one.start()

        def wait_send(self):
            self.whole.wait_send()

    to_far = copy(trade.rows_for(trade.far_group, 0, units), rows_out.at[:, z], 0, far)
    to_far.start()
    i = lax.broadcasted_iota(jnp.int32, (2 * heads, LANES), 0)
    j = lax.broadcasted_iota(jnp.int32, (2 * heads, LANES), 1)
    for side, kept in ((core, dt_mine), (1 - core, dt_other)):
        chosen = jnp.where((i == j + side * heads) & (j < heads), 1.0, 0.0).astype(BF16)
        kept[...] = dot(w_dt[...], chosen).astype(BF16)
    to_partner, to_x, to_y = Thirds(1 - core, 1, partner), Thirds(core, 2, over_x), Thirds(core, 3, over_y)
    for one in (to_partner, to_x, to_y):
        one.start()
    to_near = copy(trade.rows_for(trade.near_group, 0, units), rows_out.at[:, z], 4, near)
    keep_rows = pltpu.make_async_copy(trade.rows_for(trade.near_group, 0, units), rows_out.at[:, z], local.at[0])

    @pl.when(stays)
    def _():
        keep_rows.start()

    @pl.when(jnp.logical_not(stays))
    def _():
        to_near.start()

    own = part(chip, core)
    keeps = [
        pltpu.make_async_copy(
            w_x.at[:, pl.ds(pl.multiple_of(core * inner, inner), inner)], own.at[:, pl.ds(0, inner)], local.at[1]
        ),
        pltpu.make_async_copy(w_bc, own.at[:, pl.ds(inner, 2 * LANES)], local.at[2]),
        pltpu.make_async_copy(dt_mine, own.at[:, pl.ds(inner + 2 * LANES, LANES)], local.at[3]),
    ]
    for keep in keeps:
        keep.start()

    share = conv_x.shape[0]
    per_norm, per_bc, per_head = norm_gain.shape[1], conv_bc.shape[0], dt_bias.shape[1]
    built = jnp.zeros((SMALL_ROWS, share), F32)
    taps = dot_tn(conv_x[...], one_hot(share, share, 0))
    gains = dot(norm_gain[...], one_hot(per_norm, share, per_norm * (f % 2)))
    spread_bc = one_hot(per_bc, 2 * LANES, per_bc * f)
    taps_bc, bias_bc = dot_tn(conv_bc[...], spread_bc), dot(conv_bc_bias[...], spread_bc)
    spread_heads = one_hot(per_head, LANES, per_head * (f % 4))
    by_head = [dot(v[...], spread_heads) for v in (dt_bias, a_log, skip_d)]
    small[...] = built
    small[0:4] = taps
    small[4:5] = conv_x_bias[...].astype(F32)
    small[5:6] = gate_gain[...].astype(F32)
    for k in range(4):
        small[6 + k : 7 + k] = jnp.where(f // 2 == k, gains, 0.0)
    small[10:14, : 2 * LANES] = taps_bc
    small[14:15, : 2 * LANES] = bias_bc
    for side in range(2):
        for n, values in enumerate(by_head):
            small[15 + side : 16 + side, n * LANES : (n + 1) * LANES] = jnp.where(f // 4 == side, values, 0.0)

    def small_copy(k, at):
        return pltpu.make_async_remote_copy(
            src_ref=small, dst_ref=small_all.at[at],
            send_sem=small_sends.at[k], recv_sem=small_receives.at[at],
            device_id=((f + k) % shards, z), device_id_type=MESH,
        )

    for k in range(1, shards):
        small_copy(k, f).start()
    small_all[f] = small[...]

    copy(part(chip, core), part(chip, 1 - core), 1, partner).wait_recv()
    again_x = copy(part(chip, 1 - core), part(chip, 1 - core), 5, over_x)
    again_x.start()
    again_y = copy(part(chip, 1 - core), part(chip, 1 - core), 6, over_y)
    again_y.start()

    near_at, far_at = trade.near_at, trade.far_at

    @pl.when(stays)
    def _():
        keep_rows.wait()

    @pl.when(jnp.logical_not(stays))
    def _():
        copy(trade.rows_for(trade.near_group, 0, units), rows_out.at[:, near_at], 4, near).wait_recv()

    near_on = copy(rows_out.at[:, near_at], rows_out.at[:, near_at], 7, partner)
    near_on.start()

    for k in range(1, shards):
        small_copy(k, (f + k) % shards).wait_recv()
    cx[...] = jnp.zeros_like(cx)
    for k in range(4):
        block = small_all[4 * core + k]
        lanes = slice(k * share, (k + 1) * share)
        cx[0:5, lanes] = block[0:5]
        gain_rows[:, lanes] = jnp.broadcast_to(block[5:6], (8, share))
    summed = small_all[0]
    for k in range(1, shards):
        summed = summed + small_all[k]
    for k in range(4):
        gain_in[:, k * share : (k + 1) * share] = jnp.broadcast_to(summed[6 + k : 7 + k], (8, share))
    cbc[...] = jnp.zeros_like(cbc)
    cbc[0:5] = summed[10:15, : 2 * LANES]
    ours = jnp.where(core == 0, summed[15:16], summed[16:17])
    lane = lax.broadcasted_iota(jnp.int32, (1, LANES), 1)
    hp[...] = jnp.zeros_like(hp)
    hp[0:1] = jnp.where(lane < heads, jnp.exp(ours[:, LANES : 2 * LANES]), 0.0)
    hp[1:2] = ours[:, :LANES]
    skips = ours[:, 2 * LANES :]
    for pair in range(inner // LANES):
        cx[5:6, pair * LANES : (pair + 1) * LANES] = two_heads(skips, pair, lane < LANES // 2)

    copy(part(by_x, core), part(by_x, core), 2, over_x).wait_recv()
    on_y = copy(part(by_x, core), part(by_x, core), 8, over_y)
    on_y.start()
    copy(part(by_y, core), part(by_y, core), 3, over_y).wait_recv()
    copy(part(by_x, 1 - core), part(by_x, 1 - core), 5, over_x).wait_recv()
    copy(part(by_y, 1 - core), part(by_y, 1 - core), 6, over_y).wait_recv()
    on_x = copy(part(by_y, 1 - core), part(by_y, 1 - core), 9, over_x)
    on_x.start()

    copy(trade.rows_for(trade.far_group, 0, units), rows_out.at[:, far_at], 0, far).wait_recv()
    far_on = copy(rows_out.at[:, far_at], rows_out.at[:, far_at], 10, partner)
    far_on.start()

    corner = (by_x + 2) % 4
    copy(part(corner, core), part(corner, core), 8, over_y).wait_recv()
    copy(part(corner, 1 - core), part(corner, 1 - core), 9, over_x).wait_recv()
    copy(rows_out.at[:, near_at], rows_out.at[:, trade.swapped(near_at)], 7, partner).wait_recv()
    copy(rows_out.at[:, far_at], rows_out.at[:, trade.swapped(far_at)], 10, partner).wait_recv()
    for sent in (to_far, to_partner, to_x, to_y, again_x, again_y, near_on, on_y, on_x, far_on):
        sent.wait_send()

    @pl.when(jnp.logical_not(stays))
    def _():
        to_near.wait_send()

    for k in range(1, shards):
        small_copy(k, f).wait_send()
    for keep in keeps:
        keep.wait()


class Reduction:
    def __init__(self, pieces, sends, receives, base, special=None):
        self.f, self.z, self.core, self.chip, self.by_x, self.by_y = places()
        self.corner, self.bit = (self.by_x + 2) % 4, self.z % 2
        self.sends, self.receives, self.base, self.special = sends, receives, base, special
        self.pieces, z_start = [], 0
        for n, (start, width, way) in enumerate(pieces):
            wide = width + LANES if start == special else 2 * width
            self.pieces.append((n, start, width, way, z_start, wide))
            z_start += wide
        self.wide = z_start
        self.partner = (self.f + 1 - 2 * self.core, self.z)
        self.over = {"x": (2 * self.by_x + self.core, self.z), "y": (2 * self.by_y + self.core, self.z)}
        self.near, self.far = (self.f, self.z + 1 - 2 * self.bit), (self.f, (self.z + 2) % 4)

    @staticmethod
    def at(i, size):
        return pl.ds(pl.multiple_of(i * size, size), size)

    def copy(self, src, dst, n, k, device):
        return remote(src, dst, self.sends, self.receives, self.base + 7 * n + k, device)

    def over_chips(self, source, own, passed, r1, s2, r2, sp, rp, total):
        self.source, self.own, self.passed = source, own, passed
        self.r1, self.s2, self.r2, self.sp, self.rp, self.total = r1, s2, r2, sp, rp, total
        self.rows = r2.shape[0]

    def first_copies(self, piece):
        n, start, width, way, _, _ = piece
        columns = pl.ds(start, width)
        to = self.by_x if way == "x" else self.by_y
        return [
            self.copy(self.source(i, columns), self.r1.at[k, :, columns], n, k, self.over[way])
            for k, i in enumerate((to, self.corner))
        ]

    def second_copy(self, piece):
        n, start, width, way, _, _ = piece
        columns = pl.ds(start, width)
        other = "y" if way == "x" else "x"
        return self.copy(self.s2.at[:, columns], self.r2.at[:, columns], n, 2, self.over[other])

    def pair_copy(self, piece):
        n, start, width, _, _, _ = piece
        columns = pl.ds(start, width)
        return self.copy(self.sp.at[:, columns], self.rp.at[:, columns], n, 3, self.partner)

    def start(self):
        for piece in self.pieces:
            for copy in self.first_copies(piece):
                copy.start()

    def after_first(self, piece):
        _, start, width, way, _, _ = piece
        if self.source is not None:
            for copy in self.first_copies(piece):
                copy.wait_recv()
        columns = pl.ds(start, width)
        passed = self.passed(self.by_y if way == "x" else self.by_x, columns)
        self.s2[:, columns] = (passed.astype(F32) + self.r1[1, :, columns].astype(F32)).astype(BF16)
        self.second_copy(piece).start()

    def chip_sum(self, piece, side):
        columns = pl.ds(piece[1], piece[2])
        there = self.at(side, self.rows // 2)
        own = self.own(side, columns).astype(F32)
        return own + self.r1[0, there, columns].astype(F32) + self.r2[there, columns].astype(F32)

    def lanes_at(self, start, side, width):
        return pl.ds(pl.multiple_of(start + side * width, LANES), width)

    def after_second(self, piece):
        _, start, width, _, z_at, _ = piece
        self.second_copy(piece).wait_recv()
        self.sp[:, pl.ds(start, width)] = self.chip_sum(piece, 1 - self.core).astype(BF16)
        self.pair_copy(piece).start()

    def after_pair(self, piece):
        _, start, width, _, z_at, _ = piece
        self.pair_copy(piece).wait_recv()
        own = self.chip_sum(piece, self.core)
        came = self.rp[:, pl.ds(start, width)]
        if start == self.special:
            both = 2 * LANES
            self.total[:, pl.ds(z_at, both)] = (own[:, :both] + came[:, :both].astype(F32)).astype(BF16)
            self.total[:, self.lanes_at(z_at + both, self.core, LANES)] = own[:, both:].astype(BF16)
            self.total[:, self.lanes_at(z_at + both, 1 - self.core, LANES)] = came[:, both:]
        else:
            self.total[:, self.lanes_at(z_at, self.core, width)] = own.astype(BF16)
            self.total[:, self.lanes_at(z_at, 1 - self.core, width)] = came

    def drain_chips(self):
        for piece in self.pieces:
            firsts = [] if self.source is None else self.first_copies(piece)
            for copy in firsts + [self.second_copy(piece), self.pair_copy(piece)]:
                copy.wait_send()

    def over_members(self, total, came, sums, across, last, store):
        self.total, self.store = total, store
        self.came, self.sums, self.across, self.last = came, sums, across, last
        self.half = total.shape[0] // 2

    def z_copy(self, piece, k):
        n, _, _, _, start, wide = piece
        columns = pl.ds(start, wide)
        src, dst, device = (
            (self.total.at[self.at(1 - self.bit, self.half), columns], self.came, self.near),
            (self.sums.at[0, :, columns], self.across, self.far),
            (self.sums.at[1, :, columns], self.last, self.near),
        )[k]
        return self.copy(src, dst.at[:, columns], n, 4 + k, device)

    def start_members(self, piece):
        self.z_copy(piece, 0).start()

    def after_near(self, piece):
        columns = pl.ds(piece[4], piece[5])
        self.z_copy(piece, 0).wait_recv()
        own = self.total[self.at(self.bit, self.half), columns].astype(F32)
        self.sums[0, :, columns] = (own + self.came[:, columns].astype(F32)).astype(BF16)
        self.z_copy(piece, 1).start()

    def after_far(self, piece):
        columns = pl.ds(piece[4], piece[5])
        self.z_copy(piece, 1).wait_recv()
        total = self.sums[0, :, columns].astype(F32) + self.across[:, columns].astype(F32)
        self.sums[1, :, columns] = total.astype(BF16)
        self.z_copy(piece, 2).start()
        self.store(piece, self.at(self.bit, self.half), total.astype(BF16).astype(F32))

    def after_last(self, piece):
        self.z_copy(piece, 2).wait_recv()
        values = self.last[:, pl.ds(piece[4], piece[5])].astype(F32)
        self.store(piece, self.at(1 - self.bit, self.half), values)

    def drain_members(self):
        for piece in self.pieces:
            for k in range(3):
                self.z_copy(piece, k).wait_send()


def chip_scratch(rows, width):
    return [
        pltpu.VMEM((2, 2 * rows, width), BF16),
        pltpu.VMEM((2 * rows, width), BF16),
        pltpu.VMEM((2 * rows, width), BF16),
        pltpu.VMEM((rows, width), BF16),
        pltpu.VMEM((rows, width), BF16),
    ]


def member_scratch(rows, wide):
    half = (rows // 2, wide)
    return [
        pltpu.VMEM(half, BF16), pltpu.VMEM((2,) + half, BF16),
        pltpu.VMEM(half, BF16), pltpu.VMEM(half, BF16),
    ]


FIRST_PIECES = ((0, 512, "x"), (1024, 512, "y"), (512, 512, "x"), (1536, 384, "y"))
HALF_PIECES = ((0, 768, "x"), (768, 768, "y"))


def tail_kernel(
    g, g_x, g_bc, g_heads, g_gate, g_norm, d_part, out_x, out_bc, out_dt, vec_out, d_out,
    d_came, d_sum, local, r1, s2, r2, sp, rp, total, came, sums, across, last,
    vs, vr, sends, receives, vec_sends, vec_receives,
):
    f, z, core, chip, by_x, by_y = places()
    rows = g.shape[0] // 4
    inner = out_x.shape[1] // 2
    bit, upper, units = z % 2, z // 2, d_part.shape[0]
    first = Reduction(FIRST_PIECES, sends, receives, 0, inner)
    slot = 7 * len(FIRST_PIECES)
    partner, near, far = first.partner, first.near, first.far
    token_near, token_far = (2 * chip + bit, 2 * upper + core), (2 * chip + bit, 2 * (1 - upper) + core)
    stays = bit == core

    barrier = pltpu.get_barrier_semaphore()
    for device in (partner, first.over["x"], first.over["y"], near, far, token_far):
        pl.semaphore_signal(barrier, inc=1, device_id=device, device_id_type=MESH)

    @pl.when(jnp.logical_not(stays))
    def _():
        pl.semaphore_signal(barrier, inc=1, device_id=token_near, device_id_type=MESH)

    pl.semaphore_wait(barrier, 6 + (bit + core) % 2)

    def d_pair(k, n):
        return remote(d_part.at[:, k, 1 - core], d_came.at[:, k], sends, receives, slot + n, partner)

    def d_trade(k, n, device, group):
        return remote(
            d_sum.at[:, k], d_out.at[pl.ds(group * units, units)], sends, receives, slot + 2 + n, device
        )

    def d_add(k):
        for u in range(units):
            d_sum[u, k] = (d_part[u, k, core].astype(F32) + d_came[u, k].astype(F32)).astype(BF16)

    d_pair(1 - upper, 0).start()
    d_pair(upper, 1).start()
    d_keep = pltpu.make_async_copy(d_sum.at[:, upper], d_out.at[pl.ds(upper * units, units)], local.at[0])

    first.over_chips(
        lambda i, columns: g.at[first.at(i, rows), columns],
        lambda side, columns: g[pl.ds(pl.multiple_of(chip * rows + side * (rows // 2), rows // 2), rows // 2), columns],
        lambda i, columns: g[first.at(i, rows), columns],
        r1, s2, r2, sp, rp, total,
    )

    def store_first(piece, there, values):
        _, start, width, _, _, _ = piece
        if start == inner:
            out_bc[there, :] = values[:, : 2 * LANES]
            out_dt[there, :] = values[:, 2 * LANES :]
        else:
            out_x[there, pl.ds(start, width)] = values[:, :width]
            out_x[there, pl.ds(inner + start, width)] = values[:, width:]

    first.over_members(total, came, sums, across, last, store_first)

    vs[0] = jnp.zeros(vs.shape[1:], F32)
    for k in range(5):
        vs[0, k : k + 1] = jnp.sum(g_x[8 * k : 8 * k + 8], axis=0, keepdims=True)
        vs[0, 8 + k : 9 + k, : 2 * LANES] = jnp.sum(g_bc[8 * k : 8 * k + 8], axis=0, keepdims=True)
    vs[0, 5:6] = g_gate[...]
    vs[0, 6:7] = g_norm[...]
    for k in range(3):
        vs[0, 7:8, k * LANES : (k + 1) * LANES] = jnp.sum(
            g_heads[8 * k : 8 * k + 8], axis=0, keepdims=True
        )
    vec_ways = [first.over["x"], first.over["y"], near, far]

    def vec_copy(k):
        return remote(vs.at[k], vr.at[k], vec_sends, vec_receives, k, vec_ways[k])

    def vec_last(side):
        return remote(vec_out.at[core], vec_out.at[side], vec_sends, vec_receives, 4, partner)

    def vec_step(k):
        if k:
            vec_copy(k - 1).wait_recv()
            summed = vs[k - 1] + vr[k - 1]
            if k < 4:
                vs[k] = summed
            else:
                vec_out[core] = summed
        if k < 4:
            vec_copy(k).start()
        else:
            vec_last(core).start()

    first.start()
    vec_step(0)
    d_pair(1 - upper, 0).wait_recv()
    d_add(1 - upper)
    d_trade(1 - upper, 0, token_far, upper).start()
    d_pair(upper, 1).wait_recv()
    d_add(upper)

    @pl.when(stays)
    def _():
        d_keep.start()

    @pl.when(jnp.logical_not(stays))
    def _():
        d_trade(upper, 1, token_near, upper).start()

    early, late = first.pieces[:2], first.pieces[2:]

    def pair_on(piece):
        first.after_pair(piece)
        first.start_members(piece)

    order = (
        (first.after_first, early), (1, ()), (first.after_first, late), (2, ()),
        (first.after_second, early), (3, ()), (pair_on, early), (first.after_second, late), (4, ()),
        (first.after_near, early), (pair_on, late), (first.after_far, early),
        (first.after_near, late), (first.after_last, early),
        (first.after_far, late), (first.after_last, late),
    )
    for stage, pieces in order:
        if not pieces:
            vec_step(stage)
        for piece in pieces:
            stage(piece)
    vec_last(1 - core).wait_recv()
    d_trade(1 - upper, 0, token_far, 1 - upper).wait_recv()

    @pl.when(stays)
    def _():
        d_keep.wait()

    @pl.when(jnp.logical_not(stays))
    def _():
        d_trade(upper, 1, token_near, upper).wait()

    d_trade(1 - upper, 0, token_far, upper).wait_send()
    d_pair(1 - upper, 0).wait_send()
    d_pair(upper, 1).wait_send()
    first.drain_chips()
    first.drain_members()
    for k in range(4):
        vec_copy(k).wait_send()
    vec_last(core).wait_send()


def trade_steps(source, target, local, sends, receives):
    f, z, core, chip, _, _ = places()
    units = source.shape[0]
    bit, upper = z % 2, z // 2
    near, far = (2 * chip + bit, 2 * upper + core), (2 * chip + bit, 2 * (1 - upper) + core)
    stays = bit == core

    def copy(k, n, device, group):
        return remote(source.at[:, k], target.at[pl.ds(group * units, units)], sends, receives, n, device)

    keep = pltpu.make_async_copy(source.at[:, upper], target.at[pl.ds(upper * units, units)], local.at[0])

    def start():
        copy(1 - upper, 0, far, upper).start()

        @pl.when(stays)
        def _():
            keep.start()

        @pl.when(jnp.logical_not(stays))
        def _():
            copy(upper, 1, near, upper).start()

    def finish():
        copy(1 - upper, 0, far, 1 - upper).wait_recv()
        copy(1 - upper, 0, far, upper).wait_send()

        @pl.when(stays)
        def _():
            keep.wait()

        @pl.when(jnp.logical_not(stays))
        def _():
            copy(upper, 1, near, upper).wait()

    return start, finish, far, near, stays


class Segments:
    def __init__(self):
        self.f, self.z, self.core, self.chip, _, _ = places()
        self.group = self.z // 2
        self.me = self.chip * 2 + self.z % 2
        self.count = 8

    def device(self, i):
        return ((i // 2) * 2 + self.core, self.group * 2 + i % 2)

    def peer(self, k):
        other = (self.me + k) % self.count
        return other, self.device(other)


def middle_kernel(
    dno, gated, gate, y_pull, stats, gain, bcs, acum_pull, decays, normed, g_out, came_left, came_right, projected,
    x, xp, bc, bcp, dt, halo, cx, cbc, hp, y, st, incoming, acum, pick,
    d_all, heads_x, heads_bc, g_x, g_bc, g_heads, d_gate_out, tokens_out, total_out, z_out,
    dy_all, dgate_all, pulled, own, after, parts, results, blocks, g_z, out_own,
    o_r1, o_s2, o_r2, o_sp, o_rp, o_total, o_came, o_sums, o_across, o_last, o_final,
    z_rp, z_total, z_came, z_sums, z_across, z_last, z_final,
    xe, be, adjoint, dpx, dpb, ends,
    local, block_sems, trade_local, trade_sends, trade_receives, sends, receives,
    state_sends, state_receives, back_sends, back_receives,
):
    i = pl.program_id(0)
    chunks = (pl.num_programs(0) - 1) // 2
    f, z, core, chip, by_x, by_y = places()
    segments = Segments()
    me, count = segments.me, segments.count
    units, share = own.shape[0], parts.shape[2]
    rows = g_z.shape[0] // 4
    half = rows // 2
    inner = g_z.shape[1]

    def at(k, size):
        return pl.ds(pl.multiple_of(k * size, size), size)

    start_trade, finish_trade, trade_far, trade_near, stays = trade_steps(
        projected, tokens_out, trade_local, trade_sends, trade_receives
    )
    out = Reduction(HALF_PIECES, sends, receives, 0)
    gz = Reduction(HALF_PIECES, sends, receives, 7 * len(HALF_PIECES))
    out.over_chips(
        None,
        lambda side, columns: out_own[at(side, half), columns],
        lambda k, columns: o_s2[:, columns],
        o_r1, o_s2, o_r2, o_sp, o_rp, o_total,
    )

    def store_to(target):
        def store(piece, there, values):
            _, start, width, _, _, _ = piece
            target[there, pl.ds(start, width)] = values[:, :width].astype(BF16)
            target[there, pl.ds(inner + start, width)] = values[:, width:].astype(BF16)

        return store

    out.over_members(o_total, o_came, o_sums, o_across, o_last, store_to(o_final))
    gz.over_chips(
        lambda k, columns: g_z.at[at(k, rows), columns],
        lambda side, columns: g_z[pl.ds(pl.multiple_of(chip * rows + side * half, half), half), columns],
        lambda k, columns: g_z[at(k, rows), columns],
        o_r1, o_s2, o_r2, o_sp, z_rp, z_total,
    )
    gz.over_members(z_total, z_came, z_sums, z_across, z_last, store_to(z_final))
    left, right = (pl.ds(start, width) for start, width, _ in HALF_PIECES)
    own_rows = pltpu.make_async_copy(g_out.at[at(chip, rows)], out_own, local.at[0])
    pass_left = pltpu.make_async_copy(g_out.at[at(by_y, rows), left], o_s2.at[:, left], local.at[1])
    pass_right = pltpu.make_async_copy(g_out.at[at(by_x, rows), right], o_s2.at[:, right], local.at[2])
    keep_gate = pltpu.make_async_copy(dgate_all, d_gate_out, local.at[3])
    take_left = pltpu.make_async_copy(came_left, o_r1.at[:, :, left], local.at[4])
    take_right = pltpu.make_async_copy(came_right, o_r1.at[:, :, right], local.at[5])
    keep_out = pltpu.make_async_copy(o_final, total_out, local.at[6])
    keep_z = pltpu.make_async_copy(z_final, z_out, local.at[7])
    taken = (own_rows, pass_left, pass_right, take_left, take_right)

    def fetch(k):
        columns = pl.ds(k * 256, 256)
        return pltpu.make_async_copy(normed.at[:, columns], blocks.at[k % 2], block_sems.at[k % 2])

    @pl.when(i == 0)
    def _():
        barrier = pltpu.get_barrier_semaphore()
        for k in range(1, count):
            pl.semaphore_signal(barrier, inc=1, device_id=segments.peer(k)[1], device_id_type=MESH)
        for device in (out.partner, out.far, trade_far):
            pl.semaphore_signal(barrier, inc=1, device_id=device, device_id_type=MESH)

        @pl.when(jnp.logical_not(stays))
        def _():
            pl.semaphore_signal(barrier, inc=1, device_id=trade_near, device_id_type=MESH)

        pl.semaphore_wait(barrier, count + 2 + (z + core) % 2)
        for copy in taken:
            copy.start()
        start_trade()

    @pl.when(i == 2)
    def _():
        for copy in taken:
            copy.wait()
        for piece in out.pieces:
            out.after_first(piece)

    @pl.when(i == chunks - 2)
    def _():
        for piece in out.pieces:
            out.after_second(piece)

    @pl.when(i < chunks)
    def _():
        place = at(i, CHUNK)
        pull_kernel(
            dno, gated, gate, y_pull, stats, gain, bcs, acum_pull,
            dy_all.at[place], dgate_all.at[place], own.at[pl.ds(i // PER_UNIT, 1)],
            pulled, chunk=i % PER_UNIT,
        )

    def state_copy(k, at_me):
        other, device = segments.peer(k)
        src, slot = (own.at[:, at(other, share)], me) if at_me else (own.at[:, at(me, share)], other)
        return pltpu.make_async_remote_copy(
            src_ref=src, dst_ref=parts.at[slot],
            send_sem=state_sends.at[k], recv_sem=state_receives.at[slot],
            device_id=device, device_id_type=MESH,
        )

    def back_copy(k, at_me):
        other, device = segments.peer(k)
        slot = me if at_me else other
        return pltpu.make_async_remote_copy(
            src_ref=results.at[other], dst_ref=after.at[:, at(slot, share)],
            send_sem=back_sends.at[k], recv_sem=back_receives.at[slot],
            device_id=device, device_id_type=MESH,
        )

    def multiply(k):
        if k < 5:
            fetch(k + 1).start()
        fetch(k).wait()

        def part(n, carry):
            columns = pl.ds(pl.multiple_of(n * 256, 256), 256)
            product = dot_tn(blocks[k % 2], dgate_all[:, columns])
            g_z[pl.ds(k * 256, 256), columns] = product.astype(BF16)
            return carry

        lax.fori_loop(0, inner // 256, part, 0)

    @pl.when(i == chunks)
    def _():
        for k in range(1, count):
            state_copy(k, True).start()
        fetch(0).start()
        keep_gate.start()
        parts[me] = own[:, at(me, share)]
        for k in range(3):
            multiply(k)
        for piece in out.pieces:
            out.after_pair(piece)
        for k in range(1, count):
            state_copy(k, False).wait_recv()
        running = [jnp.zeros((share, inner), F32) for _ in range(units)]
        for n in range(count - 1, -1, -1):
            for u in range(units):
                results[n, u] = running[u].astype(BF16)
                running[u] = running[u] * decays[n, u : u + 1] + parts[n, u].astype(F32)
        after[:, at(me, share)] = results[me]
        for k in range(1, count):
            back_copy(k, True).start()
        for k in range(3, 6):
            multiply(k)
        for k in range(1, count):
            back_copy(k, False).wait_recv()
        out.drain_chips()
        gz.start()
        for k in range(1, count):
            state_copy(k, True).wait_send()
            back_copy(k, True).wait_send()
        for piece in out.pieces:
            out.start_members(piece)

    def at_step(n, *stages):
        @pl.when(i == chunks + 1 + n)
        def _():
            for stage, reduction in stages:
                for piece in reduction.pieces:
                    stage(piece)

    @pl.when(i > chunks)
    def _():
        n = i - chunks - 1
        unit, chunk = n // PER_UNIT, n % PER_UNIT
        place = at(unit * PER_UNIT + PER_UNIT - 1 - chunk, CHUNK)
        backward_kernel(
            x, xp, bc, bcp, dt, halo, cx, cbc, hp, dy_all.at[place], y, st, incoming, acum,
            after.at[pl.ds(unit, 1)], pick, d_all, heads_x, heads_bc, g_x, g_bc, g_heads,
            xe, be, adjoint, dpx, dpb, ends, place=(unit, chunk),
        )

    at_step(2, (out.after_near, out))
    at_step(4, (gz.after_first, gz))
    at_step(6, (out.after_far, out), (gz.after_second, gz))
    at_step(7, (gz.after_pair, gz), (gz.start_members, gz))
    at_step(8, (out.after_last, out))
    at_step(9, (gz.after_near, gz))

    @pl.when(i == 2 * chunks)
    def _():
        finish_trade()
        out.drain_members()
        keep_out.start()
        gz.drain_chips()
        for stage in (gz.after_far, gz.after_last):
            for piece in gz.pieces:
                stage(piece)
        keep_z.start()
        gz.drain_members()
        keep_gate.wait()
        keep_out.wait()
        keep_z.wait()


class Plan:
    def __init__(self, batch, tokens):
        self.shards, self.members = lax.axis_size("fs"), lax.axis_size("sp")
        self.f, self.z = lax.axis_index("fs"), lax.axis_index("sp")
        self.core = self.f % 2
        self.chips = self.shards // 2
        self.chip = self.f // 2
        self.batch, self.tokens = batch, tokens
        self.units = batch // 2
        self.joints = self.members // 2
        self.count = self.chips * self.joints
        self.group, self.joint = self.z // self.joints, self.z % self.joints
        self.fast = self.chips == 4 and self.members == 4

    def at(self, f, z):
        return f * self.members + z

    def send(self, x, pairs):
        return lax.ppermute(x, ("fs", "sp"), pairs)

    def swap(self, x, df=0, dz=0):
        pairs = [
            (self.at(f, z), self.at(f ^ df, z ^ dz))
            for f in range(self.shards)
            for z in range(self.members)
        ]
        return self.send(x, pairs)

    def along(self, x, by):
        pairs = []
        for f in range(self.shards):
            for z in range(self.members):
                place = (f // 2) * self.joints + z % self.joints + by
                if 0 <= place < self.count:
                    there = (place // self.joints) * 2 + f % 2
                    pairs.append(
                        (self.at(f, z), self.at(there, z - z % self.joints + place % self.joints))
                    )
        return self.send(x, pairs)

    def by_core(self, mine, other):
        first = self.core == 0
        return jnp.where(first, mine, other), jnp.where(first, other, mine)

    def head(self, hidden, w_x, w_bc, w_dt, conv_x, conv_bc, *vectors):
        anywhere, vmem = pl.BlockSpec(memory_space=pl.ANY), pl.BlockSpec(memory_space=pltpu.VMEM)
        conv_x_bias, gate_gain, norm_gain, conv_bc_bias, dt_bias, a_log, skip_d = (v[None] for v in vectors)
        rows, inner = w_x.shape[0], w_x.shape[1] // 2
        small = (SMALL_ROWS, conv_x.shape[0])
        dma = pltpu.SemaphoreType.DMA
        shape = jax.ShapeDtypeStruct
        units, first, *params = pl.pallas_call(
            head_kernel,
            out_shape=[
                shape((self.units, 4, self.tokens, hidden.shape[-1]), BF16),
                shape((4, 2, rows, inner + 3 * LANES), BF16),
                shape((8, inner), F32), shape((8, 2 * LANES), F32), shape((8, LANES), F32),
                shape((8, hidden.shape[-1]), F32), shape((8, inner), F32),
            ],
            in_specs=[anywhere] * 3 + [vmem] * 10,
            out_specs=[anywhere] * 2 + [vmem] * 5,
            scratch_shapes=[
                pltpu.VMEM((rows, LANES), BF16), pltpu.VMEM((rows, LANES), BF16),
                pltpu.VMEM(small, F32), pltpu.VMEM((self.shards,) + small, F32),
                dma((4,)), dma((11,)), dma((11,)), dma((self.shards,)), dma((self.shards,)),
            ],
            compiler_params=pltpu.CompilerParams(
                collective_id=2, has_side_effects=True, vmem_limit_bytes=VMEM_LIMIT
            ),
            cost_estimate=cost(55),
            name="head",
        )(
            hidden, w_x, w_bc, w_dt, conv_x, conv_x_bias, gate_gain, norm_gain, conv_bc, conv_bc_bias,
            dt_bias, a_log, skip_d,
        )
        return units.reshape(-1, hidden.shape[-1]), first.reshape(-1, inner + 3 * LANES), *params

    def tail(self, g, g_x, g_bc, g_heads, g_gate, g_norm, d_normed):
        rows, inner = g.shape[0] // self.shards, g_x.shape[1]
        if not self.fast:
            g = self.reduce_chips(g)
            low = self.core == 0
            kept, given = jnp.where(low, g[:rows], g[rows:]), jnp.where(low, g[rows:], g[:rows])
            came = self.swap(given.astype(BF16), df=1).astype(F32)
            total = self.reduce_members(
                jnp.concatenate(
                    list(self.by_core(kept[:, :inner], came[:, :inner]))
                    + [kept[:, inner : inner + 2 * LANES] + came[:, inner : inner + 2 * LANES]]
                    + list(self.by_core(kept[:, inner + 2 * LANES :], came[:, inner + 2 * LANES :])),
                    axis=1,
                )
            )
            wide = ((0, 0), (0, inner - 2 * LANES))
            heads = g_heads.reshape(3, 8, LANES).sum(axis=1).reshape(1, -1)
            vec = jnp.concatenate(
                [
                    g_x.reshape(5, 8, inner).sum(axis=1), g_gate, g_norm,
                    jnp.pad(heads, ((0, 0), (0, inner - 3 * LANES))),
                    jnp.pad(g_bc.reshape(5, 8, 2 * LANES).sum(axis=1), wide),
                ]
            )
            vec = self.sum_all(jnp.pad(vec, ((0, 3), (0, 0))))
            vec = jnp.stack(self.by_core(vec, self.swap(vec, df=1)))
            cut = 2 * inner + 2 * LANES
            d_rows = self.to_tokens(self.cores_sum(d_normed))
            return total[:, : 2 * inner], total[:, 2 * inner : cut], total[:, cut:], vec, d_rows
        width = g.shape[1]
        wide = 2 * inner + 4 * LANES
        vmem = pl.BlockSpec(memory_space=pltpu.VMEM)
        vec = (16, inner)
        d_shape = (self.units, 2, self.tokens, d_normed.shape[1])
        slots = 7 * len(FIRST_PIECES) + 4
        return pl.pallas_call(
            tail_kernel,
            out_shape=[
                jax.ShapeDtypeStruct((rows, 2 * inner), F32),
                jax.ShapeDtypeStruct((rows, 2 * LANES), F32),
                jax.ShapeDtypeStruct((rows, 2 * LANES), F32),
                jax.ShapeDtypeStruct((2,) + vec, F32),
                jax.ShapeDtypeStruct((self.batch, self.tokens, d_normed.shape[1]), BF16),
            ],
            in_specs=[vmem] * 7,
            out_specs=[vmem] * 5,
            scratch_shapes=[pltpu.VMEM(d_shape, BF16)] * 2
            + [pltpu.SemaphoreType.DMA((1,))]
            + chip_scratch(rows, width)
            + [pltpu.VMEM((rows, wide), BF16)]
            + member_scratch(rows, wide)
            + [pltpu.VMEM((4,) + vec, F32)] * 2
            + [pltpu.SemaphoreType.DMA((slots,))] * 2
            + [pltpu.SemaphoreType.DMA((5,))] * 2,
            compiler_params=pltpu.CompilerParams(
                collective_id=3, has_side_effects=True, vmem_limit_bytes=TAIL_LIMIT
            ),
            cost_estimate=cost(90),
            name="tail",
        )(
            g, g_x, g_bc, g_heads, g_gate, g_norm,
            d_normed.reshape(self.units, 2, 2, self.tokens, d_normed.shape[1]),
        )

    def first_hop(self, g):
        rows = g.shape[0] // 4
        by_x, by_y = self.chip + 1 - 2 * (self.chip % 2), (self.chip + 2) % 4
        corner = (by_x + 2) % 4
        blocks = g.reshape(4, rows, g.shape[1])
        found = []
        for (start, width, _), to, df in zip(HALF_PIECES, (by_x, by_y), (2, 4)):
            columns = blocks[:, :, start : start + width]
            given = [lax.dynamic_index_in_dim(columns, k, 0, False) for k in (to, corner)]
            found.append(self.swap(jnp.stack(given), df=df))
        return found

    def gather(self, x):
        groups = [list(range(c, self.shards, 2)) for c in range(2)]
        return lax.all_gather(x, "fs", axis=0, tiled=True, axis_index_groups=groups)

    def reduce_chips(self, g):
        groups = [list(range(c, self.shards, 2)) for c in range(2)]
        return lax.psum_scatter(
            g, "fs", scatter_dimension=0, tiled=True, axis_index_groups=groups
        ).astype(F32)

    def reduce_members(self, g):
        return lax.psum(g.astype(BF16), "sp").astype(F32)

    def traded(self, x, far):
        pairs = [
            (self.at(f, z), self.at(f - f % 2 + z % 2, ((z // 2) ^ far) * 2 + f % 2))
            for f in range(self.shards)
            for z in range(self.members)
        ]
        return self.send(x, pairs)

    def to_units(self, rows):
        units, width = self.units, rows.shape[-1]
        if self.fast:
            low, high = rows[:units], rows[units:]
            upper = self.z // 2 == 1
            far = self.traded(jnp.where(upper, low, high), 1)
            near = self.traded(jnp.where(upper, high, low), 0)
            mine = jnp.stack([jnp.where(upper, far, near), jnp.where(upper, near, far)], axis=1)
            pair = self.by_core(mine, self.swap(mine, df=1))
            block = jnp.stack(pair, axis=2)
        else:
            other = self.swap(rows, df=1)
            everything = lax.all_gather(jnp.stack(self.by_core(rows, other)), "sp")
            per_core = self.joints // 2
            block = lax.dynamic_slice(
                everything,
                ((self.joint % per_core) * 4, self.joint // per_core, self.group * units, 0, 0),
                (4, 1, units) + rows.shape[1:],
            )[:, 0]
            block = jnp.moveaxis(block, 0, 1)
        return block.reshape(units * 4 * self.tokens, width)

    def cores_sum(self, partial):
        units, width = self.units, partial.shape[-1]
        if self.fast:
            block = partial.reshape(units, 2, 2, self.tokens, width)
            even = self.core == 0
            mine = jnp.where(even, block[:, :, 0], block[:, :, 1])
            given = jnp.where(even, block[:, :, 1], block[:, :, 0]).astype(BF16)
            return (mine.astype(F32) + self.swap(given, df=1).astype(F32)).astype(BF16)
        return partial.astype(BF16).reshape(units, 4, self.tokens, width)

    def to_tokens(self, total):
        units, width = self.units, total.shape[-1]
        if self.fast:
            upper = self.z // 2 == 1
            far = self.traded(jnp.where(upper, total[:, 0], total[:, 1]), 1)
            near = self.traded(jnp.where(upper, total[:, 1], total[:, 0]), 0)
            return jnp.concatenate(
                [jnp.where(upper, far, near), jnp.where(upper, near, far)], axis=0
            )
        per_core = self.joints // 2
        block = total
        wide = jnp.zeros((self.members, 2, self.batch, self.tokens, width), BF16)
        wide = lax.dynamic_update_slice(
            wide,
            jnp.moveaxis(block, 1, 0)[:, None],
            ((self.joint % per_core) * 4, self.joint // per_core, self.group * units, 0, 0),
        )
        summed = lax.psum_scatter(wide, "sp", scatter_dimension=0, tiled=False)
        first = self.core == 0
        mine, given = jnp.where(first, summed[0], summed[1]), jnp.where(first, summed[1], summed[0])
        return (mine.astype(F32) + self.swap(given, df=1).astype(F32)).astype(BF16)

    def sum_all(self, x):
        if not self.fast:
            groups = [list(range(c, self.shards, 2)) for c in range(2)]
            return lax.psum(lax.psum(x, "fs", axis_index_groups=groups), "sp")
        for df, dz in ((2, 0), (4, 0), (0, 1), (0, 2)):
            x = x + self.swap(x, df, dz)
        return x


def row_scale(values):
    return lax.rsqrt(jnp.mean(values * values, axis=-1, keepdims=True) + EPSILON)


def rows_spec(width, column=0, back=False):
    def place(u, c):
        return (u * PER_UNIT + (PER_UNIT - 1 - c if back else c), column)

    return pl.BlockSpec((CHUNK, width), place)


def chunk_spec(shape, back=False):
    def place(u, c):
        return (u * PER_UNIT + (PER_UNIT - 1 - c if back else c), 0, 0)

    return pl.BlockSpec((1,) + shape, place)


def unit_spec(shape):
    return pl.BlockSpec((1,) + shape, lambda u, c: (u, 0, 0))


def whole_spec(shape):
    return pl.BlockSpec(shape, lambda u, c: (0,) * len(shape))


def cost(microseconds):
    return pl.CostEstimate(flops=int(microseconds * 1.15e9), bytes_accessed=0, transcendentals=0)


def params():
    return pltpu.CompilerParams(
        dimension_semantics=("arbitrary", "arbitrary"), vmem_limit_bytes=VMEM_LIMIT
    )


def slow_exchange(plan, own, decays, back):
    count, units = plan.count, own.shape[0]
    rates, pieces = decays[:units, None], own.astype(F32)

    def hop(_, before):
        return plan.along((before * rates + pieces).astype(BF16), -1 if back else 1).astype(F32)

    return lax.fori_loop(0, count - 1, hop, jnp.zeros(own.shape, F32)).astype(BF16)


def exchange(plan, own, decays, cot, near, far):
    units, depth, width = own.shape
    count, share = plan.count, depth // plan.count
    dec_shape = (count, 8, width)
    vmem, anywhere = pl.BlockSpec(memory_space=pltpu.VMEM), pl.BlockSpec(memory_space=pl.ANY)
    dma = pltpu.SemaphoreType.DMA
    rows_shape = (units, 4, plan.tokens, cot.shape[-1])
    incoming, all_decays, rows = pl.pallas_call(
        exchange_kernel,
        out_shape=[
            jax.ShapeDtypeStruct(own.shape, BF16),
            jax.ShapeDtypeStruct(dec_shape, F32),
            jax.ShapeDtypeStruct(rows_shape, BF16),
        ],
        in_specs=[vmem, vmem, anywhere, anywhere, anywhere],
        out_specs=[vmem, vmem, anywhere],
        scratch_shapes=[
            pltpu.VMEM((count, units, share, width), BF16),
            pltpu.VMEM(dec_shape, F32),
            pltpu.VMEM((count, units, share, width), BF16),
        ]
        + [dma((count,))] * 6
        + [dma((4,)), dma((4,)), dma((2,))],
        compiler_params=pltpu.CompilerParams(
            collective_id=0, has_side_effects=True, vmem_limit_bytes=VMEM_LIMIT
        ),
        cost_estimate=cost(35),
        name="states",
    )(own, decays, cot, near, far)
    return incoming, all_decays, rows.reshape(-1, cot.shape[-1])


def body(
    hidden, norm_gain, w_z, w_x, w_bc, w_dt, w_out, conv_x, conv_x_bias, conv_bc, conv_bc_bias,
    dt_bias, a_log, skip_d, gate_gain, cotangent,
):
    batch, tokens, model = hidden.shape
    plan = Plan(batch, tokens)
    core = plan.core
    inner = w_z.shape[1] // 2
    heads = w_dt.shape[1] // 2
    head_size = inner // heads
    units = plan.units
    rows = units * 4 * tokens
    chunks = rows // CHUNK

    def halves(w):
        half = w.shape[1] // 2
        return jnp.where(core == 0, w[:, :half], w[:, half:]), jnp.where(core == 0, w[:, half:], w[:, :half])

    z_mine, z_other = halves(w_z)
    o_mine, o_other = halves(w_out)

    def rows_of_chip(mine, other):
        return jnp.concatenate(plan.by_core(mine, plan.swap(other, df=1)), axis=0)

    vectors = (conv_x_bias, gate_gain, norm_gain, conv_bc_bias, dt_bias, a_log, skip_d)
    if plan.fast:
        hidden_rows, weight_first, cx, cbc, hp, gain_in, gain_rows = plan.head(
            hidden, w_x, w_bc, w_dt, conv_x, conv_bc, *vectors
        )
        gain_in, gain_out = gain_in[0], gain_rows[0]
    else:
        x_mine, x_other = halves(w_x)
        dt_mine, dt_other = halves(w_dt)
        fill = jnp.zeros((w_dt.shape[0], LANES - heads), BF16)
        weight_first = plan.gather(
            rows_of_chip(
                jnp.concatenate([x_mine, w_bc, dt_mine, fill], axis=1),
                jnp.concatenate([x_other, w_bc, dt_other, fill], axis=1),
            )
        )
        hidden_rows, cot_rows = plan.to_units(hidden), plan.to_units(cotangent)

        def whole_of(v):
            return lax.all_gather(v.astype(F32), "fs", axis=0, tiled=True)

        def mine_of(v):
            half = v.shape[0] // 2
            return lax.dynamic_slice_in_dim(v, core * half, half, 0)

        bias_x, gain_out, gain_in, bias_bc, shift, rate_log, skip = (whole_of(v) for v in vectors)
        taps_x, taps_bc = mine_of(whole_of(conv_x)), whole_of(conv_bc)
        bias_x, gain_out, skip, shift, rate_log = (
            mine_of(v) for v in (bias_x, gain_out, skip, shift, rate_log)
        )
        nothing = jnp.zeros((2, inner), F32)
        cx = jnp.concatenate([taps_x.T, bias_x[None], jnp.repeat(skip, head_size)[None], nothing])
        cbc = jnp.concatenate([taps_bc.T, bias_bc[None], jnp.zeros((3, bias_bc.size), F32)])
        pad_heads = (0, LANES - heads)
        hp = jnp.stack([jnp.pad(jnp.exp(rate_log), pad_heads), jnp.pad(shift, pad_heads)])
        hp = jnp.pad(hp, ((0, 6), (0, 0)))
        gain_rows = jnp.broadcast_to(gain_out[None], (8, inner))
    weight_gate = plan.gather(rows_of_chip(z_mine, z_other))
    weight_out = plan.gather(rows_of_chip(o_mine, o_other))
    pick = (jnp.arange(inner)[:, None] // head_size == jnp.arange(LANES)[None, :]).astype(BF16)

    hidden_rows = hidden_rows.astype(F32)
    scale_in = row_scale(hidden_rows)
    unit_in = hidden_rows * scale_in
    normed = (unit_in * gain_in[None]).astype(BF16)

    first = dot(normed, weight_first).astype(BF16)
    def shaped(*shape, dtype=BF16):
        return jax.ShapeDtypeStruct(shape, dtype)

    states = (LANES, inner)
    edge = (units, 16, inner + 2 * LANES)
    in_specs = [
        rows_spec(inner), rows_spec(2 * LANES, inner // (2 * LANES)),
        rows_spec(LANES, (inner + 2 * LANES) // LANES),
    ]
    consts = [whole_spec(cx.shape), whole_spec(cbc.shape), whole_spec(hp.shape)]
    out_specs = [
        rows_spec(inner), chunk_spec(states), unit_spec(states), unit_spec((8, inner)),
        rows_spec(2 * LANES), rows_spec(LANES),
    ]
    out_shape = [
        shaped(rows, inner), shaped(chunks, *states), shaped(units, *states),
        shaped(units, 8, inner, dtype=F32), shaped(rows, 2 * LANES), shaped(rows, LANES, dtype=F32),
    ]
    scratch = [
        pltpu.VMEM((CHUNK + 8, inner), F32), pltpu.VMEM((CHUNK + 8, 2 * LANES), F32),
        pltpu.VMEM(states, F32), pltpu.VMEM((8, LANES), F32),
    ]
    by_unit = first.reshape(units, 4 * tokens, first.shape[1])
    if plan.fast:
        anywhere = pl.BlockSpec(memory_space=pl.ANY)
        dma = pltpu.SemaphoreType.DMA
        y_own, starts, own, decays, shared, reach, halo, near, far = pl.pallas_call(
            scan_forward_kernel,
            grid=(units, PER_UNIT),
            in_specs=in_specs + [anywhere, anywhere] + consts,
            out_specs=out_specs + [whole_spec(edge), anywhere, anywhere],
            out_shape=out_shape
            + [shaped(*edge), shaped(units, tokens, model), shaped(EARLY_UNITS, tokens, model)],
            scratch_shapes=scratch
            + [pltpu.VMEM(edge, BF16), dma((1,)), dma((1,)), dma((2,)), dma((2,)), dma((1,))],
            compiler_params=pltpu.CompilerParams(
                dimension_semantics=("arbitrary", "arbitrary"), vmem_limit_bytes=VMEM_LIMIT,
                collective_id=1, has_side_effects=True,
            ),
            cost_estimate=cost(31),
            name="scan_forward",
        )(first, first, first, by_unit, cotangent, cx, cbc, hp)
    else:
        halo = plan.along(by_unit[:, 4 * tokens - 16 :, : inner + 2 * LANES], 1)
        y_own, starts, own, decays, shared, reach = pl.pallas_call(
            forward_kernel,
            grid=(units, PER_UNIT),
            in_specs=in_specs + [whole_spec(edge)] + consts,
            out_specs=out_specs,
            out_shape=out_shape,
            scratch_shapes=scratch,
            compiler_params=params(),
            name="scan_forward",
        )(first, first, first, halo, cx, cbc, hp)

    decay_rows = jnp.concatenate([decays[:, 0], jnp.zeros((8 - units, inner), F32)])
    if plan.fast:
        incoming, all_decays, cot_rows = exchange(plan, own, decay_rows, cotangent, near, far)
    else:
        incoming = slow_exchange(plan, own, decay_rows, False)
    gate_in = dot(normed, weight_gate).astype(BF16)

    y, gated, squares = pl.pallas_call(
        gate_kernel,
        grid=(units, PER_UNIT),
        in_specs=[
            rows_spec(inner), rows_spec(inner), rows_spec(2 * LANES), rows_spec(LANES), unit_spec(states),
        ],
        out_specs=[rows_spec(inner), rows_spec(inner), rows_spec(LANES)],
        out_shape=[shaped(rows, inner), shaped(rows, inner), shaped(rows, LANES, dtype=F32)],
        compiler_params=params(),
        cost_estimate=cost(14),
        name="gate_forward",
    )(y_own, gate_in, shared, reach, incoming)

    def pair_sum(v):
        return v + plan.swap(v, df=1)

    squares = pair_sum(squares[:, 0].reshape(chunks, CHUNK))
    scale_out = lax.rsqrt(squares / (2 * inner) + EPSILON).reshape(rows, 1)
    unit_out = gated.astype(F32) * scale_out
    normed_out = (unit_out * gain_out[None]).astype(BF16)
    projected = plan.cores_sum(dot_nt(normed_out, weight_out))

    g_out = dot_tn(cot_rows, normed_out).astype(BF16)
    g_out, weight_out, cot_rows = lax.optimization_barrier((g_out, weight_out, cot_rows))
    d_normed_out = dot(cot_rows, weight_out).astype(BF16)
    wide = d_normed_out.astype(F32)
    g_gate_gain = jnp.sum(wide * unit_out, axis=0)
    mean = pair_sum(jnp.sum(wide * gain_out[None] * unit_out, axis=1).reshape(chunks, CHUNK))
    mean = (mean / (2 * inner)).reshape(rows, 1)
    stats = jnp.concatenate([scale_out, mean, jnp.zeros((rows, LANES - 2), F32)], axis=1)

    width = inner + 3 * LANES
    back = functools.partial(rows_spec, back=True)
    if plan.fast:
        came_left, came_right = plan.first_hop(g_out)
        spots = 2 * chunks + 1
        shard_rows = model // plan.shards
        segments = plan.count
        share = LANES // segments

        def pulls(columns, column=0):
            return pl.BlockSpec((CHUNK, columns), lambda i: (jnp.minimum(i, chunks - 1), column))

        def scan_at(i):
            n = jnp.maximum(i - chunks - 1, 0)
            return n - n % PER_UNIT + PER_UNIT - 1 - n % PER_UNIT

        def scans(columns, column=0):
            return pl.BlockSpec((CHUNK, columns), lambda i: (scan_at(i), column))

        def edges(columns, column=0):
            return pl.BlockSpec((16, columns), lambda i: (jnp.maximum(scan_at(i) * 8 - 1, 0), column))

        def scan_chunk(shape):
            return pl.BlockSpec((1,) + shape, lambda i: (scan_at(i), 0, 0))

        def scan_unit(shape):
            return pl.BlockSpec((1,) + shape, lambda i: (scan_at(i) // PER_UNIT, 0, 0))

        def every(shape):
            return pl.BlockSpec(shape, lambda i: (0,) * len(shape), pipeline_mode=pl.Buffered(1))

        def whole(shape):
            return pl.BlockSpec(shape, lambda i: (0,) * len(shape))

        anywhere = pl.BlockSpec(memory_space=pl.ANY)
        dma = pltpu.SemaphoreType.DMA
        d_all, heads_x, heads_bc, g_x, g_bc, g_heads, d_gate, projected, total_out, total_z = pl.pallas_call(
            middle_kernel,
            grid=(spots,),
            in_specs=[
                pulls(inner), pulls(inner), pulls(inner), pulls(inner), pulls(LANES), every((8, inner)),
                pulls(2 * LANES), pulls(LANES), every(all_decays.shape), anywhere, anywhere, anywhere, anywhere, anywhere,
                scans(inner), edges(inner),
                scans(2 * LANES, inner // (2 * LANES)), edges(2 * LANES, inner // (2 * LANES)),
                scans(LANES, (inner + 2 * LANES) // LANES), every(edge), every(cx.shape), every(cbc.shape), every(hp.shape),
                scans(inner), scan_chunk(states), scan_unit(states), scans(LANES), every(pick.shape),
            ],
            out_specs=[
                scans(width), scan_unit((8, inner)), scan_unit((8, 2 * LANES)),
                whole((40, inner)), whole((40, 2 * LANES)), whole((24, LANES)),
                anywhere, anywhere, anywhere, anywhere,
            ],
            out_shape=[
                shaped(rows, width), shaped(units, 8, inner, dtype=F32), shaped(units, 8, 2 * LANES, dtype=F32),
                shaped(40, inner, dtype=F32), shaped(40, 2 * LANES, dtype=F32), shaped(24, LANES, dtype=F32),
                shaped(rows, inner), shaped(batch, tokens, model),
                shaped(shard_rows, 2 * inner), shaped(shard_rows, 2 * inner),
            ],
            scratch_shapes=[
                pltpu.VMEM((rows, inner), BF16), pltpu.VMEM((rows, inner), BF16), pltpu.VMEM(states, F32),
                pltpu.VMEM((units,) + states, BF16), pltpu.VMEM((units,) + states, BF16),
                pltpu.VMEM((segments, units, share, inner), BF16),
                pltpu.VMEM((segments, units, share, inner), BF16),
                pltpu.VMEM((2, rows, 256), BF16), pltpu.VMEM((model, inner), BF16),
                pltpu.VMEM((model // 4, inner), BF16),
            ]
            + chip_scratch(shard_rows, inner)
            + [pltpu.VMEM((shard_rows, 2 * inner), BF16)]
            + member_scratch(shard_rows, 2 * inner)
            + [pltpu.VMEM((shard_rows, 2 * inner), BF16)]
            + [pltpu.VMEM((shard_rows, inner), BF16), pltpu.VMEM((shard_rows, 2 * inner), BF16)]
            + member_scratch(shard_rows, 2 * inner)
            + [pltpu.VMEM((shard_rows, 2 * inner), BF16)]
            + [
                pltpu.VMEM((CHUNK + 8, inner), F32), pltpu.VMEM((CHUNK + 8, 2 * LANES), F32),
                pltpu.VMEM(states, F32),
                pltpu.VMEM((CHUNK + 8, inner), F32), pltpu.VMEM((CHUNK + 8, 2 * LANES), F32),
                pltpu.VMEM((8, inner), F32),
                dma((8,)), dma((2,)), dma((1,)), dma((2,)), dma((2,)),
                dma((14 * len(HALF_PIECES),)), dma((14 * len(HALF_PIECES),)),
                dma((segments,)), dma((segments,)), dma((segments,)), dma((segments,)),
            ],
            compiler_params=pltpu.CompilerParams(
                dimension_semantics=("arbitrary",), vmem_limit_bytes=MIDDLE_LIMIT,
                collective_id=4, has_side_effects=True,
            ),
            cost_estimate=cost(125),
            name="middle",
        )(
            d_normed_out, gated, gate_in, y, stats, gain_rows, shared, reach, all_decays, normed, g_out,
            came_left, came_right, projected, first, first, first, first, first, halo, cx, cbc, hp, y, starts, incoming,
            reach, pick,
        )
    else:

        def edges(columns, column=0):
            def place(u, c):
                return (jnp.maximum((u * PER_UNIT + PER_UNIT - 1 - c) * 8 - 1, 0), column)

            return pl.BlockSpec((16, columns), place)

        dy, d_gate, pull = pl.pallas_call(
            pull_kernel,
            grid=(units, PER_UNIT),
            in_specs=[
                rows_spec(inner), rows_spec(inner), rows_spec(inner), rows_spec(inner), rows_spec(LANES),
                whole_spec((8, inner)), rows_spec(2 * LANES), rows_spec(LANES),
            ],
            out_specs=[rows_spec(inner), rows_spec(inner), unit_spec(states)],
            out_shape=[shaped(rows, inner), shaped(rows, inner), shaped(units, *states)],
            scratch_shapes=[pltpu.VMEM(states, F32)],
            compiler_params=params(),
            name="gate_backward",
        )(d_normed_out, gated, gate_in, y, stats, gain_rows, shared, reach)
        after = slow_exchange(plan, pull, decay_rows, True)
        d_all, heads_x, heads_bc, g_x, g_bc, g_heads = pl.pallas_call(
            backward_kernel,
            grid=(units, PER_UNIT),
            in_specs=[
                back(inner), edges(inner),
                back(2 * LANES, inner // (2 * LANES)), edges(2 * LANES, inner // (2 * LANES)),
                back(LANES, (inner + 2 * LANES) // LANES), whole_spec(edge), whole_spec(cx.shape), whole_spec(cbc.shape), whole_spec(hp.shape),
                back(inner), back(inner), chunk_spec(states, True), unit_spec(states), back(LANES),
                unit_spec(states), whole_spec(pick.shape),
            ],
            out_specs=[
                back(width), unit_spec((8, inner)), unit_spec((8, 2 * LANES)),
                whole_spec((40, inner)), whole_spec((40, 2 * LANES)), whole_spec((24, LANES)),
            ],
            out_shape=[
                shaped(rows, width), shaped(units, 8, inner, dtype=F32), shaped(units, 8, 2 * LANES, dtype=F32),
                shaped(40, inner, dtype=F32), shaped(40, 2 * LANES, dtype=F32), shaped(24, LANES, dtype=F32),
            ],
            scratch_shapes=[
                pltpu.VMEM((CHUNK + 8, inner), F32), pltpu.VMEM((CHUNK + 8, 2 * LANES), F32),
                pltpu.VMEM(states, F32),
                pltpu.VMEM((CHUNK + 8, inner), F32), pltpu.VMEM((CHUNK + 8, 2 * LANES), F32),
                pltpu.VMEM((8, inner), F32),
            ],
            compiler_params=params(),
            name="scan_backward",
        )(
            first, first, first, first, first, halo, cx, cbc, hp,
            dy, y, starts, incoming, reach, after, pick,
        )
        projected = plan.to_tokens(projected)

        def over_everything(g):
            g = plan.reduce_chips(g)
            half = g.shape[0] // 2
            low = core == 0
            mine, other = jnp.where(low, g[:half], g[half:]), jnp.where(low, g[half:], g[:half])
            other = plan.swap(other.astype(BF16), df=1).astype(F32)
            return plan.reduce_members(jnp.concatenate(plan.by_core(mine, other), axis=1))

        total_out = over_everything(g_out)
        total_z = over_everything(dot_tn(normed, d_gate).astype(BF16))
    output = (hidden.astype(F32) + projected.astype(F32)).astype(BF16)

    later = plan.along(jnp.concatenate([heads_x, heads_bc], axis=2)[:, :3].astype(BF16), -1).astype(F32)
    taps = jnp.concatenate([cx[:4], cbc[:4]], axis=1)
    extra = jnp.stack(
        [sum(taps[k][None] * later[:, i - k] for k in range(i + 1)) for i in range(3)], axis=1
    )
    tail_rows = d_all.reshape(units, 4 * tokens, width)[:, 4 * tokens - 16 :].astype(F32)
    extra = jnp.pad(extra, ((0, 0), (13, 0), (0, width - extra.shape[2])))
    d_all = d_all.reshape(units, 4 * tokens, width)
    d_all = lax.dynamic_update_slice(d_all, (tail_rows + extra).astype(BF16), (0, 4 * tokens - 16, 0))
    d_all = d_all.reshape(rows, width)

    g_first = dot_tn(normed, d_all).astype(BF16)
    d_normed = dot_nt(d_gate, weight_gate) + dot_nt(d_all, weight_first)
    g_norm_gain = jnp.sum(d_normed * unit_in, axis=0)

    total_x, total_bc, total_dt, vec, grad_rows = plan.tail(
        g_first, g_x, g_bc, g_heads, g_gate_gain[None], g_norm_gain[None], d_normed.astype(BF16)
    )
    grad_rows = grad_rows.astype(F32)
    resid = hidden.astype(F32)
    own_scale = row_scale(resid)
    own_unit = resid * own_scale
    dv = grad_rows * gain_in[None, None]
    grad_hidden = cotangent.astype(F32) + own_scale * (
        dv - own_unit * jnp.mean(dv * own_unit, axis=-1, keepdims=True)
    )

    total_dt = jnp.concatenate([total_dt[:, :heads], total_dt[:, LANES : LANES + heads]], axis=1)
    whole_x = jnp.moveaxis(vec[:, :6], 0, 1).reshape(6, 2 * inner)
    whole_heads = jnp.moveaxis(vec[:, 7, : 3 * LANES].reshape(2, 3, LANES)[:, :, :heads], 0, 1)
    whole_heads = whole_heads.reshape(3, 2 * heads)
    whole_norm = vec[0, 6] + vec[1, 6]
    whole_bc = vec[0, 8:13, : 2 * LANES] + vec[1, 8:13, : 2 * LANES]

    def shard(v):
        share = v.shape[-1] // plan.shards
        return lax.dynamic_slice_in_dim(v, plan.f * share, share, v.ndim - 1)

    shard_x, shard_bc, shard_heads = shard(whole_x), shard(whole_bc), shard(whole_heads)
    return (
        output,
        grad_hidden,
        shard(whole_norm),
        total_z.astype(F32),
        total_x,
        total_bc,
        total_dt,
        total_out.astype(F32),
        shard_x[:4].T,
        shard_x[4],
        shard_bc[:4].T,
        shard_bc[4],
        shard_heads[0],
        shard_heads[1],
        shard_heads[2],
        shard_x[5],
    )


def solution(mesh):
    one, two = P("fs"), P("fs", None)
    tokens = P(None, ("fs", "sp"), None)
    return jax.shard_map(
        body,
        mesh=mesh,
        in_specs=(tokens, one, two, two, two, two, two, two, one, two, one, one, one, one, one, tokens),
        out_specs=(tokens, tokens, one, two, two, two, two, two, two, one, two, one, one, one, one, one),
        check_vma=False,
    )
```

```python
import functools

import jax
import jax.numpy as jnp
from jax import lax
from jax.experimental import pallas as pl
from jax.experimental.pallas import tpu as pltpu
from jax.sharding import PartitionSpec as P

EPSILON = 1e-05
F32, BF16 = jnp.float32, jnp.bfloat16
MESH = pl.DeviceIdType.MESH
CHUNK = 128
LANES = 128
PER_UNIT = 4
VMEM_LIMIT = 56 * 1024 * 1024
TAIL_LIMIT = 56 * 1024 * 1024
MIDDLE_LIMIT = 58 * 1024 * 1024


def dot(a, b):
    return jnp.dot(a, b, preferred_element_type=F32)


def dot_nt(a, b):
    return lax.dot_general(a, b, (((1,), (1,)), ((), ())), preferred_element_type=F32)


def dot_tn(a, b):
    return lax.dot_general(a, b, (((0,), (0,)), ((), ())), preferred_element_type=F32)


def pieces_of(v):
    high = v.astype(BF16)
    rest = v - high.astype(F32)
    middle = rest.astype(BF16)
    return high, middle, (rest - middle.astype(F32)).astype(BF16)


def exact_left(ones, v):
    return sum(dot(ones, part) for part in pieces_of(v))


def exact_right(v, ones):
    return sum(dot(part, ones) for part in pieces_of(v))


def sigmoid(v):
    return 0.5 * jnp.tanh(0.5 * v) + 0.5


def grid_iotas():
    rows = lax.broadcasted_iota(jnp.int32, (CHUNK, CHUNK), 0)
    columns = lax.broadcasted_iota(jnp.int32, (CHUNK, CHUNK), 1)
    return rows, columns


def two_heads(v, pair, low):
    return jnp.where(low, v[:, 2 * pair : 2 * pair + 1], v[:, 2 * pair + 1 : 2 * pair + 2])


def conv_of(ext, lanes, taps):
    total = taps[4:5, lanes]
    for k in range(4):
        total = total + ext[5 + k : 5 + k + CHUNK, lanes] * taps[k : k + 1, lanes]
    return total


def step_of(dt_ref, hp_ref):
    shifted = dt_ref[...].astype(F32) + hp_ref[1:2]
    return shifted, jnp.maximum(shifted, 0.0) + jnp.log1p(jnp.exp(-jnp.abs(shifted)))


def forward_kernel(
    x_ref, bc_ref, dt_ref, halo_ref, cx_ref, cbc_ref, hp_ref,
    y_ref, st_ref, own_ref, dec_ref, bcs_ref, acum_ref,
    xe, be, state, base,
):
    unit, chunk = pl.program_id(0), pl.program_id(1)
    inner = x_ref.shape[1]

    @pl.when(chunk == 0)
    def _():
        state[...] = jnp.zeros_like(state)
        base[...] = jnp.zeros_like(base)
        xe[0:8] = halo_ref[unit, :, :inner].astype(F32)[8:]
        be[0:8] = halo_ref[unit, :, inner:].astype(F32)[8:]

    @pl.when(chunk != 0)
    def _():
        xe[0:8] = xe[CHUNK:]
        be[0:8] = be[CHUNK:]

    xe[8:] = x_ref[...].astype(F32)
    be[8:] = bc_ref[...].astype(F32)
    shared = []
    for k in range(2):
        pre = conv_of(be, slice(k * LANES, (k + 1) * LANES), cbc_ref)
        shared.append(pre * sigmoid(pre))
    keys, reads = shared
    bcs_ref[:, :LANES] = keys.astype(BF16)
    bcs_ref[:, LANES:] = reads.astype(BF16)
    keys_t = keys.T.astype(BF16)
    keys, reads = keys.astype(BF16), reads.astype(BF16)
    rows, columns = grid_iotas()
    causal = rows >= columns
    _, step = step_of(dt_ref, hp_ref)
    running = exact_left(jnp.where(causal, 1.0, 0.0).astype(BF16), -step * hp_ref[0:1])
    acum_ref[...] = base[0:1] + running
    total = running[CHUNK - 1 : CHUNK]
    base[...] = base[...] + total
    running_t = running.T
    scores = jnp.where(causal, dot_nt(reads, keys), 0.0)
    low = columns < LANES // 2
    low_row = low[0:1]

    for pair in range(inner // LANES):
        lanes = slice(pair * LANES, (pair + 1) * LANES)
        pre = conv_of(xe, lanes, cx_ref)
        xs = pre * sigmoid(pre)
        weighted = xs * two_heads(step, pair, low)
        first = jnp.broadcast_to(running[:, 2 * pair : 2 * pair + 1], (CHUNK, CHUNK))
        second = jnp.broadcast_to(running[:, 2 * pair + 1 : 2 * pair + 2], (CHUNK, CHUNK))
        mix = jnp.concatenate(
            [
                (jnp.exp(jnp.minimum(first - running_t[2 * pair : 2 * pair + 1], 0.0)) * scores).astype(BF16),
                (jnp.exp(jnp.minimum(second - running_t[2 * pair + 1 : 2 * pair + 2], 0.0)) * scores).astype(BF16),
            ],
            axis=1,
        )
        own = weighted.astype(BF16)
        zero = jnp.zeros_like(own)
        stacked = jnp.concatenate([jnp.where(low, own, zero), jnp.where(low, zero, own)], axis=0)
        at = jnp.where(low, first, second)
        at_end = two_heads(total, pair, low_row)
        before = state[:, lanes]
        before_low = before.astype(BF16)
        st_ref[0, :, lanes] = before_low
        y = dot(mix, stacked) + dot(reads, before_low) * jnp.exp(at) + cx_ref[5:6, lanes] * xs
        y_ref[:, lanes] = y.astype(BF16)
        late = (weighted * jnp.exp(at_end - at)).astype(BF16)
        state[:, lanes] = before * jnp.exp(at_end) + dot(keys_t, late)

    @pl.when(chunk == PER_UNIT - 1)
    def _():
        own_ref[0] = state[...].astype(BF16)
        for pair in range(inner // LANES):
            lanes = slice(pair * LANES, (pair + 1) * LANES)
            dec_ref[0, :, lanes] = jnp.broadcast_to(
                jnp.exp(two_heads(base[0:1], pair, low_row)), (8, LANES)
            )


def gate_kernel(y0_ref, gate_ref, bcs_ref, acum_ref, in_ref, y_ref, gated_ref, ss_ref):
    _, columns = grid_iotas()
    low = columns < LANES // 2
    reads = bcs_ref[:, LANES:]
    reach = acum_ref[...]
    squares = jnp.zeros((CHUNK, LANES), F32)
    for pair in range(y0_ref.shape[1] // LANES):
        lanes = slice(pair * LANES, (pair + 1) * LANES)
        y = y0_ref[:, lanes].astype(F32) + dot(reads, in_ref[0, :, lanes]) * jnp.exp(
            two_heads(reach, pair, low)
        )
        y_ref[:, lanes] = y.astype(BF16)
        gate = gate_ref[:, lanes].astype(F32)
        gated = (y * gate * sigmoid(gate)).astype(BF16)
        gated_ref[:, lanes] = gated
        wide = gated.astype(F32)
        squares = squares + wide * wide
    ss_ref[...] = jnp.broadcast_to(jnp.sum(squares, axis=1, keepdims=True), (CHUNK, LANES))


def pull_kernel(
    dno_ref, gated_ref, gate_ref, y_ref, stats_ref, gain_ref, bcs_ref, acum_ref,
    dy_ref, dgate_ref, pull_ref,
    total, chunk=None,
):
    chunk = pl.program_id(1) if chunk is None else chunk

    @pl.when(chunk == 0)
    def _():
        total[...] = jnp.zeros_like(total)

    _, columns = grid_iotas()
    low = columns < LANES // 2
    scale = jnp.broadcast_to(stats_ref[:, 0:1], (CHUNK, LANES))
    mean = jnp.broadcast_to(stats_ref[:, 1:2], (CHUNK, LANES))
    reads_t = bcs_ref[:, LANES:].astype(F32).T.astype(BF16)
    reach = acum_ref[...]
    for pair in range(dno_ref.shape[1] // LANES):
        lanes = slice(pair * LANES, (pair + 1) * LANES)
        unit = gated_ref[:, lanes].astype(F32) * scale
        du = dno_ref[:, lanes].astype(F32) * gain_ref[0:1, lanes]
        d_gated = (scale * (du - unit * mean)).astype(BF16).astype(F32)
        gate = gate_ref[:, lanes].astype(F32)
        sg = sigmoid(gate)
        silu = gate * sg
        dy = d_gated * silu
        dy_ref[:, lanes] = dy.astype(BF16)
        dgate = d_gated * y_ref[:, lanes].astype(F32) * (sg + silu * (1.0 - sg))
        dgate_ref[:, lanes] = dgate.astype(BF16)
        total[:, lanes] += dot(reads_t, (dy * jnp.exp(two_heads(reach, pair, low))).astype(BF16))

    @pl.when(chunk == PER_UNIT - 1)
    def _():
        pull_ref[0] = total[...].astype(BF16)


def backward_kernel(
    x_ref, xp_ref, bc_ref, bcp_ref, dt_ref, halo_ref, cx_ref, cbc_ref, hp_ref,
    dy_ref, y_ref, st_ref, in_ref, acum_ref, after_ref, pick_ref,
    dall_ref, head_ref, head_bc_ref, gx_ref, gbc_ref, gh_ref,
    xe, be, adjoint, dpx, dpb, ends, place=None,
):
    unit, chunk = (pl.program_id(0), pl.program_id(1)) if place is None else place
    inner = x_ref.shape[1]

    @pl.when((unit == 0) & (chunk == 0))
    def _():
        gx_ref[...] = jnp.zeros_like(gx_ref)
        gbc_ref[...] = jnp.zeros_like(gbc_ref)
        gh_ref[...] = jnp.zeros_like(gh_ref)

    @pl.when(chunk == 0)
    def _():
        adjoint[...] = after_ref[0].astype(F32)
        dpx[CHUNK:] = jnp.zeros((8, inner), F32)
        dpb[CHUNK:] = jnp.zeros((8, 2 * LANES), F32)

    inside = chunk != PER_UNIT - 1
    xe[0:8] = jnp.where(inside, xp_ref[...].astype(F32)[8:], halo_ref[unit, :, :inner].astype(F32)[8:])
    xe[8:] = x_ref[...].astype(F32)
    be[0:8] = jnp.where(inside, bcp_ref[...].astype(F32)[8:], halo_ref[unit, :, inner:].astype(F32)[8:])
    be[8:] = bc_ref[...].astype(F32)
    shared, slopes = [], []
    for k in range(2):
        pre = conv_of(be, slice(k * LANES, (k + 1) * LANES), cbc_ref)
        sg = sigmoid(pre)
        shared.append(pre * sg)
        slopes.append(sg + pre * sg * (1.0 - sg))
    keys, reads = shared
    reads_t = reads.T.astype(BF16)
    keys, reads = keys.astype(BF16), reads.astype(BF16)
    rows, columns = grid_iotas()
    causal = rows >= columns
    shifted_dt, step = step_of(dt_ref, hp_ref)
    rate = hp_ref[0:1]
    log_decay = -step * rate
    running = exact_left(jnp.where(causal, 1.0, 0.0).astype(BF16), log_decay)
    total = running[CHUNK - 1 : CHUNK]
    base = acum_ref[0:1] - running[0:1]
    running_t = running.T
    scores_t = jnp.where(rows <= columns, dot_nt(keys, reads), 0.0)
    low = columns < LANES // 2
    low_row = low[0:1]
    d_scores = jnp.zeros((CHUNK, CHUNK), F32)
    d_reads = jnp.zeros((CHUNK, LANES), F32)
    d_keys = jnp.zeros((CHUNK, LANES), F32)
    sums = jnp.zeros((3 * CHUNK, LANES), F32)

    for pair in range(inner // LANES):
        lanes = slice(pair * LANES, (pair + 1) * LANES)
        shifted = [xe[5 + k : 5 + k + CHUNK, lanes] for k in range(4)]
        pre = cx_ref[4:5, lanes] + sum(shifted[k] * cx_ref[k : k + 1, lanes] for k in range(4))
        sg = sigmoid(pre)
        xs = pre * sg
        slope = sg + xs * (1.0 - sg)
        step_wide = two_heads(step, pair, low)
        weighted = xs * step_wide
        first = jnp.broadcast_to(running[:, 2 * pair : 2 * pair + 1], (CHUNK, CHUNK))
        second = jnp.broadcast_to(running[:, 2 * pair + 1 : 2 * pair + 2], (CHUNK, CHUNK))
        gap0 = first - running_t[2 * pair : 2 * pair + 1]
        gap1 = second - running_t[2 * pair + 1 : 2 * pair + 2]
        mix_t = jnp.concatenate(
            [
                (jnp.exp(jnp.minimum(-gap0, 0.0)) * scores_t).astype(BF16),
                (jnp.exp(jnp.minimum(-gap1, 0.0)) * scores_t).astype(BF16),
            ],
            axis=1,
        )
        dy_low = dy_ref[:, lanes]
        dy = dy_low.astype(F32)
        zero = jnp.zeros_like(dy_low)
        dy_two = jnp.concatenate([jnp.where(low, dy_low, zero), jnp.where(low, zero, dy_low)], axis=0)
        d_mix = dot_nt(dy_two, weighted.astype(BF16))
        d_scores = d_scores + (
            jnp.exp(jnp.minimum(gap0, 0.0)) * d_mix[:CHUNK]
            + jnp.exp(jnp.minimum(gap1, 0.0)) * d_mix[CHUNK:]
        )
        at = jnp.where(low, first, second)
        at_end = two_heads(total, pair, low_row)
        tail = jnp.exp(at_end - at)
        end_decay = jnp.exp(at_end)
        later = adjoint[:, lanes]
        later_low = later.astype(BF16)
        from_state = dot(keys, later_low) * tail
        d_weighted = dot(mix_t, dy_two) + from_state
        before = st_ref[0, :, lanes].astype(F32) + in_ref[0, :, lanes].astype(F32) * jnp.exp(
            two_heads(base, pair, low_row)
        )
        d_read = (dy * jnp.exp(at)).astype(BF16)
        d_reads = d_reads + dot_nt(d_read, before.astype(BF16))
        d_keys = d_keys + dot_nt((weighted * tail).astype(BF16), later_low)
        skip = cx_ref[5:6, lanes]
        y = y_ref[:, lanes].astype(F32) - skip * xs
        d_run = dy * y - weighted * d_weighted
        pick = pick_ref[lanes, :]
        sums = sums + dot(
            jnp.concatenate(
                [d_run.astype(BF16), (xs * d_weighted).astype(BF16), (dy * xs).astype(BF16)], axis=0
            ),
            pick,
        )
        ends[:, lanes] = jnp.broadcast_to(
            jnp.sum(weighted * from_state, axis=0, keepdims=True)
            + end_decay * jnp.sum(later * before, axis=0, keepdims=True),
            (8, LANES),
        )
        d_pre = (step_wide * d_weighted + skip * dy) * slope
        dpx[0:CHUNK, lanes] = d_pre
        adjoint[:, lanes] = later * end_decay + dot(reads_t, d_read)
        d_x = jnp.zeros((CHUNK, LANES), F32)
        for k in range(4):
            d_x = d_x + dpx[3 - k : 3 - k + CHUNK, lanes] * cx_ref[k : k + 1, lanes]
            gx_ref[8 * k : 8 * k + 8, lanes] += jnp.sum(
                (d_pre * shifted[k]).reshape(CHUNK // 8, 8, LANES), axis=0
            )
        gx_ref[32:40, lanes] += jnp.sum(d_pre.reshape(CHUNK // 8, 8, LANES), axis=0)
        dall_ref[:, lanes] = d_x.astype(BF16)

    d_scores_low = jnp.where(causal, d_scores, 0.0)
    d_reads = d_reads + dot(d_scores_low.astype(BF16), keys)
    d_keys = d_keys + dot(d_scores_low.T.astype(BF16), reads)
    for k, part in enumerate((d_keys, d_reads)):
        lanes = slice(k * LANES, (k + 1) * LANES)
        d_pre = part * slopes[k]
        dpb[0:CHUNK, lanes] = d_pre
        d_x = jnp.zeros((CHUNK, LANES), F32)
        for tap in range(4):
            d_x = d_x + dpb[3 - tap : 3 - tap + CHUNK, lanes] * cbc_ref[tap : tap + 1, lanes]
            gbc_ref[8 * tap : 8 * tap + 8, lanes] += jnp.sum(
                (d_pre * be[5 + tap : 5 + tap + CHUNK, lanes]).reshape(CHUNK // 8, 8, LANES), axis=0
            )
        gbc_ref[32:40, lanes] += jnp.sum(d_pre.reshape(CHUNK // 8, 8, LANES), axis=0)
        dall_ref[:, inner + k * LANES : inner + (k + 1) * LANES] = d_x.astype(BF16)

    at_end = exact_right(ends[...], pick_ref[...])[0:1]
    d_log = exact_left(jnp.where(rows <= columns, 1.0, 0.0).astype(BF16), sums[:CHUNK]) + at_end
    d_step = sums[CHUNK : 2 * CHUNK] - d_log * rate
    d_dt = d_step * sigmoid(shifted_dt)
    dall_ref[:, inner + 2 * LANES :] = d_dt.astype(BF16)
    for k, part in enumerate((d_dt, d_log * log_decay, sums[2 * CHUNK :])):
        gh_ref[8 * k : 8 * k + 8] += jnp.sum(part.reshape(CHUNK // 8, 8, LANES), axis=0)
    dpx[CHUNK:] = dpx[0:8]
    dpb[CHUNK:] = dpb[0:8]

    @pl.when(chunk == PER_UNIT - 1)
    def _():
        head_ref[0] = dpx[0:8]
        head_bc_ref[0] = dpb[0:8]


def places():
    f, z = lax.axis_index("fs"), lax.axis_index("sp")
    core, chip = f % 2, f // 2
    by_x, by_y = chip + 1 - 2 * (chip % 2), (chip + 2) % 4
    return f, z, core, chip, by_x, by_y


def remote(src, dst, sends, receives, slot, device):
    return pltpu.make_async_remote_copy(
        src_ref=src, dst_ref=dst, send_sem=sends.at[slot], recv_sem=receives.at[slot],
        device_id=device, device_id_type=MESH,
    )


class Trade:
    def __init__(self, source, sends, receives):
        self.f, self.z, self.core, self.chip, _, _ = places()
        self.source, self.sends, self.receives = source, sends, receives
        self.units = source.shape[0] // 2
        self.near_group, self.far_group = self.z // 2, 1 - self.z // 2
        across = 2 * self.chip + self.z % 2
        self.near, self.far = (across, 2 * self.near_group + self.core), (across, 2 * self.far_group + self.core)
        self.near_at, self.far_at = 2 * self.near_group + self.core, 2 * self.far_group + self.core
        self.partner = (self.f + 1 - 2 * self.core, self.z)
        self.stays = self.z % 2 == self.core
        self.moves = (self.z + self.core) % 2

    def rows_for(self, group, first, last):
        return self.source.at[pl.ds(group * self.units + first, last - first)]

    def swapped(self, at):
        return at + 1 - 2 * (at % 2)

    def send(self, src, dst, slot, device):
        return remote(src, dst, self.sends, self.receives, slot, device)


class Gather:
    def __init__(self, weight, target, sends, receives, local):
        f, z, self.core, self.chip, self.by_x, self.by_y = places()
        self.weight, self.target, self.sends, self.receives = weight, target, sends, receives
        self.partner = (f + 1 - 2 * self.core, z)
        self.over_x, self.over_y = (2 * self.by_x + self.core, z), (2 * self.by_y + self.core, z)
        self.keep = pltpu.make_async_copy(self.columns(self.core), self.part(self.chip, self.core), local.at[0])

    def columns(self, side):
        width = self.weight.shape[1] // 2
        return self.weight.at[:, pl.ds(pl.multiple_of(side * width, width), width)]

    def part(self, chip, core):
        return self.target.at[chip, core]

    def copy(self, src, dst, slot, device):
        return remote(src, dst, self.sends, self.receives, slot, device)

    def sent(self, slot):
        own, other = (self.chip, self.core), (self.chip, 1 - self.core)
        src, dst, device = (
            (self.columns(1 - self.core), own, self.partner),
            (self.columns(self.core), own, self.over_x),
            (self.columns(self.core), own, self.over_y),
            (self.part(*other), other, self.over_x),
            (self.part(*other), other, self.over_y),
            (self.part(self.by_x, self.core), (self.by_x, self.core), self.over_y),
            (self.part(self.by_y, 1 - self.core), (self.by_y, 1 - self.core), self.over_x),
        )[slot]
        return self.copy(src, self.part(*dst), slot, device)

    def arrives(self, slot):
        corner = (self.by_x + 2) % 4
        chip, core = (
            (self.chip, 1 - self.core), (self.by_x, self.core), (self.by_y, self.core),
            (self.by_x, 1 - self.core), (self.by_y, 1 - self.core), (corner, self.core), (corner, 1 - self.core),
        )[slot]
        device = (self.partner, self.over_x, self.over_y, self.over_x, self.over_y, self.over_y, self.over_x)[slot]
        there = self.part(chip, core)
        self.copy(there, there, slot, device).wait_recv()

    def start(self):
        for slot in range(3):
            self.sent(slot).start()
        self.keep.start()

    def second(self):
        self.arrives(0)
        for slot in (3, 4):
            self.sent(slot).start()

    def third(self):
        self.arrives(1)
        self.sent(5).start()

    def fourth(self):
        self.arrives(4)
        self.sent(6).start()

    def finish(self):
        for slot in (2, 3, 5, 6):
            self.arrives(slot)
        for slot in range(7):
            self.sent(slot).wait_send()
        self.keep.wait()


EARLY_UNITS = 2


def scan_forward_kernel(
    x, bc, dt, first, cot, weight, cx, cbc, hp,
    y, st, own, dec, bcs, acum, halo_out, near_out, far_out, gathered,
    xe, be, state, base, halo, halo_sends, halo_receives, sends, receives, local,
    w_sends, w_receives, w_local,
):
    gather = Gather(weight, gathered, w_sends, w_receives, w_local)
    unit, chunk = pl.program_id(0), pl.program_id(1)
    segments, trade = Segments(), Trade(cot, sends, receives)
    me, last = segments.me, segments.count - 1
    units, depth, width = halo.shape

    def halo_copy():
        at = pl.ds(first.shape[1] - depth, depth)
        device = segments.device((me + 1) % segments.count)
        return remote(first.at[:, at, pl.ds(0, width)], halo, halo_sends, halo_receives, 0, device)

    far_copy = trade.send(trade.rows_for(trade.far_group, 0, EARLY_UNITS), far_out, 0, trade.far)
    near_copy = trade.send(trade.rows_for(trade.near_group, 0, units), near_out, 1, trade.near)
    keep = pltpu.make_async_copy(trade.rows_for(trade.near_group, 0, units), near_out, local.at[0])

    @pl.when((unit == 0) & (chunk == 0))
    def _():
        barrier = pltpu.get_barrier_semaphore()
        pl.semaphore_signal(barrier, inc=1, device_id=trade.far, device_id_type=MESH)

        @pl.when(jnp.logical_not(trade.stays))
        def _():
            pl.semaphore_signal(barrier, inc=1, device_id=trade.near, device_id_type=MESH)

        @pl.when(me > 0)
        def _():
            pl.semaphore_signal(
                barrier, inc=1, device_id=segments.device((me + last) % segments.count), device_id_type=MESH
            )

        for device in (gather.partner, gather.over_x, gather.over_y):
            pl.semaphore_signal(barrier, inc=1, device_id=device, device_id_type=MESH)
        pl.semaphore_wait(barrier, 4 + trade.moves + jnp.where(me < last, 1, 0))

        @pl.when(me < last)
        def _():
            halo_copy().start()

        gather.start()
        far_copy.start()

        @pl.when(trade.stays)
        def _():
            keep.start()

        @pl.when(jnp.logical_not(trade.stays))
        def _():
            near_copy.start()

        @pl.when(me > 0)
        def _():
            halo_copy().wait_recv()

        @pl.when(me == 0)
        def _():
            halo[...] = jnp.zeros_like(halo)

        halo_out[...] = halo[...]

    forward_kernel(x, bc, dt, halo, cx, cbc, hp, y, st, own, dec, bcs, acum, xe, be, state, base)

    for at_unit, at_chunk, stage in ((0, 0, gather.second), (1, 1, gather.third), (1, 3, gather.fourth)):

        @pl.when((unit == at_unit) & (chunk == at_chunk))
        def _(stage=stage):
            stage()

    @pl.when((unit == units - 1) & (chunk == PER_UNIT - 1))
    def _():
        gather.finish()

        @pl.when(me < last)
        def _():
            halo_copy().wait_send()

        far_copy.wait()

        @pl.when(trade.stays)
        def _():
            keep.wait()

        @pl.when(jnp.logical_not(trade.stays))
        def _():
            near_copy.wait()


def one_hot(rows, columns, offset):
    i = lax.broadcasted_iota(jnp.int32, (rows, columns), 0)
    j = lax.broadcasted_iota(jnp.int32, (rows, columns), 1)
    return jnp.where(j == i + offset, 1.0, 0.0).astype(BF16)


SMALL_ROWS = 32


def head_kernel(
    hidden, w_x, w_bc, w_dt, conv_x, conv_x_bias, gate_gain, norm_gain, conv_bc, conv_bc_bias, dt_bias, a_log, skip_d,
    rows_out, first_out, cx, cbc, hp, gain_in, gain_rows,
    dt_mine, dt_other, small, small_all, local, sends, receives, small_sends, small_receives,
):
    f, z, core, chip, by_x, by_y = places()
    trade = Trade(hidden, sends, receives)
    partner, over_x, over_y = trade.partner, (2 * by_x + core, z), (2 * by_y + core, z)
    far, near, stays = trade.far, trade.near, trade.stays
    units, inner, shards = rows_out.shape[0], cx.shape[1], small_all.shape[0]
    heads = w_dt.shape[1] // 2

    barrier = pltpu.get_barrier_semaphore()
    for k in range(1, shards):
        pl.semaphore_signal(barrier, inc=1, device_id=((f + k) % shards, z), device_id_type=MESH)
    pl.semaphore_signal(barrier, inc=1, device_id=far, device_id_type=MESH)

    @pl.when(jnp.logical_not(stays))
    def _():
        pl.semaphore_signal(barrier, inc=1, device_id=near, device_id_type=MESH)

    pl.semaphore_wait(barrier, shards + trade.moves)

    def part(chip_at, core_at):
        return first_out.at[chip_at, core_at]

    def copy(src, dst, slot, device):
        return remote(src, dst, sends, receives, slot, device)

    class Thirds:
        def __init__(self, side, slot, device):
            columns = pl.ds(pl.multiple_of(side * inner, inner), inner)
            self.whole = copy(part(chip, core), part(chip, core), slot, device)
            dst, wide = part(chip, core), 2 * LANES
            dt = dt_mine if device is not partner else dt_other
            self.copies = [
                copy(w_x.at[:, columns], dst.at[:, pl.ds(0, inner)], slot, device),
                copy(w_bc, dst.at[:, pl.ds(inner, wide)], slot, device),
                copy(dt, dst.at[:, pl.ds(inner + wide, LANES)], slot, device),
            ]

        def start(self):
            for one in self.copies:
                one.start()

        def wait_send(self):
            self.whole.wait_send()

    to_far = copy(trade.rows_for(trade.far_group, 0, units), rows_out.at[:, z], 0, far)
    to_far.start()
    i = lax.broadcasted_iota(jnp.int32, (2 * heads, LANES), 0)
    j = lax.broadcasted_iota(jnp.int32, (2 * heads, LANES), 1)
    for side, kept in ((core, dt_mine), (1 - core, dt_other)):
        chosen = jnp.where((i == j + side * heads) & (j < heads), 1.0, 0.0).astype(BF16)
        kept[...] = dot(w_dt[...], chosen).astype(BF16)
    to_partner, to_x, to_y = Thirds(1 - core, 1, partner), Thirds(core, 2, over_x), Thirds(core, 3, over_y)
    for one in (to_partner, to_x, to_y):
        one.start()
    to_near = copy(trade.rows_for(trade.near_group, 0, units), rows_out.at[:, z], 4, near)
    keep_rows = pltpu.make_async_copy(trade.rows_for(trade.near_group, 0, units), rows_out.at[:, z], local.at[0])

    @pl.when(stays)
    def _():
        keep_rows.start()

    @pl.when(jnp.logical_not(stays))
    def _():
        to_near.start()

    own = part(chip, core)
    keeps = [
        pltpu.make_async_copy(
            w_x.at[:, pl.ds(pl.multiple_of(core * inner, inner), inner)], own.at[:, pl.ds(0, inner)], local.at[1]
        ),
        pltpu.make_async_copy(w_bc, own.at[:, pl.ds(inner, 2 * LANES)], local.at[2]),
        pltpu.make_async_copy(dt_mine, own.at[:, pl.ds(inner + 2 * LANES, LANES)], local.at[3]),
    ]
    for keep in keeps:
        keep.start()

    share = conv_x.shape[0]
    per_norm, per_bc, per_head = norm_gain.shape[1], conv_bc.shape[0], dt_bias.shape[1]
    built = jnp.zeros((SMALL_ROWS, share), F32)
    taps = dot_tn(conv_x[...], one_hot(share, share, 0))
    gains = dot(norm_gain[...], one_hot(per_norm, share, per_norm * (f % 2)))
    spread_bc = one_hot(per_bc, 2 * LANES, per_bc * f)
    taps_bc, bias_bc = dot_tn(conv_bc[...], spread_bc), dot(conv_bc_bias[...], spread_bc)
    spread_heads = one_hot(per_head, LANES, per_head * (f % 4))
    by_head = [dot(v[...], spread_heads) for v in (dt_bias, a_log, skip_d)]
    small[...] = built
    small[0:4] = taps
    small[4:5] = conv_x_bias[...].astype(F32)
    small[5:6] = gate_gain[...].astype(F32)
    for k in range(4):
        small[6 + k : 7 + k] = jnp.where(f // 2 == k, gains, 0.0)
    small[10:14, : 2 * LANES] = taps_bc
    small[14:15, : 2 * LANES] = bias_bc
    for side in range(2):
        for n, values in enumerate(by_head):
            small[15 + side : 16 + side, n * LANES : (n + 1) * LANES] = jnp.where(f // 4 == side, values, 0.0)

    def small_copy(k, at):
        return pltpu.make_async_remote_copy(
            src_ref=small, dst_ref=small_all.at[at],
            send_sem=small_sends.at[k], recv_sem=small_receives.at[at],
            device_id=((f + k) % shards, z), device_id_type=MESH,
        )

    for k in range(1, shards):
        small_copy(k, f).start()
    small_all[f] = small[...]

    copy(part(chip, core), part(chip, 1 - core), 1, partner).wait_recv()
    again_x = copy(part(chip, 1 - core), part(chip, 1 - core), 5, over_x)
    again_x.start()
    again_y = copy(part(chip, 1 - core), part(chip, 1 - core), 6, over_y)
    again_y.start()

    near_at, far_at = trade.near_at, trade.far_at

    @pl.when(stays)
    def _():
        keep_rows.wait()

    @pl.when(jnp.logical_not(stays))
    def _():
        copy(trade.rows_for(trade.near_group, 0, units), rows_out.at[:, near_at], 4, near).wait_recv()

    near_on = copy(rows_out.at[:, near_at], rows_out.at[:, near_at], 7, partner)
    near_on.start()

    for k in range(1, shards):
        small_copy(k, (f + k) % shards).wait_recv()
    cx[...] = jnp.zeros_like(cx)
    for k in range(4):
        block = small_all[4 * core + k]
        lanes = slice(k * share, (k + 1) * share)
        cx[0:5, lanes] = block[0:5]
        gain_rows[:, lanes] = jnp.broadcast_to(block[5:6], (8, share))
    summed = small_all[0]
    for k in range(1, shards):
        summed = summed + small_all[k]
    for k in range(4):
        gain_in[:, k * share : (k + 1) * share] = jnp.broadcast_to(summed[6 + k : 7 + k], (8, share))
    cbc[...] = jnp.zeros_like(cbc)
    cbc[0:5] = summed[10:15, : 2 * LANES]
    ours = jnp.where(core == 0, summed[15:16], summed[16:17])
    lane = lax.broadcasted_iota(jnp.int32, (1, LANES), 1)
    hp[...] = jnp.zeros_like(hp)
    hp[0:1] = jnp.where(lane < heads, jnp.exp(ours[:, LANES : 2 * LANES]), 0.0)
    hp[1:2] = ours[:, :LANES]
    skips = ours[:, 2 * LANES :]
    for pair in range(inner // LANES):
        cx[5:6, pair * LANES : (pair + 1) * LANES] = two_heads(skips, pair, lane < LANES // 2)

    copy(part(by_x, core), part(by_x, core), 2, over_x).wait_recv()
    on_y = copy(part(by_x, core), part(by_x, core), 8, over_y)
    on_y.start()
    copy(part(by_y, core), part(by_y, core), 3, over_y).wait_recv()
    copy(part(by_x, 1 - core), part(by_x, 1 - core), 5, over_x).wait_recv()
    copy(part(by_y, 1 - core), part(by_y, 1 - core), 6, over_y).wait_recv()
    on_x = copy(part(by_y, 1 - core), part(by_y, 1 - core), 9, over_x)
    on_x.start()

    copy(trade.rows_for(trade.far_group, 0, units), rows_out.at[:, far_at], 0, far).wait_recv()
    far_on = copy(rows_out.at[:, far_at], rows_out.at[:, far_at], 10, partner)
    far_on.start()

    corner = (by_x + 2) % 4
    copy(part(corner, core), part(corner, core), 8, over_y).wait_recv()
    copy(part(corner, 1 - core), part(corner, 1 - core), 9, over_x).wait_recv()
    copy(rows_out.at[:, near_at], rows_out.at[:, trade.swapped(near_at)], 7, partner).wait_recv()
    copy(rows_out.at[:, far_at], rows_out.at[:, trade.swapped(far_at)], 10, partner).wait_recv()
    for sent in (to_far, to_partner, to_x, to_y, again_x, again_y, near_on, on_y, on_x, far_on):
        sent.wait_send()

    @pl.when(jnp.logical_not(stays))
    def _():
        to_near.wait_send()

    for k in range(1, shards):
        small_copy(k, f).wait_send()
    for keep in keeps:
        keep.wait()


def states_kernel(
    own, dec, cot, near_rows, far_rows, normed, w_gate, w_out, y0, bcs, acum,
    dec_out, rows_out, gathered, gate_out, incoming_out, y, gated, squares,
    incoming, parts, decs, results, weight, gate, blocks,
    sends, receives, dec_sends, dec_receives, back_sends, back_receives,
    row_sends, row_receives, w_sends, w_receives, local, w_local, block_sems,
):
    i = pl.program_id(0)
    chunks = pl.num_programs(0) - 1
    segments, trade = Segments(), Trade(cot, row_sends, row_receives)
    gather = Gather(w_out, gathered, w_sends, w_receives, w_local)
    me, count, z = segments.me, segments.count, segments.z
    units, share = own.shape[0], parts.shape[2]
    early = far_rows.shape[0]
    near_at, far_at = trade.near_at, trade.far_at
    block = blocks.shape[1]
    count_blocks = gate.shape[0] // block

    def rows_of(k):
        return pl.ds(pl.multiple_of(k * share, share), share)

    def out_copy(k, at_me):
        other, device = segments.peer(k)
        src, slot = (own.at[:, rows_of(other)], me) if at_me else (own.at[:, rows_of(me)], other)
        return pltpu.make_async_remote_copy(
            src_ref=src, dst_ref=parts.at[slot], send_sem=sends.at[k], recv_sem=receives.at[slot],
            device_id=device, device_id_type=MESH,
        )

    def dec_copy(k, at_me):
        other, device = segments.peer(k)
        slot = me if at_me else other
        return pltpu.make_async_remote_copy(
            src_ref=dec, dst_ref=decs.at[slot], send_sem=dec_sends.at[k], recv_sem=dec_receives.at[slot],
            device_id=device, device_id_type=MESH,
        )

    def back_copy(k, at_me):
        other, device = segments.peer(k)
        slot = me if at_me else other
        return pltpu.make_async_remote_copy(
            src_ref=results.at[other], dst_ref=incoming.at[:, rows_of(slot)],
            send_sem=back_sends.at[k], recv_sem=back_receives.at[slot],
            device_id=device, device_id_type=MESH,
        )

    def fetch(k):
        return pltpu.make_async_copy(normed.at[pl.ds(k * block, block)], blocks.at[k % 2], block_sems.at[k % 2])

    def multiply(k):
        if k + 1 < count_blocks:
            fetch(k + 1).start()
        fetch(k).wait()

        def part(n, carry):
            columns = pl.ds(pl.multiple_of(n * 384, 384), 384)
            gate[pl.ds(k * block, block), columns] = dot(blocks[k % 2], weight[:, columns]).astype(BF16)
            return carry

        lax.fori_loop(0, gate.shape[1] // 384, part, 0)

    last = trade.send(trade.rows_for(trade.far_group, early, units), rows_out.at[early:, z], 0, trade.far)
    last_came = trade.send(
        trade.rows_for(trade.far_group, early, units), rows_out.at[early:, far_at], 0, trade.far
    )
    near_on = trade.send(near_rows, rows_out.at[:, near_at], 1, trade.partner)
    far_on = trade.send(far_rows, rows_out.at[:early, far_at], 2, trade.partner)
    last_on = trade.send(rows_out.at[early:, far_at], rows_out.at[early:, far_at], 3, trade.partner)
    near_keep = pltpu.make_async_copy(near_rows, rows_out.at[:, near_at], local.at[0])
    far_keep = pltpu.make_async_copy(far_rows, rows_out.at[:early, far_at], local.at[1])
    take_weight = pltpu.make_async_copy(w_gate, weight, local.at[2])
    keep_gate = pltpu.make_async_copy(gate, gate_out, local.at[3])
    keep_states = pltpu.make_async_copy(incoming, incoming_out, local.at[4])

    @pl.when(i == 0)
    def _():
        barrier = pltpu.get_barrier_semaphore()
        for k in range(1, count):
            pl.semaphore_signal(barrier, inc=1, device_id=segments.peer(k)[1], device_id_type=MESH)
        for device in (trade.partner, trade.far):
            pl.semaphore_signal(barrier, inc=1, device_id=device, device_id_type=MESH)
        pl.semaphore_wait(barrier, count + 1)
        for k in range(1, count):
            dec_copy(k, True).start()
            out_copy(k, True).start()
        take_weight.start()
        fetch(0).start()
        last.start()
        near_on.start()
        far_on.start()
        near_keep.start()
        far_keep.start()
        parts[me] = own[:, rows_of(me)]
        decs[me] = dec[...]
        take_weight.wait()
        for k in range(count_blocks // 2):
            multiply(k)
        for k in range(1, count):
            dec_copy(k, False).wait_recv()
            out_copy(k, False).wait_recv()
        dec_out[...] = decs[...]
        running = [jnp.zeros((share, own.shape[2]), F32) for _ in range(units)]
        for n in range(count):
            for u in range(units):
                results[n, u] = running[u].astype(BF16)
                running[u] = running[u] * decs[n, u : u + 1] + parts[n, u].astype(F32)
        incoming[:, rows_of(me)] = results[me]
        for k in range(1, count):
            back_copy(k, True).start()
        gather.start()
        multiply(count_blocks // 2)
        gather.second()
        for k in range(count_blocks // 2 + 1, count_blocks):
            multiply(k)
        keep_gate.start()
        last_came.wait_recv()
        last_on.start()
        for k in range(1, count):
            back_copy(k, False).wait_recv()
        keep_states.start()

    @pl.when(i > 0)
    def _():
        place = pl.ds(pl.multiple_of((i - 1) * CHUNK, CHUNK), CHUNK)
        gate_kernel(
            y0, gate.at[place], bcs, acum, incoming.at[pl.ds((i - 1) // PER_UNIT, 1)], y, gated, squares
        )

    @pl.when(i == 3)
    def _():
        gather.third()

    @pl.when(i == 6)
    def _():
        gather.fourth()

    @pl.when(i == chunks)
    def _():
        other_near, other_far = trade.swapped(near_at), trade.swapped(far_at)
        trade.send(near_rows, rows_out.at[:, other_near], 1, trade.partner).wait_recv()
        trade.send(far_rows, rows_out.at[:early, other_far], 2, trade.partner).wait_recv()
        trade.send(rows_out.at[early:, far_at], rows_out.at[early:, other_far], 3, trade.partner).wait_recv()
        for copy in (last, near_on, far_on, last_on):
            copy.wait_send()
        for k in range(1, count):
            dec_copy(k, True).wait_send()
            out_copy(k, True).wait_send()
            back_copy(k, True).wait_send()
        for copy in (near_keep, far_keep, keep_gate, keep_states):
            copy.wait()
        gather.finish()


class Reduction:
    def __init__(self, pieces, sends, receives, base, special=None):
        self.f, self.z, self.core, self.chip, self.by_x, self.by_y = places()
        self.corner, self.bit = (self.by_x + 2) % 4, self.z % 2
        self.sends, self.receives, self.base, self.special = sends, receives, base, special
        self.pieces, z_start = [], 0
        for n, (start, width, way) in enumerate(pieces):
            wide = width + LANES if start == special else 2 * width
            self.pieces.append((n, start, width, way, z_start, wide))
            z_start += wide
        self.wide = z_start
        self.partner = (self.f + 1 - 2 * self.core, self.z)
        self.over = {"x": (2 * self.by_x + self.core, self.z), "y": (2 * self.by_y + self.core, self.z)}
        self.near, self.far = (self.f, self.z + 1 - 2 * self.bit), (self.f, (self.z + 2) % 4)

    @staticmethod
    def at(i, size):
        return pl.ds(pl.multiple_of(i * size, size), size)

    def copy(self, src, dst, n, k, device):
        return remote(src, dst, self.sends, self.receives, self.base + 7 * n + k, device)

    def over_chips(self, source, own, passed, r1, s2, r2, sp, rp, total):
        self.source, self.own, self.passed = source, own, passed
        self.r1, self.s2, self.r2, self.sp, self.rp, self.total = r1, s2, r2, sp, rp, total
        self.rows = r2.shape[0]

    def first_copies(self, piece):
        n, start, width, way, _, _ = piece
        columns = pl.ds(start, width)
        to = self.by_x if way == "x" else self.by_y
        return [
            self.copy(self.source(i, columns), self.r1.at[k, :, columns], n, k, self.over[way])
            for k, i in enumerate((to, self.corner))
        ]

    def second_copy(self, piece):
        n, start, width, way, _, _ = piece
        columns = pl.ds(start, width)
        other = "y" if way == "x" else "x"
        return self.copy(self.s2.at[:, columns], self.r2.at[:, columns], n, 2, self.over[other])

    def pair_copy(self, piece):
        n, start, width, _, _, _ = piece
        columns = pl.ds(start, width)
        return self.copy(self.sp.at[:, columns], self.rp.at[:, columns], n, 3, self.partner)

    def start(self, pieces=None):
        for piece in self.pieces if pieces is None else pieces:
            for copy in self.first_copies(piece):
                copy.start()

    def after_first(self, piece):
        _, start, width, way, _, _ = piece
        if self.source is not None:
            for copy in self.first_copies(piece):
                copy.wait_recv()
        columns = pl.ds(start, width)
        passed = self.passed(self.by_y if way == "x" else self.by_x, columns)
        self.s2[:, columns] = (passed.astype(F32) + self.r1[1, :, columns].astype(F32)).astype(BF16)
        self.second_copy(piece).start()

    def chip_sum(self, piece, side):
        columns = pl.ds(piece[1], piece[2])
        there = self.at(side, self.rows // 2)
        own = self.own(side, columns).astype(F32)
        return own + self.r1[0, there, columns].astype(F32) + self.r2[there, columns].astype(F32)

    def lanes_at(self, start, side, width):
        return pl.ds(pl.multiple_of(start + side * width, LANES), width)

    def after_second(self, piece):
        _, start, width, _, z_at, _ = piece
        self.second_copy(piece).wait_recv()
        self.sp[:, pl.ds(start, width)] = self.chip_sum(piece, 1 - self.core).astype(BF16)
        self.pair_copy(piece).start()

    def after_pair(self, piece):
        _, start, width, _, z_at, _ = piece
        self.pair_copy(piece).wait_recv()
        own = self.chip_sum(piece, self.core)
        came = self.rp[:, pl.ds(start, width)]
        if start == self.special:
            both = 2 * LANES
            self.total[:, pl.ds(z_at, both)] = (own[:, :both] + came[:, :both].astype(F32)).astype(BF16)
            self.total[:, self.lanes_at(z_at + both, self.core, LANES)] = own[:, both:].astype(BF16)
            self.total[:, self.lanes_at(z_at + both, 1 - self.core, LANES)] = came[:, both:]
        else:
            self.total[:, self.lanes_at(z_at, self.core, width)] = own.astype(BF16)
            self.total[:, self.lanes_at(z_at, 1 - self.core, width)] = came

    def drain_chips(self):
        for piece in self.pieces:
            firsts = [] if self.source is None else self.first_copies(piece)
            for copy in firsts + [self.second_copy(piece), self.pair_copy(piece)]:
                copy.wait_send()

    def over_members(self, total, came, sums, across, last, store):
        self.total, self.store = total, store
        self.came, self.sums, self.across, self.last = came, sums, across, last
        self.half = total.shape[0] // 2

    def z_copy(self, piece, k):
        n, _, _, _, start, wide = piece
        columns = pl.ds(start, wide)
        src, dst, device = (
            (self.total.at[self.at(1 - self.bit, self.half), columns], self.came, self.near),
            (self.sums.at[0, :, columns], self.across, self.far),
            (self.sums.at[1, :, columns], self.last, self.near),
        )[k]
        return self.copy(src, dst.at[:, columns], n, 4 + k, device)

    def start_members(self, piece):
        self.z_copy(piece, 0).start()

    def after_near(self, piece):
        columns = pl.ds(piece[4], piece[5])
        self.z_copy(piece, 0).wait_recv()
        own = self.total[self.at(self.bit, self.half), columns].astype(F32)
        self.sums[0, :, columns] = (own + self.came[:, columns].astype(F32)).astype(BF16)
        self.z_copy(piece, 1).start()

    def after_far(self, piece):
        columns = pl.ds(piece[4], piece[5])
        self.z_copy(piece, 1).wait_recv()
        total = self.sums[0, :, columns].astype(F32) + self.across[:, columns].astype(F32)
        self.sums[1, :, columns] = total.astype(BF16)
        self.z_copy(piece, 2).start()
        self.store(piece, self.at(self.bit, self.half), total.astype(BF16).astype(F32))

    def after_last(self, piece):
        self.z_copy(piece, 2).wait_recv()
        values = self.last[:, pl.ds(piece[4], piece[5])].astype(F32)
        self.store(piece, self.at(1 - self.bit, self.half), values)

    def drain_members(self):
        for piece in self.pieces:
            for k in range(3):
                self.z_copy(piece, k).wait_send()


def chip_scratch(rows, width):
    return [
        pltpu.VMEM((2, 2 * rows, width), BF16),
        pltpu.VMEM((2 * rows, width), BF16),
        pltpu.VMEM((2 * rows, width), BF16),
        pltpu.VMEM((rows, width), BF16),
        pltpu.VMEM((rows, width), BF16),
    ]


def member_scratch(rows, wide):
    half = (rows // 2, wide)
    return [
        pltpu.VMEM(half, BF16), pltpu.VMEM((2,) + half, BF16),
        pltpu.VMEM(half, BF16), pltpu.VMEM(half, BF16),
    ]


FIRST_PIECES = ((0, 512, "x"), (1024, 512, "y"), (512, 512, "x"), (1536, 384, "y"))
HALF_PIECES = ((0, 768, "x"), (768, 768, "y"))


def tail_kernel(
    normed, d_all, d_base, w_first, unit_rows, g_x, g_bc, g_heads, g_gate, z_total,
    out_x, out_bc, out_dt, vec_out, d_out, out_z,
    turned, g, d_part, d_came, local, r1, s2, r2, sp, rp, total, came, sums, across, last,
    z_came, z_sums, z_across, z_last, end_x, end_bc, end_dt, end_z,
    vs, vr, vec_all, sends, receives, vec_sends, vec_receives,
):
    i = pl.program_id(0)
    steps = pl.num_programs(0) // 2
    f, z, core, chip, by_x, by_y = places()
    rows = g.shape[0] // 4
    inner = out_x.shape[1] // 2
    wide = normed.shape[1]
    bit, upper, units = z % 2, z // 2, d_part.shape[0]
    first = Reduction(FIRST_PIECES, sends, receives, 0, inner)
    gate = Reduction(HALF_PIECES, sends, receives, 7 * len(FIRST_PIECES))
    slot = 7 * (len(FIRST_PIECES) + len(HALF_PIECES))
    partner, near, far = first.partner, first.near, first.far
    token_near, token_far = (2 * chip + bit, 2 * upper + core), (2 * chip + bit, 2 * (1 - upper) + core)
    stays = bit == core

    def d_pair(k, n):
        return remote(d_part.at[:, k, 1 - core], d_came.at[:, k], sends, receives, slot + n, partner)

    def d_trade(k, n, device, group):
        return remote(
            d_part.at[:, k, core], d_out.at[pl.ds(group * units, units)], sends, receives, slot + 2 + n, device
        )

    def d_add(k):
        for u in range(units):
            d_part[u, k, core] = (d_part[u, k, core].astype(F32) + d_came[u, k].astype(F32)).astype(BF16)

    d_keep = pltpu.make_async_copy(d_part.at[:, upper, core], d_out.at[pl.ds(upper * units, units)], local.at[0])

    first.over_chips(
        lambda i, columns: g.at[first.at(i, rows), columns],
        lambda side, columns: g[pl.ds(pl.multiple_of(chip * rows + side * (rows // 2), rows // 2), rows // 2), columns],
        lambda i, columns: g[first.at(i, rows), columns],
        r1, s2, r2, sp, rp, total,
    )

    def store_first(piece, there, values):
        _, start, width, _, _, _ = piece
        if start == inner:
            end_bc[there, :] = values[:, : 2 * LANES]
            end_dt[there, :] = values[:, 2 * LANES :]
        else:
            end_x[there, pl.ds(start, width)] = values[:, :width]
            end_x[there, pl.ds(inner + start, width)] = values[:, width:]

    def store_gate(piece, there, values):
        _, start, width, _, _, _ = piece
        end_z[there, pl.ds(start, width)] = values[:, :width]
        end_z[there, pl.ds(inner + start, width)] = values[:, width:]

    gate.over_members(z_total, z_came, z_sums, z_across, z_last, store_gate)
    first.over_members(total, came, sums, across, last, store_first)

    vec_ways = [first.over["x"], first.over["y"], near, far]

    def vec_copy(k):
        return remote(vs.at[k], vr.at[k], vec_sends, vec_receives, k, vec_ways[k])

    def vec_last(side):
        return remote(vec_all.at[core], vec_all.at[side], vec_sends, vec_receives, 4, partner)

    def vec_step(k):
        if k:
            vec_copy(k - 1).wait_recv()
            summed = vs[k - 1] + vr[k - 1]
            if k < 4:
                vs[k] = summed
            else:
                vec_all[core] = summed
        if k < 4:
            vec_copy(k).start()
        else:
            vec_last(core).start()

    early, late = first.pieces[:2], first.pieces[2:]

    def pair_on(piece):
        first.after_pair(piece)
        first.start_members(piece)

    @pl.when(i == 0)
    def _():
        barrier = pltpu.get_barrier_semaphore()
        for device in (partner, first.over["x"], first.over["y"], near, far, token_far):
            pl.semaphore_signal(barrier, inc=1, device_id=device, device_id_type=MESH)

        @pl.when(jnp.logical_not(stays))
        def _():
            pl.semaphore_signal(barrier, inc=1, device_id=token_near, device_id_type=MESH)

        pl.semaphore_wait(barrier, 6 + (bit + core) % 2)
        for piece in gate.pieces:
            gate.start_members(piece)
        vs[0] = jnp.zeros(vs.shape[1:], F32)

    @pl.when(i < steps)
    def _():
        def part(n, carry):
            columns = pl.ds(pl.multiple_of(n * 384, 384), 384)
            g[pl.ds(pl.multiple_of(i * wide, wide), wide), columns] = dot(
                turned[...], d_all[:, columns]
            ).astype(BF16)
            return carry

        turned[...] = normed[...].T
        lax.fori_loop(0, g.shape[1] // 384, part, 0)

    @pl.when(i == steps - 1)
    def _():
        first.start(early)

    @pl.when(i == steps + 4)
    def _():
        for piece in early:
            first.after_first(piece)
        first.start(late)

    @pl.when(i >= steps)
    def _():
        columns = pl.ds(pl.multiple_of((i - steps) * wide, wide), wide)
        per = d_all.shape[0] // units

        def part(u, carry):
            there = pl.ds(pl.multiple_of(u * per, per), per)
            product = d_base[there, :].astype(F32) + dot_nt(d_all[there, :], w_first[...])
            d_part[u, :, :, :, columns] = product.astype(BF16).reshape(2, 2, per // 4, wide)
            return carry + jnp.sum(product * unit_rows[there, :].astype(F32), axis=0, keepdims=True)

        vs[0, 6:7, columns] = lax.fori_loop(0, units, part, jnp.zeros((1, wide), F32))

    @pl.when(i == steps)
    def _():
        for piece in gate.pieces:
            gate.after_near(piece)

    @pl.when(i == 2 * steps - 1)
    def _():
        d_pair(1 - upper, 0).start()
        d_pair(upper, 1).start()
        for k in range(5):
            vs[0, k : k + 1] = jnp.sum(g_x[8 * k : 8 * k + 8], axis=0, keepdims=True)
            vs[0, 8 + k : 9 + k, : 2 * LANES] = jnp.sum(g_bc[8 * k : 8 * k + 8], axis=0, keepdims=True)
        vs[0, 5:6] = g_gate[...]
        for k in range(3):
            vs[0, 7:8, k * LANES : (k + 1) * LANES] = jnp.sum(
                g_heads[8 * k : 8 * k + 8], axis=0, keepdims=True
            )
        vec_step(0)
        d_pair(1 - upper, 0).wait_recv()
        d_add(1 - upper)
        d_trade(1 - upper, 0, token_far, upper).start()
        d_pair(upper, 1).wait_recv()
        d_add(upper)

        @pl.when(stays)
        def _():
            d_keep.start()

        @pl.when(jnp.logical_not(stays))
        def _():
            d_trade(upper, 1, token_near, upper).start()

        order = (
            (first.after_second, early), (1, ()), (pair_on, early), (2, ()), (first.after_first, late),
            (gate.after_far, gate.pieces), (3, ()), (first.after_second, late), (4, ()),
            (first.after_near, early), (pair_on, late), (gate.after_last, gate.pieces), (first.after_far, early),
            (first.after_near, late), (first.after_last, early), (first.after_far, late), (first.after_last, late),
        )
        for stage, pieces in order:
            if not pieces:
                vec_step(stage)
            for piece in pieces:
                stage(piece)
        ends = [
            pltpu.make_async_copy(src, dst, local.at[1 + n])
            for n, (src, dst) in enumerate(
                ((end_x, out_x), (end_bc, out_bc), (end_dt, out_dt), (end_z, out_z))
            )
        ]
        for end in ends:
            end.start()
        vec_last(1 - core).wait_recv()
        vec_out[...] = vec_all[...]
        d_trade(1 - upper, 0, token_far, 1 - upper).wait_recv()

        @pl.when(stays)
        def _():
            d_keep.wait()

        @pl.when(jnp.logical_not(stays))
        def _():
            d_trade(upper, 1, token_near, upper).wait()

        d_trade(1 - upper, 0, token_far, upper).wait_send()
        d_pair(1 - upper, 0).wait_send()
        d_pair(upper, 1).wait_send()
        first.drain_chips()
        first.drain_members()
        gate.drain_members()
        for k in range(4):
            vec_copy(k).wait_send()
        vec_last(core).wait_send()
        for end in ends:
            end.wait()


def trade_steps(source, target, local, sends, receives):
    f, z, core, chip, _, _ = places()
    units = source.shape[0]
    bit, upper = z % 2, z // 2
    near, far = (2 * chip + bit, 2 * upper + core), (2 * chip + bit, 2 * (1 - upper) + core)
    stays = bit == core

    def copy(k, n, device, group):
        return remote(source.at[:, k], target.at[pl.ds(group * units, units)], sends, receives, n, device)

    keep = pltpu.make_async_copy(source.at[:, upper], target.at[pl.ds(upper * units, units)], local.at[0])

    def start():
        copy(1 - upper, 0, far, upper).start()

        @pl.when(stays)
        def _():
            keep.start()

        @pl.when(jnp.logical_not(stays))
        def _():
            copy(upper, 1, near, upper).start()

    def finish():
        copy(1 - upper, 0, far, 1 - upper).wait_recv()
        copy(1 - upper, 0, far, upper).wait_send()

        @pl.when(stays)
        def _():
            keep.wait()

        @pl.when(jnp.logical_not(stays))
        def _():
            copy(upper, 1, near, upper).wait()

    return start, finish, far, near, stays


class Segments:
    def __init__(self):
        self.f, self.z, self.core, self.chip, _, _ = places()
        self.group = self.z // 2
        self.me = self.chip * 2 + self.z % 2
        self.count = 8

    def device(self, i):
        return ((i // 2) * 2 + self.core, self.group * 2 + i % 2)

    def peer(self, k):
        other = (self.me + k) % self.count
        return other, self.device(other)


def middle_kernel(
    dno, gated, gate, y_pull, stats, gain, bcs, acum_pull, decays, normed, w_gate, g_out, projected,
    x, xp, bc, bcp, dt, halo, cx, cbc, hp, y, st, incoming, acum, pick,
    d_all, heads_x, heads_bc, g_x, g_bc, g_heads, d_base_out, tokens_out, total_out, z_out,
    dy_all, dgate_all, pulled, own, after, parts, results, blocks, turned, w_blocks, products, g_z, out_own,
    o_r1, o_s2, o_r2, o_sp, o_rp, o_total, o_came, o_sums, o_across, o_last,
    z_r1, z_r2, z_rp, z_total,
    xe, be, adjoint, dpx, dpb, ends,
    local, keep_sems, block_sems, w_sems, product_sems, trade_local, trade_sends, trade_receives, sends, receives,
    state_sends, state_receives, back_sends, back_receives,
):
    i = pl.program_id(0)
    chunks = (pl.num_programs(0) - 1) // 2
    f, z, core, chip, by_x, by_y = places()
    segments = Segments()
    me, count = segments.me, segments.count
    units, share = own.shape[0], parts.shape[2]
    rows = g_z.shape[0] // 4
    half = rows // 2
    inner = g_z.shape[1]

    def at(k, size):
        return pl.ds(pl.multiple_of(k * size, size), size)

    start_trade, finish_trade, trade_far, trade_near, stays = trade_steps(
        projected, tokens_out, trade_local, trade_sends, trade_receives
    )
    out = Reduction(HALF_PIECES, sends, receives, 0)
    gz = Reduction(HALF_PIECES, sends, receives, 7 * len(HALF_PIECES))
    out.over_chips(
        lambda k, columns: g_out.at[at(k, rows), columns],
        lambda side, columns: out_own[at(side, half), columns],
        lambda k, columns: o_s2[:, columns],
        o_r1, o_s2, o_r2, o_sp, o_rp, o_total,
    )

    out.over_members(o_total, o_came, o_sums, o_across, o_last, lambda piece, there, values: None)
    gz.over_chips(
        lambda k, columns: g_z.at[at(k, rows), columns],
        lambda side, columns: g_z[pl.ds(pl.multiple_of(chip * rows + side * half, half), half), columns],
        lambda k, columns: g_z[at(k, rows), columns],
        z_r1, o_s2, z_r2, o_sp, z_rp, z_total,
    )
    left, right = (pl.ds(start, width) for start, width, _ in HALF_PIECES)
    own_rows = pltpu.make_async_copy(g_out.at[at(chip, rows)], out_own, local.at[0])
    pass_left = pltpu.make_async_copy(g_out.at[at(by_y, rows), left], o_s2.at[:, left], local.at[1])
    pass_right = pltpu.make_async_copy(g_out.at[at(by_x, rows), right], o_s2.at[:, right], local.at[2])

    def keep_out():
        copies = []
        for piece in out.pieces:
            n, start, width, _, z_at, _ = piece
            for side, (src, half_at) in enumerate(((o_sums.at[1], out.bit), (o_last, 1 - out.bit))):
                for part in range(2):
                    slot = 4 * n + 2 * side + part
                    copies.append(
                        pltpu.make_async_copy(
                            src.at[:, pl.ds(z_at + part * width, width)],
                            total_out.at[out.at(half_at, out.half), pl.ds(part * inner + start, width)],
                            keep_sems.at[slot],
                        )
                    )
        return copies

    keep_z = pltpu.make_async_copy(z_total, z_out, local.at[7])
    taken = (own_rows, pass_left, pass_right)

    def fetch(k):
        columns = pl.ds(k * 256, 256)
        return pltpu.make_async_copy(normed.at[:, columns], blocks.at[k % 2], block_sems.at[k % 2])

    @pl.when(i == 0)
    def _():
        barrier = pltpu.get_barrier_semaphore()
        for k in range(1, count):
            pl.semaphore_signal(barrier, inc=1, device_id=segments.peer(k)[1], device_id_type=MESH)
        for device in (out.partner, out.far, trade_far):
            pl.semaphore_signal(barrier, inc=1, device_id=device, device_id_type=MESH)

        @pl.when(jnp.logical_not(stays))
        def _():
            pl.semaphore_signal(barrier, inc=1, device_id=trade_near, device_id_type=MESH)

        pl.semaphore_wait(barrier, count + 2 + (z + core) % 2)
        out.start()
        for copy in taken:
            copy.start()
        start_trade()

    @pl.when(i < chunks)
    def _():
        place = at(i, CHUNK)
        pull_kernel(
            dno, gated, gate, y_pull, stats, gain, bcs, acum_pull,
            dy_all.at[place], dgate_all.at[place], own.at[pl.ds(i // PER_UNIT, 1)],
            pulled, chunk=i % PER_UNIT,
        )

    def state_copy(k, at_me):
        other, device = segments.peer(k)
        src, slot = (own.at[:, at(other, share)], me) if at_me else (own.at[:, at(me, share)], other)
        return pltpu.make_async_remote_copy(
            src_ref=src, dst_ref=parts.at[slot],
            send_sem=state_sends.at[k], recv_sem=state_receives.at[slot],
            device_id=device, device_id_type=MESH,
        )

    def back_copy(k, at_me):
        other, device = segments.peer(k)
        slot = me if at_me else other
        return pltpu.make_async_remote_copy(
            src_ref=results.at[other], dst_ref=after.at[:, at(slot, share)],
            send_sem=back_sends.at[k], recv_sem=back_receives.at[slot],
            device_id=device, device_id_type=MESH,
        )

    def multiply(k):
        if k < 5:
            fetch(k + 1).start()
        fetch(k).wait()

        turned[...] = blocks[k % 2].T

        def part(n, carry):
            columns = pl.ds(pl.multiple_of(n * 256, 256), 256)
            product = dot(turned[...], dgate_all[:, columns])
            g_z[pl.ds(k * 256, 256), columns] = product.astype(BF16)
            return carry

        lax.fori_loop(0, inner // 256, part, 0)

    def fetch_w(k):
        return pltpu.make_async_copy(w_gate.at[pl.ds(k * 256, 256)], w_blocks.at[k % 2], w_sems.at[k % 2])

    def put(k):
        return pltpu.make_async_copy(
            products.at[k % 2], d_base_out.at[:, pl.ds(k * 256, 256)], product_sems.at[k % 2]
        )

    def project(k):
        if k < 5:
            fetch_w(k + 1).start()
        fetch_w(k).wait()
        if k > 1:
            put(k - 2).wait()
        per = dgate_all.shape[0] // units

        def part(n, carry):
            there = pl.ds(pl.multiple_of(n * per, per), per)
            products[k % 2, there, :] = dot_nt(dgate_all[there, :], w_blocks[k % 2]).astype(BF16)
            return carry

        lax.fori_loop(0, units, part, 0)
        put(k).start()

    @pl.when(i == chunks)
    def _():
        for k in range(1, count):
            state_copy(k, True).start()
        fetch(0).start()
        fetch_w(0).start()
        parts[me] = own[:, at(me, share)]
        for k in range(6):
            multiply(k)
        for k in range(1, count):
            state_copy(k, False).wait_recv()
        running = [jnp.zeros((share, inner), F32) for _ in range(units)]
        for n in range(count - 1, -1, -1):
            for u in range(units):
                results[n, u] = running[u].astype(BF16)
                running[u] = running[u] * decays[n, u : u + 1] + parts[n, u].astype(F32)
        after[:, at(me, share)] = results[me]
        for k in range(1, count):
            back_copy(k, True).start()
        for k in range(6):
            project(k)
        put(4).wait()
        put(5).wait()
        for k in range(1, count):
            back_copy(k, False).wait_recv()
        for k in range(1, count):
            state_copy(k, True).wait_send()
            back_copy(k, True).wait_send()
        for copy in taken:
            copy.wait()
        for piece in out.pieces:
            out.after_first(piece)
        gz.start()

    def at_step(n, *stages):
        @pl.when(i == chunks + 1 + n)
        def _():
            for stage, reduction in stages:
                for piece in reduction.pieces:
                    stage(piece)

    @pl.when(i > chunks)
    def _():
        n = i - chunks - 1
        unit, chunk = n // PER_UNIT, n % PER_UNIT
        place = at(unit * PER_UNIT + PER_UNIT - 1 - chunk, CHUNK)
        backward_kernel(
            x, xp, bc, bcp, dt, halo, cx, cbc, hp, dy_all.at[place], y, st, incoming, acum,
            after.at[pl.ds(unit, 1)], pick, d_all, heads_x, heads_bc, g_x, g_bc, g_heads,
            xe, be, adjoint, dpx, dpb, ends, place=(unit, chunk),
        )

    at_step(2, (out.after_second, out))
    at_step(3, (out.after_pair, out), (out.start_members, out))
    at_step(5, (out.after_near, out))

    @pl.when(i == chunks + 1 + 6)
    def _():
        for piece in out.pieces:
            out.second_copy(piece).wait_send()
            out.pair_copy(piece).wait_send()
            gz.after_first(piece)

    at_step(8, (gz.after_second, gz))
    at_step(9, (out.after_far, out), (gz.after_pair, gz))

    @pl.when(i == 2 * chunks)
    def _():
        finish_trade()
        for piece in out.pieces:
            out.after_last(piece)
            for copy in out.first_copies(piece):
                copy.wait_send()
        out.drain_members()
        for copy in keep_out():
            copy.start()
        keep_z.start()
        gz.drain_chips()
        for copy in keep_out():
            copy.wait()
        keep_z.wait()


class Plan:
    def __init__(self, batch, tokens):
        self.shards, self.members = lax.axis_size("fs"), lax.axis_size("sp")
        self.f, self.z = lax.axis_index("fs"), lax.axis_index("sp")
        self.core = self.f % 2
        self.chips = self.shards // 2
        self.chip = self.f // 2
        self.batch, self.tokens = batch, tokens
        self.units = batch // 2
        self.joints = self.members // 2
        self.count = self.chips * self.joints
        self.group, self.joint = self.z // self.joints, self.z % self.joints
        self.fast = self.chips == 4 and self.members == 4

    def at(self, f, z):
        return f * self.members + z

    def send(self, x, pairs):
        return lax.ppermute(x, ("fs", "sp"), pairs)

    def swap(self, x, df=0, dz=0):
        pairs = [
            (self.at(f, z), self.at(f ^ df, z ^ dz))
            for f in range(self.shards)
            for z in range(self.members)
        ]
        return self.send(x, pairs)

    def along(self, x, by):
        pairs = []
        for f in range(self.shards):
            for z in range(self.members):
                place = (f // 2) * self.joints + z % self.joints + by
                if 0 <= place < self.count:
                    there = (place // self.joints) * 2 + f % 2
                    pairs.append(
                        (self.at(f, z), self.at(there, z - z % self.joints + place % self.joints))
                    )
        return self.send(x, pairs)

    def by_core(self, mine, other):
        first = self.core == 0
        return jnp.where(first, mine, other), jnp.where(first, other, mine)

    def head(self, hidden, w_x, w_bc, w_dt, conv_x, conv_bc, *vectors):
        anywhere, vmem = pl.BlockSpec(memory_space=pl.ANY), pl.BlockSpec(memory_space=pltpu.VMEM)
        conv_x_bias, gate_gain, norm_gain, conv_bc_bias, dt_bias, a_log, skip_d = (v[None] for v in vectors)
        rows, inner = w_x.shape[0], w_x.shape[1] // 2
        small = (SMALL_ROWS, conv_x.shape[0])
        dma = pltpu.SemaphoreType.DMA
        shape = jax.ShapeDtypeStruct
        units, first, *params = pl.pallas_call(
            head_kernel,
            out_shape=[
                shape((self.units, 4, self.tokens, hidden.shape[-1]), BF16),
                shape((4, 2, rows, inner + 3 * LANES), BF16),
                shape((8, inner), F32), shape((8, 2 * LANES), F32), shape((8, LANES), F32),
                shape((8, hidden.shape[-1]), F32), shape((8, inner), F32),
            ],
            in_specs=[anywhere] * 3 + [vmem] * 10,
            out_specs=[anywhere] * 2 + [vmem] * 5,
            scratch_shapes=[
                pltpu.VMEM((rows, LANES), BF16), pltpu.VMEM((rows, LANES), BF16),
                pltpu.VMEM(small, F32), pltpu.VMEM((self.shards,) + small, F32),
                dma((4,)), dma((11,)), dma((11,)), dma((self.shards,)), dma((self.shards,)),
            ],
            compiler_params=pltpu.CompilerParams(
                collective_id=2, has_side_effects=True, vmem_limit_bytes=VMEM_LIMIT
            ),
            cost_estimate=cost(55),
            name="head",
        )(
            hidden, w_x, w_bc, w_dt, conv_x, conv_x_bias, gate_gain, norm_gain, conv_bc, conv_bc_bias,
            dt_bias, a_log, skip_d,
        )
        return units.reshape(-1, hidden.shape[-1]), first.reshape(-1, inner + 3 * LANES), *params

    def slow_tail(self, g, g_x, g_bc, g_heads, g_gate, g_norm, d_normed):
        rows, inner = g.shape[0] // self.shards, g_x.shape[1]
        g = self.reduce_chips(g)
        low = self.core == 0
        kept, given = jnp.where(low, g[:rows], g[rows:]), jnp.where(low, g[rows:], g[:rows])
        came = self.swap(given.astype(BF16), df=1).astype(F32)
        total = self.reduce_members(
            jnp.concatenate(
                list(self.by_core(kept[:, :inner], came[:, :inner]))
                + [kept[:, inner : inner + 2 * LANES] + came[:, inner : inner + 2 * LANES]]
                + list(self.by_core(kept[:, inner + 2 * LANES :], came[:, inner + 2 * LANES :])),
                axis=1,
            )
        )
        wide = ((0, 0), (0, inner - 2 * LANES))
        heads = g_heads.reshape(3, 8, LANES).sum(axis=1).reshape(1, -1)
        vec = jnp.concatenate(
            [
                g_x.reshape(5, 8, inner).sum(axis=1), g_gate, g_norm,
                jnp.pad(heads, ((0, 0), (0, inner - 3 * LANES))),
                jnp.pad(g_bc.reshape(5, 8, 2 * LANES).sum(axis=1), wide),
            ]
        )
        vec = self.sum_all(jnp.pad(vec, ((0, 3), (0, 0))))
        vec = jnp.stack(self.by_core(vec, self.swap(vec, df=1)))
        cut = 2 * inner + 2 * LANES
        d_rows = self.to_tokens(self.cores_sum(d_normed))
        return total[:, : 2 * inner], total[:, 2 * inner : cut], total[:, cut:], vec, d_rows
    def tail(self, normed, d_all, d_base, w_first, unit_rows, g_x, g_bc, g_heads, g_gate, z_total):
        model, inner, width = normed.shape[1], g_x.shape[1], d_all.shape[1]
        rows, count = model // self.shards, normed.shape[0]
        wide, block = 2 * inner + 4 * LANES, 256
        steps = model // block
        vec = (16, inner)
        slots = 7 * (len(FIRST_PIECES) + len(HALF_PIECES)) + 4
        anywhere, dma, shape = pl.BlockSpec(memory_space=pl.ANY), pltpu.SemaphoreType.DMA, jax.ShapeDtypeStruct

        def whole(v):
            return pl.BlockSpec(v.shape, lambda i: (0,) * v.ndim, pipeline_mode=pl.Buffered(1))

        def early(i):
            return jnp.minimum(i, steps - 1)

        def late(i):
            return jnp.maximum(i - steps, 0)

        return pl.pallas_call(
            tail_kernel,
            grid=(2 * steps,),
            in_specs=[
                pl.BlockSpec((count, block), lambda i: (0, early(i))), whole(d_all),
                pl.BlockSpec((count, block), lambda i: (0, late(i))),
                pl.BlockSpec((block, width), lambda i: (late(i), 0)),
                pl.BlockSpec((count, block), lambda i: (0, late(i))),
                whole(g_x), whole(g_bc), whole(g_heads), whole(g_gate), whole(z_total),
            ],
            out_specs=[anywhere] * 3
            + [pl.BlockSpec((2,) + vec, lambda i: (0, 0, 0))]
            + [anywhere] * 2,
            out_shape=[
                shape((rows, 2 * inner), F32), shape((rows, 2 * LANES), F32), shape((rows, 2 * LANES), F32),
                shape((2,) + vec, F32), shape((self.batch, self.tokens, model), BF16),
                shape((rows, 2 * inner), F32),
            ],
            scratch_shapes=[
                pltpu.VMEM((block, count), BF16),
                pltpu.VMEM((model, width), BF16),
                pltpu.VMEM((self.units, 2, 2, self.tokens, model), BF16),
                pltpu.VMEM((self.units, 2, self.tokens, model), BF16),
                dma((5,)),
            ]
            + chip_scratch(rows, width)
            + [pltpu.VMEM((rows, wide), BF16)]
            + member_scratch(rows, wide)
            + member_scratch(rows, 2 * inner)
            + [
                pltpu.VMEM((rows, 2 * inner), F32), pltpu.VMEM((rows, 2 * LANES), F32),
                pltpu.VMEM((rows, 2 * LANES), F32), pltpu.VMEM((rows, 2 * inner), F32),
                pltpu.VMEM((4,) + vec, F32), pltpu.VMEM((4,) + vec, F32), pltpu.VMEM((2,) + vec, F32),
                dma((slots,)), dma((slots,)), dma((5,)), dma((5,)),
            ],
            compiler_params=pltpu.CompilerParams(
                dimension_semantics=("arbitrary",), collective_id=3, has_side_effects=True,
                vmem_limit_bytes=TAIL_LIMIT,
            ),
            cost_estimate=cost(130),
            name="tail",
        )(normed, d_all, d_base, w_first, unit_rows, g_x, g_bc, g_heads, g_gate, z_total)

    def gather(self, x):
        groups = [list(range(c, self.shards, 2)) for c in range(2)]
        return lax.all_gather(x, "fs", axis=0, tiled=True, axis_index_groups=groups)

    def reduce_chips(self, g):
        groups = [list(range(c, self.shards, 2)) for c in range(2)]
        return lax.psum_scatter(
            g, "fs", scatter_dimension=0, tiled=True, axis_index_groups=groups
        ).astype(F32)

    def reduce_members(self, g):
        return lax.psum(g.astype(BF16), "sp").astype(F32)

    def traded(self, x, far):
        pairs = [
            (self.at(f, z), self.at(f - f % 2 + z % 2, ((z // 2) ^ far) * 2 + f % 2))
            for f in range(self.shards)
            for z in range(self.members)
        ]
        return self.send(x, pairs)

    def to_units(self, rows):
        units, width = self.units, rows.shape[-1]
        if self.fast:
            low, high = rows[:units], rows[units:]
            upper = self.z // 2 == 1
            far = self.traded(jnp.where(upper, low, high), 1)
            near = self.traded(jnp.where(upper, high, low), 0)
            mine = jnp.stack([jnp.where(upper, far, near), jnp.where(upper, near, far)], axis=1)
            pair = self.by_core(mine, self.swap(mine, df=1))
            block = jnp.stack(pair, axis=2)
        else:
            other = self.swap(rows, df=1)
            everything = lax.all_gather(jnp.stack(self.by_core(rows, other)), "sp")
            per_core = self.joints // 2
            block = lax.dynamic_slice(
                everything,
                ((self.joint % per_core) * 4, self.joint // per_core, self.group * units, 0, 0),
                (4, 1, units) + rows.shape[1:],
            )[:, 0]
            block = jnp.moveaxis(block, 0, 1)
        return block.reshape(units * 4 * self.tokens, width)

    def cores_sum(self, partial):
        units, width = self.units, partial.shape[-1]
        if self.fast:
            block = partial.reshape(units, 2, 2, self.tokens, width)
            even = self.core == 0
            mine = jnp.where(even, block[:, :, 0], block[:, :, 1])
            given = jnp.where(even, block[:, :, 1], block[:, :, 0]).astype(BF16)
            return (mine.astype(F32) + self.swap(given, df=1).astype(F32)).astype(BF16)
        return partial.astype(BF16).reshape(units, 4, self.tokens, width)

    def to_tokens(self, total):
        units, width = self.units, total.shape[-1]
        if self.fast:
            upper = self.z // 2 == 1
            far = self.traded(jnp.where(upper, total[:, 0], total[:, 1]), 1)
            near = self.traded(jnp.where(upper, total[:, 1], total[:, 0]), 0)
            return jnp.concatenate(
                [jnp.where(upper, far, near), jnp.where(upper, near, far)], axis=0
            )
        per_core = self.joints // 2
        block = total
        wide = jnp.zeros((self.members, 2, self.batch, self.tokens, width), BF16)
        wide = lax.dynamic_update_slice(
            wide,
            jnp.moveaxis(block, 1, 0)[:, None],
            ((self.joint % per_core) * 4, self.joint // per_core, self.group * units, 0, 0),
        )
        summed = lax.psum_scatter(wide, "sp", scatter_dimension=0, tiled=False)
        first = self.core == 0
        mine, given = jnp.where(first, summed[0], summed[1]), jnp.where(first, summed[1], summed[0])
        return (mine.astype(F32) + self.swap(given, df=1).astype(F32)).astype(BF16)

    def sum_all(self, x):
        if not self.fast:
            groups = [list(range(c, self.shards, 2)) for c in range(2)]
            return lax.psum(lax.psum(x, "fs", axis_index_groups=groups), "sp")
        for df, dz in ((2, 0), (4, 0), (0, 1), (0, 2)):
            x = x + self.swap(x, df, dz)
        return x


def row_scale(values):
    return lax.rsqrt(jnp.mean(values * values, axis=-1, keepdims=True) + EPSILON)


def rows_spec(width, column=0, back=False):
    def place(u, c):
        return (u * PER_UNIT + (PER_UNIT - 1 - c if back else c), column)

    return pl.BlockSpec((CHUNK, width), place)


def chunk_spec(shape, back=False):
    def place(u, c):
        return (u * PER_UNIT + (PER_UNIT - 1 - c if back else c), 0, 0)

    return pl.BlockSpec((1,) + shape, place)


def unit_spec(shape):
    return pl.BlockSpec((1,) + shape, lambda u, c: (u, 0, 0))


def whole_spec(shape):
    return pl.BlockSpec(shape, lambda u, c: (0,) * len(shape))


def cost(microseconds):
    return pl.CostEstimate(flops=int(microseconds * 1.15e9), bytes_accessed=0, transcendentals=0)


def params():
    return pltpu.CompilerParams(
        dimension_semantics=("arbitrary", "arbitrary"), vmem_limit_bytes=VMEM_LIMIT
    )


def slow_exchange(plan, own, decays, back):
    count, units = plan.count, own.shape[0]
    rates, pieces = decays[:units, None], own.astype(F32)

    def hop(_, before):
        return plan.along((before * rates + pieces).astype(BF16), -1 if back else 1).astype(F32)

    return lax.fori_loop(0, count - 1, hop, jnp.zeros(own.shape, F32)).astype(BF16)


def exchange(plan, own, decays, cot, near, far, normed, w_gate, w_out, y0, bcs, acum):
    units, depth, width = own.shape
    count, share = plan.count, depth // plan.count
    dec_shape, rows, model = (count, 8, width), normed.shape[0], normed.shape[1]
    chunks = rows // CHUNK
    anywhere, dma, shape = pl.BlockSpec(memory_space=pl.ANY), pltpu.SemaphoreType.DMA, jax.ShapeDtypeStruct

    def whole(v):
        return pl.BlockSpec(v.shape, lambda i: (0,) * v.ndim, pipeline_mode=pl.Buffered(1))

    def chunk(columns):
        return pl.BlockSpec((CHUNK, columns), lambda i: (jnp.maximum(i - 1, 0), 0))

    all_decays, cot_rows, weight_out, gate, incoming, y, gated, squares = pl.pallas_call(
        states_kernel,
        grid=(chunks + 1,),
        in_specs=[whole(own), whole(decays)]
        + [anywhere] * 6
        + [chunk(width), chunk(2 * LANES), chunk(LANES)],
        out_specs=[pl.BlockSpec(dec_shape, lambda i: (0, 0, 0))]
        + [anywhere] * 4
        + [chunk(width), chunk(width), chunk(LANES)],
        out_shape=[
            shape(dec_shape, F32), shape((units, 4, plan.tokens, model), BF16),
            shape((4, 2, w_out.shape[0], width), BF16), shape((rows, width), BF16), shape(own.shape, BF16),
            shape((rows, width), BF16), shape((rows, width), BF16), shape((rows, LANES), F32),
        ],
        scratch_shapes=[
            pltpu.VMEM(own.shape, BF16), pltpu.VMEM((count, units, share, width), BF16),
            pltpu.VMEM(dec_shape, F32), pltpu.VMEM((count, units, share, width), BF16),
            pltpu.VMEM(w_gate.shape, BF16), pltpu.VMEM((rows, width), BF16), pltpu.VMEM((2, 256, model), BF16),
        ]
        + [dma((count,))] * 6
        + [dma((4,)), dma((4,)), dma((7,)), dma((7,)), dma((5,)), dma((1,)), dma((2,))],
        compiler_params=pltpu.CompilerParams(
            dimension_semantics=("arbitrary",), collective_id=0, has_side_effects=True,
            vmem_limit_bytes=VMEM_LIMIT,
        ),
        cost_estimate=cost(60),
        name="states",
    )(own, decays, cot, near, far, normed, w_gate, w_out, y0, bcs, acum)
    return (
        all_decays, cot_rows.reshape(rows, model), weight_out.reshape(model, width), gate, incoming,
        y, gated, squares,
    )


def body(
    hidden, norm_gain, w_z, w_x, w_bc, w_dt, w_out, conv_x, conv_x_bias, conv_bc, conv_bc_bias,
    dt_bias, a_log, skip_d, gate_gain, cotangent,
):
    batch, tokens, model = hidden.shape
    plan = Plan(batch, tokens)
    core = plan.core
    inner = w_z.shape[1] // 2
    heads = w_dt.shape[1] // 2
    head_size = inner // heads
    units = plan.units
    rows = units * 4 * tokens
    chunks = rows // CHUNK

    def halves(w):
        half = w.shape[1] // 2
        return jnp.where(core == 0, w[:, :half], w[:, half:]), jnp.where(core == 0, w[:, half:], w[:, :half])

    def rows_of_chip(mine, other):
        return jnp.concatenate(plan.by_core(mine, plan.swap(other, df=1)), axis=0)

    vectors = (conv_x_bias, gate_gain, norm_gain, conv_bc_bias, dt_bias, a_log, skip_d)
    if plan.fast:
        hidden_rows, weight_first, cx, cbc, hp, gain_in, gain_rows = plan.head(
            hidden, w_x, w_bc, w_dt, conv_x, conv_bc, *vectors
        )
        gain_in, gain_out = gain_in[0], gain_rows[0]
    else:
        x_mine, x_other = halves(w_x)
        dt_mine, dt_other = halves(w_dt)
        fill = jnp.zeros((w_dt.shape[0], LANES - heads), BF16)
        weight_first = plan.gather(
            rows_of_chip(
                jnp.concatenate([x_mine, w_bc, dt_mine, fill], axis=1),
                jnp.concatenate([x_other, w_bc, dt_other, fill], axis=1),
            )
        )
        hidden_rows, cot_rows = plan.to_units(hidden), plan.to_units(cotangent)

        def whole_of(v):
            return lax.all_gather(v.astype(F32), "fs", axis=0, tiled=True)

        def mine_of(v):
            half = v.shape[0] // 2
            return lax.dynamic_slice_in_dim(v, core * half, half, 0)

        bias_x, gain_out, gain_in, bias_bc, shift, rate_log, skip = (whole_of(v) for v in vectors)
        taps_x, taps_bc = mine_of(whole_of(conv_x)), whole_of(conv_bc)
        bias_x, gain_out, skip, shift, rate_log = (
            mine_of(v) for v in (bias_x, gain_out, skip, shift, rate_log)
        )
        nothing = jnp.zeros((2, inner), F32)
        cx = jnp.concatenate([taps_x.T, bias_x[None], jnp.repeat(skip, head_size)[None], nothing])
        cbc = jnp.concatenate([taps_bc.T, bias_bc[None], jnp.zeros((3, bias_bc.size), F32)])
        pad_heads = (0, LANES - heads)
        hp = jnp.stack([jnp.pad(jnp.exp(rate_log), pad_heads), jnp.pad(shift, pad_heads)])
        hp = jnp.pad(hp, ((0, 6), (0, 0)))
        gain_rows = jnp.broadcast_to(gain_out[None], (8, inner))
        weight_gate = plan.gather(rows_of_chip(*halves(w_z)))
        weight_out = plan.gather(rows_of_chip(*halves(w_out)))
    pick = (jnp.arange(inner)[:, None] // head_size == jnp.arange(LANES)[None, :]).astype(BF16)

    hidden_rows = hidden_rows.astype(F32)
    scale_in = row_scale(hidden_rows)
    unit_in = hidden_rows * scale_in
    normed = (unit_in * gain_in[None]).astype(BF16)
    unit_low = unit_in.astype(BF16)
    normed, unit_low = lax.optimization_barrier((normed, unit_low))

    first = dot(normed, weight_first).astype(BF16)
    def shaped(*shape, dtype=BF16):
        return jax.ShapeDtypeStruct(shape, dtype)

    states = (LANES, inner)
    edge = (units, 16, inner + 2 * LANES)
    in_specs = [
        rows_spec(inner), rows_spec(2 * LANES, inner // (2 * LANES)),
        rows_spec(LANES, (inner + 2 * LANES) // LANES),
    ]
    consts = [whole_spec(cx.shape), whole_spec(cbc.shape), whole_spec(hp.shape)]
    out_specs = [
        rows_spec(inner), chunk_spec(states), unit_spec(states), unit_spec((8, inner)),
        rows_spec(2 * LANES), rows_spec(LANES),
    ]
    out_shape = [
        shaped(rows, inner), shaped(chunks, *states), shaped(units, *states),
        shaped(units, 8, inner, dtype=F32), shaped(rows, 2 * LANES), shaped(rows, LANES, dtype=F32),
    ]
    scratch = [
        pltpu.VMEM((CHUNK + 8, inner), F32), pltpu.VMEM((CHUNK + 8, 2 * LANES), F32),
        pltpu.VMEM(states, F32), pltpu.VMEM((8, LANES), F32),
    ]
    by_unit = first.reshape(units, 4 * tokens, first.shape[1])
    if plan.fast:
        anywhere = pl.BlockSpec(memory_space=pl.ANY)
        dma = pltpu.SemaphoreType.DMA
        y_own, starts, own, decays, shared, reach, halo, near, far, weight_gate = pl.pallas_call(
            scan_forward_kernel,
            grid=(units, PER_UNIT),
            in_specs=in_specs + [anywhere, anywhere, anywhere] + consts,
            out_specs=out_specs + [whole_spec(edge), anywhere, anywhere, anywhere],
            out_shape=out_shape
            + [
                shaped(*edge), shaped(units, tokens, model), shaped(EARLY_UNITS, tokens, model),
                shaped(4, 2, w_z.shape[0], inner),
            ],
            scratch_shapes=scratch
            + [pltpu.VMEM(edge, BF16), dma((1,)), dma((1,)), dma((2,)), dma((2,)), dma((1,)), dma((7,)), dma((7,)), dma((1,))],
            compiler_params=pltpu.CompilerParams(
                dimension_semantics=("arbitrary", "arbitrary"), vmem_limit_bytes=VMEM_LIMIT,
                collective_id=1, has_side_effects=True,
            ),
            cost_estimate=cost(31),
            name="scan_forward",
        )(first, first, first, by_unit, cotangent, w_z, cx, cbc, hp)
    else:
        halo = plan.along(by_unit[:, 4 * tokens - 16 :, : inner + 2 * LANES], 1)
        y_own, starts, own, decays, shared, reach = pl.pallas_call(
            forward_kernel,
            grid=(units, PER_UNIT),
            in_specs=in_specs + [whole_spec(edge)] + consts,
            out_specs=out_specs,
            out_shape=out_shape,
            scratch_shapes=scratch,
            compiler_params=params(),
            name="scan_forward",
        )(first, first, first, halo, cx, cbc, hp)

    decay_rows = jnp.concatenate([decays[:, 0], jnp.zeros((8 - units, inner), F32)])
    if plan.fast:
        weight_gate = weight_gate.reshape(model, inner)
        all_decays, cot_rows, weight_out, gate_in, incoming, y, gated, squares = exchange(
            plan, own, decay_rows, cotangent, near, far, normed, weight_gate, w_out, y_own, shared, reach
        )
    else:
        incoming = slow_exchange(plan, own, decay_rows, False)
        gate_in = dot(normed, weight_gate).astype(BF16)
        y, gated, squares = pl.pallas_call(
            gate_kernel,
            grid=(units, PER_UNIT),
            in_specs=[
                rows_spec(inner), rows_spec(inner), rows_spec(2 * LANES), rows_spec(LANES), unit_spec(states),
            ],
            out_specs=[rows_spec(inner), rows_spec(inner), rows_spec(LANES)],
            out_shape=[shaped(rows, inner), shaped(rows, inner), shaped(rows, LANES, dtype=F32)],
            compiler_params=params(),
            name="gate_forward",
        )(y_own, gate_in, shared, reach, incoming)

    def pair_sum(v):
        return v + plan.swap(v, df=1)

    squares = pair_sum(squares[:, 0].reshape(chunks, CHUNK))
    scale_out = lax.rsqrt(squares / (2 * inner) + EPSILON).reshape(rows, 1)
    unit_out = gated.astype(F32) * scale_out
    normed_out = (unit_out * gain_out[None]).astype(BF16)
    g_out = dot_tn(cot_rows, normed_out).astype(BF16)
    projected = plan.cores_sum(dot_nt(normed_out, weight_out).astype(BF16))

    d_normed_out = dot(cot_rows, weight_out).astype(BF16)
    wide = d_normed_out.astype(F32)
    g_gate_gain = jnp.sum(wide * unit_out, axis=0)
    mean = pair_sum(jnp.sum(wide * gain_out[None] * unit_out, axis=1).reshape(chunks, CHUNK))
    mean = (mean / (2 * inner)).reshape(rows, 1)
    stats = jnp.concatenate([scale_out, mean, jnp.zeros((rows, LANES - 2), F32)], axis=1)

    width = inner + 3 * LANES
    back = functools.partial(rows_spec, back=True)
    if plan.fast:
        spots = 2 * chunks + 1
        shard_rows = model // plan.shards
        segments = plan.count
        share = LANES // segments

        def pulls(columns, column=0):
            return pl.BlockSpec((CHUNK, columns), lambda i: (jnp.minimum(i, chunks - 1), column))

        def scan_at(i):
            n = jnp.maximum(i - chunks - 1, 0)
            return n - n % PER_UNIT + PER_UNIT - 1 - n % PER_UNIT

        def scans(columns, column=0):
            return pl.BlockSpec((CHUNK, columns), lambda i: (scan_at(i), column))

        def edges(columns, column=0):
            return pl.BlockSpec((16, columns), lambda i: (jnp.maximum(scan_at(i) * 8 - 1, 0), column))

        def scan_chunk(shape):
            return pl.BlockSpec((1,) + shape, lambda i: (scan_at(i), 0, 0))

        def scan_unit(shape):
            return pl.BlockSpec((1,) + shape, lambda i: (scan_at(i) // PER_UNIT, 0, 0))

        def every(shape):
            return pl.BlockSpec(shape, lambda i: (0,) * len(shape), pipeline_mode=pl.Buffered(1))

        def whole(shape):
            return pl.BlockSpec(shape, lambda i: (0,) * len(shape))

        anywhere = pl.BlockSpec(memory_space=pl.ANY)
        dma = pltpu.SemaphoreType.DMA
        d_all, heads_x, heads_bc, g_x, g_bc, g_heads, d_base, projected, total_out, total_z = pl.pallas_call(
            middle_kernel,
            grid=(spots,),
            in_specs=[
                pulls(inner), pulls(inner), pulls(inner), pulls(inner), pulls(LANES), every((8, inner)),
                pulls(2 * LANES), pulls(LANES), every(all_decays.shape), anywhere, anywhere, anywhere, anywhere,
                scans(inner), edges(inner),
                scans(2 * LANES, inner // (2 * LANES)), edges(2 * LANES, inner // (2 * LANES)),
                scans(LANES, (inner + 2 * LANES) // LANES), every(edge), every(cx.shape), every(cbc.shape), every(hp.shape),
                scans(inner), scan_chunk(states), scan_unit(states), scans(LANES), every(pick.shape),
            ],
            out_specs=[
                scans(width), scan_unit((8, inner)), scan_unit((8, 2 * LANES)),
                whole((40, inner)), whole((40, 2 * LANES)), whole((24, LANES)),
                anywhere, anywhere, anywhere, anywhere,
            ],
            out_shape=[
                shaped(rows, width), shaped(units, 8, inner, dtype=F32), shaped(units, 8, 2 * LANES, dtype=F32),
                shaped(40, inner, dtype=F32), shaped(40, 2 * LANES, dtype=F32), shaped(24, LANES, dtype=F32),
                shaped(rows, model), shaped(batch, tokens, model),
                shaped(shard_rows, 2 * inner), shaped(shard_rows, 2 * inner),
            ],
            scratch_shapes=[
                pltpu.VMEM((rows, inner), BF16), pltpu.VMEM((rows, inner), BF16), pltpu.VMEM(states, F32),
                pltpu.VMEM((units,) + states, BF16), pltpu.VMEM((units,) + states, BF16),
                pltpu.VMEM((segments, units, share, inner), BF16),
                pltpu.VMEM((segments, units, share, inner), BF16),
                pltpu.VMEM((2, rows, 256), BF16), pltpu.VMEM((256, rows), BF16),
                pltpu.VMEM((2, 256, inner), BF16), pltpu.VMEM((2, rows, 256), BF16),
                pltpu.VMEM((model, inner), BF16),
                pltpu.VMEM((model // 4, inner), BF16),
            ]
            + chip_scratch(shard_rows, inner)
            + [pltpu.VMEM((shard_rows, 2 * inner), BF16)]
            + member_scratch(shard_rows, 2 * inner)
            + [
                pltpu.VMEM((2, 2 * shard_rows, inner), BF16), pltpu.VMEM((2 * shard_rows, inner), BF16),
                pltpu.VMEM((shard_rows, inner), BF16), pltpu.VMEM((shard_rows, 2 * inner), BF16),
            ]
            + [
                pltpu.VMEM((CHUNK + 8, inner), F32), pltpu.VMEM((CHUNK + 8, 2 * LANES), F32),
                pltpu.VMEM(states, F32),
                pltpu.VMEM((CHUNK + 8, inner), F32), pltpu.VMEM((CHUNK + 8, 2 * LANES), F32),
                pltpu.VMEM((8, inner), F32),
                dma((8,)), dma((8,)), dma((2,)), dma((2,)), dma((2,)), dma((1,)), dma((2,)), dma((2,)),
                dma((14 * len(HALF_PIECES),)), dma((14 * len(HALF_PIECES),)),
                dma((segments,)), dma((segments,)), dma((segments,)), dma((segments,)),
            ],
            compiler_params=pltpu.CompilerParams(
                dimension_semantics=("arbitrary",), vmem_limit_bytes=MIDDLE_LIMIT,
                collective_id=4, has_side_effects=True,
            ),
            cost_estimate=cost(125),
            name="middle",
        )(
            d_normed_out, gated, gate_in, y, stats, gain_rows, shared, reach, all_decays, normed, weight_gate, g_out,
            projected, first, first, first, first, first, halo, cx, cbc, hp, y, starts, incoming,
            reach, pick,
        )
    else:

        def edges(columns, column=0):
            def place(u, c):
                return (jnp.maximum((u * PER_UNIT + PER_UNIT - 1 - c) * 8 - 1, 0), column)

            return pl.BlockSpec((16, columns), place)

        dy, d_gate, pull = pl.pallas_call(
            pull_kernel,
            grid=(units, PER_UNIT),
            in_specs=[
                rows_spec(inner), rows_spec(inner), rows_spec(inner), rows_spec(inner), rows_spec(LANES),
                whole_spec((8, inner)), rows_spec(2 * LANES), rows_spec(LANES),
            ],
            out_specs=[rows_spec(inner), rows_spec(inner), unit_spec(states)],
            out_shape=[shaped(rows, inner), shaped(rows, inner), shaped(units, *states)],
            scratch_shapes=[pltpu.VMEM(states, F32)],
            compiler_params=params(),
            name="gate_backward",
        )(d_normed_out, gated, gate_in, y, stats, gain_rows, shared, reach)
        after = slow_exchange(plan, pull, decay_rows, True)
        d_all, heads_x, heads_bc, g_x, g_bc, g_heads = pl.pallas_call(
            backward_kernel,
            grid=(units, PER_UNIT),
            in_specs=[
                back(inner), edges(inner),
                back(2 * LANES, inner // (2 * LANES)), edges(2 * LANES, inner // (2 * LANES)),
                back(LANES, (inner + 2 * LANES) // LANES), whole_spec(edge), whole_spec(cx.shape), whole_spec(cbc.shape), whole_spec(hp.shape),
                back(inner), back(inner), chunk_spec(states, True), unit_spec(states), back(LANES),
                unit_spec(states), whole_spec(pick.shape),
            ],
            out_specs=[
                back(width), unit_spec((8, inner)), unit_spec((8, 2 * LANES)),
                whole_spec((40, inner)), whole_spec((40, 2 * LANES)), whole_spec((24, LANES)),
            ],
            out_shape=[
                shaped(rows, width), shaped(units, 8, inner, dtype=F32), shaped(units, 8, 2 * LANES, dtype=F32),
                shaped(40, inner, dtype=F32), shaped(40, 2 * LANES, dtype=F32), shaped(24, LANES, dtype=F32),
            ],
            scratch_shapes=[
                pltpu.VMEM((CHUNK + 8, inner), F32), pltpu.VMEM((CHUNK + 8, 2 * LANES), F32),
                pltpu.VMEM(states, F32),
                pltpu.VMEM((CHUNK + 8, inner), F32), pltpu.VMEM((CHUNK + 8, 2 * LANES), F32),
                pltpu.VMEM((8, inner), F32),
            ],
            compiler_params=params(),
            name="scan_backward",
        )(
            first, first, first, first, first, halo, cx, cbc, hp,
            dy, y, starts, incoming, reach, after, pick,
        )
        projected = plan.to_tokens(projected)

        def over_everything(g):
            g = plan.reduce_chips(g)
            half = g.shape[0] // 2
            low = core == 0
            mine, other = jnp.where(low, g[:half], g[half:]), jnp.where(low, g[half:], g[:half])
            other = plan.swap(other.astype(BF16), df=1).astype(F32)
            return plan.reduce_members(jnp.concatenate(plan.by_core(mine, other), axis=1))

        total_out = over_everything(g_out)
        total_z = over_everything(dot_tn(normed, d_gate).astype(BF16))
    output = (hidden.astype(F32) + projected.astype(F32)).astype(BF16)

    later = plan.along(jnp.concatenate([heads_x, heads_bc], axis=2)[:, :3].astype(BF16), -1).astype(F32)
    taps = jnp.concatenate([cx[:4], cbc[:4]], axis=1)
    extra = jnp.stack(
        [sum(taps[k][None] * later[:, i - k] for k in range(i + 1)) for i in range(3)], axis=1
    )
    tail_rows = d_all.reshape(units, 4 * tokens, width)[:, 4 * tokens - 16 :].astype(F32)
    extra = jnp.pad(extra, ((0, 0), (13, 0), (0, width - extra.shape[2])))
    d_all = d_all.reshape(units, 4 * tokens, width)
    d_all = lax.dynamic_update_slice(d_all, (tail_rows + extra).astype(BF16), (0, 4 * tokens - 16, 0))
    d_all = d_all.reshape(rows, width)

    if plan.fast:
        total_x, total_bc, total_dt, vec, grad_rows, total_z = plan.tail(
            normed, d_all, d_base, weight_first, unit_low, g_x, g_bc, g_heads, g_gate_gain[None], total_z
        )
    else:
        g_first = dot_tn(normed, d_all).astype(BF16)
        d_normed = dot_nt(d_gate, weight_gate) + dot_nt(d_all, weight_first)
        g_norm_gain = jnp.sum(d_normed * unit_in, axis=0)
        total_x, total_bc, total_dt, vec, grad_rows = plan.slow_tail(
            g_first, g_x, g_bc, g_heads, g_gate_gain[None], g_norm_gain[None], d_normed.astype(BF16)
        )
    grad_rows = grad_rows.astype(F32)
    resid = hidden.astype(F32)
    own_scale = row_scale(resid)
    own_unit = resid * own_scale
    dv = grad_rows * gain_in[None, None]
    grad_hidden = cotangent.astype(F32) + own_scale * (
        dv - own_unit * jnp.mean(dv * own_unit, axis=-1, keepdims=True)
    )

    total_dt = jnp.concatenate([total_dt[:, :heads], total_dt[:, LANES : LANES + heads]], axis=1)
    whole_x = jnp.moveaxis(vec[:, :6], 0, 1).reshape(6, 2 * inner)
    whole_heads = jnp.moveaxis(vec[:, 7, : 3 * LANES].reshape(2, 3, LANES)[:, :, :heads], 0, 1)
    whole_heads = whole_heads.reshape(3, 2 * heads)
    whole_norm = vec[0, 6] + vec[1, 6]
    whole_bc = vec[0, 8:13, : 2 * LANES] + vec[1, 8:13, : 2 * LANES]

    def shard(v):
        share = v.shape[-1] // plan.shards
        return lax.dynamic_slice_in_dim(v, plan.f * share, share, v.ndim - 1)

    shard_x, shard_bc, shard_heads = shard(whole_x), shard(whole_bc), shard(whole_heads)
    return (
        output,
        grad_hidden,
        shard(whole_norm),
        total_z.astype(F32),
        total_x,
        total_bc,
        total_dt,
        total_out.astype(F32),
        shard_x[:4].T,
        shard_x[4],
        shard_bc[:4].T,
        shard_bc[4],
        shard_heads[0],
        shard_heads[1],
        shard_heads[2],
        shard_x[5],
    )


def solution(mesh):
    one, two = P("fs"), P("fs", None)
    tokens = P(None, ("fs", "sp"), None)
    return jax.shard_map(
        body,
        mesh=mesh,
        in_specs=(tokens, one, two, two, two, two, two, two, one, two, one, one, one, one, one, tokens),
        out_specs=(tokens, tokens, one, two, two, two, two, two, two, one, two, one, one, one, one, one),
        check_vma=False,
    )
```

```python
import functools

import jax
import jax.numpy as jnp
from jax import lax
from jax.experimental import pallas as pl
from jax.experimental.pallas import tpu as pltpu
from jax.sharding import PartitionSpec as P

EPSILON = 1e-05
F32, BF16 = jnp.float32, jnp.bfloat16
MESH = pl.DeviceIdType.MESH
CHUNK = 128
LANES = 128
PER_UNIT = 4
VMEM_LIMIT = 56 * 1024 * 1024
TAIL_LIMIT = 56 * 1024 * 1024
MIDDLE_LIMIT = 58 * 1024 * 1024


def dot(a, b):
    return jnp.dot(a, b, preferred_element_type=F32)


def dot_nt(a, b):
    return lax.dot_general(a, b, (((1,), (1,)), ((), ())), preferred_element_type=F32)


def dot_tn(a, b):
    return lax.dot_general(a, b, (((0,), (0,)), ((), ())), preferred_element_type=F32)


def pieces_of(v):
    high = v.astype(BF16)
    rest = v - high.astype(F32)
    middle = rest.astype(BF16)
    return high, middle, (rest - middle.astype(F32)).astype(BF16)


def exact_left(ones, v):
    return sum(dot(ones, part) for part in pieces_of(v))


def exact_right(v, ones):
    return sum(dot(part, ones) for part in pieces_of(v))


def sigmoid(v):
    return 0.5 * jnp.tanh(0.5 * v) + 0.5


def grid_iotas():
    rows = lax.broadcasted_iota(jnp.int32, (CHUNK, CHUNK), 0)
    columns = lax.broadcasted_iota(jnp.int32, (CHUNK, CHUNK), 1)
    return rows, columns


def two_heads(v, pair, low):
    return jnp.where(low, v[:, 2 * pair : 2 * pair + 1], v[:, 2 * pair + 1 : 2 * pair + 2])


def conv_of(ext, lanes, taps):
    total = taps[4:5, lanes]
    for k in range(4):
        total = total + ext[5 + k : 5 + k + CHUNK, lanes] * taps[k : k + 1, lanes]
    return total


def step_of(dt_ref, hp_ref):
    shifted = dt_ref[...].astype(F32) + hp_ref[1:2]
    return shifted, jnp.maximum(shifted, 0.0) + jnp.log1p(jnp.exp(-jnp.abs(shifted)))


def forward_kernel(
    x_ref, bc_ref, dt_ref, halo_ref, cx_ref, cbc_ref, hp_ref,
    y_ref, st_ref, own_ref, dec_ref, bcs_ref, acum_ref,
    xe, be, state, base,
):
    unit, chunk = pl.program_id(0), pl.program_id(1)
    inner = x_ref.shape[1]

    @pl.when(chunk == 0)
    def _():
        state[...] = jnp.zeros_like(state)
        base[...] = jnp.zeros_like(base)
        xe[0:8] = halo_ref[unit, :, :inner].astype(F32)[8:]
        be[0:8] = halo_ref[unit, :, inner:].astype(F32)[8:]

    @pl.when(chunk != 0)
    def _():
        xe[0:8] = xe[CHUNK:]
        be[0:8] = be[CHUNK:]

    xe[8:] = x_ref[...].astype(F32)
    be[8:] = bc_ref[...].astype(F32)
    shared = []
    for k in range(2):
        pre = conv_of(be, slice(k * LANES, (k + 1) * LANES), cbc_ref)
        shared.append(pre * sigmoid(pre))
    keys, reads = shared
    bcs_ref[:, :LANES] = keys.astype(BF16)
    bcs_ref[:, LANES:] = reads.astype(BF16)
    keys_t = keys.T.astype(BF16)
    keys, reads = keys.astype(BF16), reads.astype(BF16)
    rows, columns = grid_iotas()
    causal = rows >= columns
    _, step = step_of(dt_ref, hp_ref)
    running = exact_left(jnp.where(causal, 1.0, 0.0).astype(BF16), -step * hp_ref[0:1])
    acum_ref[...] = base[0:1] + running
    total = running[CHUNK - 1 : CHUNK]
    base[...] = base[...] + total
    running_t = running.T
    scores = jnp.where(causal, dot_nt(reads, keys), 0.0)
    low = columns < LANES // 2
    low_row = low[0:1]

    for pair in range(inner // LANES):
        lanes = slice(pair * LANES, (pair + 1) * LANES)
        pre = conv_of(xe, lanes, cx_ref)
        xs = pre * sigmoid(pre)
        weighted = xs * two_heads(step, pair, low)
        first = jnp.broadcast_to(running[:, 2 * pair : 2 * pair + 1], (CHUNK, CHUNK))
        second = jnp.broadcast_to(running[:, 2 * pair + 1 : 2 * pair + 2], (CHUNK, CHUNK))
        mix = jnp.concatenate(
            [
                (jnp.exp(jnp.minimum(first - running_t[2 * pair : 2 * pair + 1], 0.0)) * scores).astype(BF16),
                (jnp.exp(jnp.minimum(second - running_t[2 * pair + 1 : 2 * pair + 2], 0.0)) * scores).astype(BF16),
            ],
            axis=1,
        )
        own = weighted.astype(BF16)
        zero = jnp.zeros_like(own)
        stacked = jnp.concatenate([jnp.where(low, own, zero), jnp.where(low, zero, own)], axis=0)
        at = jnp.where(low, first, second)
        at_end = two_heads(total, pair, low_row)
        before = state[:, lanes]
        before_low = before.astype(BF16)
        st_ref[0, :, lanes] = before_low
        y = dot(mix, stacked) + dot(reads, before_low) * jnp.exp(at) + cx_ref[5:6, lanes] * xs
        y_ref[:, lanes] = y.astype(BF16)
        late = (weighted * jnp.exp(at_end - at)).astype(BF16)
        state[:, lanes] = before * jnp.exp(at_end) + dot(keys_t, late)

    @pl.when(chunk == PER_UNIT - 1)
    def _():
        own_ref[0] = state[...].astype(BF16)
        for pair in range(inner // LANES):
            lanes = slice(pair * LANES, (pair + 1) * LANES)
            dec_ref[0, :, lanes] = jnp.broadcast_to(
                jnp.exp(two_heads(base[0:1], pair, low_row)), (8, LANES)
            )


def gate_kernel(y0_ref, gate_ref, bcs_ref, acum_ref, in_ref, y_ref, gated_ref, ss_ref):
    _, columns = grid_iotas()
    low = columns < LANES // 2
    reads = bcs_ref[:, LANES:]
    reach = acum_ref[...]
    squares = jnp.zeros((CHUNK, LANES), F32)
    for pair in range(y0_ref.shape[1] // LANES):
        lanes = slice(pair * LANES, (pair + 1) * LANES)
        y = y0_ref[:, lanes].astype(F32) + dot(reads, in_ref[0, :, lanes]) * jnp.exp(
            two_heads(reach, pair, low)
        )
        y_ref[:, lanes] = y.astype(BF16)
        gate = gate_ref[:, lanes].astype(F32)
        gated = (y * gate * sigmoid(gate)).astype(BF16)
        gated_ref[:, lanes] = gated
        wide = gated.astype(F32)
        squares = squares + wide * wide
    ss_ref[...] = jnp.broadcast_to(jnp.sum(squares, axis=1, keepdims=True), (CHUNK, LANES))


def pull_kernel(
    dno_ref, gated_ref, gate_ref, y_ref, stats_ref, gain_ref, bcs_ref, acum_ref,
    dy_ref, dgate_ref, pull_ref,
    total, chunk=None,
):
    chunk = pl.program_id(1) if chunk is None else chunk

    @pl.when(chunk == 0)
    def _():
        total[...] = jnp.zeros_like(total)

    _, columns = grid_iotas()
    low = columns < LANES // 2
    scale = jnp.broadcast_to(stats_ref[:, 0:1], (CHUNK, LANES))
    mean = jnp.broadcast_to(stats_ref[:, 1:2], (CHUNK, LANES))
    reads_t = bcs_ref[:, LANES:].astype(F32).T.astype(BF16)
    reach = acum_ref[...]
    for pair in range(dno_ref.shape[1] // LANES):
        lanes = slice(pair * LANES, (pair + 1) * LANES)
        unit = gated_ref[:, lanes].astype(F32) * scale
        du = dno_ref[:, lanes].astype(F32) * gain_ref[0:1, lanes]
        d_gated = (scale * (du - unit * mean)).astype(BF16).astype(F32)
        gate = gate_ref[:, lanes].astype(F32)
        sg = sigmoid(gate)
        silu = gate * sg
        dy = d_gated * silu
        dy_ref[:, lanes] = dy.astype(BF16)
        dgate = d_gated * y_ref[:, lanes].astype(F32) * (sg + silu * (1.0 - sg))
        dgate_ref[:, lanes] = dgate.astype(BF16)
        total[:, lanes] += dot(reads_t, (dy * jnp.exp(two_heads(reach, pair, low))).astype(BF16))

    @pl.when(chunk == PER_UNIT - 1)
    def _():
        pull_ref[0] = total[...].astype(BF16)


def backward_kernel(
    x_ref, xp_ref, bc_ref, bcp_ref, dt_ref, halo_ref, cx_ref, cbc_ref, hp_ref,
    dy_ref, y_ref, st_ref, in_ref, acum_ref, after_ref, pick_ref,
    dall_ref, head_ref, head_bc_ref, gx_ref, gbc_ref, gh_ref,
    xe, be, adjoint, dpx, dpb, ends, place=None,
):
    unit, chunk = (pl.program_id(0), pl.program_id(1)) if place is None else place
    inner = x_ref.shape[1]

    @pl.when((unit == 0) & (chunk == 0))
    def _():
        gx_ref[...] = jnp.zeros_like(gx_ref)
        gbc_ref[...] = jnp.zeros_like(gbc_ref)
        gh_ref[...] = jnp.zeros_like(gh_ref)

    @pl.when(chunk == 0)
    def _():
        adjoint[...] = after_ref[0].astype(F32)
        dpx[CHUNK:] = jnp.zeros((8, inner), F32)
        dpb[CHUNK:] = jnp.zeros((8, 2 * LANES), F32)

    inside = chunk != PER_UNIT - 1
    xe[0:8] = jnp.where(inside, xp_ref[...].astype(F32)[8:], halo_ref[unit, :, :inner].astype(F32)[8:])
    xe[8:] = x_ref[...].astype(F32)
    be[0:8] = jnp.where(inside, bcp_ref[...].astype(F32)[8:], halo_ref[unit, :, inner:].astype(F32)[8:])
    be[8:] = bc_ref[...].astype(F32)
    shared, slopes = [], []
    for k in range(2):
        pre = conv_of(be, slice(k * LANES, (k + 1) * LANES), cbc_ref)
        sg = sigmoid(pre)
        shared.append(pre * sg)
        slopes.append(sg + pre * sg * (1.0 - sg))
    keys, reads = shared
    reads_t = reads.T.astype(BF16)
    keys, reads = keys.astype(BF16), reads.astype(BF16)
    rows, columns = grid_iotas()
    causal = rows >= columns
    shifted_dt, step = step_of(dt_ref, hp_ref)
    rate = hp_ref[0:1]
    log_decay = -step * rate
    running = exact_left(jnp.where(causal, 1.0, 0.0).astype(BF16), log_decay)
    total = running[CHUNK - 1 : CHUNK]
    base = acum_ref[0:1] - running[0:1]
    running_t = running.T
    scores_t = jnp.where(rows <= columns, dot_nt(keys, reads), 0.0)
    low = columns < LANES // 2
    low_row = low[0:1]
    d_scores = jnp.zeros((CHUNK, CHUNK), F32)
    d_reads = jnp.zeros((CHUNK, LANES), F32)
    d_keys = jnp.zeros((CHUNK, LANES), F32)
    sums = jnp.zeros((3 * CHUNK, LANES), F32)

    for pair in range(inner // LANES):
        lanes = slice(pair * LANES, (pair + 1) * LANES)
        shifted = [xe[5 + k : 5 + k + CHUNK, lanes] for k in range(4)]
        pre = cx_ref[4:5, lanes] + sum(shifted[k] * cx_ref[k : k + 1, lanes] for k in range(4))
        sg = sigmoid(pre)
        xs = pre * sg
        slope = sg + xs * (1.0 - sg)
        step_wide = two_heads(step, pair, low)
        weighted = xs * step_wide
        first = jnp.broadcast_to(running[:, 2 * pair : 2 * pair + 1], (CHUNK, CHUNK))
        second = jnp.broadcast_to(running[:, 2 * pair + 1 : 2 * pair + 2], (CHUNK, CHUNK))
        gap0 = first - running_t[2 * pair : 2 * pair + 1]
        gap1 = second - running_t[2 * pair + 1 : 2 * pair + 2]
        mix_t = jnp.concatenate(
            [
                (jnp.exp(jnp.minimum(-gap0, 0.0)) * scores_t).astype(BF16),
                (jnp.exp(jnp.minimum(-gap1, 0.0)) * scores_t).astype(BF16),
            ],
            axis=1,
        )
        dy_low = dy_ref[:, lanes]
        dy = dy_low.astype(F32)
        zero = jnp.zeros_like(dy_low)
        dy_two = jnp.concatenate([jnp.where(low, dy_low, zero), jnp.where(low, zero, dy_low)], axis=0)
        d_mix = dot_nt(dy_two, weighted.astype(BF16))
        d_scores = d_scores + (
            jnp.exp(jnp.minimum(gap0, 0.0)) * d_mix[:CHUNK]
            + jnp.exp(jnp.minimum(gap1, 0.0)) * d_mix[CHUNK:]
        )
        at = jnp.where(low, first, second)
        at_end = two_heads(total, pair, low_row)
        tail = jnp.exp(at_end - at)
        end_decay = jnp.exp(at_end)
        later = adjoint[:, lanes]
        later_low = later.astype(BF16)
        from_state = dot(keys, later_low) * tail
        d_weighted = dot(mix_t, dy_two) + from_state
        before = st_ref[0, :, lanes].astype(F32) + in_ref[0, :, lanes].astype(F32) * jnp.exp(
            two_heads(base, pair, low_row)
        )
        d_read = (dy * jnp.exp(at)).astype(BF16)
        d_reads = d_reads + dot_nt(d_read, before.astype(BF16))
        d_keys = d_keys + dot_nt((weighted * tail).astype(BF16), later_low)
        skip = cx_ref[5:6, lanes]
        y = y_ref[:, lanes].astype(F32) - skip * xs
        d_run = dy * y - weighted * d_weighted
        pick = pick_ref[lanes, :]
        sums = sums + dot(
            jnp.concatenate(
                [d_run.astype(BF16), (xs * d_weighted).astype(BF16), (dy * xs).astype(BF16)], axis=0
            ),
            pick,
        )
        ends[:, lanes] = jnp.broadcast_to(
            jnp.sum(weighted * from_state, axis=0, keepdims=True)
            + end_decay * jnp.sum(later * before, axis=0, keepdims=True),
            (8, LANES),
        )
        d_pre = (step_wide * d_weighted + skip * dy) * slope
        dpx[0:CHUNK, lanes] = d_pre
        adjoint[:, lanes] = later * end_decay + dot(reads_t, d_read)
        d_x = jnp.zeros((CHUNK, LANES), F32)
        for k in range(4):
            d_x = d_x + dpx[3 - k : 3 - k + CHUNK, lanes] * cx_ref[k : k + 1, lanes]
            gx_ref[8 * k : 8 * k + 8, lanes] += jnp.sum(
                (d_pre * shifted[k]).reshape(CHUNK // 8, 8, LANES), axis=0
            )
        gx_ref[32:40, lanes] += jnp.sum(d_pre.reshape(CHUNK // 8, 8, LANES), axis=0)
        dall_ref[:, lanes] = d_x.astype(BF16)

    d_scores_low = jnp.where(causal, d_scores, 0.0)
    d_reads = d_reads + dot(d_scores_low.astype(BF16), keys)
    d_keys = d_keys + dot(d_scores_low.T.astype(BF16), reads)
    for k, part in enumerate((d_keys, d_reads)):
        lanes = slice(k * LANES, (k + 1) * LANES)
        d_pre = part * slopes[k]
        dpb[0:CHUNK, lanes] = d_pre
        d_x = jnp.zeros((CHUNK, LANES), F32)
        for tap in range(4):
            d_x = d_x + dpb[3 - tap : 3 - tap + CHUNK, lanes] * cbc_ref[tap : tap + 1, lanes]
            gbc_ref[8 * tap : 8 * tap + 8, lanes] += jnp.sum(
                (d_pre * be[5 + tap : 5 + tap + CHUNK, lanes]).reshape(CHUNK // 8, 8, LANES), axis=0
            )
        gbc_ref[32:40, lanes] += jnp.sum(d_pre.reshape(CHUNK // 8, 8, LANES), axis=0)
        dall_ref[:, inner + k * LANES : inner + (k + 1) * LANES] = d_x.astype(BF16)

    at_end = exact_right(ends[...], pick_ref[...])[0:1]
    d_log = exact_left(jnp.where(rows <= columns, 1.0, 0.0).astype(BF16), sums[:CHUNK]) + at_end
    d_step = sums[CHUNK : 2 * CHUNK] - d_log * rate
    d_dt = d_step * sigmoid(shifted_dt)
    dall_ref[:, inner + 2 * LANES :] = d_dt.astype(BF16)
    for k, part in enumerate((d_dt, d_log * log_decay, sums[2 * CHUNK :])):
        gh_ref[8 * k : 8 * k + 8] += jnp.sum(part.reshape(CHUNK // 8, 8, LANES), axis=0)
    dpx[CHUNK:] = dpx[0:8]
    dpb[CHUNK:] = dpb[0:8]

    @pl.when(chunk == PER_UNIT - 1)
    def _():
        head_ref[0] = dpx[0:8]
        head_bc_ref[0] = dpb[0:8]


def places():
    f, z = lax.axis_index("fs"), lax.axis_index("sp")
    core, chip = f % 2, f // 2
    by_x, by_y = chip + 1 - 2 * (chip % 2), (chip + 2) % 4
    return f, z, core, chip, by_x, by_y


def remote(src, dst, sends, receives, slot, device):
    return pltpu.make_async_remote_copy(
        src_ref=src, dst_ref=dst, send_sem=sends.at[slot], recv_sem=receives.at[slot],
        device_id=device, device_id_type=MESH,
    )


class Bounce:
    def __init__(self, src, buffer, dst, sems, n):
        self.into = pltpu.make_async_copy(src, buffer, sems.at[2 * n])
        self.out = pltpu.make_async_copy(buffer, dst, sems.at[2 * n + 1])

    def start(self):
        self.into.start()

    def relay(self):
        self.into.wait()
        self.out.start()

    def wait(self):
        self.out.wait()


class Trade:
    def __init__(self, source, sends, receives):
        self.f, self.z, self.core, self.chip, _, _ = places()
        self.source, self.sends, self.receives = source, sends, receives
        self.units = source.shape[0] // 2
        self.near_group, self.far_group = self.z // 2, 1 - self.z // 2
        across = 2 * self.chip + self.z % 2
        self.near, self.far = (across, 2 * self.near_group + self.core), (across, 2 * self.far_group + self.core)
        self.near_at, self.far_at = 2 * self.near_group + self.core, 2 * self.far_group + self.core
        self.partner = (self.f + 1 - 2 * self.core, self.z)
        self.stays = self.z % 2 == self.core
        self.moves = (self.z + self.core) % 2

    def rows_for(self, group, first, last):
        return self.source.at[pl.ds(group * self.units + first, last - first)]

    def swapped(self, at):
        return at + 1 - 2 * (at % 2)

    def send(self, src, dst, slot, device):
        return remote(src, dst, self.sends, self.receives, slot, device)


class Gather:
    def __init__(self, weight, target, sends, receives, local, buffer):
        f, z, self.core, self.chip, self.by_x, self.by_y = places()
        self.weight, self.target, self.sends, self.receives = weight, target, sends, receives
        self.partner = (f + 1 - 2 * self.core, z)
        self.over_x, self.over_y = (2 * self.by_x + self.core, z), (2 * self.by_y + self.core, z)
        self.keep = Bounce(self.columns(self.core), buffer, self.part(self.chip, self.core), local, 0)

    def columns(self, side):
        width = self.weight.shape[1] // 2
        return self.weight.at[:, pl.ds(pl.multiple_of(side * width, width), width)]

    def part(self, chip, core):
        return self.target.at[chip, core]

    def copy(self, src, dst, slot, device):
        return remote(src, dst, self.sends, self.receives, slot, device)

    def sent(self, slot):
        own, other = (self.chip, self.core), (self.chip, 1 - self.core)
        src, dst, device = (
            (self.columns(1 - self.core), own, self.partner),
            (self.columns(self.core), own, self.over_x),
            (self.columns(self.core), own, self.over_y),
            (self.part(*other), other, self.over_x),
            (self.part(*other), other, self.over_y),
            (self.part(self.by_x, self.core), (self.by_x, self.core), self.over_y),
            (self.part(self.by_y, 1 - self.core), (self.by_y, 1 - self.core), self.over_x),
        )[slot]
        return self.copy(src, self.part(*dst), slot, device)

    def arrives(self, slot):
        corner = (self.by_x + 2) % 4
        chip, core = (
            (self.chip, 1 - self.core), (self.by_x, self.core), (self.by_y, self.core),
            (self.by_x, 1 - self.core), (self.by_y, 1 - self.core), (corner, self.core), (corner, 1 - self.core),
        )[slot]
        device = (self.partner, self.over_x, self.over_y, self.over_x, self.over_y, self.over_y, self.over_x)[slot]
        there = self.part(chip, core)
        self.copy(there, there, slot, device).wait_recv()

    def start(self):
        for slot in range(3):
            self.sent(slot).start()
        self.keep.start()

    def second(self):
        self.keep.relay()
        self.arrives(0)
        for slot in (3, 4):
            self.sent(slot).start()

    def third(self):
        self.arrives(1)
        self.sent(5).start()

    def fourth(self):
        self.arrives(4)
        self.sent(6).start()

    def finish(self):
        for slot in (2, 3, 5, 6):
            self.arrives(slot)
        for slot in range(7):
            self.sent(slot).wait_send()
        self.keep.wait()


EARLY_UNITS = 2


def scan_forward_kernel(
    x, bc, dt, first, cot, weight, cx, cbc, hp,
    y, st, own, dec, bcs, acum, halo_out, near_out, far_out, gathered,
    xe, be, state, base, halo, halo_sends, halo_receives, sends, receives, local,
    w_sends, w_receives, w_local, w_buffer, row_buffer,
):
    gather = Gather(weight, gathered, w_sends, w_receives, w_local, w_buffer)
    unit, chunk = pl.program_id(0), pl.program_id(1)
    segments, trade = Segments(), Trade(cot, sends, receives)
    me, last = segments.me, segments.count - 1
    units, depth, width = halo.shape

    def halo_copy():
        at = pl.ds(first.shape[1] - depth, depth)
        device = segments.device((me + 1) % segments.count)
        return remote(first.at[:, at, pl.ds(0, width)], halo, halo_sends, halo_receives, 0, device)

    far_copy = trade.send(trade.rows_for(trade.far_group, 0, EARLY_UNITS), far_out, 0, trade.far)
    near_copy = trade.send(trade.rows_for(trade.near_group, 0, units), near_out, 1, trade.near)
    keep = Bounce(trade.rows_for(trade.near_group, 0, units), row_buffer, near_out, local, 0)

    @pl.when((unit == 0) & (chunk == 0))
    def _():
        barrier = pltpu.get_barrier_semaphore()
        pl.semaphore_signal(barrier, inc=1, device_id=trade.far, device_id_type=MESH)

        @pl.when(jnp.logical_not(trade.stays))
        def _():
            pl.semaphore_signal(barrier, inc=1, device_id=trade.near, device_id_type=MESH)

        @pl.when(me > 0)
        def _():
            pl.semaphore_signal(
                barrier, inc=1, device_id=segments.device((me + last) % segments.count), device_id_type=MESH
            )

        for device in (gather.partner, gather.over_x, gather.over_y):
            pl.semaphore_signal(barrier, inc=1, device_id=device, device_id_type=MESH)
        pl.semaphore_wait(barrier, 4 + trade.moves + jnp.where(me < last, 1, 0))

        @pl.when(me < last)
        def _():
            halo_copy().start()

        gather.start()
        far_copy.start()

        @pl.when(trade.stays)
        def _():
            keep.start()

        @pl.when(jnp.logical_not(trade.stays))
        def _():
            near_copy.start()

        @pl.when(me > 0)
        def _():
            halo_copy().wait_recv()

        @pl.when(me == 0)
        def _():
            halo[...] = jnp.zeros_like(halo)

        halo_out[...] = halo[...]

    forward_kernel(x, bc, dt, halo, cx, cbc, hp, y, st, own, dec, bcs, acum, xe, be, state, base)

    @pl.when((unit == 0) & (chunk == 1) & trade.stays)
    def _():
        keep.relay()

    for at_unit, at_chunk, stage in ((0, 0, gather.second), (1, 1, gather.third), (1, 3, gather.fourth)):

        @pl.when((unit == at_unit) & (chunk == at_chunk))
        def _(stage=stage):
            stage()

    @pl.when((unit == units - 1) & (chunk == PER_UNIT - 1))
    def _():
        gather.finish()

        @pl.when(me < last)
        def _():
            halo_copy().wait_send()

        far_copy.wait()

        @pl.when(trade.stays)
        def _():
            keep.wait()

        @pl.when(jnp.logical_not(trade.stays))
        def _():
            near_copy.wait()


def one_hot(rows, columns, offset):
    i = lax.broadcasted_iota(jnp.int32, (rows, columns), 0)
    j = lax.broadcasted_iota(jnp.int32, (rows, columns), 1)
    return jnp.where(j == i + offset, 1.0, 0.0).astype(BF16)


SMALL_ROWS = 32


def head_kernel(
    hidden, w_x, w_bc, w_dt, conv_x, conv_x_bias, gate_gain, norm_gain, conv_bc, conv_bc_bias, dt_bias, a_log, skip_d,
    rows_out, first_out, cx, cbc, hp, gain_in, gain_rows,
    dt_mine, dt_other, small, small_all, row_buffer, x_buffer, bc_buffer,
    local, sends, receives, small_sends, small_receives,
):
    f, z, core, chip, by_x, by_y = places()
    trade = Trade(hidden, sends, receives)
    partner, over_x, over_y = trade.partner, (2 * by_x + core, z), (2 * by_y + core, z)
    far, near, stays = trade.far, trade.near, trade.stays
    units, inner, shards = rows_out.shape[0], cx.shape[1], small_all.shape[0]
    heads = w_dt.shape[1] // 2

    barrier = pltpu.get_barrier_semaphore()
    for k in range(1, shards):
        pl.semaphore_signal(barrier, inc=1, device_id=((f + k) % shards, z), device_id_type=MESH)
    pl.semaphore_signal(barrier, inc=1, device_id=far, device_id_type=MESH)

    @pl.when(jnp.logical_not(stays))
    def _():
        pl.semaphore_signal(barrier, inc=1, device_id=near, device_id_type=MESH)

    pl.semaphore_wait(barrier, shards + trade.moves)

    def part(chip_at, core_at):
        return first_out.at[chip_at, core_at]

    def copy(src, dst, slot, device):
        return remote(src, dst, sends, receives, slot, device)

    class Thirds:
        def __init__(self, side, slot, device):
            columns = pl.ds(pl.multiple_of(side * inner, inner), inner)
            self.whole = copy(part(chip, core), part(chip, core), slot, device)
            dst, wide = part(chip, core), 2 * LANES
            dt = dt_mine if device is not partner else dt_other
            self.copies = [
                copy(w_x.at[:, columns], dst.at[:, pl.ds(0, inner)], slot, device),
                copy(w_bc, dst.at[:, pl.ds(inner, wide)], slot, device),
                copy(dt, dst.at[:, pl.ds(inner + wide, LANES)], slot, device),
            ]

        def start(self):
            for one in self.copies:
                one.start()

        def wait_send(self):
            self.whole.wait_send()

    to_far = copy(trade.rows_for(trade.far_group, 0, units), rows_out.at[:, z], 0, far)
    to_far.start()
    i = lax.broadcasted_iota(jnp.int32, (2 * heads, LANES), 0)
    j = lax.broadcasted_iota(jnp.int32, (2 * heads, LANES), 1)
    for side, kept in ((core, dt_mine), (1 - core, dt_other)):
        chosen = jnp.where((i == j + side * heads) & (j < heads), 1.0, 0.0).astype(BF16)
        kept[...] = dot(w_dt[...], chosen).astype(BF16)
    to_partner, to_x, to_y = Thirds(1 - core, 1, partner), Thirds(core, 2, over_x), Thirds(core, 3, over_y)
    for one in (to_partner, to_x, to_y):
        one.start()
    to_near = copy(trade.rows_for(trade.near_group, 0, units), rows_out.at[:, z], 4, near)
    keep_rows = Bounce(trade.rows_for(trade.near_group, 0, units), row_buffer, rows_out.at[:, z], local, 0)

    @pl.when(stays)
    def _():
        keep_rows.start()

    @pl.when(jnp.logical_not(stays))
    def _():
        to_near.start()

    own = part(chip, core)
    keeps = [
        Bounce(
            w_x.at[:, pl.ds(pl.multiple_of(core * inner, inner), inner)], x_buffer,
            own.at[:, pl.ds(0, inner)], local, 1,
        ),
        Bounce(w_bc, bc_buffer, own.at[:, pl.ds(inner, 2 * LANES)], local, 2),
    ]
    keep_dt = pltpu.make_async_copy(dt_mine, own.at[:, pl.ds(inner + 2 * LANES, LANES)], local.at[6])
    for keep in keeps:
        keep.start()
    keep_dt.start()

    share = conv_x.shape[0]
    per_norm, per_bc, per_head = norm_gain.shape[1], conv_bc.shape[0], dt_bias.shape[1]
    built = jnp.zeros((SMALL_ROWS, share), F32)
    taps = dot_tn(conv_x[...], one_hot(share, share, 0))
    gains = dot(norm_gain[...], one_hot(per_norm, share, per_norm * (f % 2)))
    spread_bc = one_hot(per_bc, 2 * LANES, per_bc * f)
    taps_bc, bias_bc = dot_tn(conv_bc[...], spread_bc), dot(conv_bc_bias[...], spread_bc)
    spread_heads = one_hot(per_head, LANES, per_head * (f % 4))
    by_head = [dot(v[...], spread_heads) for v in (dt_bias, a_log, skip_d)]
    small[...] = built
    small[0:4] = taps
    small[4:5] = conv_x_bias[...].astype(F32)
    small[5:6] = gate_gain[...].astype(F32)
    for k in range(4):
        small[6 + k : 7 + k] = jnp.where(f // 2 == k, gains, 0.0)
    small[10:14, : 2 * LANES] = taps_bc
    small[14:15, : 2 * LANES] = bias_bc
    for side in range(2):
        for n, values in enumerate(by_head):
            small[15 + side : 16 + side, n * LANES : (n + 1) * LANES] = jnp.where(f // 4 == side, values, 0.0)

    def small_copy(k, at):
        return pltpu.make_async_remote_copy(
            src_ref=small, dst_ref=small_all.at[at],
            send_sem=small_sends.at[k], recv_sem=small_receives.at[at],
            device_id=((f + k) % shards, z), device_id_type=MESH,
        )

    for k in range(1, shards):
        small_copy(k, f).start()
    small_all[f] = small[...]

    for keep in keeps:
        keep.relay()

    @pl.when(stays)
    def _():
        keep_rows.relay()

    copy(part(chip, core), part(chip, 1 - core), 1, partner).wait_recv()
    again_x = copy(part(chip, 1 - core), part(chip, 1 - core), 5, over_x)
    again_x.start()
    again_y = copy(part(chip, 1 - core), part(chip, 1 - core), 6, over_y)
    again_y.start()

    near_at, far_at = trade.near_at, trade.far_at

    @pl.when(stays)
    def _():
        keep_rows.wait()

    @pl.when(jnp.logical_not(stays))
    def _():
        copy(trade.rows_for(trade.near_group, 0, units), rows_out.at[:, near_at], 4, near).wait_recv()

    near_on = copy(rows_out.at[:, near_at], rows_out.at[:, near_at], 7, partner)
    near_on.start()

    for k in range(1, shards):
        small_copy(k, (f + k) % shards).wait_recv()
    cx[...] = jnp.zeros_like(cx)
    for k in range(4):
        block = small_all[4 * core + k]
        lanes = slice(k * share, (k + 1) * share)
        cx[0:5, lanes] = block[0:5]
        gain_rows[:, lanes] = jnp.broadcast_to(block[5:6], (8, share))
    summed = small_all[0]
    for k in range(1, shards):
        summed = summed + small_all[k]
    for k in range(4):
        gain_in[:, k * share : (k + 1) * share] = jnp.broadcast_to(summed[6 + k : 7 + k], (8, share))
    cbc[...] = jnp.zeros_like(cbc)
    cbc[0:5] = summed[10:15, : 2 * LANES]
    ours = jnp.where(core == 0, summed[15:16], summed[16:17])
    lane = lax.broadcasted_iota(jnp.int32, (1, LANES), 1)
    hp[...] = jnp.zeros_like(hp)
    hp[0:1] = jnp.where(lane < heads, jnp.exp(ours[:, LANES : 2 * LANES]), 0.0)
    hp[1:2] = ours[:, :LANES]
    skips = ours[:, 2 * LANES :]
    for pair in range(inner // LANES):
        cx[5:6, pair * LANES : (pair + 1) * LANES] = two_heads(skips, pair, lane < LANES // 2)

    copy(part(by_x, core), part(by_x, core), 2, over_x).wait_recv()
    on_y = copy(part(by_x, core), part(by_x, core), 8, over_y)
    on_y.start()
    copy(part(by_y, core), part(by_y, core), 3, over_y).wait_recv()
    copy(part(by_x, 1 - core), part(by_x, 1 - core), 5, over_x).wait_recv()
    copy(part(by_y, 1 - core), part(by_y, 1 - core), 6, over_y).wait_recv()
    on_x = copy(part(by_y, 1 - core), part(by_y, 1 - core), 9, over_x)
    on_x.start()

    copy(trade.rows_for(trade.far_group, 0, units), rows_out.at[:, far_at], 0, far).wait_recv()
    far_on = copy(rows_out.at[:, far_at], rows_out.at[:, far_at], 10, partner)
    far_on.start()

    corner = (by_x + 2) % 4
    copy(part(corner, core), part(corner, core), 8, over_y).wait_recv()
    copy(part(corner, 1 - core), part(corner, 1 - core), 9, over_x).wait_recv()
    copy(rows_out.at[:, near_at], rows_out.at[:, trade.swapped(near_at)], 7, partner).wait_recv()
    copy(rows_out.at[:, far_at], rows_out.at[:, trade.swapped(far_at)], 10, partner).wait_recv()
    for sent in (to_far, to_partner, to_x, to_y, again_x, again_y, near_on, on_y, on_x, far_on):
        sent.wait_send()

    @pl.when(jnp.logical_not(stays))
    def _():
        to_near.wait_send()

    for k in range(1, shards):
        small_copy(k, f).wait_send()
    for keep in keeps:
        keep.wait()
    keep_dt.wait()


def states_kernel(
    own, dec, cot, near_rows, far_rows, normed, w_gate, w_out, y0, bcs, acum,
    dec_out, rows_out, gathered, gate_out, incoming_out, y, gated, squares,
    incoming, parts, decs, results, weight, gate, blocks,
    sends, receives, dec_sends, dec_receives, back_sends, back_receives,
    row_sends, row_receives, w_sends, w_receives, local, w_local, block_sems,
    w_buffer, near_buffer, far_buffer, row_local,
):
    i = pl.program_id(0)
    chunks = pl.num_programs(0) - 1
    segments, trade = Segments(), Trade(cot, row_sends, row_receives)
    gather = Gather(w_out, gathered, w_sends, w_receives, w_local, w_buffer)
    me, count, z = segments.me, segments.count, segments.z
    units, share = own.shape[0], parts.shape[2]
    early = far_rows.shape[0]
    near_at, far_at = trade.near_at, trade.far_at
    block = blocks.shape[1]
    count_blocks = gate.shape[0] // block

    def rows_of(k):
        return pl.ds(pl.multiple_of(k * share, share), share)

    def out_copy(k, at_me):
        other, device = segments.peer(k)
        src, slot = (own.at[:, rows_of(other)], me) if at_me else (own.at[:, rows_of(me)], other)
        return pltpu.make_async_remote_copy(
            src_ref=src, dst_ref=parts.at[slot], send_sem=sends.at[k], recv_sem=receives.at[slot],
            device_id=device, device_id_type=MESH,
        )

    def dec_copy(k, at_me):
        other, device = segments.peer(k)
        slot = me if at_me else other
        return pltpu.make_async_remote_copy(
            src_ref=dec, dst_ref=decs.at[slot], send_sem=dec_sends.at[k], recv_sem=dec_receives.at[slot],
            device_id=device, device_id_type=MESH,
        )

    def back_copy(k, at_me):
        other, device = segments.peer(k)
        slot = me if at_me else other
        return pltpu.make_async_remote_copy(
            src_ref=results.at[other], dst_ref=incoming.at[:, rows_of(slot)],
            send_sem=back_sends.at[k], recv_sem=back_receives.at[slot],
            device_id=device, device_id_type=MESH,
        )

    def fetch(k):
        return pltpu.make_async_copy(normed.at[pl.ds(k * block, block)], blocks.at[k % 2], block_sems.at[k % 2])

    def multiply(k):
        if k + 1 < count_blocks:
            fetch(k + 1).start()
        fetch(k).wait()

        def part(n, carry):
            columns = pl.ds(pl.multiple_of(n * 384, 384), 384)
            gate[pl.ds(k * block, block), columns] = dot(blocks[k % 2], weight[:, columns]).astype(BF16)
            return carry

        lax.fori_loop(0, gate.shape[1] // 384, part, 0)

    last = trade.send(trade.rows_for(trade.far_group, early, units), rows_out.at[early:, z], 0, trade.far)
    last_came = trade.send(
        trade.rows_for(trade.far_group, early, units), rows_out.at[early:, far_at], 0, trade.far
    )
    near_on = trade.send(near_rows, rows_out.at[:, near_at], 1, trade.partner)
    far_on = trade.send(far_rows, rows_out.at[:early, far_at], 2, trade.partner)
    last_on = trade.send(rows_out.at[early:, far_at], rows_out.at[early:, far_at], 3, trade.partner)
    near_keep = Bounce(near_rows, near_buffer, rows_out.at[:, near_at], row_local, 0)
    far_keep = Bounce(far_rows, far_buffer, rows_out.at[:early, far_at], row_local, 1)
    take_weight = pltpu.make_async_copy(w_gate, weight, local.at[2])
    keep_gate = pltpu.make_async_copy(gate, gate_out, local.at[3])
    keep_states = pltpu.make_async_copy(incoming, incoming_out, local.at[4])

    @pl.when(i == 0)
    def _():
        barrier = pltpu.get_barrier_semaphore()
        for k in range(1, count):
            pl.semaphore_signal(barrier, inc=1, device_id=segments.peer(k)[1], device_id_type=MESH)
        for device in (trade.partner, trade.far):
            pl.semaphore_signal(barrier, inc=1, device_id=device, device_id_type=MESH)
        pl.semaphore_wait(barrier, count + 1)
        for k in range(1, count):
            dec_copy(k, True).start()
            out_copy(k, True).start()
        take_weight.start()
        fetch(0).start()
        last.start()
        near_on.start()
        far_on.start()
        near_keep.start()
        far_keep.start()
        parts[me] = own[:, rows_of(me)]
        decs[me] = dec[...]
        take_weight.wait()
        for k in range(count_blocks // 2):
            multiply(k)
        near_keep.relay()
        far_keep.relay()
        for k in range(1, count):
            dec_copy(k, False).wait_recv()
            out_copy(k, False).wait_recv()
        dec_out[...] = decs[...]
        running = [jnp.zeros((share, own.shape[2]), F32) for _ in range(units)]
        for n in range(count):
            for u in range(units):
                results[n, u] = running[u].astype(BF16)
                running[u] = running[u] * decs[n, u : u + 1] + parts[n, u].astype(F32)
        incoming[:, rows_of(me)] = results[me]
        for k in range(1, count):
            back_copy(k, True).start()
        gather.start()
        multiply(count_blocks // 2)
        gather.second()
        for k in range(count_blocks // 2 + 1, count_blocks):
            multiply(k)
        keep_gate.start()
        last_came.wait_recv()
        last_on.start()
        for k in range(1, count):
            back_copy(k, False).wait_recv()
        keep_states.start()

    @pl.when(i > 0)
    def _():
        place = pl.ds(pl.multiple_of((i - 1) * CHUNK, CHUNK), CHUNK)
        gate_kernel(
            y0, gate.at[place], bcs, acum, incoming.at[pl.ds((i - 1) // PER_UNIT, 1)], y, gated, squares
        )

    @pl.when(i == 3)
    def _():
        gather.third()

    @pl.when(i == 6)
    def _():
        gather.fourth()

    @pl.when(i == chunks)
    def _():
        other_near, other_far = trade.swapped(near_at), trade.swapped(far_at)
        trade.send(near_rows, rows_out.at[:, other_near], 1, trade.partner).wait_recv()
        trade.send(far_rows, rows_out.at[:early, other_far], 2, trade.partner).wait_recv()
        trade.send(rows_out.at[early:, far_at], rows_out.at[early:, other_far], 3, trade.partner).wait_recv()
        for copy in (last, near_on, far_on, last_on):
            copy.wait_send()
        for k in range(1, count):
            dec_copy(k, True).wait_send()
            out_copy(k, True).wait_send()
            back_copy(k, True).wait_send()
        for copy in (near_keep, far_keep, keep_gate, keep_states):
            copy.wait()
        gather.finish()


class Reduction:
    def __init__(self, pieces, sends, receives, base, special=None):
        self.f, self.z, self.core, self.chip, self.by_x, self.by_y = places()
        self.corner, self.bit = (self.by_x + 2) % 4, self.z % 2
        self.sends, self.receives, self.base, self.special = sends, receives, base, special
        self.pieces, z_start = [], 0
        for n, (start, width, way) in enumerate(pieces):
            wide = width + LANES if start == special else 2 * width
            self.pieces.append((n, start, width, way, z_start, wide))
            z_start += wide
        self.wide = z_start
        self.partner = (self.f + 1 - 2 * self.core, self.z)
        self.over = {"x": (2 * self.by_x + self.core, self.z), "y": (2 * self.by_y + self.core, self.z)}
        self.near, self.far = (self.f, self.z + 1 - 2 * self.bit), (self.f, (self.z + 2) % 4)

    @staticmethod
    def at(i, size):
        return pl.ds(pl.multiple_of(i * size, size), size)

    def copy(self, src, dst, n, k, device):
        return remote(src, dst, self.sends, self.receives, self.base + 7 * n + k, device)

    def over_chips(self, source, own, passed, r1, s2, r2, sp, rp, total):
        self.source, self.own, self.passed = source, own, passed
        self.r1, self.s2, self.r2, self.sp, self.rp, self.total = r1, s2, r2, sp, rp, total
        self.rows = r2.shape[0]

    def first_copies(self, piece):
        n, start, width, way, _, _ = piece
        columns = pl.ds(start, width)
        to = self.by_x if way == "x" else self.by_y
        return [
            self.copy(self.source(i, columns), self.r1.at[k, :, columns], n, k, self.over[way])
            for k, i in enumerate((to, self.corner))
        ]

    def second_copy(self, piece):
        n, start, width, way, _, _ = piece
        columns = pl.ds(start, width)
        other = "y" if way == "x" else "x"
        return self.copy(self.s2.at[:, columns], self.r2.at[:, columns], n, 2, self.over[other])

    def pair_copy(self, piece):
        n, start, width, _, _, _ = piece
        columns = pl.ds(start, width)
        return self.copy(self.sp.at[:, columns], self.rp.at[:, columns], n, 3, self.partner)

    def start(self, pieces=None):
        for piece in self.pieces if pieces is None else pieces:
            for copy in self.first_copies(piece):
                copy.start()

    def after_first(self, piece):
        _, start, width, way, _, _ = piece
        if self.source is not None:
            for copy in self.first_copies(piece):
                copy.wait_recv()
        columns = pl.ds(start, width)
        passed = self.passed(self.by_y if way == "x" else self.by_x, columns)
        self.s2[:, columns] = (passed.astype(F32) + self.r1[1, :, columns].astype(F32)).astype(BF16)
        self.second_copy(piece).start()

    def chip_sum(self, piece, side):
        columns = pl.ds(piece[1], piece[2])
        there = self.at(side, self.rows // 2)
        own = self.own(side, columns).astype(F32)
        return own + self.r1[0, there, columns].astype(F32) + self.r2[there, columns].astype(F32)

    def lanes_at(self, start, side, width):
        return pl.ds(pl.multiple_of(start + side * width, LANES), width)

    def after_second(self, piece):
        _, start, width, _, z_at, _ = piece
        self.second_copy(piece).wait_recv()
        self.sp[:, pl.ds(start, width)] = self.chip_sum(piece, 1 - self.core).astype(BF16)
        self.pair_copy(piece).start()

    def after_pair(self, piece):
        _, start, width, _, z_at, _ = piece
        self.pair_copy(piece).wait_recv()
        own = self.chip_sum(piece, self.core)
        came = self.rp[:, pl.ds(start, width)]
        if start == self.special:
            both = 2 * LANES
            self.total[:, pl.ds(z_at, both)] = (own[:, :both] + came[:, :both].astype(F32)).astype(BF16)
            self.total[:, self.lanes_at(z_at + both, self.core, LANES)] = own[:, both:].astype(BF16)
            self.total[:, self.lanes_at(z_at + both, 1 - self.core, LANES)] = came[:, both:]
        else:
            self.total[:, self.lanes_at(z_at, self.core, width)] = own.astype(BF16)
            self.total[:, self.lanes_at(z_at, 1 - self.core, width)] = came

    def drain_chips(self):
        for piece in self.pieces:
            firsts = [] if self.source is None else self.first_copies(piece)
            for copy in firsts + [self.second_copy(piece), self.pair_copy(piece)]:
                copy.wait_send()

    def over_members(self, total, came, sums, across, last, store):
        self.total, self.store = total, store
        self.came, self.sums, self.across, self.last = came, sums, across, last
        self.half = total.shape[0] // 2

    def z_copy(self, piece, k):
        n, _, _, _, start, wide = piece
        columns = pl.ds(start, wide)
        src, dst, device = (
            (self.total.at[self.at(1 - self.bit, self.half), columns], self.came, self.near),
            (self.sums.at[0, :, columns], self.across, self.far),
            (self.sums.at[1, :, columns], self.last, self.near),
        )[k]
        return self.copy(src, dst.at[:, columns], n, 4 + k, device)

    def start_members(self, piece):
        self.z_copy(piece, 0).start()

    def after_near(self, piece):
        columns = pl.ds(piece[4], piece[5])
        self.z_copy(piece, 0).wait_recv()
        own = self.total[self.at(self.bit, self.half), columns].astype(F32)
        self.sums[0, :, columns] = (own + self.came[:, columns].astype(F32)).astype(BF16)
        self.z_copy(piece, 1).start()

    def after_far(self, piece):
        columns = pl.ds(piece[4], piece[5])
        self.z_copy(piece, 1).wait_recv()
        total = self.sums[0, :, columns].astype(F32) + self.across[:, columns].astype(F32)
        self.sums[1, :, columns] = total.astype(BF16)
        self.z_copy(piece, 2).start()
        self.store(piece, self.at(self.bit, self.half), total.astype(BF16).astype(F32))

    def after_last(self, piece):
        self.z_copy(piece, 2).wait_recv()
        values = self.last[:, pl.ds(piece[4], piece[5])].astype(F32)
        self.store(piece, self.at(1 - self.bit, self.half), values)

    def drain_members(self):
        for piece in self.pieces:
            for k in range(3):
                self.z_copy(piece, k).wait_send()


def chip_scratch(rows, width):
    return [
        pltpu.VMEM((2, 2 * rows, width), BF16),
        pltpu.VMEM((2 * rows, width), BF16),
        pltpu.VMEM((2 * rows, width), BF16),
        pltpu.VMEM((rows, width), BF16),
        pltpu.VMEM((rows, width), BF16),
    ]


def member_scratch(rows, wide):
    half = (rows // 2, wide)
    return [
        pltpu.VMEM(half, BF16), pltpu.VMEM((2,) + half, BF16),
        pltpu.VMEM(half, BF16), pltpu.VMEM(half, BF16),
    ]


FIRST_PIECES = ((0, 512, "x"), (1024, 512, "y"), (512, 512, "x"), (1536, 384, "y"))
HALF_PIECES = ((0, 768, "x"), (768, 768, "y"))


def tail_kernel(
    normed, d_all, d_base, w_first, unit_rows, g_x, g_bc, g_heads, g_gate, z_total,
    out_x, out_bc, out_dt, vec_out, d_out, out_z,
    turned, g, d_part, d_came, local, r1, s2, r2, sp, rp, total, came, sums, across, last,
    z_came, z_sums, z_across, z_last, end_x, end_bc, end_dt, end_z,
    vs, vr, vec_all, sends, receives, vec_sends, vec_receives,
):
    i = pl.program_id(0)
    steps = pl.num_programs(0) // 2
    f, z, core, chip, by_x, by_y = places()
    rows = g.shape[0] // 4
    inner = out_x.shape[1] // 2
    wide = normed.shape[1]
    bit, upper, units = z % 2, z // 2, d_part.shape[0]
    first = Reduction(FIRST_PIECES, sends, receives, 0, inner)
    gate = Reduction(HALF_PIECES, sends, receives, 7 * len(FIRST_PIECES))
    slot = 7 * (len(FIRST_PIECES) + len(HALF_PIECES))
    partner, near, far = first.partner, first.near, first.far
    token_near, token_far = (2 * chip + bit, 2 * upper + core), (2 * chip + bit, 2 * (1 - upper) + core)
    stays = bit == core

    def d_pair(k, n):
        return remote(d_part.at[:, k, 1 - core], d_came.at[:, k], sends, receives, slot + n, partner)

    def d_trade(k, n, device, group):
        return remote(
            d_part.at[:, k, core], d_out.at[pl.ds(group * units, units)], sends, receives, slot + 2 + n, device
        )

    def d_add(k):
        for u in range(units):
            d_part[u, k, core] = (d_part[u, k, core].astype(F32) + d_came[u, k].astype(F32)).astype(BF16)

    d_keep = pltpu.make_async_copy(d_part.at[:, upper, core], d_out.at[pl.ds(upper * units, units)], local.at[0])

    first.over_chips(
        lambda i, columns: g.at[first.at(i, rows), columns],
        lambda side, columns: g[pl.ds(pl.multiple_of(chip * rows + side * (rows // 2), rows // 2), rows // 2), columns],
        lambda i, columns: g[first.at(i, rows), columns],
        r1, s2, r2, sp, rp, total,
    )

    def store_first(piece, there, values):
        _, start, width, _, _, _ = piece
        if start == inner:
            end_bc[there, :] = values[:, : 2 * LANES]
            end_dt[there, :] = values[:, 2 * LANES :]
        else:
            end_x[there, pl.ds(start, width)] = values[:, :width]
            end_x[there, pl.ds(inner + start, width)] = values[:, width:]

    def store_gate(piece, there, values):
        _, start, width, _, _, _ = piece
        end_z[there, pl.ds(start, width)] = values[:, :width]
        end_z[there, pl.ds(inner + start, width)] = values[:, width:]

    gate.over_members(z_total, z_came, z_sums, z_across, z_last, store_gate)
    first.over_members(total, came, sums, across, last, store_first)

    vec_ways = [first.over["x"], first.over["y"], near, far]

    def vec_copy(k):
        return remote(vs.at[k], vr.at[k], vec_sends, vec_receives, k, vec_ways[k])

    def vec_last(side):
        return remote(vec_all.at[core], vec_all.at[side], vec_sends, vec_receives, 4, partner)

    def vec_step(k):
        if k:
            vec_copy(k - 1).wait_recv()
            summed = vs[k - 1] + vr[k - 1]
            if k < 4:
                vs[k] = summed
            else:
                vec_all[core] = summed
        if k < 4:
            vec_copy(k).start()
        else:
            vec_last(core).start()

    early, late = first.pieces[:2], first.pieces[2:]

    def pair_on(piece):
        first.after_pair(piece)
        first.start_members(piece)

    @pl.when(i == 0)
    def _():
        barrier = pltpu.get_barrier_semaphore()
        for device in (partner, first.over["x"], first.over["y"], near, far, token_far):
            pl.semaphore_signal(barrier, inc=1, device_id=device, device_id_type=MESH)

        @pl.when(jnp.logical_not(stays))
        def _():
            pl.semaphore_signal(barrier, inc=1, device_id=token_near, device_id_type=MESH)

        pl.semaphore_wait(barrier, 6 + (bit + core) % 2)
        for piece in gate.pieces:
            gate.start_members(piece)
        vs[0] = jnp.zeros(vs.shape[1:], F32)

    @pl.when(i < steps)
    def _():
        def part(n, carry):
            columns = pl.ds(pl.multiple_of(n * 384, 384), 384)
            g[pl.ds(pl.multiple_of(i * wide, wide), wide), columns] = dot(
                turned[...], d_all[:, columns]
            ).astype(BF16)
            return carry

        turned[...] = normed[...].T
        lax.fori_loop(0, g.shape[1] // 384, part, 0)

    @pl.when(i == steps - 1)
    def _():
        first.start(early)

    @pl.when(i == steps + 4)
    def _():
        for piece in early:
            first.after_first(piece)
        first.start(late)

    @pl.when(i >= steps)
    def _():
        columns = pl.ds(pl.multiple_of((i - steps) * wide, wide), wide)
        per = d_all.shape[0] // units

        def part(u, carry):
            there = pl.ds(pl.multiple_of(u * per, per), per)
            product = d_base[there, :].astype(F32) + dot_nt(d_all[there, :], w_first[...])
            d_part[u, :, :, :, columns] = product.astype(BF16).reshape(2, 2, per // 4, wide)
            return carry + jnp.sum(product * unit_rows[there, :].astype(F32), axis=0, keepdims=True)

        vs[0, 6:7, columns] = lax.fori_loop(0, units, part, jnp.zeros((1, wide), F32))

    @pl.when(i == steps)
    def _():
        for piece in gate.pieces:
            gate.after_near(piece)

    @pl.when(i == 2 * steps - 1)
    def _():
        d_pair(1 - upper, 0).start()
        d_pair(upper, 1).start()
        for k in range(5):
            vs[0, k : k + 1] = jnp.sum(g_x[8 * k : 8 * k + 8], axis=0, keepdims=True)
            vs[0, 8 + k : 9 + k, : 2 * LANES] = jnp.sum(g_bc[8 * k : 8 * k + 8], axis=0, keepdims=True)
        vs[0, 5:6] = g_gate[...]
        for k in range(3):
            vs[0, 7:8, k * LANES : (k + 1) * LANES] = jnp.sum(
                g_heads[8 * k : 8 * k + 8], axis=0, keepdims=True
            )
        vec_step(0)
        d_pair(1 - upper, 0).wait_recv()
        d_add(1 - upper)
        d_trade(1 - upper, 0, token_far, upper).start()
        d_pair(upper, 1).wait_recv()
        d_add(upper)

        @pl.when(stays)
        def _():
            d_keep.start()

        @pl.when(jnp.logical_not(stays))
        def _():
            d_trade(upper, 1, token_near, upper).start()

        order = (
            (first.after_second, early), (1, ()), (pair_on, early), (2, ()), (first.after_first, late),
            (gate.after_far, gate.pieces), (3, ()), (first.after_second, late), (4, ()),
            (first.after_near, early), (pair_on, late), (gate.after_last, gate.pieces), (first.after_far, early),
            (first.after_near, late), (first.after_last, early), (first.after_far, late), (first.after_last, late),
        )
        for stage, pieces in order:
            if not pieces:
                vec_step(stage)
            for piece in pieces:
                stage(piece)
        ends = [
            pltpu.make_async_copy(src, dst, local.at[1 + n])
            for n, (src, dst) in enumerate(
                ((end_x, out_x), (end_bc, out_bc), (end_dt, out_dt), (end_z, out_z))
            )
        ]
        for end in ends:
            end.start()
        vec_last(1 - core).wait_recv()
        vec_out[...] = vec_all[...]
        d_trade(1 - upper, 0, token_far, 1 - upper).wait_recv()

        @pl.when(stays)
        def _():
            d_keep.wait()

        @pl.when(jnp.logical_not(stays))
        def _():
            d_trade(upper, 1, token_near, upper).wait()

        d_trade(1 - upper, 0, token_far, upper).wait_send()
        d_pair(1 - upper, 0).wait_send()
        d_pair(upper, 1).wait_send()
        first.drain_chips()
        first.drain_members()
        gate.drain_members()
        for k in range(4):
            vec_copy(k).wait_send()
        vec_last(core).wait_send()
        for end in ends:
            end.wait()


def trade_steps(source, target, buffer, local, sends, receives):
    f, z, core, chip, _, _ = places()
    units = source.shape[0]
    bit, upper = z % 2, z // 2
    near, far = (2 * chip + bit, 2 * upper + core), (2 * chip + bit, 2 * (1 - upper) + core)
    stays = bit == core

    def copy(k, n, device, group):
        return remote(source.at[:, k], target.at[pl.ds(group * units, units)], sends, receives, n, device)

    tokens = source.shape[2]
    keeps = [
        Bounce(
            source.at[u, upper], buffer.at[pl.ds(u * tokens, tokens)], target.at[upper * units + u], local, u
        )
        for u in range(units)
    ]

    def relay():
        @pl.when(stays)
        def _():
            for keep in keeps:
                keep.relay()

    def settle():
        @pl.when(stays)
        def _():
            for keep in keeps:
                keep.wait()

    def start():
        copy(1 - upper, 0, far, upper).start()

        @pl.when(stays)
        def _():
            for keep in keeps:
                keep.start()

        @pl.when(jnp.logical_not(stays))
        def _():
            copy(upper, 1, near, upper).start()

    def finish():
        copy(1 - upper, 0, far, 1 - upper).wait_recv()
        copy(1 - upper, 0, far, upper).wait_send()

        @pl.when(jnp.logical_not(stays))
        def _():
            copy(upper, 1, near, upper).wait()

    return start, relay, settle, finish, far, near, stays


class Segments:
    def __init__(self):
        self.f, self.z, self.core, self.chip, _, _ = places()
        self.group = self.z // 2
        self.me = self.chip * 2 + self.z % 2
        self.count = 8

    def device(self, i):
        return ((i // 2) * 2 + self.core, self.group * 2 + i % 2)

    def peer(self, k):
        other = (self.me + k) % self.count
        return other, self.device(other)


def middle_kernel(
    dno, gated, gate, y_pull, stats, gain, bcs, acum_pull, decays, normed, w_gate, g_out, projected,
    x, xp, bc, bcp, dt, halo, cx, cbc, hp, y, st, incoming, acum, pick,
    d_all, heads_x, heads_bc, g_x, g_bc, g_heads, d_base_out, tokens_out, total_out, z_out,
    dy_all, dgate_all, pulled, own, after, parts, results, blocks, turned, w_blocks, products, g_z, out_own,
    o_r1, o_s2, o_r2, o_sp, o_rp, o_total, o_came, o_sums, o_across, o_last,
    z_r1, z_r2, z_rp, z_total,
    xe, be, adjoint, dpx, dpb, ends,
    local, keep_sems, block_sems, w_sems, product_sems, trade_local, trade_sends, trade_receives, sends, receives,
    state_sends, state_receives, back_sends, back_receives,
):
    i = pl.program_id(0)
    chunks = (pl.num_programs(0) - 1) // 2
    f, z, core, chip, by_x, by_y = places()
    segments = Segments()
    me, count = segments.me, segments.count
    units, share = own.shape[0], parts.shape[2]
    rows = g_z.shape[0] // 4
    half = rows // 2
    inner = g_z.shape[1]

    def at(k, size):
        return pl.ds(pl.multiple_of(k * size, size), size)

    start_trade, relay_trade, settle_trade, finish_trade, trade_far, trade_near, stays = trade_steps(
        projected, tokens_out, g_z, trade_local, trade_sends, trade_receives
    )
    out = Reduction(HALF_PIECES, sends, receives, 0)
    gz = Reduction(HALF_PIECES, sends, receives, 7 * len(HALF_PIECES))
    out.over_chips(
        lambda k, columns: g_out.at[at(k, rows), columns],
        lambda side, columns: out_own[at(side, half), columns],
        lambda k, columns: o_s2[:, columns],
        o_r1, o_s2, o_r2, o_sp, o_rp, o_total,
    )

    out.over_members(o_total, o_came, o_sums, o_across, o_last, lambda piece, there, values: None)
    gz.over_chips(
        lambda k, columns: g_z.at[at(k, rows), columns],
        lambda side, columns: g_z[pl.ds(pl.multiple_of(chip * rows + side * half, half), half), columns],
        lambda k, columns: g_z[at(k, rows), columns],
        z_r1, o_s2, z_r2, o_sp, z_rp, z_total,
    )
    left, right = (pl.ds(start, width) for start, width, _ in HALF_PIECES)
    own_rows = pltpu.make_async_copy(g_out.at[at(chip, rows)], out_own, local.at[0])
    pass_left = pltpu.make_async_copy(g_out.at[at(by_y, rows), left], o_s2.at[:, left], local.at[1])
    pass_right = pltpu.make_async_copy(g_out.at[at(by_x, rows), right], o_s2.at[:, right], local.at[2])

    def keep_out():
        copies = []
        for piece in out.pieces:
            n, start, width, _, z_at, _ = piece
            for side, (src, half_at) in enumerate(((o_sums.at[1], out.bit), (o_last, 1 - out.bit))):
                for part in range(2):
                    slot = 4 * n + 2 * side + part
                    copies.append(
                        pltpu.make_async_copy(
                            src.at[:, pl.ds(z_at + part * width, width)],
                            total_out.at[out.at(half_at, out.half), pl.ds(part * inner + start, width)],
                            keep_sems.at[slot],
                        )
                    )
        return copies

    keep_z = pltpu.make_async_copy(z_total, z_out, local.at[7])
    taken = (own_rows, pass_left, pass_right)

    def fetch(k):
        columns = pl.ds(k * 256, 256)
        return pltpu.make_async_copy(normed.at[:, columns], blocks.at[k % 2], block_sems.at[k % 2])

    @pl.when(i == 0)
    def _():
        barrier = pltpu.get_barrier_semaphore()
        for k in range(1, count):
            pl.semaphore_signal(barrier, inc=1, device_id=segments.peer(k)[1], device_id_type=MESH)
        for device in (out.partner, out.far, trade_far):
            pl.semaphore_signal(barrier, inc=1, device_id=device, device_id_type=MESH)

        @pl.when(jnp.logical_not(stays))
        def _():
            pl.semaphore_signal(barrier, inc=1, device_id=trade_near, device_id_type=MESH)

        pl.semaphore_wait(barrier, count + 2 + (z + core) % 2)
        out.start()
        for copy in taken:
            copy.start()
        start_trade()

    @pl.when(i == 3)
    def _():
        relay_trade()

    @pl.when(i < chunks)
    def _():
        place = at(i, CHUNK)
        pull_kernel(
            dno, gated, gate, y_pull, stats, gain, bcs, acum_pull,
            dy_all.at[place], dgate_all.at[place], own.at[pl.ds(i // PER_UNIT, 1)],
            pulled, chunk=i % PER_UNIT,
        )

    def state_copy(k, at_me):
        other, device = segments.peer(k)
        src, slot = (own.at[:, at(other, share)], me) if at_me else (own.at[:, at(me, share)], other)
        return pltpu.make_async_remote_copy(
            src_ref=src, dst_ref=parts.at[slot],
            send_sem=state_sends.at[k], recv_sem=state_receives.at[slot],
            device_id=device, device_id_type=MESH,
        )

    def back_copy(k, at_me):
        other, device = segments.peer(k)
        slot = me if at_me else other
        return pltpu.make_async_remote_copy(
            src_ref=results.at[other], dst_ref=after.at[:, at(slot, share)],
            send_sem=back_sends.at[k], recv_sem=back_receives.at[slot],
            device_id=device, device_id_type=MESH,
        )

    def multiply(k):
        if k < 5:
            fetch(k + 1).start()
        fetch(k).wait()

        turned[...] = blocks[k % 2].T

        def part(n, carry):
            columns = pl.ds(pl.multiple_of(n * 256, 256), 256)
            product = dot(turned[...], dgate_all[:, columns])
            g_z[pl.ds(k * 256, 256), columns] = product.astype(BF16)
            return carry

        lax.fori_loop(0, inner // 256, part, 0)

    def fetch_w(k):
        return pltpu.make_async_copy(w_gate.at[pl.ds(k * 256, 256)], w_blocks.at[k % 2], w_sems.at[k % 2])

    def put(k):
        return pltpu.make_async_copy(
            products.at[k % 2], d_base_out.at[:, pl.ds(k * 256, 256)], product_sems.at[k % 2]
        )

    def project(k):
        if k < 5:
            fetch_w(k + 1).start()
        fetch_w(k).wait()
        if k > 1:
            put(k - 2).wait()
        per = dgate_all.shape[0] // units

        def part(n, carry):
            there = pl.ds(pl.multiple_of(n * per, per), per)
            products[k % 2, there, :] = dot_nt(dgate_all[there, :], w_blocks[k % 2]).astype(BF16)
            return carry

        lax.fori_loop(0, units, part, 0)
        put(k).start()

    @pl.when(i == chunks)
    def _():
        for k in range(1, count):
            state_copy(k, True).start()
        fetch(0).start()
        fetch_w(0).start()
        settle_trade()
        parts[me] = own[:, at(me, share)]
        for k in range(6):
            multiply(k)
        for k in range(1, count):
            state_copy(k, False).wait_recv()
        running = [jnp.zeros((share, inner), F32) for _ in range(units)]
        for n in range(count - 1, -1, -1):
            for u in range(units):
                results[n, u] = running[u].astype(BF16)
                running[u] = running[u] * decays[n, u : u + 1] + parts[n, u].astype(F32)
        after[:, at(me, share)] = results[me]
        for k in range(1, count):
            back_copy(k, True).start()
        for k in range(6):
            project(k)
        put(4).wait()
        put(5).wait()
        for k in range(1, count):
            back_copy(k, False).wait_recv()
        for k in range(1, count):
            state_copy(k, True).wait_send()
            back_copy(k, True).wait_send()
        for copy in taken:
            copy.wait()
        for piece in out.pieces:
            out.after_first(piece)
        gz.start()

    def at_step(n, *stages):
        @pl.when(i == chunks + 1 + n)
        def _():
            for stage, reduction in stages:
                for piece in reduction.pieces:
                    stage(piece)

    @pl.when(i > chunks)
    def _():
        n = i - chunks - 1
        unit, chunk = n // PER_UNIT, n % PER_UNIT
        place = at(unit * PER_UNIT + PER_UNIT - 1 - chunk, CHUNK)
        backward_kernel(
            x, xp, bc, bcp, dt, halo, cx, cbc, hp, dy_all.at[place], y, st, incoming, acum,
            after.at[pl.ds(unit, 1)], pick, d_all, heads_x, heads_bc, g_x, g_bc, g_heads,
            xe, be, adjoint, dpx, dpb, ends, place=(unit, chunk),
        )

    at_step(2, (out.after_second, out))
    at_step(3, (out.after_pair, out), (out.start_members, out))
    at_step(5, (out.after_near, out))

    @pl.when(i == chunks + 1 + 6)
    def _():
        for piece in out.pieces:
            out.second_copy(piece).wait_send()
            out.pair_copy(piece).wait_send()
            gz.after_first(piece)

    at_step(8, (gz.after_second, gz))
    at_step(9, (out.after_far, out), (gz.after_pair, gz))

    @pl.when(i == 2 * chunks)
    def _():
        finish_trade()
        for piece in out.pieces:
            out.after_last(piece)
            for copy in out.first_copies(piece):
                copy.wait_send()
        out.drain_members()
        for copy in keep_out():
            copy.start()
        keep_z.start()
        gz.drain_chips()
        for copy in keep_out():
            copy.wait()
        keep_z.wait()


class Plan:
    def __init__(self, batch, tokens):
        self.shards, self.members = lax.axis_size("fs"), lax.axis_size("sp")
        self.f, self.z = lax.axis_index("fs"), lax.axis_index("sp")
        self.core = self.f % 2
        self.chips = self.shards // 2
        self.chip = self.f // 2
        self.batch, self.tokens = batch, tokens
        self.units = batch // 2
        self.joints = self.members // 2
        self.count = self.chips * self.joints
        self.group, self.joint = self.z // self.joints, self.z % self.joints
        self.fast = self.chips == 4 and self.members == 4

    def at(self, f, z):
        return f * self.members + z

    def send(self, x, pairs):
        return lax.ppermute(x, ("fs", "sp"), pairs)

    def swap(self, x, df=0, dz=0):
        pairs = [
            (self.at(f, z), self.at(f ^ df, z ^ dz))
            for f in range(self.shards)
            for z in range(self.members)
        ]
        return self.send(x, pairs)

    def along(self, x, by):
        pairs = []
        for f in range(self.shards):
            for z in range(self.members):
                place = (f // 2) * self.joints + z % self.joints + by
                if 0 <= place < self.count:
                    there = (place // self.joints) * 2 + f % 2
                    pairs.append(
                        (self.at(f, z), self.at(there, z - z % self.joints + place % self.joints))
                    )
        return self.send(x, pairs)

    def by_core(self, mine, other):
        first = self.core == 0
        return jnp.where(first, mine, other), jnp.where(first, other, mine)

    def head(self, hidden, w_x, w_bc, w_dt, conv_x, conv_bc, *vectors):
        anywhere, vmem = pl.BlockSpec(memory_space=pl.ANY), pl.BlockSpec(memory_space=pltpu.VMEM)
        conv_x_bias, gate_gain, norm_gain, conv_bc_bias, dt_bias, a_log, skip_d = (v[None] for v in vectors)
        rows, inner = w_x.shape[0], w_x.shape[1] // 2
        small = (SMALL_ROWS, conv_x.shape[0])
        dma = pltpu.SemaphoreType.DMA
        shape = jax.ShapeDtypeStruct
        units, first, *params = pl.pallas_call(
            head_kernel,
            out_shape=[
                shape((self.units, 4, self.tokens, hidden.shape[-1]), BF16),
                shape((4, 2, rows, inner + 3 * LANES), BF16),
                shape((8, inner), F32), shape((8, 2 * LANES), F32), shape((8, LANES), F32),
                shape((8, hidden.shape[-1]), F32), shape((8, inner), F32),
            ],
            in_specs=[anywhere] * 3 + [vmem] * 10,
            out_specs=[anywhere] * 2 + [vmem] * 5,
            scratch_shapes=[
                pltpu.VMEM((rows, LANES), BF16), pltpu.VMEM((rows, LANES), BF16),
                pltpu.VMEM(small, F32), pltpu.VMEM((self.shards,) + small, F32),
                pltpu.VMEM((self.units, self.tokens, hidden.shape[-1]), BF16),
                pltpu.VMEM((rows, inner), BF16), pltpu.VMEM((rows, 2 * LANES), BF16),
                dma((7,)), dma((11,)), dma((11,)), dma((self.shards,)), dma((self.shards,)),
            ],
            compiler_params=pltpu.CompilerParams(
                collective_id=2, has_side_effects=True, vmem_limit_bytes=VMEM_LIMIT
            ),
            cost_estimate=cost(55),
            name="head",
        )(
            hidden, w_x, w_bc, w_dt, conv_x, conv_x_bias, gate_gain, norm_gain, conv_bc, conv_bc_bias,
            dt_bias, a_log, skip_d,
        )
        return units.reshape(-1, hidden.shape[-1]), first.reshape(-1, inner + 3 * LANES), *params

    def slow_tail(self, g, g_x, g_bc, g_heads, g_gate, g_norm, d_normed):
        rows, inner = g.shape[0] // self.shards, g_x.shape[1]
        g = self.reduce_chips(g)
        low = self.core == 0
        kept, given = jnp.where(low, g[:rows], g[rows:]), jnp.where(low, g[rows:], g[:rows])
        came = self.swap(given.astype(BF16), df=1).astype(F32)
        total = self.reduce_members(
            jnp.concatenate(
                list(self.by_core(kept[:, :inner], came[:, :inner]))
                + [kept[:, inner : inner + 2 * LANES] + came[:, inner : inner + 2 * LANES]]
                + list(self.by_core(kept[:, inner + 2 * LANES :], came[:, inner + 2 * LANES :])),
                axis=1,
            )
        )
        wide = ((0, 0), (0, inner - 2 * LANES))
        heads = g_heads.reshape(3, 8, LANES).sum(axis=1).reshape(1, -1)
        vec = jnp.concatenate(
            [
                g_x.reshape(5, 8, inner).sum(axis=1), g_gate, g_norm,
                jnp.pad(heads, ((0, 0), (0, inner - 3 * LANES))),
                jnp.pad(g_bc.reshape(5, 8, 2 * LANES).sum(axis=1), wide),
            ]
        )
        vec = self.sum_all(jnp.pad(vec, ((0, 3), (0, 0))))
        vec = jnp.stack(self.by_core(vec, self.swap(vec, df=1)))
        cut = 2 * inner + 2 * LANES
        d_rows = self.to_tokens(self.cores_sum(d_normed))
        return total[:, : 2 * inner], total[:, 2 * inner : cut], total[:, cut:], vec, d_rows
    def tail(self, normed, d_all, d_base, w_first, unit_rows, g_x, g_bc, g_heads, g_gate, z_total):
        model, inner, width = normed.shape[1], g_x.shape[1], d_all.shape[1]
        rows, count = model // self.shards, normed.shape[0]
        wide, block = 2 * inner + 4 * LANES, 256
        steps = model // block
        vec = (16, inner)
        slots = 7 * (len(FIRST_PIECES) + len(HALF_PIECES)) + 4
        anywhere, dma, shape = pl.BlockSpec(memory_space=pl.ANY), pltpu.SemaphoreType.DMA, jax.ShapeDtypeStruct

        def whole(v):
            return pl.BlockSpec(v.shape, lambda i: (0,) * v.ndim, pipeline_mode=pl.Buffered(1))

        def early(i):
            return jnp.minimum(i, steps - 1)

        def late(i):
            return jnp.maximum(i - steps, 0)

        return pl.pallas_call(
            tail_kernel,
            grid=(2 * steps,),
            in_specs=[
                pl.BlockSpec((count, block), lambda i: (0, early(i))), whole(d_all),
                pl.BlockSpec((count, block), lambda i: (0, late(i))),
                pl.BlockSpec((block, width), lambda i: (late(i), 0)),
                pl.BlockSpec((count, block), lambda i: (0, late(i))),
                whole(g_x), whole(g_bc), whole(g_heads), whole(g_gate), whole(z_total),
            ],
            out_specs=[anywhere] * 3
            + [pl.BlockSpec((2,) + vec, lambda i: (0, 0, 0))]
            + [anywhere] * 2,
            out_shape=[
                shape((rows, 2 * inner), F32), shape((rows, 2 * LANES), F32), shape((rows, 2 * LANES), F32),
                shape((2,) + vec, F32), shape((self.batch, self.tokens, model), BF16),
                shape((rows, 2 * inner), F32),
            ],
            scratch_shapes=[
                pltpu.VMEM((block, count), BF16),
                pltpu.VMEM((model, width), BF16),
                pltpu.VMEM((self.units, 2, 2, self.tokens, model), BF16),
                pltpu.VMEM((self.units, 2, self.tokens, model), BF16),
                dma((5,)),
            ]
            + chip_scratch(rows, width)
            + [pltpu.VMEM((rows, wide), BF16)]
            + member_scratch(rows, wide)
            + member_scratch(rows, 2 * inner)
            + [
                pltpu.VMEM((rows, 2 * inner), F32), pltpu.VMEM((rows, 2 * LANES), F32),
                pltpu.VMEM((rows, 2 * LANES), F32), pltpu.VMEM((rows, 2 * inner), F32),
                pltpu.VMEM((4,) + vec, F32), pltpu.VMEM((4,) + vec, F32), pltpu.VMEM((2,) + vec, F32),
                dma((slots,)), dma((slots,)), dma((5,)), dma((5,)),
            ],
            compiler_params=pltpu.CompilerParams(
                dimension_semantics=("arbitrary",), collective_id=3, has_side_effects=True,
                vmem_limit_bytes=TAIL_LIMIT,
            ),
            cost_estimate=cost(130),
            name="tail",
        )(normed, d_all, d_base, w_first, unit_rows, g_x, g_bc, g_heads, g_gate, z_total)

    def gather(self, x):
        groups = [list(range(c, self.shards, 2)) for c in range(2)]
        return lax.all_gather(x, "fs", axis=0, tiled=True, axis_index_groups=groups)

    def reduce_chips(self, g):
        groups = [list(range(c, self.shards, 2)) for c in range(2)]
        return lax.psum_scatter(
            g, "fs", scatter_dimension=0, tiled=True, axis_index_groups=groups
        ).astype(F32)

    def reduce_members(self, g):
        return lax.psum(g.astype(BF16), "sp").astype(F32)

    def traded(self, x, far):
        pairs = [
            (self.at(f, z), self.at(f - f % 2 + z % 2, ((z // 2) ^ far) * 2 + f % 2))
            for f in range(self.shards)
            for z in range(self.members)
        ]
        return self.send(x, pairs)

    def to_units(self, rows):
        units, width = self.units, rows.shape[-1]
        if self.fast:
            low, high = rows[:units], rows[units:]
            upper = self.z // 2 == 1
            far = self.traded(jnp.where(upper, low, high), 1)
            near = self.traded(jnp.where(upper, high, low), 0)
            mine = jnp.stack([jnp.where(upper, far, near), jnp.where(upper, near, far)], axis=1)
            pair = self.by_core(mine, self.swap(mine, df=1))
            block = jnp.stack(pair, axis=2)
        else:
            other = self.swap(rows, df=1)
            everything = lax.all_gather(jnp.stack(self.by_core(rows, other)), "sp")
            per_core = self.joints // 2
            block = lax.dynamic_slice(
                everything,
                ((self.joint % per_core) * 4, self.joint // per_core, self.group * units, 0, 0),
                (4, 1, units) + rows.shape[1:],
            )[:, 0]
            block = jnp.moveaxis(block, 0, 1)
        return block.reshape(units * 4 * self.tokens, width)

    def cores_sum(self, partial):
        units, width = self.units, partial.shape[-1]
        if self.fast:
            block = partial.reshape(units, 2, 2, self.tokens, width)
            even = self.core == 0
            mine = jnp.where(even, block[:, :, 0], block[:, :, 1])
            given = jnp.where(even, block[:, :, 1], block[:, :, 0]).astype(BF16)
            return (mine.astype(F32) + self.swap(given, df=1).astype(F32)).astype(BF16)
        return partial.astype(BF16).reshape(units, 4, self.tokens, width)

    def to_tokens(self, total):
        units, width = self.units, total.shape[-1]
        if self.fast:
            upper = self.z // 2 == 1
            far = self.traded(jnp.where(upper, total[:, 0], total[:, 1]), 1)
            near = self.traded(jnp.where(upper, total[:, 1], total[:, 0]), 0)
            return jnp.concatenate(
                [jnp.where(upper, far, near), jnp.where(upper, near, far)], axis=0
            )
        per_core = self.joints // 2
        block = total
        wide = jnp.zeros((self.members, 2, self.batch, self.tokens, width), BF16)
        wide = lax.dynamic_update_slice(
            wide,
            jnp.moveaxis(block, 1, 0)[:, None],
            ((self.joint % per_core) * 4, self.joint // per_core, self.group * units, 0, 0),
        )
        summed = lax.psum_scatter(wide, "sp", scatter_dimension=0, tiled=False)
        first = self.core == 0
        mine, given = jnp.where(first, summed[0], summed[1]), jnp.where(first, summed[1], summed[0])
        return (mine.astype(F32) + self.swap(given, df=1).astype(F32)).astype(BF16)

    def sum_all(self, x):
        if not self.fast:
            groups = [list(range(c, self.shards, 2)) for c in range(2)]
            return lax.psum(lax.psum(x, "fs", axis_index_groups=groups), "sp")
        for df, dz in ((2, 0), (4, 0), (0, 1), (0, 2)):
            x = x + self.swap(x, df, dz)
        return x


def row_scale(values):
    return lax.rsqrt(jnp.mean(values * values, axis=-1, keepdims=True) + EPSILON)


def rows_spec(width, column=0, back=False):
    def place(u, c):
        return (u * PER_UNIT + (PER_UNIT - 1 - c if back else c), column)

    return pl.BlockSpec((CHUNK, width), place)


def chunk_spec(shape, back=False):
    def place(u, c):
        return (u * PER_UNIT + (PER_UNIT - 1 - c if back else c), 0, 0)

    return pl.BlockSpec((1,) + shape, place)


def unit_spec(shape):
    return pl.BlockSpec((1,) + shape, lambda u, c: (u, 0, 0))


def whole_spec(shape):
    return pl.BlockSpec(shape, lambda u, c: (0,) * len(shape))


def cost(microseconds):
    return pl.CostEstimate(flops=int(microseconds * 1.15e9), bytes_accessed=0, transcendentals=0)


def params():
    return pltpu.CompilerParams(
        dimension_semantics=("arbitrary", "arbitrary"), vmem_limit_bytes=VMEM_LIMIT
    )


def slow_exchange(plan, own, decays, back):
    count, units = plan.count, own.shape[0]
    rates, pieces = decays[:units, None], own.astype(F32)

    def hop(_, before):
        return plan.along((before * rates + pieces).astype(BF16), -1 if back else 1).astype(F32)

    return lax.fori_loop(0, count - 1, hop, jnp.zeros(own.shape, F32)).astype(BF16)


def exchange(plan, own, decays, cot, near, far, normed, w_gate, w_out, y0, bcs, acum):
    units, depth, width = own.shape
    count, share = plan.count, depth // plan.count
    dec_shape, rows, model = (count, 8, width), normed.shape[0], normed.shape[1]
    chunks = rows // CHUNK
    anywhere, dma, shape = pl.BlockSpec(memory_space=pl.ANY), pltpu.SemaphoreType.DMA, jax.ShapeDtypeStruct

    def whole(v):
        return pl.BlockSpec(v.shape, lambda i: (0,) * v.ndim, pipeline_mode=pl.Buffered(1))

    def chunk(columns):
        return pl.BlockSpec((CHUNK, columns), lambda i: (jnp.maximum(i - 1, 0), 0))

    all_decays, cot_rows, weight_out, gate, incoming, y, gated, squares = pl.pallas_call(
        states_kernel,
        grid=(chunks + 1,),
        in_specs=[whole(own), whole(decays)]
        + [anywhere] * 6
        + [chunk(width), chunk(2 * LANES), chunk(LANES)],
        out_specs=[pl.BlockSpec(dec_shape, lambda i: (0, 0, 0))]
        + [anywhere] * 4
        + [chunk(width), chunk(width), chunk(LANES)],
        out_shape=[
            shape(dec_shape, F32), shape((units, 4, plan.tokens, model), BF16),
            shape((4, 2, w_out.shape[0], width), BF16), shape((rows, width), BF16), shape(own.shape, BF16),
            shape((rows, width), BF16), shape((rows, width), BF16), shape((rows, LANES), F32),
        ],
        scratch_shapes=[
            pltpu.VMEM(own.shape, BF16), pltpu.VMEM((count, units, share, width), BF16),
            pltpu.VMEM(dec_shape, F32), pltpu.VMEM((count, units, share, width), BF16),
            pltpu.VMEM(w_gate.shape, BF16), pltpu.VMEM((rows, width), BF16), pltpu.VMEM((2, 256, model), BF16),
        ]
        + [dma((count,))] * 6
        + [dma((4,)), dma((4,)), dma((7,)), dma((7,)), dma((5,)), dma((2,)), dma((2,))]
        + [
            pltpu.VMEM((w_out.shape[0], width), BF16), pltpu.VMEM(near.shape, BF16),
            pltpu.VMEM(far.shape, BF16), dma((4,)),
        ],
        compiler_params=pltpu.CompilerParams(
            dimension_semantics=("arbitrary",), collective_id=0, has_side_effects=True,
            vmem_limit_bytes=VMEM_LIMIT,
        ),
        cost_estimate=cost(60),
        name="states",
    )(own, decays, cot, near, far, normed, w_gate, w_out, y0, bcs, acum)
    return (
        all_decays, cot_rows.reshape(rows, model), weight_out.reshape(model, width), gate, incoming,
        y, gated, squares,
    )


def body(
    hidden, norm_gain, w_z, w_x, w_bc, w_dt, w_out, conv_x, conv_x_bias, conv_bc, conv_bc_bias,
    dt_bias, a_log, skip_d, gate_gain, cotangent,
):
    batch, tokens, model = hidden.shape
    plan = Plan(batch, tokens)
    core = plan.core
    inner = w_z.shape[1] // 2
    heads = w_dt.shape[1] // 2
    head_size = inner // heads
    units = plan.units
    rows = units * 4 * tokens
    chunks = rows // CHUNK

    def halves(w):
        half = w.shape[1] // 2
        return jnp.where(core == 0, w[:, :half], w[:, half:]), jnp.where(core == 0, w[:, half:], w[:, :half])

    def rows_of_chip(mine, other):
        return jnp.concatenate(plan.by_core(mine, plan.swap(other, df=1)), axis=0)

    vectors = (conv_x_bias, gate_gain, norm_gain, conv_bc_bias, dt_bias, a_log, skip_d)
    if plan.fast:
        hidden_rows, weight_first, cx, cbc, hp, gain_in, gain_rows = plan.head(
            hidden, w_x, w_bc, w_dt, conv_x, conv_bc, *vectors
        )
        gain_in, gain_out = gain_in[0], gain_rows[0]
    else:
        x_mine, x_other = halves(w_x)
        dt_mine, dt_other = halves(w_dt)
        fill = jnp.zeros((w_dt.shape[0], LANES - heads), BF16)
        weight_first = plan.gather(
            rows_of_chip(
                jnp.concatenate([x_mine, w_bc, dt_mine, fill], axis=1),
                jnp.concatenate([x_other, w_bc, dt_other, fill], axis=1),
            )
        )
        hidden_rows, cot_rows = plan.to_units(hidden), plan.to_units(cotangent)

        def whole_of(v):
            return lax.all_gather(v.astype(F32), "fs", axis=0, tiled=True)

        def mine_of(v):
            half = v.shape[0] // 2
            return lax.dynamic_slice_in_dim(v, core * half, half, 0)

        bias_x, gain_out, gain_in, bias_bc, shift, rate_log, skip = (whole_of(v) for v in vectors)
        taps_x, taps_bc = mine_of(whole_of(conv_x)), whole_of(conv_bc)
        bias_x, gain_out, skip, shift, rate_log = (
            mine_of(v) for v in (bias_x, gain_out, skip, shift, rate_log)
        )
        nothing = jnp.zeros((2, inner), F32)
        cx = jnp.concatenate([taps_x.T, bias_x[None], jnp.repeat(skip, head_size)[None], nothing])
        cbc = jnp.concatenate([taps_bc.T, bias_bc[None], jnp.zeros((3, bias_bc.size), F32)])
        pad_heads = (0, LANES - heads)
        hp = jnp.stack([jnp.pad(jnp.exp(rate_log), pad_heads), jnp.pad(shift, pad_heads)])
        hp = jnp.pad(hp, ((0, 6), (0, 0)))
        gain_rows = jnp.broadcast_to(gain_out[None], (8, inner))
        weight_gate = plan.gather(rows_of_chip(*halves(w_z)))
        weight_out = plan.gather(rows_of_chip(*halves(w_out)))
    pick = (jnp.arange(inner)[:, None] // head_size == jnp.arange(LANES)[None, :]).astype(BF16)

    hidden_rows = hidden_rows.astype(F32)
    scale_in = row_scale(hidden_rows)
    unit_in = hidden_rows * scale_in
    normed = (unit_in * gain_in[None]).astype(BF16)
    unit_low = unit_in.astype(BF16)
    normed, unit_low = lax.optimization_barrier((normed, unit_low))

    first = dot(normed, weight_first).astype(BF16)
    def shaped(*shape, dtype=BF16):
        return jax.ShapeDtypeStruct(shape, dtype)

    states = (LANES, inner)
    edge = (units, 16, inner + 2 * LANES)
    in_specs = [
        rows_spec(inner), rows_spec(2 * LANES, inner // (2 * LANES)),
        rows_spec(LANES, (inner + 2 * LANES) // LANES),
    ]
    consts = [whole_spec(cx.shape), whole_spec(cbc.shape), whole_spec(hp.shape)]
    out_specs = [
        rows_spec(inner), chunk_spec(states), unit_spec(states), unit_spec((8, inner)),
        rows_spec(2 * LANES), rows_spec(LANES),
    ]
    out_shape = [
        shaped(rows, inner), shaped(chunks, *states), shaped(units, *states),
        shaped(units, 8, inner, dtype=F32), shaped(rows, 2 * LANES), shaped(rows, LANES, dtype=F32),
    ]
    scratch = [
        pltpu.VMEM((CHUNK + 8, inner), F32), pltpu.VMEM((CHUNK + 8, 2 * LANES), F32),
        pltpu.VMEM(states, F32), pltpu.VMEM((8, LANES), F32),
    ]
    by_unit = first.reshape(units, 4 * tokens, first.shape[1])
    if plan.fast:
        anywhere = pl.BlockSpec(memory_space=pl.ANY)
        dma = pltpu.SemaphoreType.DMA
        y_own, starts, own, decays, shared, reach, halo, near, far, weight_gate = pl.pallas_call(
            scan_forward_kernel,
            grid=(units, PER_UNIT),
            in_specs=in_specs + [anywhere, anywhere, anywhere] + consts,
            out_specs=out_specs + [whole_spec(edge), anywhere, anywhere, anywhere],
            out_shape=out_shape
            + [
                shaped(*edge), shaped(units, tokens, model), shaped(EARLY_UNITS, tokens, model),
                shaped(4, 2, w_z.shape[0], inner),
            ],
            scratch_shapes=scratch
            + [pltpu.VMEM(edge, BF16), dma((1,)), dma((1,)), dma((2,)), dma((2,)), dma((2,)), dma((7,)), dma((7,)), dma((2,))]
            + [pltpu.VMEM((w_z.shape[0], inner), BF16), pltpu.VMEM((units, tokens, model), BF16)],
            compiler_params=pltpu.CompilerParams(
                dimension_semantics=("arbitrary", "arbitrary"), vmem_limit_bytes=VMEM_LIMIT,
                collective_id=1, has_side_effects=True,
            ),
            cost_estimate=cost(31),
            name="scan_forward",
        )(first, first, first, by_unit, cotangent, w_z, cx, cbc, hp)
    else:
        halo = plan.along(by_unit[:, 4 * tokens - 16 :, : inner + 2 * LANES], 1)
        y_own, starts, own, decays, shared, reach = pl.pallas_call(
            forward_kernel,
            grid=(units, PER_UNIT),
            in_specs=in_specs + [whole_spec(edge)] + consts,
            out_specs=out_specs,
            out_shape=out_shape,
            scratch_shapes=scratch,
            compiler_params=params(),
            name="scan_forward",
        )(first, first, first, halo, cx, cbc, hp)

    decay_rows = jnp.concatenate([decays[:, 0], jnp.zeros((8 - units, inner), F32)])
    if plan.fast:
        weight_gate = weight_gate.reshape(model, inner)
        all_decays, cot_rows, weight_out, gate_in, incoming, y, gated, squares = exchange(
            plan, own, decay_rows, cotangent, near, far, normed, weight_gate, w_out, y_own, shared, reach
        )
    else:
        incoming = slow_exchange(plan, own, decay_rows, False)
        gate_in = dot(normed, weight_gate).astype(BF16)
        y, gated, squares = pl.pallas_call(
            gate_kernel,
            grid=(units, PER_UNIT),
            in_specs=[
                rows_spec(inner), rows_spec(inner), rows_spec(2 * LANES), rows_spec(LANES), unit_spec(states),
            ],
            out_specs=[rows_spec(inner), rows_spec(inner), rows_spec(LANES)],
            out_shape=[shaped(rows, inner), shaped(rows, inner), shaped(rows, LANES, dtype=F32)],
            compiler_params=params(),
            name="gate_forward",
        )(y_own, gate_in, shared, reach, incoming)

    def pair_sum(v):
        return v + plan.swap(v, df=1)

    squares = pair_sum(squares[:, 0].reshape(chunks, CHUNK))
    scale_out = lax.rsqrt(squares / (2 * inner) + EPSILON).reshape(rows, 1)
    unit_out = gated.astype(F32) * scale_out
    normed_out = (unit_out * gain_out[None]).astype(BF16)
    g_out = dot_tn(cot_rows, normed_out).astype(BF16)
    projected = plan.cores_sum(dot_nt(normed_out, weight_out).astype(BF16))

    d_normed_out = dot(cot_rows, weight_out).astype(BF16)
    wide = d_normed_out.astype(F32)
    g_gate_gain = jnp.sum(wide * unit_out, axis=0)
    mean = pair_sum(jnp.sum(wide * gain_out[None] * unit_out, axis=1).reshape(chunks, CHUNK))
    mean = (mean / (2 * inner)).reshape(rows, 1)
    stats = jnp.concatenate([scale_out, mean, jnp.zeros((rows, LANES - 2), F32)], axis=1)

    width = inner + 3 * LANES
    back = functools.partial(rows_spec, back=True)
    if plan.fast:
        spots = 2 * chunks + 1
        shard_rows = model // plan.shards
        segments = plan.count
        share = LANES // segments

        def pulls(columns, column=0):
            return pl.BlockSpec((CHUNK, columns), lambda i: (jnp.minimum(i, chunks - 1), column))

        def scan_at(i):
            n = jnp.maximum(i - chunks - 1, 0)
            return n - n % PER_UNIT + PER_UNIT - 1 - n % PER_UNIT

        def scans(columns, column=0):
            return pl.BlockSpec((CHUNK, columns), lambda i: (scan_at(i), column))

        def edges(columns, column=0):
            return pl.BlockSpec((16, columns), lambda i: (jnp.maximum(scan_at(i) * 8 - 1, 0), column))

        def scan_chunk(shape):
            return pl.BlockSpec((1,) + shape, lambda i: (scan_at(i), 0, 0))

        def scan_unit(shape):
            return pl.BlockSpec((1,) + shape, lambda i: (scan_at(i) // PER_UNIT, 0, 0))

        def every(shape):
            return pl.BlockSpec(shape, lambda i: (0,) * len(shape), pipeline_mode=pl.Buffered(1))

        def whole(shape):
            return pl.BlockSpec(shape, lambda i: (0,) * len(shape))

        anywhere = pl.BlockSpec(memory_space=pl.ANY)
        dma = pltpu.SemaphoreType.DMA
        d_all, heads_x, heads_bc, g_x, g_bc, g_heads, d_base, projected, total_out, total_z = pl.pallas_call(
            middle_kernel,
            grid=(spots,),
            in_specs=[
                pulls(inner), pulls(inner), pulls(inner), pulls(inner), pulls(LANES), every((8, inner)),
                pulls(2 * LANES), pulls(LANES), every(all_decays.shape), anywhere, anywhere, anywhere, anywhere,
                scans(inner), edges(inner),
                scans(2 * LANES, inner // (2 * LANES)), edges(2 * LANES, inner // (2 * LANES)),
                scans(LANES, (inner + 2 * LANES) // LANES), every(edge), every(cx.shape), every(cbc.shape), every(hp.shape),
                scans(inner), scan_chunk(states), scan_unit(states), scans(LANES), every(pick.shape),
            ],
            out_specs=[
                scans(width), scan_unit((8, inner)), scan_unit((8, 2 * LANES)),
                whole((40, inner)), whole((40, 2 * LANES)), whole((24, LANES)),
                anywhere, anywhere, anywhere, anywhere,
            ],
            out_shape=[
                shaped(rows, width), shaped(units, 8, inner, dtype=F32), shaped(units, 8, 2 * LANES, dtype=F32),
                shaped(40, inner, dtype=F32), shaped(40, 2 * LANES, dtype=F32), shaped(24, LANES, dtype=F32),
                shaped(rows, model), shaped(batch, tokens, model),
                shaped(shard_rows, 2 * inner), shaped(shard_rows, 2 * inner),
            ],
            scratch_shapes=[
                pltpu.VMEM((rows, inner), BF16), pltpu.VMEM((rows, inner), BF16), pltpu.VMEM(states, F32),
                pltpu.VMEM((units,) + states, BF16), pltpu.VMEM((units,) + states, BF16),
                pltpu.VMEM((segments, units, share, inner), BF16),
                pltpu.VMEM((segments, units, share, inner), BF16),
                pltpu.VMEM((2, rows, 256), BF16), pltpu.VMEM((256, rows), BF16),
                pltpu.VMEM((2, 256, inner), BF16), pltpu.VMEM((2, rows, 256), BF16),
                pltpu.VMEM((model, inner), BF16),
                pltpu.VMEM((model // 4, inner), BF16),
            ]
            + chip_scratch(shard_rows, inner)
            + [pltpu.VMEM((shard_rows, 2 * inner), BF16)]
            + member_scratch(shard_rows, 2 * inner)
            + [
                pltpu.VMEM((2, 2 * shard_rows, inner), BF16), pltpu.VMEM((2 * shard_rows, inner), BF16),
                pltpu.VMEM((shard_rows, inner), BF16), pltpu.VMEM((shard_rows, 2 * inner), BF16),
            ]
            + [
                pltpu.VMEM((CHUNK + 8, inner), F32), pltpu.VMEM((CHUNK + 8, 2 * LANES), F32),
                pltpu.VMEM(states, F32),
                pltpu.VMEM((CHUNK + 8, inner), F32), pltpu.VMEM((CHUNK + 8, 2 * LANES), F32),
                pltpu.VMEM((8, inner), F32),
                dma((8,)), dma((8,)), dma((2,)), dma((2,)), dma((2,)), dma((6,)), dma((2,)), dma((2,)),
                dma((14 * len(HALF_PIECES),)), dma((14 * len(HALF_PIECES),)),
                dma((segments,)), dma((segments,)), dma((segments,)), dma((segments,)),
            ],
            compiler_params=pltpu.CompilerParams(
                dimension_semantics=("arbitrary",), vmem_limit_bytes=MIDDLE_LIMIT,
                collective_id=4, has_side_effects=True,
            ),
            cost_estimate=cost(125),
            name="middle",
        )(
            d_normed_out, gated, gate_in, y, stats, gain_rows, shared, reach, all_decays, normed, weight_gate, g_out,
            projected, first, first, first, first, first, halo, cx, cbc, hp, y, starts, incoming,
            reach, pick,
        )
    else:

        def edges(columns, column=0):
            def place(u, c):
                return (jnp.maximum((u * PER_UNIT + PER_UNIT - 1 - c) * 8 - 1, 0), column)

            return pl.BlockSpec((16, columns), place)

        dy, d_gate, pull = pl.pallas_call(
            pull_kernel,
            grid=(units, PER_UNIT),
            in_specs=[
                rows_spec(inner), rows_spec(inner), rows_spec(inner), rows_spec(inner), rows_spec(LANES),
                whole_spec((8, inner)), rows_spec(2 * LANES), rows_spec(LANES),
            ],
            out_specs=[rows_spec(inner), rows_spec(inner), unit_spec(states)],
            out_shape=[shaped(rows, inner), shaped(rows, inner), shaped(units, *states)],
            scratch_shapes=[pltpu.VMEM(states, F32)],
            compiler_params=params(),
            name="gate_backward",
        )(d_normed_out, gated, gate_in, y, stats, gain_rows, shared, reach)
        after = slow_exchange(plan, pull, decay_rows, True)
        d_all, heads_x, heads_bc, g_x, g_bc, g_heads = pl.pallas_call(
            backward_kernel,
            grid=(units, PER_UNIT),
            in_specs=[
                back(inner), edges(inner),
                back(2 * LANES, inner // (2 * LANES)), edges(2 * LANES, inner // (2 * LANES)),
                back(LANES, (inner + 2 * LANES) // LANES), whole_spec(edge), whole_spec(cx.shape), whole_spec(cbc.shape), whole_spec(hp.shape),
                back(inner), back(inner), chunk_spec(states, True), unit_spec(states), back(LANES),
                unit_spec(states), whole_spec(pick.shape),
            ],
            out_specs=[
                back(width), unit_spec((8, inner)), unit_spec((8, 2 * LANES)),
                whole_spec((40, inner)), whole_spec((40, 2 * LANES)), whole_spec((24, LANES)),
            ],
            out_shape=[
                shaped(rows, width), shaped(units, 8, inner, dtype=F32), shaped(units, 8, 2 * LANES, dtype=F32),
                shaped(40, inner, dtype=F32), shaped(40, 2 * LANES, dtype=F32), shaped(24, LANES, dtype=F32),
            ],
            scratch_shapes=[
                pltpu.VMEM((CHUNK + 8, inner), F32), pltpu.VMEM((CHUNK + 8, 2 * LANES), F32),
                pltpu.VMEM(states, F32),
                pltpu.VMEM((CHUNK + 8, inner), F32), pltpu.VMEM((CHUNK + 8, 2 * LANES), F32),
                pltpu.VMEM((8, inner), F32),
            ],
            compiler_params=params(),
            name="scan_backward",
        )(
            first, first, first, first, first, halo, cx, cbc, hp,
            dy, y, starts, incoming, reach, after, pick,
        )
        projected = plan.to_tokens(projected)

        def over_everything(g):
            g = plan.reduce_chips(g)
            half = g.shape[0] // 2
            low = core == 0
            mine, other = jnp.where(low, g[:half], g[half:]), jnp.where(low, g[half:], g[:half])
            other = plan.swap(other.astype(BF16), df=1).astype(F32)
            return plan.reduce_members(jnp.concatenate(plan.by_core(mine, other), axis=1))

        total_out = over_everything(g_out)
        total_z = over_everything(dot_tn(normed, d_gate).astype(BF16))
    output = (hidden.astype(F32) + projected.astype(F32)).astype(BF16)

    later = plan.along(jnp.concatenate([heads_x, heads_bc], axis=2)[:, :3].astype(BF16), -1).astype(F32)
    taps = jnp.concatenate([cx[:4], cbc[:4]], axis=1)
    extra = jnp.stack(
        [sum(taps[k][None] * later[:, i - k] for k in range(i + 1)) for i in range(3)], axis=1
    )
    tail_rows = d_all.reshape(units, 4 * tokens, width)[:, 4 * tokens - 16 :].astype(F32)
    extra = jnp.pad(extra, ((0, 0), (13, 0), (0, width - extra.shape[2])))
    d_all = d_all.reshape(units, 4 * tokens, width)
    d_all = lax.dynamic_update_slice(d_all, (tail_rows + extra).astype(BF16), (0, 4 * tokens - 16, 0))
    d_all = d_all.reshape(rows, width)

    if plan.fast:
        total_x, total_bc, total_dt, vec, grad_rows, total_z = plan.tail(
            normed, d_all, d_base, weight_first, unit_low, g_x, g_bc, g_heads, g_gate_gain[None], total_z
        )
    else:
        g_first = dot_tn(normed, d_all).astype(BF16)
        d_normed = dot_nt(d_gate, weight_gate) + dot_nt(d_all, weight_first)
        g_norm_gain = jnp.sum(d_normed * unit_in, axis=0)
        total_x, total_bc, total_dt, vec, grad_rows = plan.slow_tail(
            g_first, g_x, g_bc, g_heads, g_gate_gain[None], g_norm_gain[None], d_normed.astype(BF16)
        )
    grad_rows = grad_rows.astype(F32)
    resid = hidden.astype(F32)
    own_scale = row_scale(resid)
    own_unit = resid * own_scale
    dv = grad_rows * gain_in[None, None]
    grad_hidden = cotangent.astype(F32) + own_scale * (
        dv - own_unit * jnp.mean(dv * own_unit, axis=-1, keepdims=True)
    )

    total_dt = jnp.concatenate([total_dt[:, :heads], total_dt[:, LANES : LANES + heads]], axis=1)
    whole_x = jnp.moveaxis(vec[:, :6], 0, 1).reshape(6, 2 * inner)
    whole_heads = jnp.moveaxis(vec[:, 7, : 3 * LANES].reshape(2, 3, LANES)[:, :, :heads], 0, 1)
    whole_heads = whole_heads.reshape(3, 2 * heads)
    whole_norm = vec[0, 6] + vec[1, 6]
    whole_bc = vec[0, 8:13, : 2 * LANES] + vec[1, 8:13, : 2 * LANES]

    def shard(v):
        share = v.shape[-1] // plan.shards
        return lax.dynamic_slice_in_dim(v, plan.f * share, share, v.ndim - 1)

    shard_x, shard_bc, shard_heads = shard(whole_x), shard(whole_bc), shard(whole_heads)
    return (
        output,
        grad_hidden,
        shard(whole_norm),
        total_z.astype(F32),
        total_x,
        total_bc,
        total_dt,
        total_out.astype(F32),
        shard_x[:4].T,
        shard_x[4],
        shard_bc[:4].T,
        shard_bc[4],
        shard_heads[0],
        shard_heads[1],
        shard_heads[2],
        shard_x[5],
    )


def solution(mesh):
    one, two = P("fs"), P("fs", None)
    tokens = P(None, ("fs", "sp"), None)
    return jax.shard_map(
        body,
        mesh=mesh,
        in_specs=(tokens, one, two, two, two, two, two, two, one, two, one, one, one, one, one, tokens),
        out_specs=(tokens, tokens, one, two, two, two, two, two, two, one, two, one, one, one, one, one),
        check_vma=False,
    )
```

```python
import functools

import jax
import jax.numpy as jnp
from jax import lax
from jax.experimental import pallas as pl
from jax.experimental.pallas import tpu as pltpu
from jax.sharding import PartitionSpec as P

EPSILON = 1e-05
F32, BF16 = jnp.float32, jnp.bfloat16
MESH = pl.DeviceIdType.MESH
CHUNK = 128
LANES = 128
PER_UNIT = 4
VMEM_LIMIT = 56 * 1024 * 1024
TAIL_LIMIT = 56 * 1024 * 1024
MIDDLE_LIMIT = 58 * 1024 * 1024


def dot(a, b):
    return jnp.dot(a, b, preferred_element_type=F32)


def dot_nt(a, b):
    return lax.dot_general(a, b, (((1,), (1,)), ((), ())), preferred_element_type=F32)


def dot_tn(a, b):
    return lax.dot_general(a, b, (((0,), (0,)), ((), ())), preferred_element_type=F32)


def pieces_of(v):
    high = v.astype(BF16)
    rest = v - high.astype(F32)
    middle = rest.astype(BF16)
    return high, middle, (rest - middle.astype(F32)).astype(BF16)


def exact_left(ones, v):
    return sum(dot(ones, part) for part in pieces_of(v))


def exact_right(v, ones):
    return sum(dot(part, ones) for part in pieces_of(v))


def sigmoid(v):
    return 0.5 * jnp.tanh(0.5 * v) + 0.5


def grid_iotas():
    rows = lax.broadcasted_iota(jnp.int32, (CHUNK, CHUNK), 0)
    columns = lax.broadcasted_iota(jnp.int32, (CHUNK, CHUNK), 1)
    return rows, columns


def two_heads(v, pair, low):
    return jnp.where(low, v[:, 2 * pair : 2 * pair + 1], v[:, 2 * pair + 1 : 2 * pair + 2])


def conv_of(ext, lanes, taps):
    total = taps[4:5, lanes]
    for k in range(4):
        total = total + ext[5 + k : 5 + k + CHUNK, lanes] * taps[k : k + 1, lanes]
    return total


def step_of(dt_ref, hp_ref):
    shifted = dt_ref[...].astype(F32) + hp_ref[1:2]
    return shifted, jnp.maximum(shifted, 0.0) + jnp.log1p(jnp.exp(-jnp.abs(shifted)))


def forward_kernel(
    x_ref, bc_ref, dt_ref, halo_ref, cx_ref, cbc_ref, hp_ref,
    y_ref, st_ref, own_ref, dec_ref, bcs_ref, acum_ref,
    xe, be, state, base,
):
    unit, chunk = pl.program_id(0), pl.program_id(1)
    inner = x_ref.shape[1]

    @pl.when(chunk == 0)
    def _():
        state[...] = jnp.zeros_like(state)
        base[...] = jnp.zeros_like(base)
        xe[0:8] = halo_ref[unit, :, :inner].astype(F32)[8:]
        be[0:8] = halo_ref[unit, :, inner:].astype(F32)[8:]

    @pl.when(chunk != 0)
    def _():
        xe[0:8] = xe[CHUNK:]
        be[0:8] = be[CHUNK:]

    xe[8:] = x_ref[...].astype(F32)
    be[8:] = bc_ref[...].astype(F32)
    shared = []
    for k in range(2):
        pre = conv_of(be, slice(k * LANES, (k + 1) * LANES), cbc_ref)
        shared.append(pre * sigmoid(pre))
    keys, reads = shared
    bcs_ref[:, :LANES] = keys.astype(BF16)
    bcs_ref[:, LANES:] = reads.astype(BF16)
    keys_t = keys.T.astype(BF16)
    keys, reads = keys.astype(BF16), reads.astype(BF16)
    rows, columns = grid_iotas()
    causal = rows >= columns
    _, step = step_of(dt_ref, hp_ref)
    running = exact_left(jnp.where(causal, 1.0, 0.0).astype(BF16), -step * hp_ref[0:1])
    acum_ref[...] = base[0:1] + running
    total = running[CHUNK - 1 : CHUNK]
    base[...] = base[...] + total
    running_t = running.T
    scores = jnp.where(causal, dot_nt(reads, keys), 0.0)
    low = columns < LANES // 2
    low_row = low[0:1]

    for pair in range(inner // LANES):
        lanes = slice(pair * LANES, (pair + 1) * LANES)
        pre = conv_of(xe, lanes, cx_ref)
        xs = pre * sigmoid(pre)
        weighted = xs * two_heads(step, pair, low)
        first = jnp.broadcast_to(running[:, 2 * pair : 2 * pair + 1], (CHUNK, CHUNK))
        second = jnp.broadcast_to(running[:, 2 * pair + 1 : 2 * pair + 2], (CHUNK, CHUNK))
        mix = jnp.concatenate(
            [
                (jnp.exp(jnp.minimum(first - running_t[2 * pair : 2 * pair + 1], 0.0)) * scores).astype(BF16),
                (jnp.exp(jnp.minimum(second - running_t[2 * pair + 1 : 2 * pair + 2], 0.0)) * scores).astype(BF16),
            ],
            axis=1,
        )
        own = weighted.astype(BF16)
        zero = jnp.zeros_like(own)
        stacked = jnp.concatenate([jnp.where(low, own, zero), jnp.where(low, zero, own)], axis=0)
        at = jnp.where(low, first, second)
        at_end = two_heads(total, pair, low_row)
        before = state[:, lanes]
        before_low = before.astype(BF16)
        st_ref[0, :, lanes] = before_low
        y = dot(mix, stacked) + dot(reads, before_low) * jnp.exp(at) + cx_ref[5:6, lanes] * xs
        y_ref[:, lanes] = y.astype(BF16)
        late = (weighted * jnp.exp(at_end - at)).astype(BF16)
        state[:, lanes] = before * jnp.exp(at_end) + dot(keys_t, late)

    @pl.when(chunk == PER_UNIT - 1)
    def _():
        own_ref[0] = state[...].astype(BF16)
        for pair in range(inner // LANES):
            lanes = slice(pair * LANES, (pair + 1) * LANES)
            dec_ref[0, :, lanes] = jnp.broadcast_to(
                jnp.exp(two_heads(base[0:1], pair, low_row)), (8, LANES)
            )


def gate_kernel(y0_ref, gate_ref, bcs_ref, acum_ref, in_ref, y_ref, gated_ref, ss_ref):
    _, columns = grid_iotas()
    low = columns < LANES // 2
    reads = bcs_ref[:, LANES:]
    reach = acum_ref[...]
    squares = jnp.zeros((CHUNK, LANES), F32)
    for pair in range(y0_ref.shape[1] // LANES):
        lanes = slice(pair * LANES, (pair + 1) * LANES)
        y = y0_ref[:, lanes].astype(F32) + dot(reads, in_ref[0, :, lanes]) * jnp.exp(
            two_heads(reach, pair, low)
        )
        y_ref[:, lanes] = y.astype(BF16)
        gate = gate_ref[:, lanes].astype(F32)
        gated = (y * gate * sigmoid(gate)).astype(BF16)
        gated_ref[:, lanes] = gated
        wide = gated.astype(F32)
        squares = squares + wide * wide
    ss_ref[...] = jnp.broadcast_to(jnp.sum(squares, axis=1, keepdims=True), (CHUNK, LANES))


def pull_kernel(
    dno_ref, gated_ref, gate_ref, y_ref, stats_ref, gain_ref, bcs_ref, acum_ref,
    dy_ref, dgate_ref, pull_ref,
    total, chunk=None,
):
    chunk = pl.program_id(1) if chunk is None else chunk

    @pl.when(chunk == 0)
    def _():
        total[...] = jnp.zeros_like(total)

    _, columns = grid_iotas()
    low = columns < LANES // 2
    scale = jnp.broadcast_to(stats_ref[:, 0:1], (CHUNK, LANES))
    mean = jnp.broadcast_to(stats_ref[:, 1:2], (CHUNK, LANES))
    reads_t = bcs_ref[:, LANES:].astype(F32).T.astype(BF16)
    reach = acum_ref[...]
    for pair in range(dno_ref.shape[1] // LANES):
        lanes = slice(pair * LANES, (pair + 1) * LANES)
        unit = gated_ref[:, lanes].astype(F32) * scale
        du = dno_ref[:, lanes].astype(F32) * gain_ref[0:1, lanes]
        d_gated = (scale * (du - unit * mean)).astype(BF16).astype(F32)
        gate = gate_ref[:, lanes].astype(F32)
        sg = sigmoid(gate)
        silu = gate * sg
        dy = d_gated * silu
        dy_ref[:, lanes] = dy.astype(BF16)
        dgate = d_gated * y_ref[:, lanes].astype(F32) * (sg + silu * (1.0 - sg))
        dgate_ref[:, lanes] = dgate.astype(BF16)
        total[:, lanes] += dot(reads_t, (dy * jnp.exp(two_heads(reach, pair, low))).astype(BF16))

    @pl.when(chunk == PER_UNIT - 1)
    def _():
        pull_ref[0] = total[...].astype(BF16)


def backward_kernel(
    x_ref, xp_ref, bc_ref, bcp_ref, dt_ref, halo_ref, cx_ref, cbc_ref, hp_ref,
    dy_ref, y_ref, st_ref, in_ref, acum_ref, after_ref, pick_ref,
    dall_ref, head_ref, head_bc_ref, gx_ref, gbc_ref, gh_ref,
    xe, be, adjoint, dpx, dpb, ends, place=None,
):
    unit, chunk = (pl.program_id(0), pl.program_id(1)) if place is None else place
    inner = x_ref.shape[1]

    @pl.when((unit == 0) & (chunk == 0))
    def _():
        gx_ref[...] = jnp.zeros_like(gx_ref)
        gbc_ref[...] = jnp.zeros_like(gbc_ref)
        gh_ref[...] = jnp.zeros_like(gh_ref)

    @pl.when(chunk == 0)
    def _():
        adjoint[...] = after_ref[0].astype(F32)
        dpx[CHUNK:] = jnp.zeros((8, inner), F32)
        dpb[CHUNK:] = jnp.zeros((8, 2 * LANES), F32)

    inside = chunk != PER_UNIT - 1
    xe[0:8] = jnp.where(inside, xp_ref[...].astype(F32)[8:], halo_ref[unit, :, :inner].astype(F32)[8:])
    xe[8:] = x_ref[...].astype(F32)
    be[0:8] = jnp.where(inside, bcp_ref[...].astype(F32)[8:], halo_ref[unit, :, inner:].astype(F32)[8:])
    be[8:] = bc_ref[...].astype(F32)
    shared, slopes = [], []
    for k in range(2):
        pre = conv_of(be, slice(k * LANES, (k + 1) * LANES), cbc_ref)
        sg = sigmoid(pre)
        shared.append(pre * sg)
        slopes.append(sg + pre * sg * (1.0 - sg))
    keys, reads = shared
    reads_t = reads.T.astype(BF16)
    keys, reads = keys.astype(BF16), reads.astype(BF16)
    rows, columns = grid_iotas()
    causal = rows >= columns
    shifted_dt, step = step_of(dt_ref, hp_ref)
    rate = hp_ref[0:1]
    log_decay = -step * rate
    running = exact_left(jnp.where(causal, 1.0, 0.0).astype(BF16), log_decay)
    total = running[CHUNK - 1 : CHUNK]
    base = acum_ref[0:1] - running[0:1]
    running_t = running.T
    scores_t = jnp.where(rows <= columns, dot_nt(keys, reads), 0.0)
    low = columns < LANES // 2
    low_row = low[0:1]
    d_scores = jnp.zeros((CHUNK, CHUNK), F32)
    d_reads = jnp.zeros((CHUNK, LANES), F32)
    d_keys = jnp.zeros((CHUNK, LANES), F32)
    sums = jnp.zeros((3 * CHUNK, LANES), F32)

    for pair in range(inner // LANES):
        lanes = slice(pair * LANES, (pair + 1) * LANES)
        shifted = [xe[5 + k : 5 + k + CHUNK, lanes] for k in range(4)]
        pre = cx_ref[4:5, lanes] + sum(shifted[k] * cx_ref[k : k + 1, lanes] for k in range(4))
        sg = sigmoid(pre)
        xs = pre * sg
        slope = sg + xs * (1.0 - sg)
        step_wide = two_heads(step, pair, low)
        weighted = xs * step_wide
        first = jnp.broadcast_to(running[:, 2 * pair : 2 * pair + 1], (CHUNK, CHUNK))
        second = jnp.broadcast_to(running[:, 2 * pair + 1 : 2 * pair + 2], (CHUNK, CHUNK))
        gap0 = first - running_t[2 * pair : 2 * pair + 1]
        gap1 = second - running_t[2 * pair + 1 : 2 * pair + 2]
        mix_t = jnp.concatenate(
            [
                (jnp.exp(jnp.minimum(-gap0, 0.0)) * scores_t).astype(BF16),
                (jnp.exp(jnp.minimum(-gap1, 0.0)) * scores_t).astype(BF16),
            ],
            axis=1,
        )
        dy_low = dy_ref[:, lanes]
        dy = dy_low.astype(F32)
        zero = jnp.zeros_like(dy_low)
        dy_two = jnp.concatenate([jnp.where(low, dy_low, zero), jnp.where(low, zero, dy_low)], axis=0)
        d_mix = dot_nt(dy_two, weighted.astype(BF16))
        d_scores = d_scores + (
            jnp.exp(jnp.minimum(gap0, 0.0)) * d_mix[:CHUNK]
            + jnp.exp(jnp.minimum(gap1, 0.0)) * d_mix[CHUNK:]
        )
        at = jnp.where(low, first, second)
        at_end = two_heads(total, pair, low_row)
        tail = jnp.exp(at_end - at)
        end_decay = jnp.exp(at_end)
        later = adjoint[:, lanes]
        later_low = later.astype(BF16)
        from_state = dot(keys, later_low) * tail
        d_weighted = dot(mix_t, dy_two) + from_state
        before = st_ref[0, :, lanes].astype(F32) + in_ref[0, :, lanes].astype(F32) * jnp.exp(
            two_heads(base, pair, low_row)
        )
        d_read = (dy * jnp.exp(at)).astype(BF16)
        d_reads = d_reads + dot_nt(d_read, before.astype(BF16))
        d_keys = d_keys + dot_nt((weighted * tail).astype(BF16), later_low)
        skip = cx_ref[5:6, lanes]
        y = y_ref[:, lanes].astype(F32) - skip * xs
        d_run = dy * y - weighted * d_weighted
        pick = pick_ref[lanes, :]
        sums = sums + dot(
            jnp.concatenate(
                [d_run.astype(BF16), (xs * d_weighted).astype(BF16), (dy * xs).astype(BF16)], axis=0
            ),
            pick,
        )
        ends[:, lanes] = jnp.broadcast_to(
            jnp.sum(weighted * from_state, axis=0, keepdims=True)
            + end_decay * jnp.sum(later * before, axis=0, keepdims=True),
            (8, LANES),
        )
        d_pre = (step_wide * d_weighted + skip * dy) * slope
        dpx[0:CHUNK, lanes] = d_pre
        adjoint[:, lanes] = later * end_decay + dot(reads_t, d_read)
        d_x = jnp.zeros((CHUNK, LANES), F32)
        for k in range(4):
            d_x = d_x + dpx[3 - k : 3 - k + CHUNK, lanes] * cx_ref[k : k + 1, lanes]
            gx_ref[8 * k : 8 * k + 8, lanes] += jnp.sum(
                (d_pre * shifted[k]).reshape(CHUNK // 8, 8, LANES), axis=0
            )
        gx_ref[32:40, lanes] += jnp.sum(d_pre.reshape(CHUNK // 8, 8, LANES), axis=0)
        dall_ref[:, lanes] = d_x.astype(BF16)

    d_scores_low = jnp.where(causal, d_scores, 0.0)
    d_reads = d_reads + dot(d_scores_low.astype(BF16), keys)
    d_keys = d_keys + dot(d_scores_low.T.astype(BF16), reads)
    for k, part in enumerate((d_keys, d_reads)):
        lanes = slice(k * LANES, (k + 1) * LANES)
        d_pre = part * slopes[k]
        dpb[0:CHUNK, lanes] = d_pre
        d_x = jnp.zeros((CHUNK, LANES), F32)
        for tap in range(4):
            d_x = d_x + dpb[3 - tap : 3 - tap + CHUNK, lanes] * cbc_ref[tap : tap + 1, lanes]
            gbc_ref[8 * tap : 8 * tap + 8, lanes] += jnp.sum(
                (d_pre * be[5 + tap : 5 + tap + CHUNK, lanes]).reshape(CHUNK // 8, 8, LANES), axis=0
            )
        gbc_ref[32:40, lanes] += jnp.sum(d_pre.reshape(CHUNK // 8, 8, LANES), axis=0)
        dall_ref[:, inner + k * LANES : inner + (k + 1) * LANES] = d_x.astype(BF16)

    at_end = exact_right(ends[...], pick_ref[...])[0:1]
    d_log = exact_left(jnp.where(rows <= columns, 1.0, 0.0).astype(BF16), sums[:CHUNK]) + at_end
    d_step = sums[CHUNK : 2 * CHUNK] - d_log * rate
    d_dt = d_step * sigmoid(shifted_dt)
    dall_ref[:, inner + 2 * LANES :] = d_dt.astype(BF16)
    for k, part in enumerate((d_dt, d_log * log_decay, sums[2 * CHUNK :])):
        gh_ref[8 * k : 8 * k + 8] += jnp.sum(part.reshape(CHUNK // 8, 8, LANES), axis=0)
    dpx[CHUNK:] = dpx[0:8]
    dpb[CHUNK:] = dpb[0:8]

    @pl.when(chunk == PER_UNIT - 1)
    def _():
        head_ref[0] = dpx[0:8]
        head_bc_ref[0] = dpb[0:8]


def places():
    f, z = lax.axis_index("fs"), lax.axis_index("sp")
    core, chip = f % 2, f // 2
    by_x, by_y = chip + 1 - 2 * (chip % 2), (chip + 2) % 4
    return f, z, core, chip, by_x, by_y


def remote(src, dst, sends, receives, slot, device):
    return pltpu.make_async_remote_copy(
        src_ref=src, dst_ref=dst, send_sem=sends.at[slot], recv_sem=receives.at[slot],
        device_id=device, device_id_type=MESH,
    )


class Bounce:
    def __init__(self, src, buffer, dst, sems, n):
        self.into = pltpu.make_async_copy(src, buffer, sems.at[2 * n])
        self.out = pltpu.make_async_copy(buffer, dst, sems.at[2 * n + 1])

    def start(self):
        self.into.start()

    def relay(self):
        self.into.wait()
        self.out.start()

    def wait(self):
        self.out.wait()


class Trade:
    def __init__(self, source, sends, receives):
        self.f, self.z, self.core, self.chip, _, _ = places()
        self.source, self.sends, self.receives = source, sends, receives
        self.units = source.shape[0] // 2
        self.near_group, self.far_group = self.z // 2, 1 - self.z // 2
        across = 2 * self.chip + self.z % 2
        self.near, self.far = (across, 2 * self.near_group + self.core), (across, 2 * self.far_group + self.core)
        self.near_at, self.far_at = 2 * self.near_group + self.core, 2 * self.far_group + self.core
        self.partner = (self.f + 1 - 2 * self.core, self.z)
        self.stays = self.z % 2 == self.core
        self.moves = (self.z + self.core) % 2

    def rows_for(self, group, first, last):
        return self.source.at[pl.ds(group * self.units + first, last - first)]

    def swapped(self, at):
        return at + 1 - 2 * (at % 2)

    def send(self, src, dst, slot, device):
        return remote(src, dst, self.sends, self.receives, slot, device)


class Gather:
    def __init__(self, weight, target, sends, receives, local, buffer):
        f, z, self.core, self.chip, self.by_x, self.by_y = places()
        self.weight, self.target, self.sends, self.receives = weight, target, sends, receives
        self.partner = (f + 1 - 2 * self.core, z)
        self.over_x, self.over_y = (2 * self.by_x + self.core, z), (2 * self.by_y + self.core, z)
        self.keep = Bounce(self.columns(self.core), buffer, self.part(self.chip, self.core), local, 0)

    def columns(self, side):
        width = self.weight.shape[1] // 2
        return self.weight.at[:, pl.ds(pl.multiple_of(side * width, width), width)]

    def part(self, chip, core):
        return self.target.at[chip, core]

    def copy(self, src, dst, slot, device):
        return remote(src, dst, self.sends, self.receives, slot, device)

    def sent(self, slot):
        own, other = (self.chip, self.core), (self.chip, 1 - self.core)
        src, dst, device = (
            (self.columns(1 - self.core), own, self.partner),
            (self.columns(self.core), own, self.over_x),
            (self.columns(self.core), own, self.over_y),
            (self.part(*other), other, self.over_x),
            (self.part(*other), other, self.over_y),
            (self.part(self.by_x, self.core), (self.by_x, self.core), self.over_y),
            (self.part(self.by_y, 1 - self.core), (self.by_y, 1 - self.core), self.over_x),
        )[slot]
        return self.copy(src, self.part(*dst), slot, device)

    def arrives(self, slot):
        corner = (self.by_x + 2) % 4
        chip, core = (
            (self.chip, 1 - self.core), (self.by_x, self.core), (self.by_y, self.core),
            (self.by_x, 1 - self.core), (self.by_y, 1 - self.core), (corner, self.core), (corner, 1 - self.core),
        )[slot]
        device = (self.partner, self.over_x, self.over_y, self.over_x, self.over_y, self.over_y, self.over_x)[slot]
        there = self.part(chip, core)
        self.copy(there, there, slot, device).wait_recv()

    def start(self):
        for slot in range(3):
            self.sent(slot).start()
        self.keep.start()

    def second(self):
        self.keep.relay()
        self.arrives(0)
        for slot in (3, 4):
            self.sent(slot).start()

    def third(self):
        self.arrives(1)
        self.sent(5).start()

    def fourth(self):
        self.arrives(4)
        self.sent(6).start()

    def finish(self):
        for slot in (2, 3, 5, 6):
            self.arrives(slot)
        for slot in range(7):
            self.sent(slot).wait_send()
        self.keep.wait()


EARLY_UNITS = 2


def scan_forward_kernel(
    x, bc, dt, first, cot, weight, cx, cbc, hp,
    y, st, own, dec, bcs, acum, halo_out, near_out, far_out, gathered,
    xe, be, state, base, halo, halo_sends, halo_receives, sends, receives, local,
    w_sends, w_receives, w_local, w_buffer, row_buffer,
):
    gather = Gather(weight, gathered, w_sends, w_receives, w_local, w_buffer)
    unit, chunk = pl.program_id(0), pl.program_id(1)
    segments, trade = Segments(), Trade(cot, sends, receives)
    me, last = segments.me, segments.count - 1
    units, depth, width = halo.shape

    def halo_copy():
        at = pl.ds(first.shape[1] - depth, depth)
        device = segments.device((me + 1) % segments.count)
        return remote(first.at[:, at, pl.ds(0, width)], halo, halo_sends, halo_receives, 0, device)

    far_copy = trade.send(trade.rows_for(trade.far_group, 0, EARLY_UNITS), far_out, 0, trade.far)
    near_copy = trade.send(trade.rows_for(trade.near_group, 0, units), near_out, 1, trade.near)
    keep = Bounce(trade.rows_for(trade.near_group, 0, units), row_buffer, near_out, local, 0)

    @pl.when((unit == 0) & (chunk == 0))
    def _():
        barrier = pltpu.get_barrier_semaphore()
        pl.semaphore_signal(barrier, inc=1, device_id=trade.far, device_id_type=MESH)

        @pl.when(jnp.logical_not(trade.stays))
        def _():
            pl.semaphore_signal(barrier, inc=1, device_id=trade.near, device_id_type=MESH)

        @pl.when(me > 0)
        def _():
            pl.semaphore_signal(
                barrier, inc=1, device_id=segments.device((me + last) % segments.count), device_id_type=MESH
            )

        for device in (gather.partner, gather.over_x, gather.over_y):
            pl.semaphore_signal(barrier, inc=1, device_id=device, device_id_type=MESH)
        pl.semaphore_wait(barrier, 4 + trade.moves + jnp.where(me < last, 1, 0))

        @pl.when(me < last)
        def _():
            halo_copy().start()

        gather.start()
        far_copy.start()

        @pl.when(trade.stays)
        def _():
            keep.start()

        @pl.when(jnp.logical_not(trade.stays))
        def _():
            near_copy.start()

        @pl.when(me > 0)
        def _():
            halo_copy().wait_recv()

        @pl.when(me == 0)
        def _():
            halo[...] = jnp.zeros_like(halo)

        halo_out[...] = halo[...]

    forward_kernel(x, bc, dt, halo, cx, cbc, hp, y, st, own, dec, bcs, acum, xe, be, state, base)

    @pl.when((unit == 0) & (chunk == 1) & trade.stays)
    def _():
        keep.relay()

    for at_unit, at_chunk, stage in ((0, 0, gather.second), (1, 1, gather.third), (1, 3, gather.fourth)):

        @pl.when((unit == at_unit) & (chunk == at_chunk))
        def _(stage=stage):
            stage()

    @pl.when((unit == units - 1) & (chunk == PER_UNIT - 1))
    def _():
        gather.finish()

        @pl.when(me < last)
        def _():
            halo_copy().wait_send()

        far_copy.wait()

        @pl.when(trade.stays)
        def _():
            keep.wait()

        @pl.when(jnp.logical_not(trade.stays))
        def _():
            near_copy.wait()


def one_hot(rows, columns, offset):
    i = lax.broadcasted_iota(jnp.int32, (rows, columns), 0)
    j = lax.broadcasted_iota(jnp.int32, (rows, columns), 1)
    return jnp.where(j == i + offset, 1.0, 0.0).astype(BF16)


SMALL_ROWS = 32


def head_kernel(
    hidden, w_x, w_bc, w_dt, conv_x, conv_x_bias, gate_gain, norm_gain, conv_bc, conv_bc_bias, dt_bias, a_log, skip_d,
    rows_out, first_out, cx, cbc, hp, gain_in, gain_rows,
    dt_mine, dt_other, small, small_all, row_buffer, x_buffer, bc_buffer,
    local, sends, receives, small_sends, small_receives,
):
    f, z, core, chip, by_x, by_y = places()
    trade = Trade(hidden, sends, receives)
    partner, over_x, over_y = trade.partner, (2 * by_x + core, z), (2 * by_y + core, z)
    far, near, stays = trade.far, trade.near, trade.stays
    units, inner, shards = rows_out.shape[0], cx.shape[1], small_all.shape[0]
    heads = w_dt.shape[1] // 2

    barrier = pltpu.get_barrier_semaphore()
    for k in range(1, shards):
        pl.semaphore_signal(barrier, inc=1, device_id=((f + k) % shards, z), device_id_type=MESH)
    pl.semaphore_signal(barrier, inc=1, device_id=far, device_id_type=MESH)

    @pl.when(jnp.logical_not(stays))
    def _():
        pl.semaphore_signal(barrier, inc=1, device_id=near, device_id_type=MESH)

    pl.semaphore_wait(barrier, shards + trade.moves)

    def part(chip_at, core_at):
        return first_out.at[chip_at, core_at]

    def copy(src, dst, slot, device):
        return remote(src, dst, sends, receives, slot, device)

    class Thirds:
        def __init__(self, side, slot, device):
            columns = pl.ds(pl.multiple_of(side * inner, inner), inner)
            self.whole = copy(part(chip, core), part(chip, core), slot, device)
            dst, wide = part(chip, core), 2 * LANES
            dt = dt_mine if device is not partner else dt_other
            self.copies = [
                copy(w_x.at[:, columns], dst.at[:, pl.ds(0, inner)], slot, device),
                copy(w_bc, dst.at[:, pl.ds(inner, wide)], slot, device),
                copy(dt, dst.at[:, pl.ds(inner + wide, LANES)], slot, device),
            ]

        def start(self):
            for one in self.copies:
                one.start()

        def wait_send(self):
            self.whole.wait_send()

    to_far = copy(trade.rows_for(trade.far_group, 0, units), rows_out.at[:, z], 0, far)
    to_far.start()
    i = lax.broadcasted_iota(jnp.int32, (2 * heads, LANES), 0)
    j = lax.broadcasted_iota(jnp.int32, (2 * heads, LANES), 1)
    for side, kept in ((core, dt_mine), (1 - core, dt_other)):
        chosen = jnp.where((i == j + side * heads) & (j < heads), 1.0, 0.0).astype(BF16)
        kept[...] = dot(w_dt[...], chosen).astype(BF16)
    to_partner, to_x, to_y = Thirds(1 - core, 1, partner), Thirds(core, 2, over_x), Thirds(core, 3, over_y)
    for one in (to_partner, to_x, to_y):
        one.start()
    to_near = copy(trade.rows_for(trade.near_group, 0, units), rows_out.at[:, z], 4, near)
    keep_rows = Bounce(trade.rows_for(trade.near_group, 0, units), row_buffer, rows_out.at[:, z], local, 0)

    @pl.when(stays)
    def _():
        keep_rows.start()

    @pl.when(jnp.logical_not(stays))
    def _():
        to_near.start()

    own = part(chip, core)
    keeps = [
        Bounce(
            w_x.at[:, pl.ds(pl.multiple_of(core * inner, inner), inner)], x_buffer,
            own.at[:, pl.ds(0, inner)], local, 1,
        ),
        Bounce(w_bc, bc_buffer, own.at[:, pl.ds(inner, 2 * LANES)], local, 2),
    ]
    keep_dt = pltpu.make_async_copy(dt_mine, own.at[:, pl.ds(inner + 2 * LANES, LANES)], local.at[6])
    for keep in keeps:
        keep.start()
    keep_dt.start()

    share = conv_x.shape[0]
    per_norm, per_bc, per_head = norm_gain.shape[1], conv_bc.shape[0], dt_bias.shape[1]
    built = jnp.zeros((SMALL_ROWS, share), F32)
    taps = dot_tn(conv_x[...], one_hot(share, share, 0))
    gains = dot(norm_gain[...], one_hot(per_norm, share, per_norm * (f % 2)))
    spread_bc = one_hot(per_bc, 2 * LANES, per_bc * f)
    taps_bc, bias_bc = dot_tn(conv_bc[...], spread_bc), dot(conv_bc_bias[...], spread_bc)
    spread_heads = one_hot(per_head, LANES, per_head * (f % 4))
    by_head = [dot(v[...], spread_heads) for v in (dt_bias, a_log, skip_d)]
    small[...] = built
    small[0:4] = taps
    small[4:5] = conv_x_bias[...].astype(F32)
    small[5:6] = gate_gain[...].astype(F32)
    for k in range(4):
        small[6 + k : 7 + k] = jnp.where(f // 2 == k, gains, 0.0)
    small[10:14, : 2 * LANES] = taps_bc
    small[14:15, : 2 * LANES] = bias_bc
    for side in range(2):
        for n, values in enumerate(by_head):
            small[15 + side : 16 + side, n * LANES : (n + 1) * LANES] = jnp.where(f // 4 == side, values, 0.0)

    def small_copy(k, at):
        return pltpu.make_async_remote_copy(
            src_ref=small, dst_ref=small_all.at[at],
            send_sem=small_sends.at[k], recv_sem=small_receives.at[at],
            device_id=((f + k) % shards, z), device_id_type=MESH,
        )

    for k in range(1, shards):
        small_copy(k, f).start()
    small_all[f] = small[...]

    for keep in keeps:
        keep.relay()

    @pl.when(stays)
    def _():
        keep_rows.relay()

    copy(part(chip, core), part(chip, 1 - core), 1, partner).wait_recv()
    again_x = copy(part(chip, 1 - core), part(chip, 1 - core), 5, over_x)
    again_x.start()
    again_y = copy(part(chip, 1 - core), part(chip, 1 - core), 6, over_y)
    again_y.start()

    near_at, far_at = trade.near_at, trade.far_at

    @pl.when(stays)
    def _():
        keep_rows.wait()

    @pl.when(jnp.logical_not(stays))
    def _():
        copy(trade.rows_for(trade.near_group, 0, units), rows_out.at[:, near_at], 4, near).wait_recv()

    near_on = copy(rows_out.at[:, near_at], rows_out.at[:, near_at], 7, partner)
    near_on.start()

    for k in range(1, shards):
        small_copy(k, (f + k) % shards).wait_recv()
    cx[...] = jnp.zeros_like(cx)
    for k in range(4):
        block = small_all[4 * core + k]
        lanes = slice(k * share, (k + 1) * share)
        cx[0:5, lanes] = block[0:5]
        gain_rows[:, lanes] = jnp.broadcast_to(block[5:6], (8, share))
    summed = small_all[0]
    for k in range(1, shards):
        summed = summed + small_all[k]
    for k in range(4):
        gain_in[:, k * share : (k + 1) * share] = jnp.broadcast_to(summed[6 + k : 7 + k], (8, share))
    cbc[...] = jnp.zeros_like(cbc)
    cbc[0:5] = summed[10:15, : 2 * LANES]
    ours = jnp.where(core == 0, summed[15:16], summed[16:17])
    lane = lax.broadcasted_iota(jnp.int32, (1, LANES), 1)
    hp[...] = jnp.zeros_like(hp)
    hp[0:1] = jnp.where(lane < heads, jnp.exp(ours[:, LANES : 2 * LANES]), 0.0)
    hp[1:2] = ours[:, :LANES]
    skips = ours[:, 2 * LANES :]
    for pair in range(inner // LANES):
        cx[5:6, pair * LANES : (pair + 1) * LANES] = two_heads(skips, pair, lane < LANES // 2)

    copy(part(by_x, core), part(by_x, core), 2, over_x).wait_recv()
    on_y = copy(part(by_x, core), part(by_x, core), 8, over_y)
    on_y.start()
    copy(part(by_y, core), part(by_y, core), 3, over_y).wait_recv()
    copy(part(by_x, 1 - core), part(by_x, 1 - core), 5, over_x).wait_recv()
    copy(part(by_y, 1 - core), part(by_y, 1 - core), 6, over_y).wait_recv()
    on_x = copy(part(by_y, 1 - core), part(by_y, 1 - core), 9, over_x)
    on_x.start()

    copy(trade.rows_for(trade.far_group, 0, units), rows_out.at[:, far_at], 0, far).wait_recv()
    far_on = copy(rows_out.at[:, far_at], rows_out.at[:, far_at], 10, partner)
    far_on.start()

    corner = (by_x + 2) % 4
    copy(part(corner, core), part(corner, core), 8, over_y).wait_recv()
    copy(part(corner, 1 - core), part(corner, 1 - core), 9, over_x).wait_recv()
    copy(rows_out.at[:, near_at], rows_out.at[:, trade.swapped(near_at)], 7, partner).wait_recv()
    copy(rows_out.at[:, far_at], rows_out.at[:, trade.swapped(far_at)], 10, partner).wait_recv()
    for sent in (to_far, to_partner, to_x, to_y, again_x, again_y, near_on, on_y, on_x, far_on):
        sent.wait_send()

    @pl.when(jnp.logical_not(stays))
    def _():
        to_near.wait_send()

    for k in range(1, shards):
        small_copy(k, f).wait_send()
    for keep in keeps:
        keep.wait()
    keep_dt.wait()


def states_kernel(
    own, dec, cot, near_rows, far_rows, normed, w_gate, w_out, y0, bcs, acum,
    dec_out, rows_out, gathered, gate_out, incoming_out, y, gated, squares,
    incoming, parts, decs, results, weight, gate, blocks,
    sends, receives, dec_sends, dec_receives, back_sends, back_receives,
    row_sends, row_receives, w_sends, w_receives, local, w_local, block_sems,
    w_buffer, near_buffer, far_buffer, row_local,
):
    i = pl.program_id(0)
    chunks = pl.num_programs(0) - 1
    segments, trade = Segments(), Trade(cot, row_sends, row_receives)
    gather = Gather(w_out, gathered, w_sends, w_receives, w_local, w_buffer)
    me, count, z = segments.me, segments.count, segments.z
    units, share = own.shape[0], parts.shape[2]
    early = far_rows.shape[0]
    near_at, far_at = trade.near_at, trade.far_at
    block = blocks.shape[1]
    count_blocks = gate.shape[0] // block

    def rows_of(k):
        return pl.ds(pl.multiple_of(k * share, share), share)

    def out_copy(k, at_me):
        other, device = segments.peer(k)
        src, slot = (own.at[:, rows_of(other)], me) if at_me else (own.at[:, rows_of(me)], other)
        return pltpu.make_async_remote_copy(
            src_ref=src, dst_ref=parts.at[slot], send_sem=sends.at[k], recv_sem=receives.at[slot],
            device_id=device, device_id_type=MESH,
        )

    def dec_copy(k, at_me):
        other, device = segments.peer(k)
        slot = me if at_me else other
        return pltpu.make_async_remote_copy(
            src_ref=dec, dst_ref=decs.at[slot], send_sem=dec_sends.at[k], recv_sem=dec_receives.at[slot],
            device_id=device, device_id_type=MESH,
        )

    def back_copy(k, at_me):
        other, device = segments.peer(k)
        slot = me if at_me else other
        return pltpu.make_async_remote_copy(
            src_ref=results.at[other], dst_ref=incoming.at[:, rows_of(slot)],
            send_sem=back_sends.at[k], recv_sem=back_receives.at[slot],
            device_id=device, device_id_type=MESH,
        )

    def fetch(k):
        return pltpu.make_async_copy(normed.at[pl.ds(k * block, block)], blocks.at[k % 2], block_sems.at[k % 2])

    def multiply(k):
        if k + 1 < count_blocks:
            fetch(k + 1).start()
        fetch(k).wait()

        def part(n, carry):
            columns = pl.ds(pl.multiple_of(n * 384, 384), 384)
            gate[pl.ds(k * block, block), columns] = dot(blocks[k % 2], weight[:, columns]).astype(BF16)
            return carry

        lax.fori_loop(0, gate.shape[1] // 384, part, 0)

    last = trade.send(trade.rows_for(trade.far_group, early, units), rows_out.at[early:, z], 0, trade.far)
    last_came = trade.send(
        trade.rows_for(trade.far_group, early, units), rows_out.at[early:, far_at], 0, trade.far
    )
    near_on = trade.send(near_rows, rows_out.at[:, near_at], 1, trade.partner)
    far_on = trade.send(far_rows, rows_out.at[:early, far_at], 2, trade.partner)
    last_on = trade.send(rows_out.at[early:, far_at], rows_out.at[early:, far_at], 3, trade.partner)
    near_keep = Bounce(near_rows, near_buffer, rows_out.at[:, near_at], row_local, 0)
    far_keep = Bounce(far_rows, far_buffer, rows_out.at[:early, far_at], row_local, 1)
    take_weight = pltpu.make_async_copy(w_gate, weight, local.at[2])
    keep_gate = pltpu.make_async_copy(gate, gate_out, local.at[3])
    keep_states = pltpu.make_async_copy(incoming, incoming_out, local.at[4])

    @pl.when(i == 0)
    def _():
        barrier = pltpu.get_barrier_semaphore()
        for k in range(1, count):
            pl.semaphore_signal(barrier, inc=1, device_id=segments.peer(k)[1], device_id_type=MESH)
        for device in (trade.partner, trade.far):
            pl.semaphore_signal(barrier, inc=1, device_id=device, device_id_type=MESH)
        pl.semaphore_wait(barrier, count + 1)
        for k in range(1, count):
            dec_copy(k, True).start()
            out_copy(k, True).start()
        gather.start()
        take_weight.start()
        fetch(0).start()
        last.start()
        near_on.start()
        far_on.start()
        near_keep.start()
        far_keep.start()
        parts[me] = own[:, rows_of(me)]
        decs[me] = dec[...]
        take_weight.wait()
        multiply(0)
        gather.second()
        for k in range(1, count_blocks // 2):
            multiply(k)
        near_keep.relay()
        far_keep.relay()
        for k in range(1, count):
            dec_copy(k, False).wait_recv()
            out_copy(k, False).wait_recv()
        dec_out[...] = decs[...]
        running = [jnp.zeros((share, own.shape[2]), F32) for _ in range(units)]
        for n in range(count):
            for u in range(units):
                results[n, u] = running[u].astype(BF16)
                running[u] = running[u] * decs[n, u : u + 1] + parts[n, u].astype(F32)
        incoming[:, rows_of(me)] = results[me]
        for k in range(1, count):
            back_copy(k, True).start()
        gather.third()
        for k in range(count_blocks // 2, count_blocks):
            multiply(k)
        keep_gate.start()
        last_came.wait_recv()
        last_on.start()
        for k in range(1, count):
            back_copy(k, False).wait_recv()
        keep_states.start()

    @pl.when(i > 0)
    def _():
        place = pl.ds(pl.multiple_of((i - 1) * CHUNK, CHUNK), CHUNK)
        gate_kernel(
            y0, gate.at[place], bcs, acum, incoming.at[pl.ds((i - 1) // PER_UNIT, 1)], y, gated, squares
        )

    @pl.when(i == 1)
    def _():
        gather.fourth()

    @pl.when(i == chunks)
    def _():
        other_near, other_far = trade.swapped(near_at), trade.swapped(far_at)
        trade.send(near_rows, rows_out.at[:, other_near], 1, trade.partner).wait_recv()
        trade.send(far_rows, rows_out.at[:early, other_far], 2, trade.partner).wait_recv()
        trade.send(rows_out.at[early:, far_at], rows_out.at[early:, other_far], 3, trade.partner).wait_recv()
        for copy in (last, near_on, far_on, last_on):
            copy.wait_send()
        for k in range(1, count):
            dec_copy(k, True).wait_send()
            out_copy(k, True).wait_send()
            back_copy(k, True).wait_send()
        for copy in (near_keep, far_keep, keep_gate, keep_states):
            copy.wait()
        gather.finish()


class Reduction:
    def __init__(self, pieces, sends, receives, base, special=None):
        self.f, self.z, self.core, self.chip, self.by_x, self.by_y = places()
        self.corner, self.bit = (self.by_x + 2) % 4, self.z % 2
        self.sends, self.receives, self.base, self.special = sends, receives, base, special
        self.pieces, z_start = [], 0
        for n, (start, width, way) in enumerate(pieces):
            wide = width + LANES if start == special else 2 * width
            self.pieces.append((n, start, width, way, z_start, wide))
            z_start += wide
        self.wide = z_start
        self.partner = (self.f + 1 - 2 * self.core, self.z)
        self.over = {"x": (2 * self.by_x + self.core, self.z), "y": (2 * self.by_y + self.core, self.z)}
        self.near, self.far = (self.f, self.z + 1 - 2 * self.bit), (self.f, (self.z + 2) % 4)

    @staticmethod
    def at(i, size):
        return pl.ds(pl.multiple_of(i * size, size), size)

    def copy(self, src, dst, n, k, device):
        return remote(src, dst, self.sends, self.receives, self.base + 7 * n + k, device)

    def over_chips(self, source, own, passed, r1, s2, r2, sp, rp, total):
        self.source, self.own, self.passed = source, own, passed
        self.r1, self.s2, self.r2, self.sp, self.rp, self.total = r1, s2, r2, sp, rp, total
        self.rows = r2.shape[0]

    def first_copies(self, piece):
        n, start, width, way, _, _ = piece
        columns = pl.ds(start, width)
        to = self.by_x if way == "x" else self.by_y
        return [
            self.copy(self.source(i, columns), self.r1.at[k, :, columns], n, k, self.over[way])
            for k, i in enumerate((to, self.corner))
        ]

    def second_copy(self, piece):
        n, start, width, way, _, _ = piece
        columns = pl.ds(start, width)
        other = "y" if way == "x" else "x"
        return self.copy(self.s2.at[:, columns], self.r2.at[:, columns], n, 2, self.over[other])

    def pair_copy(self, piece):
        n, start, width, _, _, _ = piece
        columns = pl.ds(start, width)
        return self.copy(self.sp.at[:, columns], self.rp.at[:, columns], n, 3, self.partner)

    def start(self, pieces=None):
        for piece in self.pieces if pieces is None else pieces:
            for copy in self.first_copies(piece):
                copy.start()

    def after_first(self, piece):
        _, start, width, way, _, _ = piece
        if self.source is not None:
            for copy in self.first_copies(piece):
                copy.wait_recv()
        columns = pl.ds(start, width)
        passed = self.passed(self.by_y if way == "x" else self.by_x, columns)
        self.s2[:, columns] = (passed.astype(F32) + self.r1[1, :, columns].astype(F32)).astype(BF16)
        self.second_copy(piece).start()

    def chip_sum(self, piece, side):
        columns = pl.ds(piece[1], piece[2])
        there = self.at(side, self.rows // 2)
        own = self.own(side, columns).astype(F32)
        return own + self.r1[0, there, columns].astype(F32) + self.r2[there, columns].astype(F32)

    def lanes_at(self, start, side, width):
        return pl.ds(pl.multiple_of(start + side * width, LANES), width)

    def after_second(self, piece):
        _, start, width, _, z_at, _ = piece
        self.second_copy(piece).wait_recv()
        self.sp[:, pl.ds(start, width)] = self.chip_sum(piece, 1 - self.core).astype(BF16)
        self.pair_copy(piece).start()

    def after_pair(self, piece):
        _, start, width, _, z_at, _ = piece
        self.pair_copy(piece).wait_recv()
        own = self.chip_sum(piece, self.core)
        came = self.rp[:, pl.ds(start, width)]
        if start == self.special:
            both = 2 * LANES
            self.total[:, pl.ds(z_at, both)] = (own[:, :both] + came[:, :both].astype(F32)).astype(BF16)
            self.total[:, self.lanes_at(z_at + both, self.core, LANES)] = own[:, both:].astype(BF16)
            self.total[:, self.lanes_at(z_at + both, 1 - self.core, LANES)] = came[:, both:]
        else:
            self.total[:, self.lanes_at(z_at, self.core, width)] = own.astype(BF16)
            self.total[:, self.lanes_at(z_at, 1 - self.core, width)] = came

    def drain_chips(self):
        for piece in self.pieces:
            firsts = [] if self.source is None else self.first_copies(piece)
            for copy in firsts + [self.second_copy(piece), self.pair_copy(piece)]:
                copy.wait_send()

    def over_members(self, total, came, sums, across, last, store):
        self.total, self.store = total, store
        self.came, self.sums, self.across, self.last = came, sums, across, last
        self.half = total.shape[0] // 2

    def z_copy(self, piece, k):
        n, _, _, _, start, wide = piece
        columns = pl.ds(start, wide)
        src, dst, device = (
            (self.total.at[self.at(1 - self.bit, self.half), columns], self.came, self.near),
            (self.sums.at[0, :, columns], self.across, self.far),
            (self.sums.at[1, :, columns], self.last, self.near),
        )[k]
        return self.copy(src, dst.at[:, columns], n, 4 + k, device)

    def start_members(self, piece):
        self.z_copy(piece, 0).start()

    def after_near(self, piece):
        columns = pl.ds(piece[4], piece[5])
        self.z_copy(piece, 0).wait_recv()
        own = self.total[self.at(self.bit, self.half), columns].astype(F32)
        self.sums[0, :, columns] = (own + self.came[:, columns].astype(F32)).astype(BF16)
        self.z_copy(piece, 1).start()

    def after_far(self, piece):
        columns = pl.ds(piece[4], piece[5])
        self.z_copy(piece, 1).wait_recv()
        total = self.sums[0, :, columns].astype(F32) + self.across[:, columns].astype(F32)
        self.sums[1, :, columns] = total.astype(BF16)
        self.z_copy(piece, 2).start()
        self.store(piece, self.at(self.bit, self.half), total.astype(BF16).astype(F32))

    def after_last(self, piece):
        self.z_copy(piece, 2).wait_recv()
        values = self.last[:, pl.ds(piece[4], piece[5])].astype(F32)
        self.store(piece, self.at(1 - self.bit, self.half), values)

    def drain_members(self):
        for piece in self.pieces:
            for k in range(3):
                self.z_copy(piece, k).wait_send()


def chip_scratch(rows, width):
    return [
        pltpu.VMEM((2, 2 * rows, width), BF16),
        pltpu.VMEM((2 * rows, width), BF16),
        pltpu.VMEM((2 * rows, width), BF16),
        pltpu.VMEM((rows, width), BF16),
        pltpu.VMEM((rows, width), BF16),
    ]


def member_scratch(rows, wide):
    half = (rows // 2, wide)
    return [
        pltpu.VMEM(half, BF16), pltpu.VMEM((2,) + half, BF16),
        pltpu.VMEM(half, BF16), pltpu.VMEM(half, BF16),
    ]


FIRST_PIECES = ((0, 512, "x"), (1024, 512, "y"), (512, 512, "x"), (1536, 384, "y"))
HALF_PIECES = ((0, 768, "x"), (768, 768, "y"))


def tail_kernel(
    normed, d_all, d_base, w_first, unit_rows, g_x, g_bc, g_heads, g_gate, z_total,
    out_x, out_bc, out_dt, vec_out, d_out, out_z,
    turned, g, d_part, d_came, local, r1, s2, r2, sp, rp, total, came, sums, across, last,
    z_came, z_sums, z_across, z_last, end_x, end_bc, end_dt, end_z,
    vs, vr, vec_all, sends, receives, vec_sends, vec_receives,
):
    i = pl.program_id(0)
    steps = pl.num_programs(0) // 2
    f, z, core, chip, by_x, by_y = places()
    rows = g.shape[0] // 4
    inner = out_x.shape[1] // 2
    wide = normed.shape[1]
    bit, upper, units = z % 2, z // 2, d_part.shape[0]
    first = Reduction(FIRST_PIECES, sends, receives, 0, inner)
    gate = Reduction(HALF_PIECES, sends, receives, 7 * len(FIRST_PIECES))
    slot = 7 * (len(FIRST_PIECES) + len(HALF_PIECES))
    partner, near, far = first.partner, first.near, first.far
    token_near, token_far = (2 * chip + bit, 2 * upper + core), (2 * chip + bit, 2 * (1 - upper) + core)
    stays = bit == core

    def d_pair(k, n):
        return remote(d_part.at[:, k, 1 - core], d_came.at[:, k], sends, receives, slot + n, partner)

    def d_trade(k, n, device, group):
        return remote(
            d_part.at[:, k, core], d_out.at[pl.ds(group * units, units)], sends, receives, slot + 2 + n, device
        )

    def d_add(k):
        for u in range(units):
            d_part[u, k, core] = (d_part[u, k, core].astype(F32) + d_came[u, k].astype(F32)).astype(BF16)

    d_keep = pltpu.make_async_copy(d_part.at[:, upper, core], d_out.at[pl.ds(upper * units, units)], local.at[0])

    first.over_chips(
        lambda i, columns: g.at[first.at(i, rows), columns],
        lambda side, columns: g[pl.ds(pl.multiple_of(chip * rows + side * (rows // 2), rows // 2), rows // 2), columns],
        lambda i, columns: g[first.at(i, rows), columns],
        r1, s2, r2, sp, rp, total,
    )

    def store_first(piece, there, values):
        _, start, width, _, _, _ = piece
        if start == inner:
            end_bc[there, :] = values[:, : 2 * LANES]
            end_dt[there, :] = values[:, 2 * LANES :]
        else:
            end_x[there, pl.ds(start, width)] = values[:, :width]
            end_x[there, pl.ds(inner + start, width)] = values[:, width:]

    def store_gate(piece, there, values):
        _, start, width, _, _, _ = piece
        end_z[there, pl.ds(start, width)] = values[:, :width]
        end_z[there, pl.ds(inner + start, width)] = values[:, width:]

    gate.over_members(z_total, z_came, z_sums, z_across, z_last, store_gate)
    first.over_members(total, came, sums, across, last, store_first)

    vec_ways = [first.over["x"], first.over["y"], near, far]

    def vec_copy(k):
        return remote(vs.at[k], vr.at[k], vec_sends, vec_receives, k, vec_ways[k])

    def vec_last(side):
        return remote(vec_all.at[core], vec_all.at[side], vec_sends, vec_receives, 4, partner)

    def vec_step(k):
        if k:
            vec_copy(k - 1).wait_recv()
            summed = vs[k - 1] + vr[k - 1]
            if k < 4:
                vs[k] = summed
            else:
                vec_all[core] = summed
        if k < 4:
            vec_copy(k).start()
        else:
            vec_last(core).start()

    early, late = first.pieces[:2], first.pieces[2:]

    def pair_on(piece):
        first.after_pair(piece)
        first.start_members(piece)

    @pl.when(i == 0)
    def _():
        barrier = pltpu.get_barrier_semaphore()
        for device in (partner, first.over["x"], first.over["y"], near, far, token_far):
            pl.semaphore_signal(barrier, inc=1, device_id=device, device_id_type=MESH)

        @pl.when(jnp.logical_not(stays))
        def _():
            pl.semaphore_signal(barrier, inc=1, device_id=token_near, device_id_type=MESH)

        pl.semaphore_wait(barrier, 6 + (bit + core) % 2)
        for piece in gate.pieces:
            gate.start_members(piece)
        vs[0] = jnp.zeros(vs.shape[1:], F32)

    @pl.when(i >= steps)
    def _():
        def part(n, carry):
            columns = pl.ds(pl.multiple_of(n * 384, 384), 384)
            g[pl.ds(pl.multiple_of((i - steps) * wide, wide), wide), columns] = dot(
                turned[...], d_all[:, columns]
            ).astype(BF16)
            return carry

        turned[...] = normed[...].T
        lax.fori_loop(0, g.shape[1] // 384, part, 0)

    @pl.when(i == 2 * steps - 1)
    def _():
        first.start(early)

    @pl.when(i < steps)
    def _():
        columns = pl.ds(pl.multiple_of(i * wide, wide), wide)
        per = d_all.shape[0] // units

        def part(u, carry):
            there = pl.ds(pl.multiple_of(u * per, per), per)
            product = d_base[there, :].astype(F32) + dot_nt(d_all[there, :], w_first[...])
            d_part[u, :, :, :, columns] = product.astype(BF16).reshape(2, 2, per // 4, wide)
            return carry + jnp.sum(product * unit_rows[there, :].astype(F32), axis=0, keepdims=True)

        vs[0, 6:7, columns] = lax.fori_loop(0, units, part, jnp.zeros((1, wide), F32))

    @pl.when(i == steps - 1)
    def _():
        for piece in gate.pieces:
            gate.after_near(piece)
        d_pair(1 - upper, 0).start()
        d_pair(upper, 1).start()

    @pl.when(i == steps + 2)
    def _():
        d_pair(1 - upper, 0).wait_recv()
        d_add(1 - upper)
        d_trade(1 - upper, 0, token_far, upper).start()
        d_pair(upper, 1).wait_recv()
        d_add(upper)

        @pl.when(stays)
        def _():
            d_keep.start()

        @pl.when(jnp.logical_not(stays))
        def _():
            d_trade(upper, 1, token_near, upper).start()

    @pl.when(i == 2 * steps - 1)
    def _():
        for k in range(5):
            vs[0, k : k + 1] = jnp.sum(g_x[8 * k : 8 * k + 8], axis=0, keepdims=True)
            vs[0, 8 + k : 9 + k, : 2 * LANES] = jnp.sum(g_bc[8 * k : 8 * k + 8], axis=0, keepdims=True)
        vs[0, 5:6] = g_gate[...]
        for k in range(3):
            vs[0, 7:8, k * LANES : (k + 1) * LANES] = jnp.sum(
                g_heads[8 * k : 8 * k + 8], axis=0, keepdims=True
            )
        vec_step(0)
        for piece in early:
            first.after_first(piece)
        first.start(late)
        order = (
            (first.after_second, early), (1, ()), (pair_on, early), (2, ()), (first.after_first, late),
            (gate.after_far, gate.pieces), (3, ()), (first.after_second, late), (4, ()),
            (first.after_near, early), (pair_on, late), (gate.after_last, gate.pieces), (first.after_far, early),
            (first.after_near, late), (first.after_last, early), (first.after_far, late), (first.after_last, late),
        )
        for stage, pieces in order:
            if not pieces:
                vec_step(stage)
            for piece in pieces:
                stage(piece)
        ends = [
            pltpu.make_async_copy(src, dst, local.at[1 + n])
            for n, (src, dst) in enumerate(
                ((end_x, out_x), (end_bc, out_bc), (end_dt, out_dt), (end_z, out_z))
            )
        ]
        for end in ends:
            end.start()
        vec_last(1 - core).wait_recv()
        vec_out[...] = vec_all[...]
        d_trade(1 - upper, 0, token_far, 1 - upper).wait_recv()

        @pl.when(stays)
        def _():
            d_keep.wait()

        @pl.when(jnp.logical_not(stays))
        def _():
            d_trade(upper, 1, token_near, upper).wait()

        d_trade(1 - upper, 0, token_far, upper).wait_send()
        d_pair(1 - upper, 0).wait_send()
        d_pair(upper, 1).wait_send()
        first.drain_chips()
        first.drain_members()
        gate.drain_members()
        for k in range(4):
            vec_copy(k).wait_send()
        vec_last(core).wait_send()
        for end in ends:
            end.wait()


def trade_steps(source, target, buffer, local, sends, receives):
    f, z, core, chip, _, _ = places()
    units = source.shape[0]
    bit, upper = z % 2, z // 2
    near, far = (2 * chip + bit, 2 * upper + core), (2 * chip + bit, 2 * (1 - upper) + core)
    stays = bit == core

    def copy(k, n, device, group):
        return remote(source.at[:, k], target.at[pl.ds(group * units, units)], sends, receives, n, device)

    tokens = source.shape[2]
    keeps = [
        Bounce(
            source.at[u, upper], buffer.at[pl.ds(u * tokens, tokens)], target.at[upper * units + u], local, u
        )
        for u in range(units)
    ]

    def relay():
        @pl.when(stays)
        def _():
            for keep in keeps:
                keep.relay()

    def settle():
        @pl.when(stays)
        def _():
            for keep in keeps:
                keep.wait()

    def start():
        copy(1 - upper, 0, far, upper).start()

        @pl.when(stays)
        def _():
            for keep in keeps:
                keep.start()

        @pl.when(jnp.logical_not(stays))
        def _():
            copy(upper, 1, near, upper).start()

    def finish():
        copy(1 - upper, 0, far, 1 - upper).wait_recv()
        copy(1 - upper, 0, far, upper).wait_send()

        @pl.when(jnp.logical_not(stays))
        def _():
            copy(upper, 1, near, upper).wait()

    return start, relay, settle, finish, far, near, stays


class Segments:
    def __init__(self):
        self.f, self.z, self.core, self.chip, _, _ = places()
        self.group = self.z // 2
        self.me = self.chip * 2 + self.z % 2
        self.count = 8

    def device(self, i):
        return ((i // 2) * 2 + self.core, self.group * 2 + i % 2)

    def peer(self, k):
        other = (self.me + k) % self.count
        return other, self.device(other)


def middle_kernel(
    dno, gated, gate, y_pull, stats, gain, bcs, acum_pull, decays, normed, w_gate, g_out, projected,
    x, xp, bc, bcp, dt, halo, cx, cbc, hp, y, st, incoming, acum, pick,
    d_all, heads_x, heads_bc, g_x, g_bc, g_heads, d_base_out, tokens_out, total_out, z_out,
    dy_all, dgate_all, pulled, own, after, parts, results, blocks, turned, w_blocks, products, g_z, out_own,
    o_r1, o_s2, o_r2, o_sp, o_rp, o_total, o_came, o_sums, o_across, o_last,
    z_r1, z_r2, z_rp, z_total,
    xe, be, adjoint, dpx, dpb, ends,
    local, keep_sems, block_sems, w_sems, product_sems, trade_local, trade_sends, trade_receives, sends, receives,
    state_sends, state_receives, back_sends, back_receives,
):
    i = pl.program_id(0)
    chunks = (pl.num_programs(0) - 1) // 2
    f, z, core, chip, by_x, by_y = places()
    segments = Segments()
    me, count = segments.me, segments.count
    units, share = own.shape[0], parts.shape[2]
    rows = g_z.shape[0] // 4
    half = rows // 2
    inner = g_z.shape[1]

    def at(k, size):
        return pl.ds(pl.multiple_of(k * size, size), size)

    start_trade, relay_trade, settle_trade, finish_trade, trade_far, trade_near, stays = trade_steps(
        projected, tokens_out, g_z, trade_local, trade_sends, trade_receives
    )
    out = Reduction(HALF_PIECES, sends, receives, 0)
    gz = Reduction(HALF_PIECES, sends, receives, 7 * len(HALF_PIECES))
    out.over_chips(
        lambda k, columns: g_out.at[at(k, rows), columns],
        lambda side, columns: out_own[at(side, half), columns],
        lambda k, columns: o_s2[:, columns],
        o_r1, o_s2, o_r2, o_sp, o_rp, o_total,
    )

    out.over_members(o_total, o_came, o_sums, o_across, o_last, lambda piece, there, values: None)
    gz.over_chips(
        lambda k, columns: g_z.at[at(k, rows), columns],
        lambda side, columns: g_z[pl.ds(pl.multiple_of(chip * rows + side * half, half), half), columns],
        lambda k, columns: g_z[at(k, rows), columns],
        z_r1, o_s2, z_r2, o_sp, z_rp, z_total,
    )
    left, right = (pl.ds(start, width) for start, width, _ in HALF_PIECES)
    own_rows = pltpu.make_async_copy(g_out.at[at(chip, rows)], out_own, local.at[0])
    pass_left = pltpu.make_async_copy(g_out.at[at(by_y, rows), left], o_s2.at[:, left], local.at[1])
    pass_right = pltpu.make_async_copy(g_out.at[at(by_x, rows), right], o_s2.at[:, right], local.at[2])

    def keep_out():
        copies = []
        for piece in out.pieces:
            n, start, width, _, z_at, _ = piece
            for side, (src, half_at) in enumerate(((o_sums.at[1], out.bit), (o_last, 1 - out.bit))):
                for part in range(2):
                    slot = 4 * n + 2 * side + part
                    copies.append(
                        pltpu.make_async_copy(
                            src.at[:, pl.ds(z_at + part * width, width)],
                            total_out.at[out.at(half_at, out.half), pl.ds(part * inner + start, width)],
                            keep_sems.at[slot],
                        )
                    )
        return copies

    keep_z = pltpu.make_async_copy(z_total, z_out, local.at[7])
    taken = (own_rows, pass_left, pass_right)

    def fetch(k):
        columns = pl.ds(k * 256, 256)
        return pltpu.make_async_copy(normed.at[:, columns], blocks.at[k % 2], block_sems.at[k % 2])

    @pl.when(i == 0)
    def _():
        barrier = pltpu.get_barrier_semaphore()
        for k in range(1, count):
            pl.semaphore_signal(barrier, inc=1, device_id=segments.peer(k)[1], device_id_type=MESH)
        for device in (out.partner, out.far, trade_far):
            pl.semaphore_signal(barrier, inc=1, device_id=device, device_id_type=MESH)

        @pl.when(jnp.logical_not(stays))
        def _():
            pl.semaphore_signal(barrier, inc=1, device_id=trade_near, device_id_type=MESH)

        pl.semaphore_wait(barrier, count + 2 + (z + core) % 2)
        out.start()
        for copy in taken:
            copy.start()
        start_trade()

    @pl.when(i == 3)
    def _():
        relay_trade()

    @pl.when(i < chunks)
    def _():
        place = at(i, CHUNK)
        pull_kernel(
            dno, gated, gate, y_pull, stats, gain, bcs, acum_pull,
            dy_all.at[place], dgate_all.at[place], own.at[pl.ds(i // PER_UNIT, 1)],
            pulled, chunk=i % PER_UNIT,
        )

    def state_copy(k, at_me):
        other, device = segments.peer(k)
        src, slot = (own.at[:, at(other, share)], me) if at_me else (own.at[:, at(me, share)], other)
        return pltpu.make_async_remote_copy(
            src_ref=src, dst_ref=parts.at[slot],
            send_sem=state_sends.at[k], recv_sem=state_receives.at[slot],
            device_id=device, device_id_type=MESH,
        )

    def back_copy(k, at_me):
        other, device = segments.peer(k)
        slot = me if at_me else other
        return pltpu.make_async_remote_copy(
            src_ref=results.at[other], dst_ref=after.at[:, at(slot, share)],
            send_sem=back_sends.at[k], recv_sem=back_receives.at[slot],
            device_id=device, device_id_type=MESH,
        )

    def multiply(k):
        if k < 5:
            fetch(k + 1).start()
        fetch(k).wait()

        turned[...] = blocks[k % 2].T

        def part(n, carry):
            columns = pl.ds(pl.multiple_of(n * 256, 256), 256)
            product = dot(turned[...], dgate_all[:, columns])
            g_z[pl.ds(k * 256, 256), columns] = product.astype(BF16)
            return carry

        lax.fori_loop(0, inner // 256, part, 0)

    def fetch_w(k):
        return pltpu.make_async_copy(w_gate.at[pl.ds(k * 256, 256)], w_blocks.at[k % 2], w_sems.at[k % 2])

    def put(k):
        return pltpu.make_async_copy(
            products.at[k % 2], d_base_out.at[:, pl.ds(k * 256, 256)], product_sems.at[k % 2]
        )

    def project(k):
        if k < 5:
            fetch_w(k + 1).start()
        fetch_w(k).wait()
        if k > 1:
            put(k - 2).wait()
        per = dgate_all.shape[0] // units

        def part(n, carry):
            there = pl.ds(pl.multiple_of(n * per, per), per)
            products[k % 2, there, :] = dot_nt(dgate_all[there, :], w_blocks[k % 2]).astype(BF16)
            return carry

        lax.fori_loop(0, units, part, 0)
        put(k).start()

    @pl.when(i == chunks)
    def _():
        for k in range(1, count):
            state_copy(k, True).start()
        fetch(0).start()
        fetch_w(0).start()
        settle_trade()
        parts[me] = own[:, at(me, share)]
        for k in range(6):
            multiply(k)
        for k in range(1, count):
            state_copy(k, False).wait_recv()
        running = [jnp.zeros((share, inner), F32) for _ in range(units)]
        for n in range(count - 1, -1, -1):
            for u in range(units):
                results[n, u] = running[u].astype(BF16)
                running[u] = running[u] * decays[n, u : u + 1] + parts[n, u].astype(F32)
        after[:, at(me, share)] = results[me]
        for k in range(1, count):
            back_copy(k, True).start()
        for k in range(6):
            project(k)
        put(4).wait()
        put(5).wait()
        for k in range(1, count):
            back_copy(k, False).wait_recv()
        for k in range(1, count):
            state_copy(k, True).wait_send()
            back_copy(k, True).wait_send()
        for copy in taken:
            copy.wait()
        for piece in out.pieces:
            out.after_first(piece)
        gz.start()

    def at_step(n, *stages):
        @pl.when(i == chunks + 1 + n)
        def _():
            for stage, reduction in stages:
                for piece in reduction.pieces:
                    stage(piece)

    @pl.when(i > chunks)
    def _():
        n = i - chunks - 1
        unit, chunk = n // PER_UNIT, n % PER_UNIT
        place = at(unit * PER_UNIT + PER_UNIT - 1 - chunk, CHUNK)
        backward_kernel(
            x, xp, bc, bcp, dt, halo, cx, cbc, hp, dy_all.at[place], y, st, incoming, acum,
            after.at[pl.ds(unit, 1)], pick, d_all, heads_x, heads_bc, g_x, g_bc, g_heads,
            xe, be, adjoint, dpx, dpb, ends, place=(unit, chunk),
        )

    at_step(2, (out.after_second, out))
    at_step(3, (out.after_pair, out), (out.start_members, out))
    at_step(5, (out.after_near, out))

    @pl.when(i == chunks + 1 + 6)
    def _():
        for piece in out.pieces:
            out.second_copy(piece).wait_send()
            out.pair_copy(piece).wait_send()
            gz.after_first(piece)

    at_step(8, (gz.after_second, gz))
    at_step(9, (out.after_far, out), (gz.after_pair, gz))

    @pl.when(i == 2 * chunks)
    def _():
        finish_trade()
        for piece in out.pieces:
            out.after_last(piece)
            for copy in out.first_copies(piece):
                copy.wait_send()
        out.drain_members()
        for copy in keep_out():
            copy.start()
        keep_z.start()
        gz.drain_chips()
        for copy in keep_out():
            copy.wait()
        keep_z.wait()


class Plan:
    def __init__(self, batch, tokens):
        self.shards, self.members = lax.axis_size("fs"), lax.axis_size("sp")
        self.f, self.z = lax.axis_index("fs"), lax.axis_index("sp")
        self.core = self.f % 2
        self.chips = self.shards // 2
        self.chip = self.f // 2
        self.batch, self.tokens = batch, tokens
        self.units = batch // 2
        self.joints = self.members // 2
        self.count = self.chips * self.joints
        self.group, self.joint = self.z // self.joints, self.z % self.joints
        self.fast = self.chips == 4 and self.members == 4

    def at(self, f, z):
        return f * self.members + z

    def send(self, x, pairs):
        return lax.ppermute(x, ("fs", "sp"), pairs)

    def swap(self, x, df=0, dz=0):
        pairs = [
            (self.at(f, z), self.at(f ^ df, z ^ dz))
            for f in range(self.shards)
            for z in range(self.members)
        ]
        return self.send(x, pairs)

    def along(self, x, by):
        pairs = []
        for f in range(self.shards):
            for z in range(self.members):
                place = (f // 2) * self.joints + z % self.joints + by
                if 0 <= place < self.count:
                    there = (place // self.joints) * 2 + f % 2
                    pairs.append(
                        (self.at(f, z), self.at(there, z - z % self.joints + place % self.joints))
                    )
        return self.send(x, pairs)

    def by_core(self, mine, other):
        first = self.core == 0
        return jnp.where(first, mine, other), jnp.where(first, other, mine)

    def head(self, hidden, w_x, w_bc, w_dt, conv_x, conv_bc, *vectors):
        anywhere, vmem = pl.BlockSpec(memory_space=pl.ANY), pl.BlockSpec(memory_space=pltpu.VMEM)
        conv_x_bias, gate_gain, norm_gain, conv_bc_bias, dt_bias, a_log, skip_d = (v[None] for v in vectors)
        rows, inner = w_x.shape[0], w_x.shape[1] // 2
        small = (SMALL_ROWS, conv_x.shape[0])
        dma = pltpu.SemaphoreType.DMA
        shape = jax.ShapeDtypeStruct
        units, first, *params = pl.pallas_call(
            head_kernel,
            out_shape=[
                shape((self.units, 4, self.tokens, hidden.shape[-1]), BF16),
                shape((4, 2, rows, inner + 3 * LANES), BF16),
                shape((8, inner), F32), shape((8, 2 * LANES), F32), shape((8, LANES), F32),
                shape((8, hidden.shape[-1]), F32), shape((8, inner), F32),
            ],
            in_specs=[anywhere] * 3 + [vmem] * 10,
            out_specs=[anywhere] * 2 + [vmem] * 5,
            scratch_shapes=[
                pltpu.VMEM((rows, LANES), BF16), pltpu.VMEM((rows, LANES), BF16),
                pltpu.VMEM(small, F32), pltpu.VMEM((self.shards,) + small, F32),
                pltpu.VMEM((self.units, self.tokens, hidden.shape[-1]), BF16),
                pltpu.VMEM((rows, inner), BF16), pltpu.VMEM((rows, 2 * LANES), BF16),
                dma((7,)), dma((11,)), dma((11,)), dma((self.shards,)), dma((self.shards,)),
            ],
            compiler_params=pltpu.CompilerParams(
                collective_id=2, has_side_effects=True, vmem_limit_bytes=VMEM_LIMIT
            ),
            cost_estimate=cost(55),
            name="head",
        )(
            hidden, w_x, w_bc, w_dt, conv_x, conv_x_bias, gate_gain, norm_gain, conv_bc, conv_bc_bias,
            dt_bias, a_log, skip_d,
        )
        return units.reshape(-1, hidden.shape[-1]), first.reshape(-1, inner + 3 * LANES), *params

    def slow_tail(self, g, g_x, g_bc, g_heads, g_gate, g_norm, d_normed):
        rows, inner = g.shape[0] // self.shards, g_x.shape[1]
        g = self.reduce_chips(g)
        low = self.core == 0
        kept, given = jnp.where(low, g[:rows], g[rows:]), jnp.where(low, g[rows:], g[:rows])
        came = self.swap(given.astype(BF16), df=1).astype(F32)
        total = self.reduce_members(
            jnp.concatenate(
                list(self.by_core(kept[:, :inner], came[:, :inner]))
                + [kept[:, inner : inner + 2 * LANES] + came[:, inner : inner + 2 * LANES]]
                + list(self.by_core(kept[:, inner + 2 * LANES :], came[:, inner + 2 * LANES :])),
                axis=1,
            )
        )
        wide = ((0, 0), (0, inner - 2 * LANES))
        heads = g_heads.reshape(3, 8, LANES).sum(axis=1).reshape(1, -1)
        vec = jnp.concatenate(
            [
                g_x.reshape(5, 8, inner).sum(axis=1), g_gate, g_norm,
                jnp.pad(heads, ((0, 0), (0, inner - 3 * LANES))),
                jnp.pad(g_bc.reshape(5, 8, 2 * LANES).sum(axis=1), wide),
            ]
        )
        vec = self.sum_all(jnp.pad(vec, ((0, 3), (0, 0))))
        vec = jnp.stack(self.by_core(vec, self.swap(vec, df=1)))
        cut = 2 * inner + 2 * LANES
        d_rows = self.to_tokens(self.cores_sum(d_normed))
        return total[:, : 2 * inner], total[:, 2 * inner : cut], total[:, cut:], vec, d_rows
    def tail(self, normed, d_all, d_base, w_first, unit_rows, g_x, g_bc, g_heads, g_gate, z_total):
        model, inner, width = normed.shape[1], g_x.shape[1], d_all.shape[1]
        rows, count = model // self.shards, normed.shape[0]
        wide, block = 2 * inner + 4 * LANES, 256
        steps = model // block
        vec = (16, inner)
        slots = 7 * (len(FIRST_PIECES) + len(HALF_PIECES)) + 4
        anywhere, dma, shape = pl.BlockSpec(memory_space=pl.ANY), pltpu.SemaphoreType.DMA, jax.ShapeDtypeStruct

        def whole(v):
            return pl.BlockSpec(v.shape, lambda i: (0,) * v.ndim, pipeline_mode=pl.Buffered(1))

        def early(i):
            return jnp.minimum(i, steps - 1)

        def late(i):
            return jnp.maximum(i - steps, 0)

        return pl.pallas_call(
            tail_kernel,
            grid=(2 * steps,),
            in_specs=[
                pl.BlockSpec((count, block), lambda i: (0, late(i))), whole(d_all),
                pl.BlockSpec((count, block), lambda i: (0, early(i))),
                pl.BlockSpec((block, width), lambda i: (early(i), 0)),
                pl.BlockSpec((count, block), lambda i: (0, early(i))),
                whole(g_x), whole(g_bc), whole(g_heads), whole(g_gate), whole(z_total),
            ],
            out_specs=[anywhere] * 3
            + [pl.BlockSpec((2,) + vec, lambda i: (0, 0, 0))]
            + [anywhere] * 2,
            out_shape=[
                shape((rows, 2 * inner), F32), shape((rows, 2 * LANES), F32), shape((rows, 2 * LANES), F32),
                shape((2,) + vec, F32), shape((self.batch, self.tokens, model), BF16),
                shape((rows, 2 * inner), F32),
            ],
            scratch_shapes=[
                pltpu.VMEM((block, count), BF16),
                pltpu.VMEM((model, width), BF16),
                pltpu.VMEM((self.units, 2, 2, self.tokens, model), BF16),
                pltpu.VMEM((self.units, 2, self.tokens, model), BF16),
                dma((5,)),
            ]
            + chip_scratch(rows, width)
            + [pltpu.VMEM((rows, wide), BF16)]
            + member_scratch(rows, wide)
            + member_scratch(rows, 2 * inner)
            + [
                pltpu.VMEM((rows, 2 * inner), F32), pltpu.VMEM((rows, 2 * LANES), F32),
                pltpu.VMEM((rows, 2 * LANES), F32), pltpu.VMEM((rows, 2 * inner), F32),
                pltpu.VMEM((4,) + vec, F32), pltpu.VMEM((4,) + vec, F32), pltpu.VMEM((2,) + vec, F32),
                dma((slots,)), dma((slots,)), dma((5,)), dma((5,)),
            ],
            compiler_params=pltpu.CompilerParams(
                dimension_semantics=("arbitrary",), collective_id=3, has_side_effects=True,
                vmem_limit_bytes=TAIL_LIMIT,
            ),
            cost_estimate=cost(130),
            name="tail",
        )(normed, d_all, d_base, w_first, unit_rows, g_x, g_bc, g_heads, g_gate, z_total)

    def gather(self, x):
        groups = [list(range(c, self.shards, 2)) for c in range(2)]
        return lax.all_gather(x, "fs", axis=0, tiled=True, axis_index_groups=groups)

    def reduce_chips(self, g):
        groups = [list(range(c, self.shards, 2)) for c in range(2)]
        return lax.psum_scatter(
            g, "fs", scatter_dimension=0, tiled=True, axis_index_groups=groups
        ).astype(F32)

    def reduce_members(self, g):
        return lax.psum(g.astype(BF16), "sp").astype(F32)

    def traded(self, x, far):
        pairs = [
            (self.at(f, z), self.at(f - f % 2 + z % 2, ((z // 2) ^ far) * 2 + f % 2))
            for f in range(self.shards)
            for z in range(self.members)
        ]
        return self.send(x, pairs)

    def to_units(self, rows):
        units, width = self.units, rows.shape[-1]
        if self.fast:
            low, high = rows[:units], rows[units:]
            upper = self.z // 2 == 1
            far = self.traded(jnp.where(upper, low, high), 1)
            near = self.traded(jnp.where(upper, high, low), 0)
            mine = jnp.stack([jnp.where(upper, far, near), jnp.where(upper, near, far)], axis=1)
            pair = self.by_core(mine, self.swap(mine, df=1))
            block = jnp.stack(pair, axis=2)
        else:
            other = self.swap(rows, df=1)
            everything = lax.all_gather(jnp.stack(self.by_core(rows, other)), "sp")
            per_core = self.joints // 2
            block = lax.dynamic_slice(
                everything,
                ((self.joint % per_core) * 4, self.joint // per_core, self.group * units, 0, 0),
                (4, 1, units) + rows.shape[1:],
            )[:, 0]
            block = jnp.moveaxis(block, 0, 1)
        return block.reshape(units * 4 * self.tokens, width)

    def cores_sum(self, partial):
        units, width = self.units, partial.shape[-1]
        if self.fast:
            block = partial.reshape(units, 2, 2, self.tokens, width)
            even = self.core == 0
            mine = jnp.where(even, block[:, :, 0], block[:, :, 1])
            given = jnp.where(even, block[:, :, 1], block[:, :, 0]).astype(BF16)
            return (mine.astype(F32) + self.swap(given, df=1).astype(F32)).astype(BF16)
        return partial.astype(BF16).reshape(units, 4, self.tokens, width)

    def to_tokens(self, total):
        units, width = self.units, total.shape[-1]
        if self.fast:
            upper = self.z // 2 == 1
            far = self.traded(jnp.where(upper, total[:, 0], total[:, 1]), 1)
            near = self.traded(jnp.where(upper, total[:, 1], total[:, 0]), 0)
            return jnp.concatenate(
                [jnp.where(upper, far, near), jnp.where(upper, near, far)], axis=0
            )
        per_core = self.joints // 2
        block = total
        wide = jnp.zeros((self.members, 2, self.batch, self.tokens, width), BF16)
        wide = lax.dynamic_update_slice(
            wide,
            jnp.moveaxis(block, 1, 0)[:, None],
            ((self.joint % per_core) * 4, self.joint // per_core, self.group * units, 0, 0),
        )
        summed = lax.psum_scatter(wide, "sp", scatter_dimension=0, tiled=False)
        first = self.core == 0
        mine, given = jnp.where(first, summed[0], summed[1]), jnp.where(first, summed[1], summed[0])
        return (mine.astype(F32) + self.swap(given, df=1).astype(F32)).astype(BF16)

    def sum_all(self, x):
        if not self.fast:
            groups = [list(range(c, self.shards, 2)) for c in range(2)]
            return lax.psum(lax.psum(x, "fs", axis_index_groups=groups), "sp")
        for df, dz in ((2, 0), (4, 0), (0, 1), (0, 2)):
            x = x + self.swap(x, df, dz)
        return x


def row_scale(values):
    return lax.rsqrt(jnp.mean(values * values, axis=-1, keepdims=True) + EPSILON)


def rows_spec(width, column=0, back=False):
    def place(u, c):
        return (u * PER_UNIT + (PER_UNIT - 1 - c if back else c), column)

    return pl.BlockSpec((CHUNK, width), place)


def chunk_spec(shape, back=False):
    def place(u, c):
        return (u * PER_UNIT + (PER_UNIT - 1 - c if back else c), 0, 0)

    return pl.BlockSpec((1,) + shape, place)


def unit_spec(shape):
    return pl.BlockSpec((1,) + shape, lambda u, c: (u, 0, 0))


def whole_spec(shape):
    return pl.BlockSpec(shape, lambda u, c: (0,) * len(shape))


def cost(microseconds):
    return pl.CostEstimate(flops=int(microseconds * 1.15e9), bytes_accessed=0, transcendentals=0)


def params():
    return pltpu.CompilerParams(
        dimension_semantics=("arbitrary", "arbitrary"), vmem_limit_bytes=VMEM_LIMIT
    )


def slow_exchange(plan, own, decays, back):
    count, units = plan.count, own.shape[0]
    rates, pieces = decays[:units, None], own.astype(F32)

    def hop(_, before):
        return plan.along((before * rates + pieces).astype(BF16), -1 if back else 1).astype(F32)

    return lax.fori_loop(0, count - 1, hop, jnp.zeros(own.shape, F32)).astype(BF16)


def exchange(plan, own, decays, cot, near, far, normed, w_gate, w_out, y0, bcs, acum):
    units, depth, width = own.shape
    count, share = plan.count, depth // plan.count
    dec_shape, rows, model = (count, 8, width), normed.shape[0], normed.shape[1]
    chunks = rows // CHUNK
    anywhere, dma, shape = pl.BlockSpec(memory_space=pl.ANY), pltpu.SemaphoreType.DMA, jax.ShapeDtypeStruct

    def whole(v):
        return pl.BlockSpec(v.shape, lambda i: (0,) * v.ndim, pipeline_mode=pl.Buffered(1))

    def chunk(columns):
        return pl.BlockSpec((CHUNK, columns), lambda i: (jnp.maximum(i - 1, 0), 0))

    all_decays, cot_rows, weight_out, gate, incoming, y, gated, squares = pl.pallas_call(
        states_kernel,
        grid=(chunks + 1,),
        in_specs=[whole(own), whole(decays)]
        + [anywhere] * 6
        + [chunk(width), chunk(2 * LANES), chunk(LANES)],
        out_specs=[pl.BlockSpec(dec_shape, lambda i: (0, 0, 0))]
        + [anywhere] * 4
        + [chunk(width), chunk(width), chunk(LANES)],
        out_shape=[
            shape(dec_shape, F32), shape((units, 4, plan.tokens, model), BF16),
            shape((4, 2, w_out.shape[0], width), BF16), shape((rows, width), BF16), shape(own.shape, BF16),
            shape((rows, width), BF16), shape((rows, width), BF16), shape((rows, LANES), F32),
        ],
        scratch_shapes=[
            pltpu.VMEM(own.shape, BF16), pltpu.VMEM((count, units, share, width), BF16),
            pltpu.VMEM(dec_shape, F32), pltpu.VMEM((count, units, share, width), BF16),
            pltpu.VMEM(w_gate.shape, BF16), pltpu.VMEM((rows, width), BF16), pltpu.VMEM((2, 256, model), BF16),
        ]
        + [dma((count,))] * 6
        + [dma((4,)), dma((4,)), dma((7,)), dma((7,)), dma((5,)), dma((2,)), dma((2,))]
        + [
            pltpu.VMEM((w_out.shape[0], width), BF16), pltpu.VMEM(near.shape, BF16),
            pltpu.VMEM(far.shape, BF16), dma((4,)),
        ],
        compiler_params=pltpu.CompilerParams(
            dimension_semantics=("arbitrary",), collective_id=0, has_side_effects=True,
            vmem_limit_bytes=VMEM_LIMIT,
        ),
        cost_estimate=cost(60),
        name="states",
    )(own, decays, cot, near, far, normed, w_gate, w_out, y0, bcs, acum)
    return (
        all_decays, cot_rows.reshape(rows, model), weight_out.reshape(model, width), gate, incoming,
        y, gated, squares,
    )


def body(
    hidden, norm_gain, w_z, w_x, w_bc, w_dt, w_out, conv_x, conv_x_bias, conv_bc, conv_bc_bias,
    dt_bias, a_log, skip_d, gate_gain, cotangent,
):
    batch, tokens, model = hidden.shape
    plan = Plan(batch, tokens)
    core = plan.core
    inner = w_z.shape[1] // 2
    heads = w_dt.shape[1] // 2
    head_size = inner // heads
    units = plan.units
    rows = units * 4 * tokens
    chunks = rows // CHUNK

    def halves(w):
        half = w.shape[1] // 2
        return jnp.where(core == 0, w[:, :half], w[:, half:]), jnp.where(core == 0, w[:, half:], w[:, :half])

    def rows_of_chip(mine, other):
        return jnp.concatenate(plan.by_core(mine, plan.swap(other, df=1)), axis=0)

    vectors = (conv_x_bias, gate_gain, norm_gain, conv_bc_bias, dt_bias, a_log, skip_d)
    if plan.fast:
        hidden_rows, weight_first, cx, cbc, hp, gain_in, gain_rows = plan.head(
            hidden, w_x, w_bc, w_dt, conv_x, conv_bc, *vectors
        )
        gain_in, gain_out = gain_in[0], gain_rows[0]
    else:
        x_mine, x_other = halves(w_x)
        dt_mine, dt_other = halves(w_dt)
        fill = jnp.zeros((w_dt.shape[0], LANES - heads), BF16)
        weight_first = plan.gather(
            rows_of_chip(
                jnp.concatenate([x_mine, w_bc, dt_mine, fill], axis=1),
                jnp.concatenate([x_other, w_bc, dt_other, fill], axis=1),
            )
        )
        hidden_rows, cot_rows = plan.to_units(hidden), plan.to_units(cotangent)

        def whole_of(v):
            return lax.all_gather(v.astype(F32), "fs", axis=0, tiled=True)

        def mine_of(v):
            half = v.shape[0] // 2
            return lax.dynamic_slice_in_dim(v, core * half, half, 0)

        bias_x, gain_out, gain_in, bias_bc, shift, rate_log, skip = (whole_of(v) for v in vectors)
        taps_x, taps_bc = mine_of(whole_of(conv_x)), whole_of(conv_bc)
        bias_x, gain_out, skip, shift, rate_log = (
            mine_of(v) for v in (bias_x, gain_out, skip, shift, rate_log)
        )
        nothing = jnp.zeros((2, inner), F32)
        cx = jnp.concatenate([taps_x.T, bias_x[None], jnp.repeat(skip, head_size)[None], nothing])
        cbc = jnp.concatenate([taps_bc.T, bias_bc[None], jnp.zeros((3, bias_bc.size), F32)])
        pad_heads = (0, LANES - heads)
        hp = jnp.stack([jnp.pad(jnp.exp(rate_log), pad_heads), jnp.pad(shift, pad_heads)])
        hp = jnp.pad(hp, ((0, 6), (0, 0)))
        gain_rows = jnp.broadcast_to(gain_out[None], (8, inner))
        weight_gate = plan.gather(rows_of_chip(*halves(w_z)))
        weight_out = plan.gather(rows_of_chip(*halves(w_out)))
    pick = (jnp.arange(inner)[:, None] // head_size == jnp.arange(LANES)[None, :]).astype(BF16)

    hidden_rows = hidden_rows.astype(F32)
    scale_in = row_scale(hidden_rows)
    unit_in = hidden_rows * scale_in
    normed = (unit_in * gain_in[None]).astype(BF16)
    unit_low = unit_in.astype(BF16)
    normed, unit_low = lax.optimization_barrier((normed, unit_low))

    first = dot(normed, weight_first).astype(BF16)
    def shaped(*shape, dtype=BF16):
        return jax.ShapeDtypeStruct(shape, dtype)

    states = (LANES, inner)
    edge = (units, 16, inner + 2 * LANES)
    in_specs = [
        rows_spec(inner), rows_spec(2 * LANES, inner // (2 * LANES)),
        rows_spec(LANES, (inner + 2 * LANES) // LANES),
    ]
    consts = [whole_spec(cx.shape), whole_spec(cbc.shape), whole_spec(hp.shape)]
    out_specs = [
        rows_spec(inner), chunk_spec(states), unit_spec(states), unit_spec((8, inner)),
        rows_spec(2 * LANES), rows_spec(LANES),
    ]
    out_shape = [
        shaped(rows, inner), shaped(chunks, *states), shaped(units, *states),
        shaped(units, 8, inner, dtype=F32), shaped(rows, 2 * LANES), shaped(rows, LANES, dtype=F32),
    ]
    scratch = [
        pltpu.VMEM((CHUNK + 8, inner), F32), pltpu.VMEM((CHUNK + 8, 2 * LANES), F32),
        pltpu.VMEM(states, F32), pltpu.VMEM((8, LANES), F32),
    ]
    by_unit = first.reshape(units, 4 * tokens, first.shape[1])
    if plan.fast:
        anywhere = pl.BlockSpec(memory_space=pl.ANY)
        dma = pltpu.SemaphoreType.DMA
        y_own, starts, own, decays, shared, reach, halo, near, far, weight_gate = pl.pallas_call(
            scan_forward_kernel,
            grid=(units, PER_UNIT),
            in_specs=in_specs + [anywhere, anywhere, anywhere] + consts,
            out_specs=out_specs + [whole_spec(edge), anywhere, anywhere, anywhere],
            out_shape=out_shape
            + [
                shaped(*edge), shaped(units, tokens, model), shaped(EARLY_UNITS, tokens, model),
                shaped(4, 2, w_z.shape[0], inner),
            ],
            scratch_shapes=scratch
            + [pltpu.VMEM(edge, BF16), dma((1,)), dma((1,)), dma((2,)), dma((2,)), dma((2,)), dma((7,)), dma((7,)), dma((2,))]
            + [pltpu.VMEM((w_z.shape[0], inner), BF16), pltpu.VMEM((units, tokens, model), BF16)],
            compiler_params=pltpu.CompilerParams(
                dimension_semantics=("arbitrary", "arbitrary"), vmem_limit_bytes=VMEM_LIMIT,
                collective_id=1, has_side_effects=True,
            ),
            cost_estimate=cost(31),
            name="scan_forward",
        )(first, first, first, by_unit, cotangent, w_z, cx, cbc, hp)
    else:
        halo = plan.along(by_unit[:, 4 * tokens - 16 :, : inner + 2 * LANES], 1)
        y_own, starts, own, decays, shared, reach = pl.pallas_call(
            forward_kernel,
            grid=(units, PER_UNIT),
            in_specs=in_specs + [whole_spec(edge)] + consts,
            out_specs=out_specs,
            out_shape=out_shape,
            scratch_shapes=scratch,
            compiler_params=params(),
            name="scan_forward",
        )(first, first, first, halo, cx, cbc, hp)

    decay_rows = jnp.concatenate([decays[:, 0], jnp.zeros((8 - units, inner), F32)])
    if plan.fast:
        weight_gate = weight_gate.reshape(model, inner)
        all_decays, cot_rows, weight_out, gate_in, incoming, y, gated, squares = exchange(
            plan, own, decay_rows, cotangent, near, far, normed, weight_gate, w_out, y_own, shared, reach
        )
    else:
        incoming = slow_exchange(plan, own, decay_rows, False)
        gate_in = dot(normed, weight_gate).astype(BF16)
        y, gated, squares = pl.pallas_call(
            gate_kernel,
            grid=(units, PER_UNIT),
            in_specs=[
                rows_spec(inner), rows_spec(inner), rows_spec(2 * LANES), rows_spec(LANES), unit_spec(states),
            ],
            out_specs=[rows_spec(inner), rows_spec(inner), rows_spec(LANES)],
            out_shape=[shaped(rows, inner), shaped(rows, inner), shaped(rows, LANES, dtype=F32)],
            compiler_params=params(),
            name="gate_forward",
        )(y_own, gate_in, shared, reach, incoming)

    def pair_sum(v):
        return v + plan.swap(v, df=1)

    squares = pair_sum(squares[:, 0].reshape(chunks, CHUNK))
    scale_out = lax.rsqrt(squares / (2 * inner) + EPSILON).reshape(rows, 1)
    unit_out = gated.astype(F32) * scale_out
    normed_out = (unit_out * gain_out[None]).astype(BF16)
    g_out = dot_tn(cot_rows, normed_out).astype(BF16)
    projected = plan.cores_sum(dot_nt(normed_out, weight_out).astype(BF16))

    d_normed_out = dot(cot_rows, weight_out).astype(BF16)
    wide = d_normed_out.astype(F32)
    g_gate_gain = jnp.sum(wide * unit_out, axis=0)
    mean = pair_sum(jnp.sum(wide * gain_out[None] * unit_out, axis=1).reshape(chunks, CHUNK))
    mean = (mean / (2 * inner)).reshape(rows, 1)
    stats = jnp.concatenate([scale_out, mean, jnp.zeros((rows, LANES - 2), F32)], axis=1)

    width = inner + 3 * LANES
    back = functools.partial(rows_spec, back=True)
    if plan.fast:
        spots = 2 * chunks + 1
        shard_rows = model // plan.shards
        segments = plan.count
        share = LANES // segments

        def pulls(columns, column=0):
            return pl.BlockSpec((CHUNK, columns), lambda i: (jnp.minimum(i, chunks - 1), column))

        def scan_at(i):
            n = jnp.maximum(i - chunks - 1, 0)
            return n - n % PER_UNIT + PER_UNIT - 1 - n % PER_UNIT

        def scans(columns, column=0):
            return pl.BlockSpec((CHUNK, columns), lambda i: (scan_at(i), column))

        def edges(columns, column=0):
            return pl.BlockSpec((16, columns), lambda i: (jnp.maximum(scan_at(i) * 8 - 1, 0), column))

        def scan_chunk(shape):
            return pl.BlockSpec((1,) + shape, lambda i: (scan_at(i), 0, 0))

        def scan_unit(shape):
            return pl.BlockSpec((1,) + shape, lambda i: (scan_at(i) // PER_UNIT, 0, 0))

        def every(shape):
            return pl.BlockSpec(shape, lambda i: (0,) * len(shape), pipeline_mode=pl.Buffered(1))

        def whole(shape):
            return pl.BlockSpec(shape, lambda i: (0,) * len(shape))

        anywhere = pl.BlockSpec(memory_space=pl.ANY)
        dma = pltpu.SemaphoreType.DMA
        d_all, heads_x, heads_bc, g_x, g_bc, g_heads, d_base, projected, total_out, total_z = pl.pallas_call(
            middle_kernel,
            grid=(spots,),
            in_specs=[
                pulls(inner), pulls(inner), pulls(inner), pulls(inner), pulls(LANES), every((8, inner)),
                pulls(2 * LANES), pulls(LANES), every(all_decays.shape), anywhere, anywhere, anywhere, anywhere,
                scans(inner), edges(inner),
                scans(2 * LANES, inner // (2 * LANES)), edges(2 * LANES, inner // (2 * LANES)),
                scans(LANES, (inner + 2 * LANES) // LANES), every(edge), every(cx.shape), every(cbc.shape), every(hp.shape),
                scans(inner), scan_chunk(states), scan_unit(states), scans(LANES), every(pick.shape),
            ],
            out_specs=[
                scans(width), scan_unit((8, inner)), scan_unit((8, 2 * LANES)),
                whole((40, inner)), whole((40, 2 * LANES)), whole((24, LANES)),
                anywhere, anywhere, anywhere, anywhere,
            ],
            out_shape=[
                shaped(rows, width), shaped(units, 8, inner, dtype=F32), shaped(units, 8, 2 * LANES, dtype=F32),
                shaped(40, inner, dtype=F32), shaped(40, 2 * LANES, dtype=F32), shaped(24, LANES, dtype=F32),
                shaped(rows, model), shaped(batch, tokens, model),
                shaped(shard_rows, 2 * inner), shaped(shard_rows, 2 * inner),
            ],
            scratch_shapes=[
                pltpu.VMEM((rows, inner), BF16), pltpu.VMEM((rows, inner), BF16), pltpu.VMEM(states, F32),
                pltpu.VMEM((units,) + states, BF16), pltpu.VMEM((units,) + states, BF16),
                pltpu.VMEM((segments, units, share, inner), BF16),
                pltpu.VMEM((segments, units, share, inner), BF16),
                pltpu.VMEM((2, rows, 256), BF16), pltpu.VMEM((256, rows), BF16),
                pltpu.VMEM((2, 256, inner), BF16), pltpu.VMEM((2, rows, 256), BF16),
                pltpu.VMEM((model, inner), BF16),
                pltpu.VMEM((model // 4, inner), BF16),
            ]
            + chip_scratch(shard_rows, inner)
            + [pltpu.VMEM((shard_rows, 2 * inner), BF16)]
            + member_scratch(shard_rows, 2 * inner)
            + [
                pltpu.VMEM((2, 2 * shard_rows, inner), BF16), pltpu.VMEM((2 * shard_rows, inner), BF16),
                pltpu.VMEM((shard_rows, inner), BF16), pltpu.VMEM((shard_rows, 2 * inner), BF16),
            ]
            + [
                pltpu.VMEM((CHUNK + 8, inner), F32), pltpu.VMEM((CHUNK + 8, 2 * LANES), F32),
                pltpu.VMEM(states, F32),
                pltpu.VMEM((CHUNK + 8, inner), F32), pltpu.VMEM((CHUNK + 8, 2 * LANES), F32),
                pltpu.VMEM((8, inner), F32),
                dma((8,)), dma((8,)), dma((2,)), dma((2,)), dma((2,)), dma((6,)), dma((2,)), dma((2,)),
                dma((14 * len(HALF_PIECES),)), dma((14 * len(HALF_PIECES),)),
                dma((segments,)), dma((segments,)), dma((segments,)), dma((segments,)),
            ],
            compiler_params=pltpu.CompilerParams(
                dimension_semantics=("arbitrary",), vmem_limit_bytes=MIDDLE_LIMIT,
                collective_id=4, has_side_effects=True,
            ),
            cost_estimate=cost(125),
            name="middle",
        )(
            d_normed_out, gated, gate_in, y, stats, gain_rows, shared, reach, all_decays, normed, weight_gate, g_out,
            projected, first, first, first, first, first, halo, cx, cbc, hp, y, starts, incoming,
            reach, pick,
        )
    else:

        def edges(columns, column=0):
            def place(u, c):
                return (jnp.maximum((u * PER_UNIT + PER_UNIT - 1 - c) * 8 - 1, 0), column)

            return pl.BlockSpec((16, columns), place)

        dy, d_gate, pull = pl.pallas_call(
            pull_kernel,
            grid=(units, PER_UNIT),
            in_specs=[
                rows_spec(inner), rows_spec(inner), rows_spec(inner), rows_spec(inner), rows_spec(LANES),
                whole_spec((8, inner)), rows_spec(2 * LANES), rows_spec(LANES),
            ],
            out_specs=[rows_spec(inner), rows_spec(inner), unit_spec(states)],
            out_shape=[shaped(rows, inner), shaped(rows, inner), shaped(units, *states)],
            scratch_shapes=[pltpu.VMEM(states, F32)],
            compiler_params=params(),
            name="gate_backward",
        )(d_normed_out, gated, gate_in, y, stats, gain_rows, shared, reach)
        after = slow_exchange(plan, pull, decay_rows, True)
        d_all, heads_x, heads_bc, g_x, g_bc, g_heads = pl.pallas_call(
            backward_kernel,
            grid=(units, PER_UNIT),
            in_specs=[
                back(inner), edges(inner),
                back(2 * LANES, inner // (2 * LANES)), edges(2 * LANES, inner // (2 * LANES)),
                back(LANES, (inner + 2 * LANES) // LANES), whole_spec(edge), whole_spec(cx.shape), whole_spec(cbc.shape), whole_spec(hp.shape),
                back(inner), back(inner), chunk_spec(states, True), unit_spec(states), back(LANES),
                unit_spec(states), whole_spec(pick.shape),
            ],
            out_specs=[
                back(width), unit_spec((8, inner)), unit_spec((8, 2 * LANES)),
                whole_spec((40, inner)), whole_spec((40, 2 * LANES)), whole_spec((24, LANES)),
            ],
            out_shape=[
                shaped(rows, width), shaped(units, 8, inner, dtype=F32), shaped(units, 8, 2 * LANES, dtype=F32),
                shaped(40, inner, dtype=F32), shaped(40, 2 * LANES, dtype=F32), shaped(24, LANES, dtype=F32),
            ],
            scratch_shapes=[
                pltpu.VMEM((CHUNK + 8, inner), F32), pltpu.VMEM((CHUNK + 8, 2 * LANES), F32),
                pltpu.VMEM(states, F32),
                pltpu.VMEM((CHUNK + 8, inner), F32), pltpu.VMEM((CHUNK + 8, 2 * LANES), F32),
                pltpu.VMEM((8, inner), F32),
            ],
            compiler_params=params(),
            name="scan_backward",
        )(
            first, first, first, first, first, halo, cx, cbc, hp,
            dy, y, starts, incoming, reach, after, pick,
        )
        projected = plan.to_tokens(projected)

        def over_everything(g):
            g = plan.reduce_chips(g)
            half = g.shape[0] // 2
            low = core == 0
            mine, other = jnp.where(low, g[:half], g[half:]), jnp.where(low, g[half:], g[:half])
            other = plan.swap(other.astype(BF16), df=1).astype(F32)
            return plan.reduce_members(jnp.concatenate(plan.by_core(mine, other), axis=1))

        total_out = over_everything(g_out)
        total_z = over_everything(dot_tn(normed, d_gate).astype(BF16))
    output = (hidden.astype(F32) + projected.astype(F32)).astype(BF16)

    later = plan.along(jnp.concatenate([heads_x, heads_bc], axis=2)[:, :3].astype(BF16), -1).astype(F32)
    taps = jnp.concatenate([cx[:4], cbc[:4]], axis=1)
    extra = jnp.stack(
        [sum(taps[k][None] * later[:, i - k] for k in range(i + 1)) for i in range(3)], axis=1
    )
    tail_rows = d_all.reshape(units, 4 * tokens, width)[:, 4 * tokens - 16 :].astype(F32)
    extra = jnp.pad(extra, ((0, 0), (13, 0), (0, width - extra.shape[2])))
    d_all = d_all.reshape(units, 4 * tokens, width)
    d_all = lax.dynamic_update_slice(d_all, (tail_rows + extra).astype(BF16), (0, 4 * tokens - 16, 0))
    d_all = d_all.reshape(rows, width)

    if plan.fast:
        total_x, total_bc, total_dt, vec, grad_rows, total_z = plan.tail(
            normed, d_all, d_base, weight_first, unit_low, g_x, g_bc, g_heads, g_gate_gain[None], total_z
        )
    else:
        g_first = dot_tn(normed, d_all).astype(BF16)
        d_normed = dot_nt(d_gate, weight_gate) + dot_nt(d_all, weight_first)
        g_norm_gain = jnp.sum(d_normed * unit_in, axis=0)
        total_x, total_bc, total_dt, vec, grad_rows = plan.slow_tail(
            g_first, g_x, g_bc, g_heads, g_gate_gain[None], g_norm_gain[None], d_normed.astype(BF16)
        )
    grad_rows = grad_rows.astype(F32)
    resid = hidden.astype(F32)
    own_scale = row_scale(resid)
    own_unit = resid * own_scale
    dv = grad_rows * gain_in[None, None]
    grad_hidden = cotangent.astype(F32) + own_scale * (
        dv - own_unit * jnp.mean(dv * own_unit, axis=-1, keepdims=True)
    )

    total_dt = jnp.concatenate([total_dt[:, :heads], total_dt[:, LANES : LANES + heads]], axis=1)
    whole_x = jnp.moveaxis(vec[:, :6], 0, 1).reshape(6, 2 * inner)
    whole_heads = jnp.moveaxis(vec[:, 7, : 3 * LANES].reshape(2, 3, LANES)[:, :, :heads], 0, 1)
    whole_heads = whole_heads.reshape(3, 2 * heads)
    whole_norm = vec[0, 6] + vec[1, 6]
    whole_bc = vec[0, 8:13, : 2 * LANES] + vec[1, 8:13, : 2 * LANES]

    def shard(v):
        share = v.shape[-1] // plan.shards
        return lax.dynamic_slice_in_dim(v, plan.f * share, share, v.ndim - 1)

    shard_x, shard_bc, shard_heads = shard(whole_x), shard(whole_bc), shard(whole_heads)
    return (
        output,
        grad_hidden,
        shard(whole_norm),
        total_z.astype(F32),
        total_x,
        total_bc,
        total_dt,
        total_out.astype(F32),
        shard_x[:4].T,
        shard_x[4],
        shard_bc[:4].T,
        shard_bc[4],
        shard_heads[0],
        shard_heads[1],
        shard_heads[2],
        shard_x[5],
    )


def solution(mesh):
    one, two = P("fs"), P("fs", None)
    tokens = P(None, ("fs", "sp"), None)
    return jax.shard_map(
        body,
        mesh=mesh,
        in_specs=(tokens, one, two, two, two, two, two, two, one, two, one, one, one, one, one, tokens),
        out_specs=(tokens, tokens, one, two, two, two, two, two, two, one, two, one, one, one, one, one),
        check_vma=False,
    )
```
